32 devices in a mesh: seq: 8 (over z, x), head: 4 (over y, core).
Axes of the slice: x: 2, y: 2, z: 4, core: 2. Of those that a mesh axis runs over, the one named last changes fastest.
Arguments:
- qkv: bfloat16 [3, 8, 512, 4096], P(None, 'seq', None, 'head'), may hold values from -6 to 6
- out_weight: bfloat16 [4096, 4096], P('head', 'seq'), may hold values from -0.09375 to 0.09375
Outputs:
- layer_out: bfloat16 [512, 8, 4096], P('head', 'seq')
The draws below stay inside these ranges and needn't reach their ends.
All inputs are finite; a program needn't handle non-finite values.
Results may differ from the reference program's by a relative error of at most 0.017.
Values may be sent and summed in bfloat16 or wider, within the bound.
No kernel may reach another device: no remote copies, remote signals or barrier semaphores. Data moves between devices by JAX's collectives and lax.ppermute only.
A program may use at most 128 MiB of HBM per device.

```python
import math
import jax
import jax.numpy as jnp
from jax import lax

HEADS = 32
HEAD = 128
D = 4096
COLS = 512
ROWS = 8


def draw_qkv(key, part):
    shape = (3, ROWS, COLS, HEADS * HEAD)
    keys = jax.random.split(key, 6)
    drawn = jax.random.normal(keys[5], shape, jnp.float32)
    return jnp.clip(drawn, -6.0, 6.0).astype(jnp.bfloat16)


def levels(key, shape, cuts, least, top_value):
    def one(position, shards_of):
        heights = jax.random.uniform(jax.random.fold_in(jax.random.fold_in(key, 6), position), (shards_of,), jnp.float32, least / len(cuts), top_value / len(cuts))
        return jnp.repeat(jnp.exp(heights), shape[position] // shards_of).reshape((-1,) + (1,) * (len(shape) - position - 1))

    level = one(*cuts[0])
    for cut in cuts[1:]:
        level = level * one(*cut)
    return level


def bell_draw(key, extent, deviation, most, cuts=(), kind=jnp.bfloat16):
    array = deviation * jax.random.normal(key, extent, jnp.float32)
    if cuts:
        array = array * levels(key, extent, cuts, -0.22, 0.18)
    return jnp.clip(array, -most, most).astype(kind)


def setup_inputs(seed: int = 0) -> dict:
    splits = jax.random.split(jax.random.key(seed), 3)
    return {
        "qkv": draw_qkv(jax.random.fold_in(splits[2], 71), 0),
        "out_weight": bell_draw(splits[1], (HEADS * HEAD, D), (HEADS * HEAD) ** -0.5, 0.09375, ((0, 4), (1, 8))),
    }


def to_bf16_f32(values):
    return lax.optimization_barrier(values.astype(jnp.bfloat16)).astype(jnp.float32)

def reference(qkv, out_weight):
    scale = 1.0 / math.sqrt(HEAD)
    whole = qkv.reshape(3, ROWS, COLS, HEADS, HEAD)
    zero_row = jnp.zeros((2, 1, COLS, HEADS, HEAD), qkv.dtype)
    keys_ext = jnp.concatenate([zero_row, whole[1:3]], axis=1)
    key_idx = lax.broadcasted_iota(jnp.int32, (COLS, 2 * COLS), 1)
    query_idx = lax.broadcasted_iota(jnp.int32, (COLS, 2 * COLS), 0)

    def one_row(index):
        queries = lax.dynamic_index_in_dim(whole[0], index, 0, keepdims=False).astype(jnp.float32)
        pair = lax.dynamic_slice_in_dim(keys_ext, index, 2, axis=1).reshape(2, 2 * COLS, HEADS, HEAD).astype(jnp.float32)
        scores = jnp.einsum('qhd,khd->hqk', queries, pair[0]) * scale
        allowed = (key_idx < COLS) & (index > 0) | (key_idx >= COLS) & (key_idx - COLS <= query_idx)
        masked = jnp.where(allowed[None], scores, jnp.float32(-1e+30))
        peak = lax.optimization_barrier(jnp.max(masked, axis=-1))
        weights = jnp.where(allowed[None], jnp.exp(masked - peak[..., None]), jnp.float32(0.0))
        total = lax.optimization_barrier(jnp.sum(weights, axis=-1))
        mixed = jnp.einsum('hqk,khd->qhd', to_bf16_f32(weights), pair[1])
        row_out = mixed / jnp.transpose(total)[..., None]
        row_lse = jnp.transpose(peak + jnp.log(total))
        return (row_out, row_lse)
    row_out, row_lse = lax.map(one_row, jnp.arange(ROWS, dtype=jnp.int32))
    r_idx = lax.broadcasted_iota(jnp.int32, (ROWS, ROWS), 0)
    s_idx = lax.broadcasted_iota(jnp.int32, (ROWS, ROWS), 1)
    col_allowed = s_idx <= r_idx - 2

    def one_head(head):
        part = lax.dynamic_index_in_dim(whole, head, 3, keepdims=False).astype(jnp.float32)
        scores = jnp.einsum('rcd,scd->crs', part[0], part[1]) * scale
        masked = jnp.where(col_allowed[None], scores, jnp.float32(-1e+30))
        peak = lax.optimization_barrier(jnp.max(masked, axis=-1))
        weights = jnp.where(col_allowed[None], jnp.exp(masked - peak[..., None]), jnp.float32(0.0))
        total = jnp.maximum(lax.optimization_barrier(jnp.sum(weights, axis=-1)), jnp.float32(1.0))
        mixed = jnp.einsum('crs,scd->rcd', to_bf16_f32(weights), part[2])
        col_out = to_bf16_f32(mixed / jnp.transpose(total)[..., None])
        col_lse = jnp.transpose(peak + jnp.log(total))
        return (col_out, col_lse)
    col_out, col_lse = lax.map(one_head, jnp.arange(HEADS, dtype=jnp.int32))
    col_out = jnp.moveaxis(col_out, 0, 2)
    col_lse = jnp.moveaxis(col_lse, 0, 2)
    top = jnp.maximum(row_lse, col_lse)
    left = jnp.exp(row_lse - top)
    right = jnp.exp(col_lse - top)
    attended = (left[..., None] * row_out + right[..., None] * col_out) / (left + right)[..., None]
    attended = attended.astype(jnp.bfloat16).reshape(ROWS * COLS, HEADS * HEAD)
    projected = jnp.dot(attended, out_weight, preferred_element_type=jnp.float32).astype(jnp.bfloat16)
    return jnp.transpose(projected.reshape(ROWS, COLS, D), (1, 0, 2))
```

```python
import functools
import jax
import jax.numpy as jnp
from jax import lax
from jax.experimental import pallas as pl
from jax.experimental.pallas import tpu as pltpu
from jax.sharding import PartitionSpec as P

HEAD = 128
LOG2E = 1.4426950408889634
NEG = -1e30
QB = 128
VMEM = 48 * 1024 * 1024
F32, BF16 = jnp.float32, jnp.bfloat16


def shifted(shard, axis, by):
    size = lax.axis_size(axis)
    pairs = [(i, i + by) for i in range(size) if 0 <= i + by < size]
    return lax.ppermute(shard, axis, pairs)


def column_part(part):
    queries, keys_part, values = (part[0], part[1], part[2])
    rows = queries.shape[0]
    scale = queries.shape[-1] ** (-0.5)
    scores = (
        jnp.einsum("rchd,schd->chrs", queries, keys_part, preferred_element_type=jnp.float32)
        * scale
    )
    r_idx = lax.broadcasted_iota(jnp.int32, (rows, rows), 0)
    s_idx = lax.broadcasted_iota(jnp.int32, (rows, rows), 1)
    allowed = s_idx <= r_idx - 2
    masked = jnp.where(allowed, scores, jnp.float32(-1e30))
    peak = jnp.max(masked, axis=-1)
    weights = jnp.where(allowed, jnp.exp(masked - peak[..., None]), jnp.float32(0.0))
    total = jnp.maximum(jnp.sum(weights, axis=-1), jnp.float32(1.0))
    rounded = weights.astype(jnp.bfloat16)
    mixed = jnp.einsum("chrs,schd->rchd", rounded, values, preferred_element_type=jnp.float32)
    col_out = (mixed / jnp.transpose(total, (2, 0, 1))[..., None]).astype(jnp.bfloat16)
    col_lse = jnp.transpose(peak + jnp.log(total), (2, 0, 1))
    return (col_out, col_lse)


def row_part(local, previous, first_row):
    rows_dev, cols, heads_local, head_size = (
        local.shape[1],
        local.shape[2],
        local.shape[3],
        local.shape[4],
    )
    scale = head_size ** (-0.5)
    keys_ext = jnp.concatenate([previous, local[1:3]], axis=1)
    key_idx = lax.broadcasted_iota(jnp.int32, (cols, 2 * cols), 1)
    query_idx = lax.broadcasted_iota(jnp.int32, (cols, 2 * cols), 0)

    def one_row(index):
        queries = lax.dynamic_index_in_dim(local[0], index, 0, keepdims=False)
        pair = keys_ext.reshape(2, 2 * cols, heads_local, head_size)
        scores = (
            jnp.einsum("qhd,khd->hqk", queries, pair[0], preferred_element_type=jnp.float32) * scale
        )
        allowed = (key_idx < cols) & (first_row + index > 0) | (key_idx >= cols) & (
            key_idx - cols <= query_idx
        )
        masked = jnp.where(allowed[None], scores, jnp.float32(-1e30))
        peak = jnp.max(masked, axis=-1)
        weights = jnp.where(allowed[None], jnp.exp(masked - peak[..., None]), jnp.float32(0.0))
        total = jnp.sum(weights, axis=-1)
        rounded = weights.astype(jnp.bfloat16)
        mixed = jnp.einsum("hqk,khd->qhd", rounded, pair[1], preferred_element_type=jnp.float32)
        return (mixed / jnp.transpose(total)[..., None], jnp.transpose(peak + jnp.log(total)))

    return lax.map(one_row, jnp.arange(rows_dev, dtype=jnp.int32))


def body_any(qkv, out_weight):
    rows_dev, cols, features = (qkv.shape[1], qkv.shape[2], qkv.shape[3])
    head_size = HEAD
    heads_local = features // head_size
    local = qkv.reshape(3, rows_dev, cols, heads_local, head_size)
    previous = shifted(local[1:3, rows_dev - 1 : rows_dev], "seq", 1)
    first_row = lax.axis_index("seq") * rows_dev
    row_out, row_lse = row_part(local, previous, first_row)
    columns = lax.all_to_all(local, "seq", split_axis=2, concat_axis=1, tiled=True)
    col_part_out, col_part_lse = column_part(columns)
    col_out, col_lse = (
        lax.all_to_all(col_part_out, "seq", split_axis=0, concat_axis=1, tiled=True),
        lax.all_to_all(
            col_part_lse.astype(jnp.bfloat16), "seq", split_axis=0, concat_axis=1, tiled=True
        ).astype(col_part_lse.dtype),
    )
    top = jnp.maximum(row_lse, col_lse)
    left = jnp.exp(row_lse - top)
    right = jnp.exp(col_lse - top)
    attended = (left[..., None] * row_out + right[..., None] * col_out.astype(jnp.float32)) / (
        left + right
    )[..., None]
    attended = attended.astype(jnp.bfloat16).reshape(rows_dev, cols, features)
    terms = jnp.einsum(
        "rcf,fd->crd",
        attended,
        lax.all_gather(out_weight, "seq", axis=1, tiled=True),
        preferred_element_type=jnp.float32,
    )
    summed = lax.psum_scatter(terms.astype(jnp.bfloat16), "head", scatter_dimension=0, tiled=True)
    return summed


def dense_scores(q, k):
    return lax.dot_general(q, k, (((1,), (1,)), ((), ())), preferred_element_type=F32)


def col_scores(q, k):
    prod = q.astype(F32) * k.astype(F32)
    high = prod.astype(BF16)
    low = (prod - high.astype(F32)).astype(BF16)
    ones = jnp.ones((2 * HEAD, HEAD), BF16)
    return jnp.dot(jnp.concatenate([high, low], axis=1), ones, preferred_element_type=F32)


def attend(q, dense, cols, coef):
    rows = q.shape[0]
    scores = []
    for k, _, offset in dense:
        s = dense_scores(q, k)
        if offset is not None:
            q_idx = lax.broadcasted_iota(jnp.int32, s.shape, 0) + offset
            k_idx = lax.broadcasted_iota(jnp.int32, s.shape, 1)
            s = jnp.where(k_idx <= q_idx, s, NEG)
        scores.append(s)
    singles = []
    for k, _, allowed in cols:
        c = col_scores(q, k)
        singles.append(c if allowed is None else jnp.where(allowed, c, NEG))
    peak = None
    for s in scores:
        m = jnp.broadcast_to(jnp.max(s, axis=1, keepdims=True), (rows, HEAD))
        peak = m if peak is None else jnp.maximum(peak, m)
    for c in singles:
        peak = c if peak is None else jnp.maximum(peak, c)
    total = jnp.zeros((rows, HEAD), F32)
    out = jnp.zeros((rows, HEAD), F32)
    for s, (_, v, _) in zip(scores, dense):
        p = jnp.exp2((s - peak[:, :1]) * coef)
        total = total + jnp.broadcast_to(jnp.sum(p, axis=1, keepdims=True), (rows, HEAD))
        out = out + jnp.dot(p.astype(BF16), v, preferred_element_type=F32)
    for c, (_, v, _) in zip(singles, cols):
        w = jnp.exp2((c - peak) * coef)
        total = total + w
        out = out + w * v.astype(F32)
    return out / total, peak * coef + jnp.log2(total)


def pack_lse(even, odd):
    lane = lax.broadcasted_iota(jnp.int32, even.shape, 1)
    return jnp.transpose(jnp.where(lane == 0, even, odd))[:8]


def unpack_lse(packed):
    cols = jnp.transpose(packed)
    rows = cols.shape[0]
    return [jnp.broadcast_to(cols[:, i : i + 1], (rows, HEAD)) for i in range(2)]


def own_kernel(coef, cols, at, keep, oq, okv, low_m, low_o, out, lse):
    x, z = at[0], at[1]
    first = x == 0

    def pair(a, b):
        return jnp.where(first, a, b), jnp.where(first, b, a)

    q_e, q_o = pair(keep[0], oq[...])
    k_e, k_o = pair(keep[1], okv[0])
    v_e, v_o = pair(keep[2], okv[1])
    lk_e, lk_o = pair(low_m[0], low_o[0])
    lv_e, lv_o = pair(low_m[1], low_o[1])
    below = z == 1
    lses = []
    for part in range(cols // QB):
        a, b = part * QB, (part + 1) * QB
        mine = slice(a, b)
        col_e = (lk_e[mine], lv_e[mine], below)
        col_o = (lk_o[mine], lv_o[mine], below)
        q1, q2 = q_e[mine], q_o[mine]

        def even(dense, singles):
            return attend(q1, [(k_e[:b], v_e[:b], a)] + dense, singles, coef)

        o1, l1 = even([], [])
        o2, l2 = attend(q2, [(k_o[:b], v_o[:b], a), (k_e, v_e, None)], [col_e, col_o], coef)
        ob, lb = attend(q1, [(lk_o, lv_o, None)], [col_e], coef)
        lb = jnp.where(below, lb, NEG)
        top = jnp.maximum(l1, lb)
        w1, wb = jnp.exp2(l1 - top), jnp.exp2(lb - top)
        out[0, mine] = (w1 * o1 + wb * ob) / (w1 + wb)
        out[1, mine] = o2
        lses.append(pack_lse(top + jnp.log2(w1 + wb), l2))
    lse[0] = jnp.concatenate(lses, axis=1)


def upper_kernel(coef, cols, at, keep, okv, low_m, low_o, qa_m, qa_o, qb_m, qb_o, out_a, lse_a, out_b, lse_b):
    x, z = at[0], at[1]
    first = x == 0

    def pair(a, b):
        return jnp.where(first, a, b), jnp.where(first, b, a)

    k_e, k_o = pair(keep[0], okv[0])
    v_e, v_o = pair(keep[1], okv[1])
    lk_e, lk_o = pair(low_m[0], low_o[0])
    lv_e, lv_o = pair(low_m[1], low_o[1])
    below = z == 1
    a_e, a_o = pair(qa_m[...], qa_o[...])
    b_e, b_o = pair(qb_m[...], qb_o[...])
    la, lb = [], []
    for part in range(cols // QB):
        mine = slice(part * QB, (part + 1) * QB)
        ce, co = (k_e[mine], v_e[mine], None), (k_o[mine], v_o[mine], None)
        le, lo = (lk_e[mine], lv_e[mine], below), (lk_o[mine], lv_o[mine], below)
        o1, l1 = attend(a_e[mine], [(k_o, v_o, None)], [ce, le, lo], coef)
        o2, l2 = attend(a_o[mine], [], [ce, co, le, lo], coef)
        out_a[0, mine] = o1.astype(BF16)
        out_a[1, mine] = o2.astype(BF16)
        la.append(pack_lse(l1, l2))
        o1, l1 = attend(b_e[mine], [], [ce, co, le, lo], coef)
        o2, l2 = attend(b_o[mine], [], [ce, co, le, lo], coef)
        out_b[0, mine] = o1.astype(BF16)
        out_b[1, mine] = o2.astype(BF16)
        lb.append(pack_lse(l1, l2))
    lse_a[0] = jnp.concatenate(la, axis=1)
    lse_b[0] = jnp.concatenate(lb, axis=1)


def merge_kernel(at, own, own_lse, oa, la, ob, lb, out):
    z = at[1]
    ls, lsa, lsb = unpack_lse(own_lse[0]), unpack_lse(la[0]), unpack_lse(lb[0])
    for row in range(2):
        l0 = ls[row]
        l1 = jnp.where(z >= 2, lsa[row], NEG)
        l2 = jnp.where(z >= 3, lsb[row], NEG)
        top = jnp.maximum(l0, jnp.maximum(l1, l2))
        w0, w1, w2 = jnp.exp2(l0 - top), jnp.exp2(l1 - top), jnp.exp2(l2 - top)
        mixed = w0 * own[row] + w1 * oa[row].astype(F32) + w2 * ob[row].astype(F32)
        out[row] = (mixed / (w0 + w1 + w2)).astype(BF16)


def head_call(kernel, at, args, outs, cols, heads, name):
    def spec(shape, packed):
        if packed:
            return pl.BlockSpec((1,) + shape[1:], lambda h, at: (h, 0, 0))
        lead = len(shape) - 1
        return pl.BlockSpec(shape[:-1] + (HEAD,), lambda h, at: (0,) * lead + (h,))

    def packed(shape):
        return tuple(shape) == (heads, 8, cols)

    return pl.pallas_call(
        kernel,
        out_shape=outs,
        grid_spec=pltpu.PrefetchScalarGridSpec(
            num_scalar_prefetch=1,
            grid=(heads,),
            in_specs=[spec(a.shape, packed(a.shape)) for a in args],
            out_specs=[spec(o.shape, packed(o.shape)) for o in outs],
        ),
        compiler_params=pltpu.CompilerParams(vmem_limit_bytes=VMEM),
        name=name,
    )(at, *args)


def project_kernel(at, a_own, a_other, *refs):
    x, core = at[0], at[2]
    slots = (len(refs) - 2)
    weights, send, keep = refs[:slots], refs[slots], refs[slots + 1]
    half = a_own.shape[-1]
    tokens = a_own.shape[3]
    near = pl.ds(pl.multiple_of(x * half, half), half)
    far = pl.ds(pl.multiple_of((1 - x) * half, half), half)
    for who, out in ((1 - core, send), (core, keep)):
        left = jnp.concatenate([a_own[r, y, who] for r in range(2) for y in range(2)], axis=0)
        right = jnp.concatenate([a_other[r, y, who] for r in range(2) for y in range(2)], axis=0)
        for s, w in enumerate(weights):
            c = jnp.dot(left, w[near], preferred_element_type=F32)
            c = c + jnp.dot(right, w[far], preferred_element_type=F32)
            c = c.astype(BF16).reshape(2, 2, tokens, w.shape[1])
            for y in range(2):
                for r in range(2):
                    out[s, y, r] = c[r, y]


def project(at, a_own, a_other, weights):
    cols = a_own.shape[1]
    shape = (2, 2, 2, cols // 4, a_own.shape[2])
    outs = [jax.ShapeDtypeStruct((len(weights), 2, 2, cols // 4, weights[0].shape[1]), BF16)] * 2
    return pl.pallas_call(
        project_kernel,
        out_shape=outs,
        in_specs=[pl.BlockSpec(memory_space=pltpu.SMEM)]
        + [pl.BlockSpec(memory_space=pltpu.VMEM)] * (2 + len(weights)),
        out_specs=[pl.BlockSpec(memory_space=pltpu.VMEM)] * 2,
        compiler_params=pltpu.CompilerParams(vmem_limit_bytes=VMEM),
        name="project",
    )(at, a_own.reshape(shape), a_other.reshape(shape), *weights)


def place_kernel(order, near, out):
    out[...] = near[0, 0]


def place(order, blocks):
    _, _, tokens, width = blocks.shape
    return pl.pallas_call(
        place_kernel,
        out_shape=jax.ShapeDtypeStruct((tokens, 8 * width), BF16),
        grid_spec=pltpu.PrefetchScalarGridSpec(
            num_scalar_prefetch=1,
            grid=(8,),
            in_specs=[pl.BlockSpec((1, 1, tokens, width), lambda i, o: (o[i] // 2, o[i] % 2, 0, 0))],
            out_specs=pl.BlockSpec((tokens, width), lambda i, o: (0, i)),
        ),
        name="place",
    )(order, blocks)


def added(a, b):
    return (a.astype(F32) + b.astype(F32)).astype(BF16)


def body_eight(qkv, out_weight):
    _, _, cols, features = qkv.shape
    half = features // 2
    heads = half // HEAD
    coef = HEAD ** (-0.5) * LOG2E
    me = lax.axis_index("seq")
    who = lax.axis_index("head")
    z, x, core, y = me // 2, me % 2, who % 2, who // 2
    at = jnp.stack([x, z, core]).astype(jnp.int32)
    local = qkv.reshape(3, cols, features)
    keep = lax.dynamic_slice_in_dim(local, x * half, half, axis=2)
    give = lax.dynamic_slice_in_dim(local, (1 - x) * half, half, axis=2)

    def seq_perm(array, layers, cross):
        pairs = [(2 * a + i, 2 * b + (1 - i if cross else i)) for a, b in layers for i in range(2)]
        return lax.ppermute(array, "seq", pairs)

    def head_perm(array, flip):
        return lax.ppermute(array, "head", [(i, i ^ flip) for i in range(4)])

    here = [(i, i) for i in range(4)]
    one_down, two_down = [(2, 1), (3, 2)], [(3, 1)]
    one_up, two_up = [(1, 2), (2, 3)], [(1, 3)]

    qa_m, qa_o = seq_perm(keep[0], one_down, False), seq_perm(give[0], one_down, True)
    qb_m, qb_o = seq_perm(keep[0], two_down, False), seq_perm(give[0], two_down, True)
    okv = seq_perm(give[1:], here, True)
    low_m, low_o = seq_perm(keep[1:], [(0, 1)], False), seq_perm(give[1:], [(0, 1)], True)
    oq = seq_perm(give[0], here, True)
    w_up = seq_perm(out_weight, [(0, 2), (1, 3)], False)

    struct = jax.ShapeDtypeStruct
    own, own_lse = head_call(
        functools.partial(own_kernel, coef, cols), at, [keep, oq, okv, low_m, low_o],
        [struct((2, cols, half), F32), struct((heads, 8, cols), F32)], cols, heads, "own_rows")
    oa, la, ob, lb = head_call(
        functools.partial(upper_kernel, coef, cols), at,
        [keep[1:], okv, low_m, low_o, qa_m, qa_o, qb_m, qb_o],
        [struct((2, cols, half), BF16), struct((heads, 8, cols), F32)] * 2, cols, heads, "upper_rows")
    la, lb = seq_perm(la, one_up, False), seq_perm(lb, two_up, False)
    oa, ob = seq_perm(oa, one_up, False), seq_perm(ob, two_up, False)
    weight, _ = lax.optimization_barrier((out_weight, (qa_m, qb_m)))
    w_down = seq_perm(weight, [(2, 0), (3, 1)], False)
    w2 = jnp.where(z >= 2, w_up, w_down)
    w1 = seq_perm(out_weight, [(0, 1), (1, 0), (2, 3), (3, 2)], False)
    w3 = seq_perm(w2, [(0, 1), (1, 0), (2, 3), (3, 2)], False)

    (a_own,) = head_call(
        merge_kernel, at, [own, own_lse, oa, la, ob, lb], [struct((2, cols, half), BF16)], cols, heads, "merge")
    a_other = seq_perm(a_own, here, True)

    mine, theirs = [], []
    for weights in ([out_weight, w2], [w1, w3]):
        send, kept = project(at, a_own, a_other, weights)
        part = added(kept, head_perm(send, 1))
        to_y = lax.dynamic_index_in_dim(part, 1 - y, 1, keepdims=False)
        stay = lax.dynamic_index_in_dim(part, y, 1, keepdims=False)
        done = added(stay, head_perm(to_y, 2))
        to_x = lax.dynamic_index_in_dim(done, 1 - x, 1, keepdims=False)
        mine.append(lax.dynamic_index_in_dim(done, x, 1, keepdims=False))
        theirs.append(seq_perm(to_x, here, True))
    blocks = jnp.stack([jnp.concatenate(mine), jnp.concatenate(theirs)], axis=1)
    slot_of = jnp.array([0, 2, 1, 3], jnp.int32)
    index = jnp.arange(8, dtype=jnp.int32)
    order = slot_of[jnp.bitwise_xor(index // 2, z)] * 2 + jnp.bitwise_xor(index % 2, x)
    return place(order.astype(jnp.int32), blocks).reshape(cols // 4, 1, 8 * out_weight.shape[1])


def solution(mesh):
    in_specs = (P(None, "seq", None, "head"), P("head", "seq"))
    out_specs = P("head", "seq", None)
    small = mesh.shape["seq"] == 8 and mesh.shape["head"] == 4

    def body(qkv, out_weight):
        if small and qkv.shape[1] == 1:
            return body_eight(qkv, out_weight)
        return body_any(qkv, out_weight)

    return jax.shard_map(body, mesh=mesh, in_specs=in_specs, out_specs=out_specs, check_vma=False)
```

```python
import functools
import jax
import jax.numpy as jnp
from jax import lax
from jax.experimental import pallas as pl
from jax.experimental.pallas import tpu as pltpu
from jax.sharding import PartitionSpec as P

HEAD = 128
LOG2E = 1.4426950408889634
NEG = -1e30
QB = 128
VMEM = 48 * 1024 * 1024
F32, BF16 = jnp.float32, jnp.bfloat16


def shifted(shard, axis, by):
    size = lax.axis_size(axis)
    pairs = [(i, i + by) for i in range(size) if 0 <= i + by < size]
    return lax.ppermute(shard, axis, pairs)


def column_part(part):
    queries, keys_part, values = (part[0], part[1], part[2])
    rows = queries.shape[0]
    scale = queries.shape[-1] ** (-0.5)
    scores = (
        jnp.einsum("rchd,schd->chrs", queries, keys_part, preferred_element_type=jnp.float32)
        * scale
    )
    r_idx = lax.broadcasted_iota(jnp.int32, (rows, rows), 0)
    s_idx = lax.broadcasted_iota(jnp.int32, (rows, rows), 1)
    allowed = s_idx <= r_idx - 2
    masked = jnp.where(allowed, scores, jnp.float32(-1e30))
    peak = jnp.max(masked, axis=-1)
    weights = jnp.where(allowed, jnp.exp(masked - peak[..., None]), jnp.float32(0.0))
    total = jnp.maximum(jnp.sum(weights, axis=-1), jnp.float32(1.0))
    rounded = weights.astype(jnp.bfloat16)
    mixed = jnp.einsum("chrs,schd->rchd", rounded, values, preferred_element_type=jnp.float32)
    col_out = (mixed / jnp.transpose(total, (2, 0, 1))[..., None]).astype(jnp.bfloat16)
    col_lse = jnp.transpose(peak + jnp.log(total), (2, 0, 1))
    return (col_out, col_lse)


def row_part(local, previous, first_row):
    rows_dev, cols, heads_local, head_size = (
        local.shape[1],
        local.shape[2],
        local.shape[3],
        local.shape[4],
    )
    scale = head_size ** (-0.5)
    keys_ext = jnp.concatenate([previous, local[1:3]], axis=1)
    key_idx = lax.broadcasted_iota(jnp.int32, (cols, 2 * cols), 1)
    query_idx = lax.broadcasted_iota(jnp.int32, (cols, 2 * cols), 0)

    def one_row(index):
        queries = lax.dynamic_index_in_dim(local[0], index, 0, keepdims=False)
        pair = keys_ext.reshape(2, 2 * cols, heads_local, head_size)
        scores = (
            jnp.einsum("qhd,khd->hqk", queries, pair[0], preferred_element_type=jnp.float32) * scale
        )
        allowed = (key_idx < cols) & (first_row + index > 0) | (key_idx >= cols) & (
            key_idx - cols <= query_idx
        )
        masked = jnp.where(allowed[None], scores, jnp.float32(-1e30))
        peak = jnp.max(masked, axis=-1)
        weights = jnp.where(allowed[None], jnp.exp(masked - peak[..., None]), jnp.float32(0.0))
        total = jnp.sum(weights, axis=-1)
        rounded = weights.astype(jnp.bfloat16)
        mixed = jnp.einsum("hqk,khd->qhd", rounded, pair[1], preferred_element_type=jnp.float32)
        return (mixed / jnp.transpose(total)[..., None], jnp.transpose(peak + jnp.log(total)))

    return lax.map(one_row, jnp.arange(rows_dev, dtype=jnp.int32))


def body_any(qkv, out_weight):
    rows_dev, cols, features = (qkv.shape[1], qkv.shape[2], qkv.shape[3])
    head_size = HEAD
    heads_local = features // head_size
    local = qkv.reshape(3, rows_dev, cols, heads_local, head_size)
    previous = shifted(local[1:3, rows_dev - 1 : rows_dev], "seq", 1)
    first_row = lax.axis_index("seq") * rows_dev
    row_out, row_lse = row_part(local, previous, first_row)
    columns = lax.all_to_all(local, "seq", split_axis=2, concat_axis=1, tiled=True)
    col_part_out, col_part_lse = column_part(columns)
    col_out, col_lse = (
        lax.all_to_all(col_part_out, "seq", split_axis=0, concat_axis=1, tiled=True),
        lax.all_to_all(
            col_part_lse.astype(jnp.bfloat16), "seq", split_axis=0, concat_axis=1, tiled=True
        ).astype(col_part_lse.dtype),
    )
    top = jnp.maximum(row_lse, col_lse)
    left = jnp.exp(row_lse - top)
    right = jnp.exp(col_lse - top)
    attended = (left[..., None] * row_out + right[..., None] * col_out.astype(jnp.float32)) / (
        left + right
    )[..., None]
    attended = attended.astype(jnp.bfloat16).reshape(rows_dev, cols, features)
    terms = jnp.einsum(
        "rcf,fd->crd",
        attended,
        lax.all_gather(out_weight, "seq", axis=1, tiled=True),
        preferred_element_type=jnp.float32,
    )
    summed = lax.psum_scatter(terms.astype(jnp.bfloat16), "head", scatter_dimension=0, tiled=True)
    return summed


def dense_scores(q, k):
    return lax.dot_general(q, k, (((1,), (1,)), ((), ())), preferred_element_type=F32)


def col_scores(q, k):
    prod = q * k
    high = prod.astype(BF16)
    low = (prod - high.astype(F32)).astype(BF16)
    ones = jnp.ones((2 * HEAD, HEAD), BF16)
    return jnp.dot(jnp.concatenate([high, low], axis=1), ones, preferred_element_type=F32)


def with_ones(v):
    return jnp.concatenate([v, jnp.ones_like(v)], axis=1)


def attend(q, dense, cols, coef):
    rows = q.shape[0]
    scores = []
    for k, _, allowed in dense:
        s = dense_scores(q, k)
        scores.append(s if allowed is None else jnp.where(allowed, s, NEG))
    singles = []
    if cols:
        wide = q.astype(F32)
    for k, _, allowed in cols:
        c = col_scores(wide, k)
        singles.append(c if allowed is None else jnp.where(allowed, c, NEG))
    peak = None
    for s in scores:
        for j in range(s.shape[1] // HEAD):
            part = s[:, j * HEAD : (j + 1) * HEAD]
            peak = part if peak is None else jnp.maximum(peak, part)
    if peak is not None:
        peak = jnp.broadcast_to(jnp.max(peak, axis=1, keepdims=True), (rows, HEAD))
    for c in singles:
        peak = c if peak is None else jnp.maximum(peak, c)
    peak = peak * coef
    both = None
    for s, (_, v, _) in zip(scores, dense):
        tiled = jnp.concatenate([peak] * (s.shape[1] // HEAD), axis=1)
        p = jnp.exp2(s * coef - tiled).astype(BF16)
        term = jnp.dot(p, v, preferred_element_type=F32)
        both = term if both is None else both + term
    out = None if both is None else both[:, :HEAD]
    total = None if both is None else both[:, HEAD:]
    for c, (_, v, _) in zip(singles, cols):
        w = jnp.exp2(c * coef - peak)
        total = w if total is None else total + w
        out = w * v if out is None else out + w * v
    return out / total, peak + jnp.log2(total)


def lse_rows(even, odd):
    lane = lax.broadcasted_iota(jnp.int32, (HEAD, HEAD), 1)
    evens, odds = [], []
    for t in range(even.shape[0] // HEAD):
        block = slice(t * HEAD, (t + 1) * HEAD)
        turned = jnp.transpose(jnp.where(lane == 0, even[block], odd[block]))
        evens.append(turned[0:1])
        odds.append(turned[1:2])
    return evens, odds


def put_lse(ref, base, evens, odds):
    rows = jnp.concatenate(evens + odds, axis=0)
    pad = (-rows.shape[0]) % 16
    if pad:
        rows = jnp.concatenate([rows, jnp.zeros((pad, HEAD), F32)], axis=0)
    count = rows.shape[0]
    for piece in range(3):
        part = rows.astype(BF16)
        ref[pl.ds(base + piece * count, count), :] = part
        rows = rows - part.astype(F32)


def get_lse(ref, base, cols):
    blocks = cols // HEAD
    count = -(-2 * blocks // 16) * 16
    rows = sum(ref[pl.ds(base + piece * count, count), :].astype(F32) for piece in range(3))
    turned = [
        jnp.transpose(jnp.broadcast_to(rows[t : t + 1], (HEAD, HEAD))) for t in range(2 * blocks)
    ]
    return jnp.concatenate(turned[:blocks], axis=0), jnp.concatenate(turned[blocks:], axis=0)


def lse_height(cols):
    return 3 * (-(-2 * (cols // HEAD) // 16) * 16)


def own_kernel(coef, cols, at, q, kv_m, kv_o, low_m, low_o, out):
    x, z = at[0], at[1]
    below = z == 1
    block = 256
    tri = lax.broadcasted_iota(jnp.int32, (block, block), 1) <= lax.broadcasted_iota(
        jnp.int32, (block, block), 0
    )
    first = x == 0
    k_e, k_o = jnp.where(first, kv_m[0], kv_o[0]), jnp.where(first, kv_o[0], kv_m[0])
    v_e, v_o = jnp.where(first, kv_m[1], kv_o[1]), jnp.where(first, kv_o[1], kv_m[1])
    v_e, v_o = with_ones(v_e), with_ones(v_o)
    lk_e = jnp.where(first, low_m[0], low_o[0])
    lk_o = jnp.where(first, low_o[0], low_m[0])
    lv_e = jnp.where(first, low_m[1], low_o[1])
    lv_o = jnp.where(first, low_o[1], low_m[1])
    lv_o1 = with_ones(lv_o)
    evens, odds = [], []
    for part in range(cols // block):
        a, b = part * block, (part + 1) * block
        mine = slice(a, b)
        col_e = (lk_e[mine].astype(F32), lv_e[mine].astype(F32), below)
        col_o = (lk_o[mine].astype(F32), lv_o[mine].astype(F32), below)

        def causal(k, v):
            blocks = [(k[a:b], v[a:b], tri)]
            return blocks if part == 0 else [(k[:a], v[:a], None)] + blocks

        o1, l1 = attend(q[0, mine], causal(k_e, v_e) + [(lk_o, lv_o1, below)], [col_e], coef)
        o2, l2 = attend(q[1, mine], causal(k_o, v_o) + [(k_e, v_e, None)], [col_e, col_o], coef)
        out[mine] = o1.astype(BF16)
        out[cols + a : cols + b] = o2.astype(BF16)
        e, o = lse_rows(l1, l2)
        evens, odds = evens + e, odds + o
    put_lse(out, 2 * cols, evens, odds)


def upper_kernel(coef, cols, at, qa, qb, kv_m, kv_o, low_m, low_o, out_a, out_b):
    x, z = at[0], at[1]
    below = z == 1
    first = x == 0
    block = 256
    k_e, k_o = jnp.where(first, kv_m[0], kv_o[0]), jnp.where(first, kv_o[0], kv_m[0])
    v_e, v_o = jnp.where(first, kv_m[1], kv_o[1]), jnp.where(first, kv_o[1], kv_m[1])
    v_o1 = with_ones(v_o)
    rows_a, rows_b = ([], []), ([], [])
    for part in range(cols // block):
        a, b = part * block, (part + 1) * block
        mine = slice(a, b)
        m_k, m_v = low_m[0, mine].astype(F32), low_m[1, mine].astype(F32)
        o_k, o_v = low_o[0, mine].astype(F32), low_o[1, mine].astype(F32)
        ce = (k_e[mine].astype(F32), v_e[mine].astype(F32), None)
        co = (k_o[mine].astype(F32), v_o[mine].astype(F32), None)
        low = [(m_k, m_v, below), (o_k, o_v, below)]
        for q, out, rows, dense, singles in (
            (qa, out_a, rows_a, [(k_o, v_o1, None)], [ce]),
            (qb, out_b, rows_b, [], [ce, co]),
        ):
            o1, l1 = attend(q[0, mine], dense, singles + low, coef)
            o2, l2 = attend(q[1, mine], [], [ce, co] + low, coef)
            out[mine] = o1.astype(BF16)
            out[cols + a : cols + b] = o2.astype(BF16)
            e, o = lse_rows(l1, l2)
            rows[0].extend(e)
            rows[1].extend(o)
    put_lse(out_a, 2 * cols, *rows_a)
    put_lse(out_b, 2 * cols, *rows_b)


def merge_kernel(cols, at, own, oa, ob, out):
    z = at[1]
    own_l, a_l, b_l = (get_lse(ref, 2 * cols, cols) for ref in (own, oa, ob))
    for row in range(2):
        tokens = slice(row * cols, (row + 1) * cols)
        l0 = own_l[row]
        l1 = jnp.where(z >= 2, a_l[row], NEG)
        l2 = jnp.where(z >= 3, b_l[row], NEG)
        top = jnp.maximum(l0, jnp.maximum(l1, l2))
        w0, w1, w2 = jnp.exp2(l0 - top), jnp.exp2(l1 - top), jnp.exp2(l2 - top)
        mixed = w0 * own[tokens].astype(F32) + w1 * oa[tokens].astype(F32) + w2 * ob[tokens].astype(F32)
        out[row] = (mixed / (w0 + w1 + w2)).astype(BF16)


def cost(us):
    return pl.CostEstimate(flops=int(us * 1.1e9), bytes_accessed=int(us * 1e6), transcendentals=0)


def head_call(kernel, at, args, outs, heads, name, us):
    def spec(shape):
        lead = len(shape) - 1
        return pl.BlockSpec(tuple(shape[:-1]) + (HEAD,), lambda h, at: (0,) * lead + (h,))

    return pl.pallas_call(
        kernel,
        out_shape=outs,
        grid_spec=pltpu.PrefetchScalarGridSpec(
            num_scalar_prefetch=1,
            grid=(heads,),
            in_specs=[spec(a.shape) for a in args],
            out_specs=[spec(o.shape) for o in outs],
        ),
        compiler_params=pltpu.CompilerParams(vmem_limit_bytes=VMEM),
        cost_estimate=cost(us),
        name=name,
    )(at, *args)


def project_kernel(chunks, at, *refs):
    x, core = at[0], at[2]
    near, far = refs[:chunks], refs[chunks : 2 * chunks]
    weights, send, keep = refs[2 * chunks : -2], refs[-2], refs[-1]
    width = near[0].shape[-1]
    tokens = near[0].shape[3]
    half = width * chunks
    for who, out in ((1 - core, send), (core, keep)):

        def rows(ref):
            return jnp.concatenate([ref[r, y, who] for y in range(2) for r in range(2)], axis=0)

        left = jnp.concatenate([rows(ref) for ref in near], axis=1)
        right = jnp.concatenate([rows(ref) for ref in far], axis=1)
        for s, w in enumerate(weights):
            c = jnp.dot(left, w[pl.ds(pl.multiple_of(x * half, half), half)], preferred_element_type=F32)
            c = c + jnp.dot(right, w[pl.ds(pl.multiple_of((1 - x) * half, half), half)], preferred_element_type=F32)
            out[s] = c.astype(BF16).reshape(2, 2, tokens, w.shape[1])


def project(at, near, far, weights):
    _, cols, width = near[0].shape
    shape = (2, 2, 2, cols // 4, width)
    outs = [jax.ShapeDtypeStruct((len(weights), 2, 2, cols // 4, weights[0].shape[1]), BF16)] * 2
    args = [a.reshape(shape) for a in near + far] + weights
    return pl.pallas_call(
        functools.partial(project_kernel, len(near)),
        out_shape=outs,
        in_specs=[pl.BlockSpec(memory_space=pltpu.SMEM)] + [pl.BlockSpec(memory_space=pltpu.VMEM)] * len(args),
        out_specs=[pl.BlockSpec(memory_space=pltpu.VMEM)] * 2,
        compiler_params=pltpu.CompilerParams(vmem_limit_bytes=VMEM),
        cost_estimate=cost(4),
        name="project",
    )(at, *args)


def place_kernel(at, layer, *refs):
    x, out = at[0], refs[-1]
    slot = 0
    for mine, theirs in zip(refs[:-1:2], refs[1:-1:2]):
        width = mine.shape[-1]
        for s in range(mine.shape[0]):
            base = layer[slot] * 2
            out[:, pl.ds(pl.multiple_of((base + x) * width, width), width)] = mine[s]
            out[:, pl.ds(pl.multiple_of((base + 1 - x) * width, width), width)] = theirs[s]
            slot += 1


def place(at, layer, parts):
    _, tokens, width = parts[0].shape
    total = sum(p.shape[0] for p in parts)
    return pl.pallas_call(
        place_kernel,
        out_shape=jax.ShapeDtypeStruct((tokens, total * width), BF16),
        in_specs=[pl.BlockSpec(memory_space=pltpu.SMEM)] * 2 + [pl.BlockSpec(memory_space=pltpu.VMEM)] * len(parts),
        out_specs=pl.BlockSpec(memory_space=pltpu.VMEM),
        cost_estimate=cost(2),
        name="place",
    )(at, layer, *parts)


def added(a, b):
    return (a.astype(F32) + b.astype(F32)).astype(BF16)


def after(value, *earlier):
    return lax.optimization_barrier((value, earlier))[0]


def body_eight(qkv, out_weight):
    _, _, cols, features = qkv.shape
    half = features // 2
    chunks = 2
    width = half // chunks
    heads = width // HEAD
    coef = HEAD ** (-0.5) * LOG2E
    me = lax.axis_index("seq")
    who = lax.axis_index("head")
    z, x, core, y = me // 2, me % 2, who % 2, who // 2
    at = jnp.stack([x, z, core]).astype(jnp.int32)
    local = qkv.reshape(3, cols, features)
    first = x == 0

    def seq_perm(array, *layers, cross=False):
        pairs = [(2 * a + i, 2 * b + (1 - i if cross else i)) for a, b in layers for i in range(2)]
        return lax.ppermute(array, "seq", pairs)

    def swap(array):
        return seq_perm(array, (0, 0), (1, 1), (2, 2), (3, 3), cross=True)

    def head_perm(array, flip):
        return lax.ppermute(array, "head", [(i, i ^ flip) for i in range(4)])

    def keep(array, lo, hi, c):
        return lax.dynamic_slice(array, (lo, 0, x * half + c * width), (hi - lo, cols, width))

    def give(array, lo, hi, c):
        return lax.dynamic_slice(array, (lo, 0, (1 - x) * half + c * width), (hi - lo, cols, width))

    q, kv, low, qa, qb = [], [], [], [], []
    w_first = seq_perm(out_weight, (1, 2), (2, 3))
    for c in range(chunks):
        if c == 0:
            for_q = for_low = local
        else:
            for_q = after(local, kv[0][1])
            for_low = after(local, low[0])
        mine, other = keep(for_q, 0, 1, c), swap(give(for_q, 0, 1, c))
        q.append(jnp.concatenate([jnp.where(first, mine, other), jnp.where(first, other, mine)]))
        low.append((seq_perm(keep(for_low, 1, 3, c), (0, 1)), seq_perm(give(for_low, 1, 3, c), (0, 1), cross=True)))
        for_kv = after(local, other) if c == 0 else for_q
        kv.append((keep(for_kv, 1, 3, c), swap(give(for_kv, 1, 3, c))))
        going = q[c] if c == 0 else after(q[c], qa[0], qb[0])
        qa.append(seq_perm(going, (2, 1), (3, 2)))
        qb.append(seq_perm(going, (3, 1)))

    struct = jax.ShapeDtypeStruct
    partial = struct((2 * cols + lse_height(cols), width), BF16)
    oa, ob, own, sent = [], [], [], []
    for c in range(chunks):
        at_c = at if c == 0 else after(at, own[0])
        a, b = head_call(
            functools.partial(upper_kernel, coef, cols), at_c, [qa[c], qb[c], *kv[c], *low[c]],
            [partial] * 2, heads, "upper_rows", 4)
        sent.append(a)
        oa.append(seq_perm(a, (1, 2), (2, 3)))
        ob.append(seq_perm(b, (1, 3)))
        (mine,) = head_call(
            functools.partial(own_kernel, coef, cols), after(at, a), [q[c], *kv[c], *low[c]], [partial],
            heads, "own_rows", 4)
        own.append(mine)

    w_second = seq_perm(after(out_weight, low[1]), (0, 1), (1, 0), (3, 2))
    w_third = seq_perm(after(out_weight, qa[1], qb[1]), (2, 1))
    w_fourth = seq_perm(w_first, (2, 3))
    w_fifth = seq_perm(jnp.where(z == 1, w_third, w_second), (1, 0), (2, 1))
    w_sixth = seq_perm(w_second, (1, 2))
    w_last = seq_perm(jnp.where(z == 1, w_fifth, w_sixth), (1, 0), (2, 3))
    slot_a = jnp.where(z == 3, w_fourth, w_second)
    slot_b = jnp.where(z == 0, w_fifth, jnp.where(z == 1, w_third, w_first))
    slot_c = jnp.where(z == 1, w_fifth, jnp.where(z == 2, w_sixth, w_last))
    layer = jnp.stack([
        z,
        jnp.array([1, 0, 3, 1], jnp.int32)[z],
        jnp.array([2, 2, 1, 2], jnp.int32)[z],
        jnp.array([3, 3, 0, 0], jnp.int32)[z],
    ]).astype(jnp.int32)

    near, far = [], []
    for c in range(chunks):
        (a,) = head_call(
            functools.partial(merge_kernel, cols), after(at, sent[-1]), [own[c], oa[c], ob[c]],
            [struct((2, cols, width), BF16)], heads, "merge", 2)
        near.append(a)
        far.append(swap(a))

    parts = []
    previous = None
    for weights in ([out_weight, slot_a], [slot_b, slot_c]):
        if previous is not None:
            weights = [after(w, previous) for w in weights]
        send, kept = project(at, near, far, weights)
        part = added(kept, head_perm(send, 1))
        previous = part
        to_y = lax.dynamic_index_in_dim(part, 1 - y, 1, keepdims=False)
        stay = lax.dynamic_index_in_dim(part, y, 1, keepdims=False)
        done = added(stay, head_perm(to_y, 2))
        theirs = swap(lax.dynamic_index_in_dim(done, 1 - x, 1, keepdims=False))
        parts += [lax.dynamic_index_in_dim(done, x, 1, keepdims=False), theirs]
    return place(at, layer, parts).reshape(cols // 4, 1, 8 * out_weight.shape[1])


def solution(mesh):
    in_specs = (P(None, "seq", None, "head"), P("head", "seq"))
    out_specs = P("head", "seq", None)
    small = mesh.shape["seq"] == 8 and mesh.shape["head"] == 4

    def body(qkv, out_weight):
        if small and qkv.shape[1] == 1:
            return body_eight(qkv, out_weight)
        return body_any(qkv, out_weight)

    return jax.shard_map(body, mesh=mesh, in_specs=in_specs, out_specs=out_specs, check_vma=False)
```

```python
import functools
import jax
import jax.numpy as jnp
from jax import lax
from jax.experimental import pallas as pl
from jax.experimental.pallas import tpu as pltpu
from jax.sharding import PartitionSpec as P

HEAD = 128
LOG2E = 1.4426950408889634
NEG = -1e30
QB = 128
VMEM = 48 * 1024 * 1024
F32, BF16 = jnp.float32, jnp.bfloat16


def shifted(shard, axis, by):
    size = lax.axis_size(axis)
    pairs = [(i, i + by) for i in range(size) if 0 <= i + by < size]
    return lax.ppermute(shard, axis, pairs)


def column_part(part):
    queries, keys_part, values = (part[0], part[1], part[2])
    rows = queries.shape[0]
    scale = queries.shape[-1] ** (-0.5)
    scores = (
        jnp.einsum("rchd,schd->chrs", queries, keys_part, preferred_element_type=jnp.float32)
        * scale
    )
    r_idx = lax.broadcasted_iota(jnp.int32, (rows, rows), 0)
    s_idx = lax.broadcasted_iota(jnp.int32, (rows, rows), 1)
    allowed = s_idx <= r_idx - 2
    masked = jnp.where(allowed, scores, jnp.float32(-1e30))
    peak = jnp.max(masked, axis=-1)
    weights = jnp.where(allowed, jnp.exp(masked - peak[..., None]), jnp.float32(0.0))
    total = jnp.maximum(jnp.sum(weights, axis=-1), jnp.float32(1.0))
    rounded = weights.astype(jnp.bfloat16)
    mixed = jnp.einsum("chrs,schd->rchd", rounded, values, preferred_element_type=jnp.float32)
    col_out = (mixed / jnp.transpose(total, (2, 0, 1))[..., None]).astype(jnp.bfloat16)
    col_lse = jnp.transpose(peak + jnp.log(total), (2, 0, 1))
    return (col_out, col_lse)


def row_part(local, previous, first_row):
    rows_dev, cols, heads_local, head_size = (
        local.shape[1],
        local.shape[2],
        local.shape[3],
        local.shape[4],
    )
    scale = head_size ** (-0.5)
    keys_ext = jnp.concatenate([previous, local[1:3]], axis=1)
    key_idx = lax.broadcasted_iota(jnp.int32, (cols, 2 * cols), 1)
    query_idx = lax.broadcasted_iota(jnp.int32, (cols, 2 * cols), 0)

    def one_row(index):
        queries = lax.dynamic_index_in_dim(local[0], index, 0, keepdims=False)
        pair = keys_ext.reshape(2, 2 * cols, heads_local, head_size)
        scores = (
            jnp.einsum("qhd,khd->hqk", queries, pair[0], preferred_element_type=jnp.float32) * scale
        )
        allowed = (key_idx < cols) & (first_row + index > 0) | (key_idx >= cols) & (
            key_idx - cols <= query_idx
        )
        masked = jnp.where(allowed[None], scores, jnp.float32(-1e30))
        peak = jnp.max(masked, axis=-1)
        weights = jnp.where(allowed[None], jnp.exp(masked - peak[..., None]), jnp.float32(0.0))
        total = jnp.sum(weights, axis=-1)
        rounded = weights.astype(jnp.bfloat16)
        mixed = jnp.einsum("hqk,khd->qhd", rounded, pair[1], preferred_element_type=jnp.float32)
        return (mixed / jnp.transpose(total)[..., None], jnp.transpose(peak + jnp.log(total)))

    return lax.map(one_row, jnp.arange(rows_dev, dtype=jnp.int32))


def body_any(qkv, out_weight):
    rows_dev, cols, features = (qkv.shape[1], qkv.shape[2], qkv.shape[3])
    head_size = HEAD
    heads_local = features // head_size
    local = qkv.reshape(3, rows_dev, cols, heads_local, head_size)
    previous = shifted(local[1:3, rows_dev - 1 : rows_dev], "seq", 1)
    first_row = lax.axis_index("seq") * rows_dev
    row_out, row_lse = row_part(local, previous, first_row)
    columns = lax.all_to_all(local, "seq", split_axis=2, concat_axis=1, tiled=True)
    col_part_out, col_part_lse = column_part(columns)
    col_out, col_lse = (
        lax.all_to_all(col_part_out, "seq", split_axis=0, concat_axis=1, tiled=True),
        lax.all_to_all(
            col_part_lse.astype(jnp.bfloat16), "seq", split_axis=0, concat_axis=1, tiled=True
        ).astype(col_part_lse.dtype),
    )
    top = jnp.maximum(row_lse, col_lse)
    left = jnp.exp(row_lse - top)
    right = jnp.exp(col_lse - top)
    attended = (left[..., None] * row_out + right[..., None] * col_out.astype(jnp.float32)) / (
        left + right
    )[..., None]
    attended = attended.astype(jnp.bfloat16).reshape(rows_dev, cols, features)
    terms = jnp.einsum(
        "rcf,fd->crd",
        attended,
        lax.all_gather(out_weight, "seq", axis=1, tiled=True),
        preferred_element_type=jnp.float32,
    )
    summed = lax.psum_scatter(terms.astype(jnp.bfloat16), "head", scatter_dimension=0, tiled=True)
    return summed


def dense_scores(q, k):
    return lax.dot_general(q, k, (((1,), (1,)), ((), ())), preferred_element_type=F32)


def col_scores(q, k):
    prod = q * k
    high = prod.astype(BF16)
    low = (prod - high.astype(F32)).astype(BF16)
    ones = jnp.ones((2 * HEAD, HEAD), BF16)
    return jnp.dot(jnp.concatenate([high, low], axis=1), ones, preferred_element_type=F32)


def with_ones(v):
    return jnp.concatenate([v, jnp.ones_like(v)], axis=1)


def attend(q, dense, cols, coef):
    rows = q.shape[0]
    scores = []
    for k, _, allowed in dense:
        s = dense_scores(q, k)
        scores.append(s if allowed is None else jnp.where(allowed, s, NEG))
    singles = []
    if cols:
        wide = q.astype(F32)
    for k, _, allowed in cols:
        c = col_scores(wide, k)
        singles.append(c if allowed is None else jnp.where(allowed, c, NEG))
    peak = None
    for s in scores:
        for j in range(s.shape[1] // HEAD):
            part = s[:, j * HEAD : (j + 1) * HEAD]
            peak = part if peak is None else jnp.maximum(peak, part)
    if peak is not None:
        peak = jnp.broadcast_to(jnp.max(peak, axis=1, keepdims=True), (rows, HEAD))
    for c in singles:
        peak = c if peak is None else jnp.maximum(peak, c)
    peak = peak * coef
    both = None
    for s, (_, v, _) in zip(scores, dense):
        tiled = jnp.concatenate([peak] * (s.shape[1] // HEAD), axis=1)
        p = jnp.exp2(s * coef - tiled).astype(BF16)
        term = jnp.dot(p, v, preferred_element_type=F32)
        both = term if both is None else both + term
    out = None if both is None else both[:, :HEAD]
    total = None if both is None else both[:, HEAD:]
    for c, (_, v, _) in zip(singles, cols):
        w = jnp.exp2(c * coef - peak)
        total = w if total is None else total + w
        out = w * v if out is None else out + w * v
    return out / total, peak + jnp.log2(total)


def lse_rows(even, odd):
    lane = lax.broadcasted_iota(jnp.int32, (HEAD, HEAD), 1)
    evens, odds = [], []
    for t in range(even.shape[0] // HEAD):
        block = slice(t * HEAD, (t + 1) * HEAD)
        turned = jnp.transpose(jnp.where(lane == 0, even[block], odd[block]))
        evens.append(turned[0:1])
        odds.append(turned[1:2])
    return evens, odds


def put_lse(ref, base, evens, odds):
    rows = jnp.concatenate(evens + odds, axis=0)
    pad = (-rows.shape[0]) % 16
    if pad:
        rows = jnp.concatenate([rows, jnp.zeros((pad, HEAD), F32)], axis=0)
    count = rows.shape[0]
    for piece in range(3):
        part = rows.astype(BF16)
        ref[pl.ds(base + piece * count, count), :] = part
        rows = rows - part.astype(F32)


def get_lse(ref, base, cols):
    blocks = cols // HEAD
    count = -(-2 * blocks // 16) * 16
    rows = sum(ref[pl.ds(base + piece * count, count), :].astype(F32) for piece in range(3))
    turned = [
        jnp.transpose(jnp.broadcast_to(rows[t : t + 1], (HEAD, HEAD))) for t in range(2 * blocks)
    ]
    return jnp.concatenate(turned[:blocks], axis=0), jnp.concatenate(turned[blocks:], axis=0)


def lse_height(cols):
    return 3 * (-(-2 * (cols // HEAD) // 16) * 16)


def own_kernel(coef, cols, at, q, kv_m, kv_o, low_m, low_o, out):
    x, z = at[0], at[1]
    below = z == 1
    block = 256
    tri = lax.broadcasted_iota(jnp.int32, (block, block), 1) <= lax.broadcasted_iota(
        jnp.int32, (block, block), 0
    )
    first = x == 0
    k_e, k_o = jnp.where(first, kv_m[0], kv_o[0]), jnp.where(first, kv_o[0], kv_m[0])
    v_e, v_o = jnp.where(first, kv_m[1], kv_o[1]), jnp.where(first, kv_o[1], kv_m[1])
    v_e, v_o = with_ones(v_e), with_ones(v_o)
    lk_e = jnp.where(first, low_m[0], low_o[0])
    lk_o = jnp.where(first, low_o[0], low_m[0])
    lv_e = jnp.where(first, low_m[1], low_o[1])
    lv_o = jnp.where(first, low_o[1], low_m[1])
    lv_o1 = with_ones(lv_o)
    evens, odds = [], []
    for part in range(cols // block):
        a, b = part * block, (part + 1) * block
        mine = slice(a, b)
        col_e = (lk_e[mine].astype(F32), lv_e[mine].astype(F32), below)
        col_o = (lk_o[mine].astype(F32), lv_o[mine].astype(F32), below)

        def causal(k, v):
            blocks = [(k[a:b], v[a:b], tri)]
            return blocks if part == 0 else [(k[:a], v[:a], None)] + blocks

        o1, l1 = attend(q[0, mine], causal(k_e, v_e) + [(lk_o, lv_o1, below)], [col_e], coef)
        o2, l2 = attend(q[1, mine], causal(k_o, v_o) + [(k_e, v_e, None)], [col_e, col_o], coef)
        out[mine] = o1.astype(BF16)
        out[cols + a : cols + b] = o2.astype(BF16)
        e, o = lse_rows(l1, l2)
        evens, odds = evens + e, odds + o
    put_lse(out, 2 * cols, evens, odds)


def upper_kernel(coef, cols, at, qa, qb, kv_m, kv_o, low_m, low_o, out_a, out_b):
    x, z = at[0], at[1]
    below = z == 1
    first = x == 0
    block = 256
    k_e, k_o = jnp.where(first, kv_m[0], kv_o[0]), jnp.where(first, kv_o[0], kv_m[0])
    v_e, v_o = jnp.where(first, kv_m[1], kv_o[1]), jnp.where(first, kv_o[1], kv_m[1])
    v_o1 = with_ones(v_o)
    rows_a, rows_b = ([], []), ([], [])
    for part in range(cols // block):
        a, b = part * block, (part + 1) * block
        mine = slice(a, b)
        m_k, m_v = low_m[0, mine].astype(F32), low_m[1, mine].astype(F32)
        o_k, o_v = low_o[0, mine].astype(F32), low_o[1, mine].astype(F32)
        ce = (k_e[mine].astype(F32), v_e[mine].astype(F32), None)
        co = (k_o[mine].astype(F32), v_o[mine].astype(F32), None)
        low = [(m_k, m_v, below), (o_k, o_v, below)]
        for q, out, rows, dense, singles in (
            (qa, out_a, rows_a, [(k_o, v_o1, None)], [ce]),
            (qb, out_b, rows_b, [], [ce, co]),
        ):
            o1, l1 = attend(q[0, mine], dense, singles + low, coef)
            o2, l2 = attend(q[1, mine], [], [ce, co] + low, coef)
            out[mine] = o1.astype(BF16)
            out[cols + a : cols + b] = o2.astype(BF16)
            e, o = lse_rows(l1, l2)
            rows[0].extend(e)
            rows[1].extend(o)
    put_lse(out_a, 2 * cols, *rows_a)
    put_lse(out_b, 2 * cols, *rows_b)


def merge_kernel(cols, at, own, oa, ob, out):
    z = at[1]
    own_l, a_l, b_l = (get_lse(ref, 2 * cols, cols) for ref in (own, oa, ob))
    for row in range(2):
        tokens = slice(row * cols, (row + 1) * cols)
        l0 = own_l[row]
        l1 = jnp.where(z >= 2, a_l[row], NEG)
        l2 = jnp.where(z >= 3, b_l[row], NEG)
        top = jnp.maximum(l0, jnp.maximum(l1, l2))
        w0, w1, w2 = jnp.exp2(l0 - top), jnp.exp2(l1 - top), jnp.exp2(l2 - top)
        mixed = w0 * own[tokens].astype(F32) + w1 * oa[tokens].astype(F32) + w2 * ob[tokens].astype(F32)
        out[row] = (mixed / (w0 + w1 + w2)).astype(BF16)


def cost(us):
    return pl.CostEstimate(flops=int(us * 1.1e9), bytes_accessed=int(us * 1e6), transcendentals=0)


def head_call(kernel, at, args, outs, heads, name, us):
    def spec(shape):
        lead = len(shape) - 1
        return pl.BlockSpec(tuple(shape[:-1]) + (HEAD,), lambda h, at: (0,) * lead + (h,))

    return pl.pallas_call(
        kernel,
        out_shape=outs,
        grid_spec=pltpu.PrefetchScalarGridSpec(
            num_scalar_prefetch=1,
            grid=(heads,),
            in_specs=[spec(a.shape) for a in args],
            out_specs=[spec(o.shape) for o in outs],
        ),
        compiler_params=pltpu.CompilerParams(vmem_limit_bytes=VMEM),
        cost_estimate=cost(us),
        name=name,
    )(at, *args)


def project_kernel(chunks, at, *refs):
    x, core = at[0], at[2]
    near, far = refs[:chunks], refs[chunks : 2 * chunks]
    weight, send, keep = refs[2 * chunks :]
    tokens, width = near[0].shape[3:]
    half = width * chunks
    top = weight[0, pl.ds(pl.multiple_of(x * half, half), half)]
    bottom = weight[0, pl.ds(pl.multiple_of((1 - x) * half, half), half)]
    for who, out in ((1 - core, send), (core, keep)):

        def rows(ref):
            return jnp.concatenate([ref[r, y, who] for y in range(2) for r in range(2)], axis=0)

        left = jnp.concatenate([rows(ref) for ref in near], axis=1)
        right = jnp.concatenate([rows(ref) for ref in far], axis=1)
        c = jnp.dot(left, top, preferred_element_type=F32) + jnp.dot(right, bottom, preferred_element_type=F32)
        out[0] = c.astype(BF16).reshape(2, 2, tokens, weight.shape[2])


def project(at, near, far, weight, start, count):
    _, cols, width = near[0].shape
    shape = (2, 2, 2, cols // 4, width)
    args = [a.reshape(shape) for a in near + far]
    _, depth, out_width = weight.shape
    out = jax.ShapeDtypeStruct((count, 2, 2, cols // 4, out_width), BF16)
    out_spec = pl.BlockSpec((1,) + out.shape[1:], lambda s, at: (s, 0, 0, 0, 0))
    return pl.pallas_call(
        functools.partial(project_kernel, len(near)),
        out_shape=[out, out],
        grid_spec=pltpu.PrefetchScalarGridSpec(
            num_scalar_prefetch=1,
            grid=(count,),
            in_specs=[pl.BlockSpec(shape, lambda s, at: (0,) * 5)] * len(args)
            + [pl.BlockSpec((1, depth, out_width), lambda s, at: (start + s, 0, 0))],
            out_specs=[out_spec, out_spec],
        ),
        compiler_params=pltpu.CompilerParams(vmem_limit_bytes=VMEM),
        cost_estimate=cost(2 * count),
        name="project",
    )(at, *args, weight)


def whole_call(kernel, at, args, outs, name, us):
    return pl.pallas_call(
        kernel,
        out_shape=outs,
        in_specs=[pl.BlockSpec(memory_space=pltpu.SMEM)] + [pl.BlockSpec(memory_space=pltpu.VMEM)] * len(args),
        out_specs=[pl.BlockSpec(memory_space=pltpu.VMEM)] * len(outs),
        compiler_params=pltpu.CompilerParams(vmem_limit_bytes=VMEM),
        cost_estimate=cost(us),
        name=name,
    )(at, *args)


def total(a, b):
    return (a.astype(F32) + b.astype(F32)).astype(BF16)


def split_kernel(at, kept, got, stay, to_y, to_x, to_xy):
    x, y = at[0], at[3]
    for s in range(kept.shape[0]):
        for out, yy, xx in ((to_xy, 1 - y, 1 - x), (to_y, 1 - y, x), (to_x, y, 1 - x), (stay, y, x)):
            out[s] = total(kept[s, yy, xx], got[s, yy, xx])


def place_kernel(at, *refs):
    x, out = at[0], refs[-1]
    layer = 0
    for stay, from_y, from_x, from_xy in zip(*(refs[i:-1:4] for i in range(4))):
        width = stay.shape[-1]
        for s in range(stay.shape[0]):
            mine = pl.ds(pl.multiple_of((2 * layer + x) * width, width), width)
            theirs = pl.ds(pl.multiple_of((2 * layer + 1 - x) * width, width), width)
            out[:, mine] = total(stay[s], from_y[s])
            out[:, theirs] = total(from_x[s], from_xy[s])
            layer += 1


def after(value, *earlier):
    return lax.optimization_barrier((value, earlier))[0]


def body_eight(qkv, out_weight):
    _, _, cols, features = qkv.shape
    half = features // 2
    chunks = 2
    width = half // chunks
    heads = width // HEAD
    coef = HEAD ** (-0.5) * LOG2E
    me = lax.axis_index("seq")
    who = lax.axis_index("head")
    z, x, core, y = me // 2, me % 2, who % 2, who // 2
    at = jnp.stack([x, z, core, y]).astype(jnp.int32)
    local = qkv.reshape(3, cols, features)
    first = x == 0

    def seq_perm(array, *layers, cross=False):
        pairs = [(2 * a + i, 2 * b + (1 - i if cross else i)) for a, b in layers for i in range(2)]
        return lax.ppermute(array, "seq", pairs)

    def swap(array):
        return seq_perm(array, (0, 0), (1, 1), (2, 2), (3, 3), cross=True)

    def head_perm(array, flip):
        return lax.ppermute(array, "head", [(i, i ^ flip) for i in range(4)])

    def keep(array, lo, hi, c):
        return lax.dynamic_slice(array, (lo, 0, x * half + c * width), (hi - lo, cols, width))

    def give(array, lo, hi, c):
        return lax.dynamic_slice(array, (lo, 0, (1 - x) * half + c * width), (hi - lo, cols, width))

    q, kv, low, qa, qb = [], [], [], [], []
    for c in range(chunks):
        source = local if c == 0 else after(local, kv[0][1])
        mine, other = keep(source, 0, 1, c), swap(give(source, 0, 1, c))
        q.append(jnp.concatenate([jnp.where(first, mine, other), jnp.where(first, other, mine)]))
        going = q[c] if c == 0 else after(q[c], qa[0], qb[0])
        qa.append(seq_perm(going, (2, 1), (3, 2)))
        qb.append(seq_perm(going, (3, 1)))
        kv.append((keep(source, 1, 3, c), swap(give(source, 1, 3, c))))
        low.append(tuple(seq_perm(half_kv, (0, 1)) for half_kv in kv[c]))
    layers = [[2 * i + j for i in range(4)] for j in range(2)]
    weight = lax.all_gather(out_weight, "seq", axis_index_groups=layers)

    struct = jax.ShapeDtypeStruct
    partial = struct((2 * cols + lse_height(cols), width), BF16)
    oa, ob, own, sent = [], [], [], []
    for c in range(chunks):
        at_c = at if c == 0 else after(at, own[0])
        a, b = head_call(
            functools.partial(upper_kernel, coef, cols), at_c, [qa[c], qb[c], *kv[c], *low[c]],
            [partial] * 2, heads, "upper_rows", 4)
        sent.append(a)
        oa.append(seq_perm(a, (1, 2), (2, 3)))
        ob.append(seq_perm(b, (1, 3)))
        (mine,) = head_call(
            functools.partial(own_kernel, coef, cols), after(at, a), [q[c], *kv[c], *low[c]], [partial],
            heads, "own_rows", 4)
        own.append(mine)

    near, far = [], []
    for c in range(chunks):
        (a,) = head_call(
            functools.partial(merge_kernel, cols), after(at, sent[-1]), [own[c], oa[c], ob[c]],
            [struct((2, cols, width), BF16)], heads, "merge", 2)
        near.append(a)
        far.append(swap(a))

    count = 2
    parts = []
    for start in range(0, 4, count):
        send, kept = project(at, near, far, weight, start, count)
        got = head_perm(send, 1)
        piece = struct((count,) + send.shape[3:], BF16)
        stay, to_y, to_x, to_xy = whole_call(split_kernel, at, [kept, got], [piece] * 4, "split", 2)
        diagonal = [((2 * i + j) * 4 + h, (2 * i + 1 - j) * 4 + (h ^ 2)) for i in range(4) for j in range(2) for h in range(4)]
        from_xy = lax.ppermute(to_xy, ("seq", "head"), diagonal)
        parts += [stay, head_perm(to_y, 2), swap(to_x), from_xy]
    (out,) = whole_call(
        place_kernel, at, parts, [struct((cols // 4, 8 * out_weight.shape[1]), BF16)], "place", 2)
    return out.reshape(cols // 4, 1, 8 * out_weight.shape[1])


def solution(mesh):
    in_specs = (P(None, "seq", None, "head"), P("head", "seq"))
    out_specs = P("head", "seq", None)
    small = mesh.shape["seq"] == 8 and mesh.shape["head"] == 4

    def body(qkv, out_weight):
        if small and qkv.shape[1] == 1:
            return body_eight(qkv, out_weight)
        return body_any(qkv, out_weight)

    return jax.shard_map(body, mesh=mesh, in_specs=in_specs, out_specs=out_specs, check_vma=False)
```

```python
import functools
import jax
import jax.numpy as jnp
from jax import lax
from jax.experimental import pallas as pl
from jax.experimental.pallas import tpu as pltpu
from jax.sharding import PartitionSpec as P

HEAD = 128
LOG2E = 1.4426950408889634
NEG = -1e30
QB = 128
VMEM = 48 * 1024 * 1024
F32, BF16 = jnp.float32, jnp.bfloat16


def shifted(shard, axis, by):
    size = lax.axis_size(axis)
    pairs = [(i, i + by) for i in range(size) if 0 <= i + by < size]
    return lax.ppermute(shard, axis, pairs)


def column_part(part):
    queries, keys_part, values = (part[0], part[1], part[2])
    rows = queries.shape[0]
    scale = queries.shape[-1] ** (-0.5)
    scores = (
        jnp.einsum("rchd,schd->chrs", queries, keys_part, preferred_element_type=jnp.float32)
        * scale
    )
    r_idx = lax.broadcasted_iota(jnp.int32, (rows, rows), 0)
    s_idx = lax.broadcasted_iota(jnp.int32, (rows, rows), 1)
    allowed = s_idx <= r_idx - 2
    masked = jnp.where(allowed, scores, jnp.float32(-1e30))
    peak = jnp.max(masked, axis=-1)
    weights = jnp.where(allowed, jnp.exp(masked - peak[..., None]), jnp.float32(0.0))
    total = jnp.maximum(jnp.sum(weights, axis=-1), jnp.float32(1.0))
    rounded = weights.astype(jnp.bfloat16)
    mixed = jnp.einsum("chrs,schd->rchd", rounded, values, preferred_element_type=jnp.float32)
    col_out = (mixed / jnp.transpose(total, (2, 0, 1))[..., None]).astype(jnp.bfloat16)
    col_lse = jnp.transpose(peak + jnp.log(total), (2, 0, 1))
    return (col_out, col_lse)


def row_part(local, previous, first_row):
    rows_dev, cols, heads_local, head_size = (
        local.shape[1],
        local.shape[2],
        local.shape[3],
        local.shape[4],
    )
    scale = head_size ** (-0.5)
    keys_ext = jnp.concatenate([previous, local[1:3]], axis=1)
    key_idx = lax.broadcasted_iota(jnp.int32, (cols, 2 * cols), 1)
    query_idx = lax.broadcasted_iota(jnp.int32, (cols, 2 * cols), 0)

    def one_row(index):
        queries = lax.dynamic_index_in_dim(local[0], index, 0, keepdims=False)
        pair = keys_ext.reshape(2, 2 * cols, heads_local, head_size)
        scores = (
            jnp.einsum("qhd,khd->hqk", queries, pair[0], preferred_element_type=jnp.float32) * scale
        )
        allowed = (key_idx < cols) & (first_row + index > 0) | (key_idx >= cols) & (
            key_idx - cols <= query_idx
        )
        masked = jnp.where(allowed[None], scores, jnp.float32(-1e30))
        peak = jnp.max(masked, axis=-1)
        weights = jnp.where(allowed[None], jnp.exp(masked - peak[..., None]), jnp.float32(0.0))
        total = jnp.sum(weights, axis=-1)
        rounded = weights.astype(jnp.bfloat16)
        mixed = jnp.einsum("hqk,khd->qhd", rounded, pair[1], preferred_element_type=jnp.float32)
        return (mixed / jnp.transpose(total)[..., None], jnp.transpose(peak + jnp.log(total)))

    return lax.map(one_row, jnp.arange(rows_dev, dtype=jnp.int32))


def body_any(qkv, out_weight):
    rows_dev, cols, features = (qkv.shape[1], qkv.shape[2], qkv.shape[3])
    head_size = HEAD
    heads_local = features // head_size
    local = qkv.reshape(3, rows_dev, cols, heads_local, head_size)
    previous = shifted(local[1:3, rows_dev - 1 : rows_dev], "seq", 1)
    first_row = lax.axis_index("seq") * rows_dev
    row_out, row_lse = row_part(local, previous, first_row)
    columns = lax.all_to_all(local, "seq", split_axis=2, concat_axis=1, tiled=True)
    col_part_out, col_part_lse = column_part(columns)
    col_out, col_lse = (
        lax.all_to_all(col_part_out, "seq", split_axis=0, concat_axis=1, tiled=True),
        lax.all_to_all(
            col_part_lse.astype(jnp.bfloat16), "seq", split_axis=0, concat_axis=1, tiled=True
        ).astype(col_part_lse.dtype),
    )
    top = jnp.maximum(row_lse, col_lse)
    left = jnp.exp(row_lse - top)
    right = jnp.exp(col_lse - top)
    attended = (left[..., None] * row_out + right[..., None] * col_out.astype(jnp.float32)) / (
        left + right
    )[..., None]
    attended = attended.astype(jnp.bfloat16).reshape(rows_dev, cols, features)
    terms = jnp.einsum(
        "rcf,fd->crd",
        attended,
        lax.all_gather(out_weight, "seq", axis=1, tiled=True),
        preferred_element_type=jnp.float32,
    )
    summed = lax.psum_scatter(terms.astype(jnp.bfloat16), "head", scatter_dimension=0, tiled=True)
    return summed


def dense_scores(q, k):
    return lax.dot_general(q, k, (((1,), (1,)), ((), ())), preferred_element_type=F32)


def col_scores(q, k):
    prod = q * k
    high = prod.astype(BF16)
    low = (prod - high.astype(F32)).astype(BF16)
    ones = jnp.ones((2 * HEAD, HEAD), BF16)
    return jnp.dot(jnp.concatenate([high, low], axis=1), ones, preferred_element_type=F32)


def with_ones(v):
    return jnp.concatenate([v, jnp.ones_like(v)], axis=1)


def attend(q, dense, cols, coef):
    rows = q.shape[0]
    scores = []
    for k, _, allowed in dense:
        s = dense_scores(q, k)
        scores.append(s if allowed is None else jnp.where(allowed, s, NEG))
    singles = []
    if cols:
        wide = q.astype(F32)
    for k, _, allowed in cols:
        c = col_scores(wide, k)
        singles.append(c if allowed is None else jnp.where(allowed, c, NEG))
    peak = None
    for s in scores:
        for j in range(s.shape[1] // HEAD):
            part = s[:, j * HEAD : (j + 1) * HEAD]
            peak = part if peak is None else jnp.maximum(peak, part)
    if peak is not None:
        peak = jnp.broadcast_to(jnp.max(peak, axis=1, keepdims=True), (rows, HEAD))
    for c in singles:
        peak = c if peak is None else jnp.maximum(peak, c)
    peak = peak * coef
    both = None
    for s, (_, v, _) in zip(scores, dense):
        tiled = jnp.concatenate([peak] * (s.shape[1] // HEAD), axis=1)
        p = jnp.exp2(s * coef - tiled).astype(BF16)
        term = jnp.dot(p, v, preferred_element_type=F32)
        both = term if both is None else both + term
    out = None if both is None else both[:, :HEAD]
    total = None if both is None else both[:, HEAD:]
    for c, (_, v, _) in zip(singles, cols):
        w = jnp.exp2(c * coef - peak)
        total = w if total is None else total + w
        out = w * v if out is None else out + w * v
    return out / total, peak + jnp.log2(total)


def lse_rows(even, odd):
    lane = lax.broadcasted_iota(jnp.int32, (HEAD, HEAD), 1)
    evens, odds = [], []
    for t in range(even.shape[0] // HEAD):
        block = slice(t * HEAD, (t + 1) * HEAD)
        turned = jnp.transpose(jnp.where(lane == 0, even[block], odd[block]))
        evens.append(turned[0:1])
        odds.append(turned[1:2])
    return evens, odds


def put_lse(ref, base, evens, odds):
    rows = jnp.concatenate(evens + odds, axis=0)
    pad = (-rows.shape[0]) % 16
    if pad:
        rows = jnp.concatenate([rows, jnp.zeros((pad, HEAD), F32)], axis=0)
    count = rows.shape[0]
    for piece in range(3):
        part = rows.astype(BF16)
        ref[pl.ds(base + piece * count, count), :] = part
        rows = rows - part.astype(F32)


def get_lse(ref, base, cols):
    blocks = cols // HEAD
    count = -(-2 * blocks // 16) * 16
    rows = sum(ref[pl.ds(base + piece * count, count), :].astype(F32) for piece in range(3))
    turned = [
        jnp.transpose(jnp.broadcast_to(rows[t : t + 1], (HEAD, HEAD))) for t in range(2 * blocks)
    ]
    return jnp.concatenate(turned[:blocks], axis=0), jnp.concatenate(turned[blocks:], axis=0)


def lse_height(cols):
    return 3 * (-(-2 * (cols // HEAD) // 16) * 16)


def stacked(refs):
    return [ref[i] for ref in refs for i in range(ref.shape[0])]


def own_kernel(coef, cols, at, q, kv_m, kv_o, *refs):
    x, z = at[0], at[1]
    below = z == 1
    block = 256
    tri = lax.broadcasted_iota(jnp.int32, (block, block), 1) <= lax.broadcasted_iota(
        jnp.int32, (block, block), 0
    )
    first = x == 0
    k_e, k_o = jnp.where(first, kv_m[0], kv_o[0]), jnp.where(first, kv_o[0], kv_m[0])
    v_e, v_o = jnp.where(first, kv_m[1], kv_o[1]), jnp.where(first, kv_o[1], kv_m[1])
    v_e, v_o = with_ones(v_e), with_ones(v_o)
    *low, out = refs
    m_k, m_v, o_k, o_v = stacked(low)
    lk_e, lk_o = jnp.where(first, m_k, o_k), jnp.where(first, o_k, m_k)
    lv_e, lv_o = jnp.where(first, m_v, o_v), jnp.where(first, o_v, m_v)
    lv_o1 = with_ones(lv_o)
    evens, odds = [], []
    for part in range(cols // block):
        a, b = part * block, (part + 1) * block
        mine = slice(a, b)
        col_e = (lk_e[mine].astype(F32), lv_e[mine].astype(F32), below)
        col_o = (lk_o[mine].astype(F32), lv_o[mine].astype(F32), below)

        def causal(k, v):
            blocks = [(k[a:b], v[a:b], tri)]
            return blocks if part == 0 else [(k[:a], v[:a], None)] + blocks

        o1, l1 = attend(q[0, mine], causal(k_e, v_e) + [(lk_o, lv_o1, below)], [col_e], coef)
        o2, l2 = attend(q[1, mine], causal(k_o, v_o) + [(k_e, v_e, None)], [col_e, col_o], coef)
        out[mine] = o1.astype(BF16)
        out[cols + a : cols + b] = o2.astype(BF16)
        e, o = lse_rows(l1, l2)
        evens, odds = evens + e, odds + o
    put_lse(out, 2 * cols, evens, odds)


def upper_kernel(coef, cols, at, qa, qb, kv_m, kv_o, *refs):
    x, z = at[0], at[1]
    below = z == 1
    first = x == 0
    block = 256
    k_e, k_o = jnp.where(first, kv_m[0], kv_o[0]), jnp.where(first, kv_o[0], kv_m[0])
    v_e, v_o = jnp.where(first, kv_m[1], kv_o[1]), jnp.where(first, kv_o[1], kv_m[1])
    v_o1 = with_ones(v_o)
    *low, out_a, out_b = refs
    lows = stacked(low)
    rows_a, rows_b = ([], []), ([], [])
    for index in range(cols // block):
        a, b = index * block, (index + 1) * block
        mine = slice(a, b)
        m_k, m_v, o_k, o_v = (part[mine].astype(F32) for part in lows)
        ce = (k_e[mine].astype(F32), v_e[mine].astype(F32), None)
        co = (k_o[mine].astype(F32), v_o[mine].astype(F32), None)
        low = [(m_k, m_v, below), (o_k, o_v, below)]
        for q, out, rows, dense, singles in (
            (qa, out_a, rows_a, [(k_o, v_o1, None)], [ce]),
            (qb, out_b, rows_b, [], [ce, co]),
        ):
            o1, l1 = attend(q[0, mine], dense, singles + low, coef)
            o2, l2 = attend(q[1, mine], [], [ce, co] + low, coef)
            out[mine] = o1.astype(BF16)
            out[cols + a : cols + b] = o2.astype(BF16)
            e, o = lse_rows(l1, l2)
            rows[0].extend(e)
            rows[1].extend(o)
    put_lse(out_a, 2 * cols, *rows_a)
    put_lse(out_b, 2 * cols, *rows_b)


def merge_kernel(cols, at, own, oa, ob, out):
    z = at[1]
    own_l, a_l, b_l = (get_lse(ref, 2 * cols, cols) for ref in (own, oa, ob))
    for row in range(2):
        tokens = slice(row * cols, (row + 1) * cols)
        l0 = own_l[row]
        l1 = jnp.where(z >= 2, a_l[row], NEG)
        l2 = jnp.where(z >= 3, b_l[row], NEG)
        top = jnp.maximum(l0, jnp.maximum(l1, l2))
        w0, w1, w2 = jnp.exp2(l0 - top), jnp.exp2(l1 - top), jnp.exp2(l2 - top)
        mixed = w0 * own[tokens].astype(F32) + w1 * oa[tokens].astype(F32) + w2 * ob[tokens].astype(F32)
        out[row] = (mixed / (w0 + w1 + w2)).astype(BF16)


def cost(us):
    return pl.CostEstimate(flops=int(us * 1.1e9), bytes_accessed=int(us * 1e6), transcendentals=0)


def head_call(kernel, at, args, outs, heads, name, us):
    def spec(shape):
        lead = len(shape) - 1
        return pl.BlockSpec(tuple(shape[:-1]) + (HEAD,), lambda h, at: (0,) * lead + (h,))

    return pl.pallas_call(
        kernel,
        out_shape=outs,
        grid_spec=pltpu.PrefetchScalarGridSpec(
            num_scalar_prefetch=1,
            grid=(heads,),
            in_specs=[spec(a.shape) for a in args],
            out_specs=[spec(o.shape) for o in outs],
        ),
        compiler_params=pltpu.CompilerParams(vmem_limit_bytes=VMEM),
        cost_estimate=cost(us),
        name=name,
    )(at, *args)


def project_kernel(chunks, at, *refs):
    x, core = at[0], at[2]
    near, far = refs[:chunks], refs[chunks : 2 * chunks]
    weight, send, keep = refs[2 * chunks :]
    tokens, width = near[0].shape[3:]
    half = width * chunks
    top = weight[0, pl.ds(pl.multiple_of(x * half, half), half)]
    bottom = weight[0, pl.ds(pl.multiple_of((1 - x) * half, half), half)]
    for who, out in ((1 - core, send), (core, keep)):

        def rows(ref):
            return jnp.concatenate([ref[r, y, who] for y in range(2) for r in range(2)], axis=0)

        left = jnp.concatenate([rows(ref) for ref in near], axis=1)
        right = jnp.concatenate([rows(ref) for ref in far], axis=1)
        c = jnp.dot(left, top, preferred_element_type=F32) + jnp.dot(right, bottom, preferred_element_type=F32)
        out[0] = c.astype(BF16).reshape(2, 2, tokens, weight.shape[2])


def project(at, near, far, weight, count, pick):
    _, cols, width = near[0].shape
    shape = (2, 2, 2, cols // 4, width)
    args = [a.reshape(shape) for a in near + far]
    _, depth, out_width = weight.shape
    out = jax.ShapeDtypeStruct((count, 2, 2, cols // 4, out_width), BF16)
    out_spec = pl.BlockSpec((1,) + out.shape[1:], lambda s, at: (s, 0, 0, 0, 0))
    return pl.pallas_call(
        functools.partial(project_kernel, len(near)),
        out_shape=[out, out],
        grid_spec=pltpu.PrefetchScalarGridSpec(
            num_scalar_prefetch=1,
            grid=(count,),
            in_specs=[pl.BlockSpec(shape, lambda s, at: (0,) * 5)] * len(args)
            + [pl.BlockSpec((1, depth, out_width), lambda s, at: (pick(s, at), 0, 0))],
            out_specs=[out_spec, out_spec],
        ),
        compiler_params=pltpu.CompilerParams(vmem_limit_bytes=VMEM),
        cost_estimate=cost(2 * count),
        name="project",
    )(at, *args, weight)


def whole_call(kernel, at, args, outs, name, us):
    return pl.pallas_call(
        kernel,
        out_shape=outs,
        in_specs=[pl.BlockSpec(memory_space=pltpu.SMEM)] + [pl.BlockSpec(memory_space=pltpu.VMEM)] * len(args),
        out_specs=[pl.BlockSpec(memory_space=pltpu.VMEM)] * len(outs),
        compiler_params=pltpu.CompilerParams(vmem_limit_bytes=VMEM),
        cost_estimate=cost(us),
        name=name,
    )(at, *args)


def total(a, b):
    return (a.astype(F32) + b.astype(F32)).astype(BF16)


def split_kernel(at, kept, got, stay, to_y, to_x, to_xy):
    x, y = at[0], at[3]
    for s in range(kept.shape[0]):
        for out, yy, xx in ((to_xy, 1 - y, 1 - x), (to_y, 1 - y, x), (to_x, y, 1 - x), (stay, y, x)):
            out[s] = total(kept[s, yy, xx], got[s, yy, xx])


def place_kernel(at, *refs):
    x, z, out = at[0], at[1], refs[-1]
    layers = [z - z % 2, z - z % 2 + 1, (z + 2) % 4, 3 - z]
    for stay, from_y, from_x, from_xy in zip(*(refs[i:-1:4] for i in range(4))):
        width = stay.shape[-1]
        for s in range(stay.shape[0]):
            base = 2 * layers.pop(0)
            mine = pl.ds(pl.multiple_of((base + x) * width, width), width)
            theirs = pl.ds(pl.multiple_of((base + 1 - x) * width, width), width)
            out[:, mine] = total(stay[s], from_y[s])
            out[:, theirs] = total(from_x[s], from_xy[s])


def after(value, *earlier):
    return lax.optimization_barrier((value, earlier))[0]


def body_eight(qkv, out_weight):
    _, _, cols, features = qkv.shape
    half = features // 2
    chunks = 2
    width = half // chunks
    heads = width // HEAD
    coef = HEAD ** (-0.5) * LOG2E
    me = lax.axis_index("seq")
    who = lax.axis_index("head")
    z, x, core, y = me // 2, me % 2, who % 2, who // 2
    at = jnp.stack([x, z, core, y]).astype(jnp.int32)
    local = qkv.reshape(3, cols, features)
    first = x == 0

    def seq_perm(array, *layers, cross=False):
        pairs = [(2 * a + i, 2 * b + (1 - i if cross else i)) for a, b in layers for i in range(2)]
        return lax.ppermute(array, "seq", pairs)

    def swap(array):
        return seq_perm(array, (0, 0), (1, 1), (2, 2), (3, 3), cross=True)

    def head_perm(array, flip):
        return lax.ppermute(array, "head", [(i, i ^ flip) for i in range(4)])

    def keep(array, lo, hi, c):
        return lax.dynamic_slice(array, (lo, 0, x * half + c * width), (hi - lo, cols, width))

    def give(array, lo, hi, c):
        return lax.dynamic_slice(array, (lo, 0, (1 - x) * half + c * width), (hi - lo, cols, width))

    w_up = seq_perm(out_weight, (0, 2), (1, 3))
    q, kv, low, qa, qb = [], [], [], [], []
    q_other = swap(lax.dynamic_slice(local, (0, 0, (1 - x) * half), (1, cols, half)))
    for c in range(chunks):
        mine, other = keep(local, 0, 1, c), q_other[:, :, c * width : (c + 1) * width]
        q.append(jnp.concatenate([jnp.where(first, mine, other), jnp.where(first, other, mine)]))
        going = q[c] if c == 0 else after(q[c], qa[0], qb[0])
        qa.append(seq_perm(going, (2, 1), (3, 2)))
        qb.append(seq_perm(going, (3, 1)))
        source = after(local, q[0]) if c == 0 else after(local, kv[0][1])
        kv.append((keep(local if c == 0 else source, 1, 3, c), swap(give(source, 1, 3, c))))
        if c == 0:
            low.append([seq_perm(half_kv, (0, 1)) for half_kv in kv[c]])
        else:
            low.append([seq_perm(after(jnp.concatenate(kv[c]), *low[0], w_up), (0, 1))])

    struct = jax.ShapeDtypeStruct
    partial = struct((2 * cols + lse_height(cols), width), BF16)
    oa, ob, own, sent = [], [], [], []
    for c in range(chunks):
        at_c = at if c == 0 else after(at, own[0])
        a, b = head_call(
            functools.partial(upper_kernel, coef, cols), at_c, [qa[c], qb[c], *kv[c], *low[c]],
            [partial] * 2, heads, "upper_rows", 4)
        sent.append(a)
        oa.append(seq_perm(a, (1, 2), (2, 3)))
        ob.append(seq_perm(b, (1, 3)))
        (mine,) = head_call(
            functools.partial(own_kernel, coef, cols), after(at, a), [q[c], *kv[c], *low[c]], [partial],
            heads, "own_rows", 4)
        own.append(mine)

    pairs = [[0, 2], [1, 3], [4, 6], [5, 7]]
    w_pair = lax.all_gather(after(out_weight, low[1][0], qa[1]), "seq", axis_index_groups=pairs)
    w_down = seq_perm(after(out_weight, qa[1], qb[1]), (2, 0), (3, 1))

    def merged(c, earlier):
        (a,) = head_call(
            functools.partial(merge_kernel, cols), after(at, earlier), [own[c], oa[c], ob[c]],
            [struct((2, cols, width), BF16)], heads, "merge", 2)
        return a, swap(a)

    first_half = merged(0, sent[1])
    w_far = jnp.where(z >= 2, w_up, after(w_down, first_half[0], own[1]))
    w_far_pair = lax.all_gather(w_far, "seq", axis_index_groups=pairs)
    near, far = map(list, zip(first_half, merged(1, w_far)))

    parts = []
    turn = at
    groups = [
        (w_pair, 2, lambda s, at: s),
        (w_far[None], 1, lambda s, at: 0),
        (w_far_pair, 1, lambda s, at: 1 - at[1] % 2),
    ]
    for weight, count, pick in groups:
        send, kept = project(turn, near, far, weight, count, pick)
        got = head_perm(send, 1)
        piece = struct((count,) + send.shape[3:], BF16)
        stay, to_y, to_x, to_xy = whole_call(split_kernel, at, [kept, got], [piece] * 4, "split", 2)
        turn = after(at, stay, *parts)
        diagonal = [((2 * i + j) * 4 + h, (2 * i + 1 - j) * 4 + (h ^ 2)) for i in range(4) for j in range(2) for h in range(4)]
        from_xy = lax.ppermute(to_xy, ("seq", "head"), diagonal)
        parts += [stay, head_perm(to_y, 2), swap(to_x), from_xy]
    (out,) = whole_call(
        place_kernel, at, parts, [struct((cols // 4, 8 * out_weight.shape[1]), BF16)], "place", 2)
    return out.reshape(cols // 4, 1, 8 * out_weight.shape[1])


def solution(mesh):
    in_specs = (P(None, "seq", None, "head"), P("head", "seq"))
    out_specs = P("head", "seq", None)
    small = mesh.shape["seq"] == 8 and mesh.shape["head"] == 4

    def body(qkv, out_weight):
        if small and qkv.shape[1] == 1:
            return body_eight(qkv, out_weight)
        return body_any(qkv, out_weight)

    return jax.shard_map(body, mesh=mesh, in_specs=in_specs, out_specs=out_specs, check_vma=False)
```

```python
import functools
import jax
import jax.numpy as jnp
from jax import lax
from jax.experimental import pallas as pl
from jax.experimental.pallas import tpu as pltpu
from jax.sharding import PartitionSpec as P

HEAD = 128
LOG2E = 1.4426950408889634
NEG = -1e30
QB = 128
VMEM = 20 * 1024 * 1024
F32, BF16 = jnp.float32, jnp.bfloat16


def shifted(shard, axis, by):
    size = lax.axis_size(axis)
    pairs = [(i, i + by) for i in range(size) if 0 <= i + by < size]
    return lax.ppermute(shard, axis, pairs)


def column_part(part):
    queries, keys_part, values = (part[0], part[1], part[2])
    rows = queries.shape[0]
    scale = queries.shape[-1] ** (-0.5)
    scores = (
        jnp.einsum("rchd,schd->chrs", queries, keys_part, preferred_element_type=jnp.float32)
        * scale
    )
    r_idx = lax.broadcasted_iota(jnp.int32, (rows, rows), 0)
    s_idx = lax.broadcasted_iota(jnp.int32, (rows, rows), 1)
    allowed = s_idx <= r_idx - 2
    masked = jnp.where(allowed, scores, jnp.float32(-1e30))
    peak = jnp.max(masked, axis=-1)
    weights = jnp.where(allowed, jnp.exp(masked - peak[..., None]), jnp.float32(0.0))
    total = jnp.maximum(jnp.sum(weights, axis=-1), jnp.float32(1.0))
    rounded = weights.astype(jnp.bfloat16)
    mixed = jnp.einsum("chrs,schd->rchd", rounded, values, preferred_element_type=jnp.float32)
    col_out = (mixed / jnp.transpose(total, (2, 0, 1))[..., None]).astype(jnp.bfloat16)
    col_lse = jnp.transpose(peak + jnp.log(total), (2, 0, 1))
    return (col_out, col_lse)


def row_part(local, previous, first_row):
    rows_dev, cols, heads_local, head_size = (
        local.shape[1],
        local.shape[2],
        local.shape[3],
        local.shape[4],
    )
    scale = head_size ** (-0.5)
    keys_ext = jnp.concatenate([previous, local[1:3]], axis=1)
    key_idx = lax.broadcasted_iota(jnp.int32, (cols, 2 * cols), 1)
    query_idx = lax.broadcasted_iota(jnp.int32, (cols, 2 * cols), 0)

    def one_row(index):
        queries = lax.dynamic_index_in_dim(local[0], index, 0, keepdims=False)
        pair = keys_ext.reshape(2, 2 * cols, heads_local, head_size)
        scores = (
            jnp.einsum("qhd,khd->hqk", queries, pair[0], preferred_element_type=jnp.float32) * scale
        )
        allowed = (key_idx < cols) & (first_row + index > 0) | (key_idx >= cols) & (
            key_idx - cols <= query_idx
        )
        masked = jnp.where(allowed[None], scores, jnp.float32(-1e30))
        peak = jnp.max(masked, axis=-1)
        weights = jnp.where(allowed[None], jnp.exp(masked - peak[..., None]), jnp.float32(0.0))
        total = jnp.sum(weights, axis=-1)
        rounded = weights.astype(jnp.bfloat16)
        mixed = jnp.einsum("hqk,khd->qhd", rounded, pair[1], preferred_element_type=jnp.float32)
        return (mixed / jnp.transpose(total)[..., None], jnp.transpose(peak + jnp.log(total)))

    return lax.map(one_row, jnp.arange(rows_dev, dtype=jnp.int32))


def body_any(qkv, out_weight):
    rows_dev, cols, features = (qkv.shape[1], qkv.shape[2], qkv.shape[3])
    head_size = HEAD
    heads_local = features // head_size
    local = qkv.reshape(3, rows_dev, cols, heads_local, head_size)
    previous = shifted(local[1:3, rows_dev - 1 : rows_dev], "seq", 1)
    first_row = lax.axis_index("seq") * rows_dev
    row_out, row_lse = row_part(local, previous, first_row)
    columns = lax.all_to_all(local, "seq", split_axis=2, concat_axis=1, tiled=True)
    col_part_out, col_part_lse = column_part(columns)
    col_out, col_lse = (
        lax.all_to_all(col_part_out, "seq", split_axis=0, concat_axis=1, tiled=True),
        lax.all_to_all(
            col_part_lse.astype(jnp.bfloat16), "seq", split_axis=0, concat_axis=1, tiled=True
        ).astype(col_part_lse.dtype),
    )
    top = jnp.maximum(row_lse, col_lse)
    left = jnp.exp(row_lse - top)
    right = jnp.exp(col_lse - top)
    attended = (left[..., None] * row_out + right[..., None] * col_out.astype(jnp.float32)) / (
        left + right
    )[..., None]
    attended = attended.astype(jnp.bfloat16).reshape(rows_dev, cols, features)
    terms = jnp.einsum(
        "rcf,fd->crd",
        attended,
        lax.all_gather(out_weight, "seq", axis=1, tiled=True),
        preferred_element_type=jnp.float32,
    )
    summed = lax.psum_scatter(terms.astype(jnp.bfloat16), "head", scatter_dimension=0, tiled=True)
    return summed


def dense_scores(q, k):
    return lax.dot_general(q, k, (((1,), (1,)), ((), ())), preferred_element_type=F32)


def col_scores(q, k):
    prod = q * k
    high = prod.astype(BF16)
    low = (prod - high.astype(F32)).astype(BF16)
    ones = jnp.ones((2 * HEAD, HEAD), BF16)
    return jnp.dot(jnp.concatenate([high, low], axis=1), ones, preferred_element_type=F32)


def with_ones(v):
    return jnp.concatenate([v, jnp.ones_like(v)], axis=1)


def attend(q, dense, cols, coef):
    rows = q.shape[0]
    scores = []
    for k, _, allowed in dense:
        s = dense_scores(q, k)
        scores.append(s if allowed is None else jnp.where(allowed, s, NEG))
    singles = []
    if cols:
        wide = q.astype(F32)
    for k, _, allowed in cols:
        c = col_scores(wide, k)
        singles.append(c if allowed is None else jnp.where(allowed, c, NEG))
    peak = None
    for s in scores:
        for j in range(s.shape[1] // HEAD):
            part = s[:, j * HEAD : (j + 1) * HEAD]
            peak = part if peak is None else jnp.maximum(peak, part)
    if peak is not None:
        peak = jnp.broadcast_to(jnp.max(peak, axis=1, keepdims=True), (rows, HEAD))
    for c in singles:
        peak = c if peak is None else jnp.maximum(peak, c)
    peak = peak * coef
    both = None
    for s, (_, v, _) in zip(scores, dense):
        tiled = jnp.concatenate([peak] * (s.shape[1] // HEAD), axis=1)
        p = jnp.exp2(s * coef - tiled).astype(BF16)
        term = jnp.dot(p, v, preferred_element_type=F32)
        both = term if both is None else both + term
    out = None if both is None else both[:, :HEAD]
    total = None if both is None else both[:, HEAD:]
    for c, (_, v, _) in zip(singles, cols):
        w = jnp.exp2(c * coef - peak)
        total = w if total is None else total + w
        out = w * v if out is None else out + w * v
    return out / total, peak + jnp.log2(total)


def lse_rows(even, odd):
    lane = lax.broadcasted_iota(jnp.int32, (HEAD, HEAD), 1)
    evens, odds = [], []
    for t in range(even.shape[0] // HEAD):
        block = slice(t * HEAD, (t + 1) * HEAD)
        turned = jnp.transpose(jnp.where(lane == 0, even[block], odd[block]))
        evens.append(turned[0:1])
        odds.append(turned[1:2])
    return evens, odds


def put_lse(ref, base, evens, odds):
    rows = jnp.concatenate(evens + odds, axis=0)
    pad = (-rows.shape[0]) % 16
    if pad:
        rows = jnp.concatenate([rows, jnp.zeros((pad, HEAD), F32)], axis=0)
    count = rows.shape[0]
    for piece in range(3):
        part = rows.astype(BF16)
        ref[pl.ds(base + piece * count, count), :] = part
        rows = rows - part.astype(F32)


def get_lse(ref, base, cols):
    blocks = cols // HEAD
    count = -(-2 * blocks // 16) * 16
    rows = sum(ref[pl.ds(base + piece * count, count), :].astype(F32) for piece in range(3))
    turned = [
        jnp.transpose(jnp.broadcast_to(rows[t : t + 1], (HEAD, HEAD))) for t in range(2 * blocks)
    ]
    return jnp.concatenate(turned[:blocks], axis=0), jnp.concatenate(turned[blocks:], axis=0)


def lse_height(cols):
    return 3 * (-(-2 * (cols // HEAD) // 16) * 16)


def stacked(refs):
    return [ref[i] for ref in refs for i in range(ref.shape[0])]


def own_kernel(coef, cols, at, q, kv_m, kv_o, *refs):
    x, z = at[0], at[1]
    below = z == 1
    block = 256
    tri = lax.broadcasted_iota(jnp.int32, (block, block), 1) <= lax.broadcasted_iota(
        jnp.int32, (block, block), 0
    )
    first = x == 0
    k_e, k_o = jnp.where(first, kv_m[0], kv_o[0]), jnp.where(first, kv_o[0], kv_m[0])
    v_e, v_o = jnp.where(first, kv_m[1], kv_o[1]), jnp.where(first, kv_o[1], kv_m[1])
    v_e, v_o = with_ones(v_e), with_ones(v_o)
    *low, out = refs
    m_k, m_v, o_k, o_v = stacked(low)
    lk_e, lk_o = jnp.where(first, m_k, o_k), jnp.where(first, o_k, m_k)
    lv_e, lv_o = jnp.where(first, m_v, o_v), jnp.where(first, o_v, m_v)
    lv_o1 = with_ones(lv_o)
    evens, odds = [], []
    for part in range(cols // block):
        a, b = part * block, (part + 1) * block
        mine = slice(a, b)
        col_e = (lk_e[mine].astype(F32), lv_e[mine].astype(F32), below)
        col_o = (lk_o[mine].astype(F32), lv_o[mine].astype(F32), below)

        def causal(k, v):
            blocks = [(k[a:b], v[a:b], tri)]
            return blocks if part == 0 else [(k[:a], v[:a], None)] + blocks

        o1, l1 = attend(q[0, mine], causal(k_e, v_e) + [(lk_o, lv_o1, below)], [col_e], coef)
        o2, l2 = attend(q[1, mine], causal(k_o, v_o) + [(k_e, v_e, None)], [col_e, col_o], coef)
        out[mine] = o1.astype(BF16)
        out[cols + a : cols + b] = o2.astype(BF16)
        e, o = lse_rows(l1, l2)
        evens, odds = evens + e, odds + o
    put_lse(out, 2 * cols, evens, odds)


def upper_kernel(coef, cols, at, qa, qb, kv_m, kv_o, *refs):
    x, z = at[0], at[1]
    below = z == 1
    first = x == 0
    block = 256
    k_e, k_o = jnp.where(first, kv_m[0], kv_o[0]), jnp.where(first, kv_o[0], kv_m[0])
    v_e, v_o = jnp.where(first, kv_m[1], kv_o[1]), jnp.where(first, kv_o[1], kv_m[1])
    v_o1 = with_ones(v_o)
    *low, out_a, out_b = refs
    lows = stacked(low)
    rows_a, rows_b = ([], []), ([], [])
    for index in range(cols // block):
        a, b = index * block, (index + 1) * block
        mine = slice(a, b)
        m_k, m_v, o_k, o_v = (part[mine].astype(F32) for part in lows)
        ce = (k_e[mine].astype(F32), v_e[mine].astype(F32), None)
        co = (k_o[mine].astype(F32), v_o[mine].astype(F32), None)
        low = [(m_k, m_v, below), (o_k, o_v, below)]
        for q, out, rows, dense, singles in (
            (qa, out_a, rows_a, [(k_o, v_o1, None)], [ce]),
            (qb, out_b, rows_b, [], [ce, co]),
        ):
            o1, l1 = attend(q[0, mine], dense, singles + low, coef)
            o2, l2 = attend(q[1, mine], [], [ce, co] + low, coef)
            out[mine] = o1.astype(BF16)
            out[cols + a : cols + b] = o2.astype(BF16)
            e, o = lse_rows(l1, l2)
            rows[0].extend(e)
            rows[1].extend(o)
    put_lse(out_a, 2 * cols, *rows_a)
    put_lse(out_b, 2 * cols, *rows_b)


def merge_kernel(cols, at, own, oa, ob, out):
    z = at[1]
    own_l, a_l, b_l = (get_lse(ref, 2 * cols, cols) for ref in (own, oa, ob))
    for row in range(2):
        tokens = slice(row * cols, (row + 1) * cols)
        l0 = own_l[row]
        l1 = jnp.where(z >= 2, a_l[row], NEG)
        l2 = jnp.where(z >= 3, b_l[row], NEG)
        top = jnp.maximum(l0, jnp.maximum(l1, l2))
        w0, w1, w2 = jnp.exp2(l0 - top), jnp.exp2(l1 - top), jnp.exp2(l2 - top)
        mixed = w0 * own[tokens].astype(F32) + w1 * oa[tokens].astype(F32) + w2 * ob[tokens].astype(F32)
        out[row] = (mixed / (w0 + w1 + w2)).astype(BF16)


def cost(us):
    return pl.CostEstimate(flops=int(us * 0.1e9), bytes_accessed=1024, transcendentals=0)


def head_call(kernel, at, args, outs, heads, name, us):
    def spec(shape, start=0):
        lead = len(shape) - 1
        return pl.BlockSpec(tuple(shape[:-1]) + (HEAD,), lambda h, at: (0,) * lead + (start + h,))

    return pl.pallas_call(
        kernel,
        out_shape=outs,
        grid_spec=pltpu.PrefetchScalarGridSpec(
            num_scalar_prefetch=1,
            grid=(heads,),
            in_specs=[spec(a.shape, start) for a, start in args],
            out_specs=[spec(o.shape) for o in outs],
        ),
        compiler_params=pltpu.CompilerParams(vmem_limit_bytes=VMEM),
        cost_estimate=cost(us),
        name=name,
    )(at, *(a for a, _ in args))


def project_kernel(chunks, at, *refs):
    x, core = at[0], at[2]
    near, far = refs[:chunks], refs[chunks : 2 * chunks]
    weight, send, keep = refs[2 * chunks :]
    tokens, width = near[0].shape[3:]
    half = width * chunks
    top = weight[0, pl.ds(pl.multiple_of(x * half, half), half)]
    bottom = weight[0, pl.ds(pl.multiple_of((1 - x) * half, half), half)]
    for who, out in ((1 - core, send), (core, keep)):

        def rows(ref):
            return jnp.concatenate([ref[r, y, who] for y in range(2) for r in range(2)], axis=0)

        left = jnp.concatenate([rows(ref) for ref in near], axis=1)
        right = jnp.concatenate([rows(ref) for ref in far], axis=1)
        c = jnp.dot(left, top, preferred_element_type=F32) + jnp.dot(right, bottom, preferred_element_type=F32)
        out[0] = c.astype(BF16).reshape(2, 2, tokens, weight.shape[2])


def project(at, near, far, weight, count, pick):
    _, cols, width = near[0].shape
    shape = (2, 2, 2, cols // 4, width)
    args = [a.reshape(shape) for a in near + far]
    _, depth, out_width = weight.shape
    out = jax.ShapeDtypeStruct((count, 2, 2, cols // 4, out_width), BF16)
    out_spec = pl.BlockSpec((1,) + out.shape[1:], lambda s, at: (s, 0, 0, 0, 0))
    return pl.pallas_call(
        functools.partial(project_kernel, len(near)),
        out_shape=[out, out],
        grid_spec=pltpu.PrefetchScalarGridSpec(
            num_scalar_prefetch=1,
            grid=(count,),
            in_specs=[pl.BlockSpec(shape, lambda s, at: (0,) * 5)] * len(args)
            + [pl.BlockSpec((1, depth, out_width), lambda s, at: (pick(s, at), 0, 0))],
            out_specs=[out_spec, out_spec],
        ),
        compiler_params=pltpu.CompilerParams(vmem_limit_bytes=VMEM),
        cost_estimate=cost(2 * count),
        name="project",
    )(at, *args, weight)


def whole_call(kernel, at, args, outs, name, us):
    return pl.pallas_call(
        kernel,
        out_shape=outs,
        in_specs=[pl.BlockSpec(memory_space=pltpu.SMEM)] + [pl.BlockSpec(memory_space=pltpu.VMEM)] * len(args),
        out_specs=[pl.BlockSpec(memory_space=pltpu.VMEM)] * len(outs),
        compiler_params=pltpu.CompilerParams(vmem_limit_bytes=VMEM),
        cost_estimate=cost(us),
        name=name,
    )(at, *args)


def total(a, b):
    return (a.astype(F32) + b.astype(F32)).astype(BF16)


def split_kernel(at, kept, got, stay, to_y, to_x, to_xy):
    x, y = at[0], at[3]
    for s in range(kept.shape[0]):
        for out, yy, xx in ((to_xy, 1 - y, 1 - x), (to_y, 1 - y, x), (to_x, y, 1 - x), (stay, y, x)):
            out[s] = total(kept[s, yy, xx], got[s, yy, xx])


def place_kernel(at, *refs):
    x, z, out = at[0], at[1], refs[-1]
    layers = [z - z % 2, z - z % 2 + 1, (z + 2) % 4, 3 - z]
    for stay, from_y, from_x, from_xy in zip(*(refs[i:-1:4] for i in range(4))):
        width = stay.shape[-1]
        for s in range(stay.shape[0]):
            base = 2 * layers.pop(0)
            mine = pl.ds(pl.multiple_of((base + x) * width, width), width)
            theirs = pl.ds(pl.multiple_of((base + 1 - x) * width, width), width)
            out[:, mine] = total(stay[s], from_y[s])
            out[:, theirs] = total(from_x[s], from_xy[s])


def after(value, *earlier):
    return lax.optimization_barrier((value, earlier))[0]


def body_eight(qkv, out_weight):
    _, _, cols, features = qkv.shape
    half = features // 2
    chunks = 2
    width = half // chunks
    heads = width // HEAD
    coef = HEAD ** (-0.5) * LOG2E
    me = lax.axis_index("seq")
    who = lax.axis_index("head")
    z, x, core, y = me // 2, me % 2, who % 2, who // 2
    at = jnp.stack([x, z, core, y]).astype(jnp.int32)
    local = qkv.reshape(3, cols, features)
    first = x == 0

    def seq_perm(array, *layers, cross=False):
        pairs = [(2 * a + i, 2 * b + (1 - i if cross else i)) for a, b in layers for i in range(2)]
        return lax.ppermute(array, "seq", pairs)

    def swap(array):
        return seq_perm(array, (0, 0), (1, 1), (2, 2), (3, 3), cross=True)

    def head_perm(array, flip):
        return lax.ppermute(array, "head", [(i, i ^ flip) for i in range(4)])

    def lanes(lo, hi, part):
        return lax.dynamic_slice(local, (lo, 0, part * half), (hi - lo, cols, half))

    mine, other = lanes(0, 1, x), swap(lanes(0, 1, 1 - x))
    q = jnp.concatenate([jnp.where(first, mine, other), jnp.where(first, other, mine)])
    kv_m, kv_give = lanes(1, 3, x), lanes(1, 3, 1 - x)
    low_m = seq_perm(kv_m, (0, 1))
    low_o = seq_perm(kv_give, (0, 1), cross=True)
    kv_o = swap(kv_give)
    qa = seq_perm(q, (2, 1), (3, 2))
    qb = seq_perm(q, (3, 1))

    struct = jax.ShapeDtypeStruct
    partial = struct((2 * cols + lse_height(cols), width), BF16)
    oa, ob = [], []
    previous = at
    for c in range(chunks):
        a, b = head_call(
            functools.partial(upper_kernel, coef, cols), previous,
            [(array, c * heads) for array in (qa, qb, kv_m, kv_o, low_m, low_o)],
            [partial] * 2, heads, "upper_rows", 4)
        previous = after(at, a)
        oa.append(seq_perm(a, (1, 2), (2, 3)))
        ob.append(seq_perm(b, (1, 3)))
    (own,) = head_call(
        functools.partial(own_kernel, coef, cols), previous,
        [(array, 0) for array in (q, kv_m, kv_o, low_m, low_o)],
        [struct((partial.shape[0], half), BF16)], chunks * heads, "own_rows", 8)

    pairs = [[0, 2], [1, 3], [4, 6], [5, 7]]
    w_pair = lax.all_gather(after(out_weight, low_m, low_o), "seq", axis_index_groups=pairs)
    w_up = seq_perm(after(out_weight, low_m, low_o), (0, 2), (1, 3))
    w_down = seq_perm(after(out_weight, qa, qb), (2, 0), (3, 1))

    def merged(c, earlier):
        (a,) = head_call(
            functools.partial(merge_kernel, cols), after(at, earlier), [(own, c * heads), (oa[c], 0), (ob[c], 0)],
            [struct((2, cols, width), BF16)], heads, "merge", 2)
        return a, swap(a)

    first_half = merged(0, previous)
    w_far = jnp.where(z >= 2, w_up, after(w_down, first_half[0], own))
    near, far = map(list, zip(first_half, merged(1, w_far)))
    w_other = seq_perm(w_far, (0, 1), (1, 0), (2, 3), (3, 2))

    parts = []
    turn = at
    groups = [
        (w_pair, 2, lambda s, at: s),
        (w_far[None], 1, lambda s, at: 0),
        (w_other[None], 1, lambda s, at: 0),
    ]
    for weight, count, pick in groups:
        send, kept = project(turn, near, far, weight, count, pick)
        got = head_perm(send, 1)
        piece = struct((count,) + send.shape[3:], BF16)
        stay, to_y, to_x, to_xy = whole_call(split_kernel, at, [kept, got], [piece] * 4, "split", 2)
        turn = after(at, stay, *parts)
        diagonal = [((2 * i + j) * 4 + h, (2 * i + 1 - j) * 4 + (h ^ 2)) for i in range(4) for j in range(2) for h in range(4)]
        from_xy = lax.ppermute(to_xy, ("seq", "head"), diagonal)
        parts += [stay, head_perm(to_y, 2), swap(to_x), from_xy]
    (out,) = whole_call(
        place_kernel, at, parts, [struct((cols // 4, 8 * out_weight.shape[1]), BF16)], "place", 2)
    return out.reshape(cols // 4, 1, 8 * out_weight.shape[1])


def solution(mesh):
    in_specs = (P(None, "seq", None, "head"), P("head", "seq"))
    out_specs = P("head", "seq", None)
    small = mesh.shape["seq"] == 8 and mesh.shape["head"] == 4

    def body(qkv, out_weight):
        if small and qkv.shape[1] == 1:
            return body_eight(qkv, out_weight)
        return body_any(qkv, out_weight)

    return jax.shard_map(body, mesh=mesh, in_specs=in_specs, out_specs=out_specs, check_vma=False)
```

```python
import functools
import jax
import jax.numpy as jnp
from jax import lax
from jax.experimental import pallas as pl
from jax.experimental.pallas import tpu as pltpu
from jax.sharding import PartitionSpec as P

HEAD = 128
LOG2E = 1.4426950408889634
NEG = -1e30
QB = 128
VMEM = 24 * 1024 * 1024
F32, BF16 = jnp.float32, jnp.bfloat16


def shifted(shard, axis, by):
    size = lax.axis_size(axis)
    pairs = [(i, i + by) for i in range(size) if 0 <= i + by < size]
    return lax.ppermute(shard, axis, pairs)


def column_part(part):
    queries, keys_part, values = (part[0], part[1], part[2])
    rows = queries.shape[0]
    scale = queries.shape[-1] ** (-0.5)
    scores = (
        jnp.einsum("rchd,schd->chrs", queries, keys_part, preferred_element_type=jnp.float32)
        * scale
    )
    r_idx = lax.broadcasted_iota(jnp.int32, (rows, rows), 0)
    s_idx = lax.broadcasted_iota(jnp.int32, (rows, rows), 1)
    allowed = s_idx <= r_idx - 2
    masked = jnp.where(allowed, scores, jnp.float32(-1e30))
    peak = jnp.max(masked, axis=-1)
    weights = jnp.where(allowed, jnp.exp(masked - peak[..., None]), jnp.float32(0.0))
    total = jnp.maximum(jnp.sum(weights, axis=-1), jnp.float32(1.0))
    rounded = weights.astype(jnp.bfloat16)
    mixed = jnp.einsum("chrs,schd->rchd", rounded, values, preferred_element_type=jnp.float32)
    col_out = (mixed / jnp.transpose(total, (2, 0, 1))[..., None]).astype(jnp.bfloat16)
    col_lse = jnp.transpose(peak + jnp.log(total), (2, 0, 1))
    return (col_out, col_lse)


def row_part(local, previous, first_row):
    rows_dev, cols, heads_local, head_size = (
        local.shape[1],
        local.shape[2],
        local.shape[3],
        local.shape[4],
    )
    scale = head_size ** (-0.5)
    keys_ext = jnp.concatenate([previous, local[1:3]], axis=1)
    key_idx = lax.broadcasted_iota(jnp.int32, (cols, 2 * cols), 1)
    query_idx = lax.broadcasted_iota(jnp.int32, (cols, 2 * cols), 0)

    def one_row(index):
        queries = lax.dynamic_index_in_dim(local[0], index, 0, keepdims=False)
        pair = keys_ext.reshape(2, 2 * cols, heads_local, head_size)
        scores = (
            jnp.einsum("qhd,khd->hqk", queries, pair[0], preferred_element_type=jnp.float32) * scale
        )
        allowed = (key_idx < cols) & (first_row + index > 0) | (key_idx >= cols) & (
            key_idx - cols <= query_idx
        )
        masked = jnp.where(allowed[None], scores, jnp.float32(-1e30))
        peak = jnp.max(masked, axis=-1)
        weights = jnp.where(allowed[None], jnp.exp(masked - peak[..., None]), jnp.float32(0.0))
        total = jnp.sum(weights, axis=-1)
        rounded = weights.astype(jnp.bfloat16)
        mixed = jnp.einsum("hqk,khd->qhd", rounded, pair[1], preferred_element_type=jnp.float32)
        return (mixed / jnp.transpose(total)[..., None], jnp.transpose(peak + jnp.log(total)))

    return lax.map(one_row, jnp.arange(rows_dev, dtype=jnp.int32))


def body_any(qkv, out_weight):
    rows_dev, cols, features = (qkv.shape[1], qkv.shape[2], qkv.shape[3])
    head_size = HEAD
    heads_local = features // head_size
    local = qkv.reshape(3, rows_dev, cols, heads_local, head_size)
    previous = shifted(local[1:3, rows_dev - 1 : rows_dev], "seq", 1)
    first_row = lax.axis_index("seq") * rows_dev
    row_out, row_lse = row_part(local, previous, first_row)
    columns = lax.all_to_all(local, "seq", split_axis=2, concat_axis=1, tiled=True)
    col_part_out, col_part_lse = column_part(columns)
    col_out, col_lse = (
        lax.all_to_all(col_part_out, "seq", split_axis=0, concat_axis=1, tiled=True),
        lax.all_to_all(
            col_part_lse.astype(jnp.bfloat16), "seq", split_axis=0, concat_axis=1, tiled=True
        ).astype(col_part_lse.dtype),
    )
    top = jnp.maximum(row_lse, col_lse)
    left = jnp.exp(row_lse - top)
    right = jnp.exp(col_lse - top)
    attended = (left[..., None] * row_out + right[..., None] * col_out.astype(jnp.float32)) / (
        left + right
    )[..., None]
    attended = attended.astype(jnp.bfloat16).reshape(rows_dev, cols, features)
    terms = jnp.einsum(
        "rcf,fd->crd",
        attended,
        lax.all_gather(out_weight, "seq", axis=1, tiled=True),
        preferred_element_type=jnp.float32,
    )
    summed = lax.psum_scatter(terms.astype(jnp.bfloat16), "head", scatter_dimension=0, tiled=True)
    return summed


def dense_scores(q, k):
    return lax.dot_general(q, k, (((1,), (1,)), ((), ())), preferred_element_type=F32)


def col_scores(q, k):
    prod = q * k
    high = prod.astype(BF16)
    low = (prod - high.astype(F32)).astype(BF16)
    ones = jnp.ones((2 * HEAD, HEAD), BF16)
    return jnp.dot(jnp.concatenate([high, low], axis=1), ones, preferred_element_type=F32)


def with_ones(v):
    return jnp.concatenate([v, jnp.ones_like(v)], axis=1)


def attend(q, dense, cols, coef):
    rows = q.shape[0]
    scores = []
    for k, _, allowed in dense:
        s = dense_scores(q, k)
        scores.append(s if allowed is None else jnp.where(allowed, s, NEG))
    singles = []
    if cols:
        wide = q.astype(F32)
    for k, _, allowed in cols:
        c = col_scores(wide, k)
        singles.append(c if allowed is None else jnp.where(allowed, c, NEG))
    peak = None
    for s in scores:
        for j in range(s.shape[1] // HEAD):
            part = s[:, j * HEAD : (j + 1) * HEAD]
            peak = part if peak is None else jnp.maximum(peak, part)
    if peak is not None:
        peak = jnp.broadcast_to(jnp.max(peak, axis=1, keepdims=True), (rows, HEAD))
    for c in singles:
        peak = c if peak is None else jnp.maximum(peak, c)
    peak = peak * coef
    both = None
    for s, (_, v, _) in zip(scores, dense):
        tiled = jnp.concatenate([peak] * (s.shape[1] // HEAD), axis=1)
        p = jnp.exp2(s * coef - tiled).astype(BF16)
        term = jnp.dot(p, v, preferred_element_type=F32)
        both = term if both is None else both + term
    out = None if both is None else both[:, :HEAD]
    total = None if both is None else both[:, HEAD:]
    for c, (_, v, _) in zip(singles, cols):
        w = jnp.exp2(c * coef - peak)
        total = w if total is None else total + w
        out = w * v if out is None else out + w * v
    return out / total, peak + jnp.log2(total)


def lse_rows(even, odd):
    lane = lax.broadcasted_iota(jnp.int32, (HEAD, HEAD), 1)
    evens, odds = [], []
    for t in range(even.shape[0] // HEAD):
        block = slice(t * HEAD, (t + 1) * HEAD)
        turned = jnp.transpose(jnp.where(lane == 0, even[block], odd[block]))
        evens.append(turned[0:1])
        odds.append(turned[1:2])
    return evens, odds


def put_lse(ref, base, evens, odds):
    rows = jnp.concatenate(evens + odds, axis=0)
    pad = (-rows.shape[0]) % 16
    if pad:
        rows = jnp.concatenate([rows, jnp.zeros((pad, HEAD), F32)], axis=0)
    count = rows.shape[0]
    for piece in range(3):
        part = rows.astype(BF16)
        ref[pl.ds(base + piece * count, count), :] = part
        rows = rows - part.astype(F32)


def get_lse(ref, base, cols):
    blocks = cols // HEAD
    count = -(-2 * blocks // 16) * 16
    rows = sum(ref[pl.ds(base + piece * count, count), :].astype(F32) for piece in range(3))
    turned = [
        jnp.transpose(jnp.broadcast_to(rows[t : t + 1], (HEAD, HEAD))) for t in range(2 * blocks)
    ]
    return jnp.concatenate(turned[:blocks], axis=0), jnp.concatenate(turned[blocks:], axis=0)


def lse_height(cols):
    return 3 * (-(-2 * (cols // HEAD) // 16) * 16)


def stacked(refs):
    return [ref[i] for ref in refs for i in range(ref.shape[0])]


def own_kernel(coef, cols, at, q_m, q_o, kv_m, kv_o, *refs):
    x, z = at[0], at[1]
    below = z == 1
    block = 256
    tri = lax.broadcasted_iota(jnp.int32, (block, block), 1) <= lax.broadcasted_iota(
        jnp.int32, (block, block), 0
    )
    first = x == 0
    k_e, k_o = jnp.where(first, kv_m[0], kv_o[0]), jnp.where(first, kv_o[0], kv_m[0])
    v_e, v_o = jnp.where(first, kv_m[1], kv_o[1]), jnp.where(first, kv_o[1], kv_m[1])
    v_e, v_o = with_ones(v_e), with_ones(v_o)
    *low, out = refs
    m_k, m_v, o_k, o_v = stacked(low)
    lk_e, lk_o = jnp.where(first, m_k, o_k), jnp.where(first, o_k, m_k)
    lv_e, lv_o = jnp.where(first, m_v, o_v), jnp.where(first, o_v, m_v)
    lv_o1 = with_ones(lv_o)
    q_e, q_o = jnp.where(first, q_m[0], q_o[0]), jnp.where(first, q_o[0], q_m[0])
    evens, odds = [], []
    for part in range(cols // block):
        a, b = part * block, (part + 1) * block
        mine = slice(a, b)
        col_e = (lk_e[mine].astype(F32), lv_e[mine].astype(F32), below)
        col_o = (lk_o[mine].astype(F32), lv_o[mine].astype(F32), below)

        def causal(k, v):
            blocks = [(k[a:b], v[a:b], tri)]
            return blocks if part == 0 else [(k[:a], v[:a], None)] + blocks

        o1, l1 = attend(q_e[mine], causal(k_e, v_e) + [(lk_o, lv_o1, below)], [col_e], coef)
        o2, l2 = attend(q_o[mine], causal(k_o, v_o) + [(k_e, v_e, None)], [col_e, col_o], coef)
        out[mine] = o1.astype(BF16)
        out[cols + a : cols + b] = o2.astype(BF16)
        e, o = lse_rows(l1, l2)
        evens, odds = evens + e, odds + o
    put_lse(out, 2 * cols, evens, odds)


def upper_kernel(coef, cols, at, qa_m, qa_o, qb_m, qb_o, kv_m, kv_o, *refs):
    x, z = at[0], at[1]
    below = z == 1
    first = x == 0
    block = 256
    k_e, k_o = jnp.where(first, kv_m[0], kv_o[0]), jnp.where(first, kv_o[0], kv_m[0])
    v_e, v_o = jnp.where(first, kv_m[1], kv_o[1]), jnp.where(first, kv_o[1], kv_m[1])
    v_o1 = with_ones(v_o)
    *low, out_a, out_b = refs
    lows = stacked(low)
    qa = jnp.where(first, qa_m[0], qa_o[0]), jnp.where(first, qa_o[0], qa_m[0])
    qb = jnp.where(first, qb_m[0], qb_o[0]), jnp.where(first, qb_o[0], qb_m[0])
    rows_a, rows_b = ([], []), ([], [])
    for index in range(cols // block):
        a, b = index * block, (index + 1) * block
        mine = slice(a, b)
        m_k, m_v, o_k, o_v = (part[mine].astype(F32) for part in lows)
        ce = (k_e[mine].astype(F32), v_e[mine].astype(F32), None)
        co = (k_o[mine].astype(F32), v_o[mine].astype(F32), None)
        low = [(m_k, m_v, below), (o_k, o_v, below)]
        for q, out, rows, dense, singles in (
            (qa, out_a, rows_a, [(k_o, v_o1, None)], [ce]),
            (qb, out_b, rows_b, [], [ce, co]),
        ):
            o1, l1 = attend(q[0][mine], dense, singles + low, coef)
            o2, l2 = attend(q[1][mine], [], [ce, co] + low, coef)
            out[mine] = o1.astype(BF16)
            out[cols + a : cols + b] = o2.astype(BF16)
            e, o = lse_rows(l1, l2)
            rows[0].extend(e)
            rows[1].extend(o)
    put_lse(out_a, 2 * cols, *rows_a)
    put_lse(out_b, 2 * cols, *rows_b)


def merge_kernel(cols, at, own, oa, ob, out):
    z = at[1]
    own_l, a_l, b_l = (get_lse(ref, 2 * cols, cols) for ref in (own, oa, ob))
    for row in range(2):
        tokens = slice(row * cols, (row + 1) * cols)
        l0 = own_l[row]
        l1 = jnp.where(z >= 2, a_l[row], NEG)
        l2 = jnp.where(z >= 3, b_l[row], NEG)
        top = jnp.maximum(l0, jnp.maximum(l1, l2))
        w0, w1, w2 = jnp.exp2(l0 - top), jnp.exp2(l1 - top), jnp.exp2(l2 - top)
        mixed = w0 * own[tokens].astype(F32) + w1 * oa[tokens].astype(F32) + w2 * ob[tokens].astype(F32)
        out[row] = (mixed / (w0 + w1 + w2)).astype(BF16)


def cost(us):
    return pl.CostEstimate(flops=int(us * 1e8), bytes_accessed=1024, transcendentals=0)


def head_call(kernel, at, args, outs, heads, name, us):
    def spec(shape, start=0):
        lead = len(shape) - 1
        return pl.BlockSpec(tuple(shape[:-1]) + (HEAD,), lambda h, at: (0,) * lead + (start + h,))

    return pl.pallas_call(
        kernel,
        out_shape=outs,
        grid_spec=pltpu.PrefetchScalarGridSpec(
            num_scalar_prefetch=1,
            grid=(heads,),
            in_specs=[spec(a.shape, start) for a, start in args],
            out_specs=[spec(o.shape) for o in outs],
        ),
        compiler_params=pltpu.CompilerParams(vmem_limit_bytes=VMEM),
        cost_estimate=cost(us),
        name=name,
    )(at, *(a for a, _ in args))


def project_kernel(chunks, at, *refs):
    x, core = at[0], at[2]
    near, far = refs[:chunks], refs[chunks : 2 * chunks]
    weights, send, keep = refs[2 * chunks : -2], refs[-2], refs[-1]
    tokens = near[0].shape[3]
    half = sum(ref.shape[4] for ref in near)
    for who, out in ((1 - core, send), (core, keep)):

        def rows(ref):
            return jnp.concatenate([ref[r, y, who] for y in range(2) for r in range(2)], axis=0)

        left = jnp.concatenate([rows(ref) for ref in near], axis=1)
        right = jnp.concatenate([rows(ref) for ref in far], axis=1)
        for s, weight in enumerate(weights):
            top = weight[0, pl.ds(pl.multiple_of(x * half, half), half)]
            bottom = weight[0, pl.ds(pl.multiple_of((1 - x) * half, half), half)]
            c = jnp.dot(left, top, preferred_element_type=F32) + jnp.dot(right, bottom, preferred_element_type=F32)
            out[s] = c.astype(BF16).reshape(2, 2, tokens, weight.shape[2])


def project(at, near, far, weights):
    cols = near[0].shape[1]
    args = [a.reshape(2, 2, 2, cols // 4, a.shape[2]) for a in near + far]
    _, depth, out_width = weights[0][0].shape
    out = jax.ShapeDtypeStruct((len(weights), 2, 2, cols // 4, out_width), BF16)

    def weight_spec(pick):
        return pl.BlockSpec((1, depth, out_width), lambda s, at: (pick(at), 0, 0))

    def whole(shape):
        return pl.BlockSpec(shape, lambda s, at: (0,) * len(shape))

    return pl.pallas_call(
        functools.partial(project_kernel, len(near)),
        out_shape=[out, out],
        grid_spec=pltpu.PrefetchScalarGridSpec(
            num_scalar_prefetch=1,
            grid=(1,),
            in_specs=[whole(a.shape) for a in args] + [weight_spec(pick) for _, pick in weights],
            out_specs=[whole(out.shape)] * 2,
        ),
        compiler_params=pltpu.CompilerParams(vmem_limit_bytes=VMEM),
        cost_estimate=cost(2 * len(weights)),
        name="project",
    )(at, *args, *(w for w, _ in weights))


def whole_call(kernel, at, args, outs, name, us):
    return pl.pallas_call(
        kernel,
        out_shape=outs,
        in_specs=[pl.BlockSpec(memory_space=pltpu.SMEM)] + [pl.BlockSpec(memory_space=pltpu.VMEM)] * len(args),
        out_specs=[pl.BlockSpec(memory_space=pltpu.VMEM)] * len(outs),
        compiler_params=pltpu.CompilerParams(vmem_limit_bytes=VMEM),
        cost_estimate=cost(us),
        name=name,
    )(at, *args)


def total(a, b):
    return (a.astype(F32) + b.astype(F32)).astype(BF16)


def split_kernel(at, kept, got, stay, to_y, to_x, to_xy):
    x, y = at[0], at[3]
    for s in range(kept.shape[0]):
        for out, yy, xx in ((to_xy, 1 - y, 1 - x), (to_y, 1 - y, x), (to_x, y, 1 - x), (stay, y, x)):
            out[s] = total(kept[s, yy, xx], got[s, yy, xx])


def place_kernel(at, *refs):
    x, z, out = at[0], at[1], refs[-1]
    layers = [z, z + 1 - 2 * (z % 2), (z + 2) % 4, 3 - z]
    for stay, from_y, from_x, from_xy in zip(*(refs[i:-1:4] for i in range(4))):
        width = stay.shape[-1]
        for s in range(stay.shape[0]):
            base = 2 * layers.pop(0)
            mine = pl.ds(pl.multiple_of((base + x) * width, width), width)
            theirs = pl.ds(pl.multiple_of((base + 1 - x) * width, width), width)
            out[:, mine] = total(stay[s], from_y[s])
            out[:, theirs] = total(from_x[s], from_xy[s])


def after(value, *earlier):
    return lax.optimization_barrier((value, earlier))[0]


def body_eight(qkv, out_weight):
    _, _, cols, features = qkv.shape
    half = features // 2
    chunks = 2
    width = half // chunks
    heads = width // HEAD
    coef = HEAD ** (-0.5) * LOG2E
    me = lax.axis_index("seq")
    who = lax.axis_index("head")
    z, x, core, y = me // 2, me % 2, who % 2, who // 2
    at = jnp.stack([x, z, core, y]).astype(jnp.int32)
    local = qkv.reshape(3, cols, features)
    first = x == 0

    def seq_perm(array, *layers, cross=False):
        pairs = [(2 * a + i, 2 * b + (1 - i if cross else i)) for a, b in layers for i in range(2)]
        return lax.ppermute(array, "seq", pairs)

    def swap(array):
        return seq_perm(array, (0, 0), (1, 1), (2, 2), (3, 3), cross=True)

    def head_perm(array, flip):
        return lax.ppermute(array, "head", [(i, i ^ flip) for i in range(4)])

    def lanes(lo, hi, part, source=local):
        return lax.dynamic_slice(source, (lo, 0, part * half), (hi - lo, cols, half))

    down, two_down = [(2, 1), (3, 2)], [(3, 1)]
    q_m = lanes(0, 1, x)
    q_o = swap(lanes(0, 1, 1 - x))
    qs = [seq_perm(q_m, *down), None, seq_perm(q_m, *two_down), None]
    kv_m, kv_give = lanes(1, 3, x), lanes(1, 3, 1 - x)
    block = out_weight.reshape(kv_m.shape)
    low_m = seq_perm(jnp.where(z == 0, kv_m, block), (0, 1), (1, 3))
    pairs = [(i, 2 + 1 - i) for i in range(2)] + [(2 + i, i) for i in range(2)] + [(4 + i, 6 + i) for i in range(2)]
    low_o = lax.ppermute(jnp.where(z == 0, kv_give, block), "seq", pairs)
    low = [low_m, low_o]
    kv_o = swap(after(kv_give, q_o))
    qs[1], qs[3] = seq_perm(q_o, *down), seq_perm(q_o, *two_down)
    w_second = seq_perm(after(out_weight, *qs), (0, 2))

    struct = jax.ShapeDtypeStruct
    partial = struct((2 * cols + lse_height(cols), width), BF16)
    oa, ob, own = [], [], []
    turn = at
    kvs = [kv_m, kv_o, low_m, low_o]
    for c in range(chunks):
        a, b = head_call(
            functools.partial(upper_kernel, coef, cols), turn, [(a, c * heads) for a in qs + kvs],
            [partial] * 2, heads, "upper_rows", 4)
        turn = after(at, a)
        oa.append(seq_perm(a, (1, 2), (2, 3)))
        ob.append(seq_perm(b, (1, 3)))
    for c in range(chunks):
        (mine,) = head_call(
            functools.partial(own_kernel, coef, cols), turn, [(a, c * heads) for a in [q_m, q_o] + kvs],
            [partial], heads, "own_rows", 4)
        own.append(mine)
        turn = after(at, mine, w_second)

    w_down = seq_perm(after(out_weight, *qs), (2, 0), (3, 1))
    w_near = seq_perm(after(out_weight, own[0]), (0, 1), (3, 2))
    w_near = jnp.where((z == 0) | (z == 3), low_o.reshape(out_weight.shape), w_near)

    def merged(c, earlier):
        (a,) = head_call(
            functools.partial(merge_kernel, cols), after(at, earlier), [(a[c], 0) for a in (own, oa, ob)],
            [struct((2, cols, width), BF16)], heads, "merge", 2)
        return a, swap(a)

    first_half = merged(0, own[1])
    w_far = jnp.where(
        z >= 2, jnp.where(z == 2, w_second, low_m.reshape(out_weight.shape)), after(w_down, first_half[0], own[1]))
    near, far = map(list, zip(first_half, merged(1, (w_far, first_half[1]))))
    w_other = seq_perm(w_far, (0, 1), (1, 0), (2, 3), (3, 2))

    parts = []
    turn = after(at, w_other)
    for weights in (
        [out_weight, w_near],
        [w_far, w_other],
    ):
        send, kept = project(turn, near, far, [(w[None], lambda at: 0) for w in weights])
        got = head_perm(send, 1)
        piece = struct(send.shape[:1] + send.shape[3:], BF16)
        stay, to_y, to_x, to_xy = whole_call(split_kernel, at, [kept, got], [piece] * 4, "split", 2)
        turn = after(at, stay)
        diagonal = [((2 * i + j) * 4 + h, (2 * i + 1 - j) * 4 + (h ^ 2)) for i in range(4) for j in range(2) for h in range(4)]
        from_xy = lax.ppermute(to_xy, ("seq", "head"), diagonal)
        parts += [stay, head_perm(to_y, 2), swap(to_x), from_xy]
    (out,) = whole_call(
        place_kernel, at, parts, [struct((cols // 4, 8 * out_weight.shape[1]), BF16)], "place", 2)
    return out.reshape(cols // 4, 1, 8 * out_weight.shape[1])


def solution(mesh):
    in_specs = (P(None, "seq", None, "head"), P("head", "seq"))
    out_specs = P("head", "seq", None)
    small = mesh.shape["seq"] == 8 and mesh.shape["head"] == 4

    def body(qkv, out_weight):
        if small and qkv.shape[1] == 1:
            return body_eight(qkv, out_weight)
        return body_any(qkv, out_weight)

    return jax.shard_map(body, mesh=mesh, in_specs=in_specs, out_specs=out_specs, check_vma=False)
```

```python
import functools
import jax
import jax.numpy as jnp
from jax import lax
from jax.experimental import pallas as pl
from jax.experimental.pallas import tpu as pltpu
from jax.sharding import PartitionSpec as P

HEAD = 128
LOG2E = 1.4426950408889634
NEG = -1e30
QB = 128
VMEM = 24 * 1024 * 1024
F32, BF16 = jnp.float32, jnp.bfloat16


def shifted(shard, axis, by):
    size = lax.axis_size(axis)
    pairs = [(i, i + by) for i in range(size) if 0 <= i + by < size]
    return lax.ppermute(shard, axis, pairs)


def column_part(part):
    queries, keys_part, values = (part[0], part[1], part[2])
    rows = queries.shape[0]
    scale = queries.shape[-1] ** (-0.5)
    scores = (
        jnp.einsum("rchd,schd->chrs", queries, keys_part, preferred_element_type=jnp.float32)
        * scale
    )
    r_idx = lax.broadcasted_iota(jnp.int32, (rows, rows), 0)
    s_idx = lax.broadcasted_iota(jnp.int32, (rows, rows), 1)
    allowed = s_idx <= r_idx - 2
    masked = jnp.where(allowed, scores, jnp.float32(-1e30))
    peak = jnp.max(masked, axis=-1)
    weights = jnp.where(allowed, jnp.exp(masked - peak[..., None]), jnp.float32(0.0))
    total = jnp.maximum(jnp.sum(weights, axis=-1), jnp.float32(1.0))
    rounded = weights.astype(jnp.bfloat16)
    mixed = jnp.einsum("chrs,schd->rchd", rounded, values, preferred_element_type=jnp.float32)
    col_out = (mixed / jnp.transpose(total, (2, 0, 1))[..., None]).astype(jnp.bfloat16)
    col_lse = jnp.transpose(peak + jnp.log(total), (2, 0, 1))
    return (col_out, col_lse)


def row_part(local, previous, first_row):
    rows_dev, cols, heads_local, head_size = (
        local.shape[1],
        local.shape[2],
        local.shape[3],
        local.shape[4],
    )
    scale = head_size ** (-0.5)
    keys_ext = jnp.concatenate([previous, local[1:3]], axis=1)
    key_idx = lax.broadcasted_iota(jnp.int32, (cols, 2 * cols), 1)
    query_idx = lax.broadcasted_iota(jnp.int32, (cols, 2 * cols), 0)

    def one_row(index):
        queries = lax.dynamic_index_in_dim(local[0], index, 0, keepdims=False)
        pair = keys_ext.reshape(2, 2 * cols, heads_local, head_size)
        scores = (
            jnp.einsum("qhd,khd->hqk", queries, pair[0], preferred_element_type=jnp.float32) * scale
        )
        allowed = (key_idx < cols) & (first_row + index > 0) | (key_idx >= cols) & (
            key_idx - cols <= query_idx
        )
        masked = jnp.where(allowed[None], scores, jnp.float32(-1e30))
        peak = jnp.max(masked, axis=-1)
        weights = jnp.where(allowed[None], jnp.exp(masked - peak[..., None]), jnp.float32(0.0))
        total = jnp.sum(weights, axis=-1)
        rounded = weights.astype(jnp.bfloat16)
        mixed = jnp.einsum("hqk,khd->qhd", rounded, pair[1], preferred_element_type=jnp.float32)
        return (mixed / jnp.transpose(total)[..., None], jnp.transpose(peak + jnp.log(total)))

    return lax.map(one_row, jnp.arange(rows_dev, dtype=jnp.int32))


def body_any(qkv, out_weight):
    rows_dev, cols, features = (qkv.shape[1], qkv.shape[2], qkv.shape[3])
    head_size = HEAD
    heads_local = features // head_size
    local = qkv.reshape(3, rows_dev, cols, heads_local, head_size)
    previous = shifted(local[1:3, rows_dev - 1 : rows_dev], "seq", 1)
    first_row = lax.axis_index("seq") * rows_dev
    row_out, row_lse = row_part(local, previous, first_row)
    columns = lax.all_to_all(local, "seq", split_axis=2, concat_axis=1, tiled=True)
    col_part_out, col_part_lse = column_part(columns)
    col_out, col_lse = (
        lax.all_to_all(col_part_out, "seq", split_axis=0, concat_axis=1, tiled=True),
        lax.all_to_all(
            col_part_lse.astype(jnp.bfloat16), "seq", split_axis=0, concat_axis=1, tiled=True
        ).astype(col_part_lse.dtype),
    )
    top = jnp.maximum(row_lse, col_lse)
    left = jnp.exp(row_lse - top)
    right = jnp.exp(col_lse - top)
    attended = (left[..., None] * row_out + right[..., None] * col_out.astype(jnp.float32)) / (
        left + right
    )[..., None]
    attended = attended.astype(jnp.bfloat16).reshape(rows_dev, cols, features)
    terms = jnp.einsum(
        "rcf,fd->crd",
        attended,
        lax.all_gather(out_weight, "seq", axis=1, tiled=True),
        preferred_element_type=jnp.float32,
    )
    summed = lax.psum_scatter(terms.astype(jnp.bfloat16), "head", scatter_dimension=0, tiled=True)
    return summed


def dense_scores(q, k):
    return lax.dot_general(q, k, (((1,), (1,)), ((), ())), preferred_element_type=F32)


def col_scores(q, k):
    prod = q * k
    high = prod.astype(BF16)
    low = (prod - high.astype(F32)).astype(BF16)
    ones = jnp.ones((2 * HEAD, HEAD), BF16)
    return jnp.dot(jnp.concatenate([high, low], axis=1), ones, preferred_element_type=F32)


def with_ones(v):
    return jnp.concatenate([v, jnp.ones_like(v)], axis=1)


def attend(q, dense, cols, coef):
    rows = q.shape[0]
    scores = []
    for k, _, allowed in dense:
        s = dense_scores(q, k)
        scores.append(s if allowed is None else jnp.where(allowed, s, NEG))
    singles = []
    if cols:
        wide = q.astype(F32)
    for k, _, allowed in cols:
        c = col_scores(wide, k)
        singles.append(c if allowed is None else jnp.where(allowed, c, NEG))
    peak = None
    for s in scores:
        for j in range(s.shape[1] // HEAD):
            part = s[:, j * HEAD : (j + 1) * HEAD]
            peak = part if peak is None else jnp.maximum(peak, part)
    if peak is not None:
        peak = jnp.broadcast_to(jnp.max(peak, axis=1, keepdims=True), (rows, HEAD))
    for c in singles:
        peak = c if peak is None else jnp.maximum(peak, c)
    peak = peak * coef
    both = None
    for s, (_, v, _) in zip(scores, dense):
        tiled = jnp.concatenate([peak] * (s.shape[1] // HEAD), axis=1)
        p = jnp.exp2(s * coef - tiled).astype(BF16)
        term = jnp.dot(p, v, preferred_element_type=F32)
        both = term if both is None else both + term
    out = None if both is None else both[:, :HEAD]
    total = None if both is None else both[:, HEAD:]
    for c, (_, v, _) in zip(singles, cols):
        w = jnp.exp2(c * coef - peak)
        total = w if total is None else total + w
        out = w * v if out is None else out + w * v
    return out / total, peak + jnp.log2(total)


def lse_rows(even, odd):
    lane = lax.broadcasted_iota(jnp.int32, (HEAD, HEAD), 1)
    evens, odds = [], []
    for t in range(even.shape[0] // HEAD):
        block = slice(t * HEAD, (t + 1) * HEAD)
        turned = jnp.transpose(jnp.where(lane == 0, even[block], odd[block]))
        evens.append(turned[0:1])
        odds.append(turned[1:2])
    return evens, odds


def put_lse(ref, base, evens, odds):
    rows = jnp.concatenate(evens + odds, axis=0)
    pad = (-rows.shape[0]) % 16
    if pad:
        rows = jnp.concatenate([rows, jnp.zeros((pad, HEAD), F32)], axis=0)
    count = rows.shape[0]
    for piece in range(3):
        part = rows.astype(BF16)
        ref[pl.ds(base + piece * count, count), :] = part
        rows = rows - part.astype(F32)


def get_lse(ref, base, cols):
    blocks = cols // HEAD
    count = -(-2 * blocks // 16) * 16
    rows = sum(ref[pl.ds(base + piece * count, count), :].astype(F32) for piece in range(3))
    turned = [
        jnp.transpose(jnp.broadcast_to(rows[t : t + 1], (HEAD, HEAD))) for t in range(2 * blocks)
    ]
    return jnp.concatenate(turned[:blocks], axis=0), jnp.concatenate(turned[blocks:], axis=0)


def lse_height(cols):
    return 3 * (-(-2 * (cols // HEAD) // 16) * 16)


def stacked(refs):
    return [ref[i] for ref in refs for i in range(ref.shape[0])]


def own_kernel(coef, cols, at, q, kv_m, kv_o, *refs):
    x, z = at[0], at[1]
    below = z == 1
    block = 256
    tri = lax.broadcasted_iota(jnp.int32, (block, block), 1) <= lax.broadcasted_iota(
        jnp.int32, (block, block), 0
    )
    first = x == 0
    k_e, k_o = jnp.where(first, kv_m[0], kv_o[0]), jnp.where(first, kv_o[0], kv_m[0])
    v_e, v_o = jnp.where(first, kv_m[1], kv_o[1]), jnp.where(first, kv_o[1], kv_m[1])
    v_e, v_o = with_ones(v_e), with_ones(v_o)
    *low, out = refs
    m_k, m_v, o_k, o_v = stacked(low)
    lk_e, lk_o = jnp.where(first, m_k, o_k), jnp.where(first, o_k, m_k)
    lv_e, lv_o = jnp.where(first, m_v, o_v), jnp.where(first, o_v, m_v)
    lv_o1 = with_ones(lv_o)
    evens, odds = [], []
    for part in range(cols // block):
        a, b = part * block, (part + 1) * block
        mine = slice(a, b)
        col_e = (lk_e[mine].astype(F32), lv_e[mine].astype(F32), below)
        col_o = (lk_o[mine].astype(F32), lv_o[mine].astype(F32), below)

        def causal(k, v):
            blocks = [(k[a:b], v[a:b], tri)]
            return blocks if part == 0 else [(k[:a], v[:a], None)] + blocks

        o1, l1 = attend(q[0, mine], causal(k_e, v_e) + [(lk_o, lv_o1, below)], [col_e], coef)
        o2, l2 = attend(q[1, mine], causal(k_o, v_o) + [(k_e, v_e, None)], [col_e, col_o], coef)
        out[mine] = o1.astype(BF16)
        out[cols + a : cols + b] = o2.astype(BF16)
        e, o = lse_rows(l1, l2)
        evens, odds = evens + e, odds + o
    put_lse(out, 2 * cols, evens, odds)


def upper_kernel(coef, cols, at, qa, qb, kv_m, kv_o, *refs):
    x, z = at[0], at[1]
    below = z == 1
    first = x == 0
    block = 256
    k_e, k_o = jnp.where(first, kv_m[0], kv_o[0]), jnp.where(first, kv_o[0], kv_m[0])
    v_e, v_o = jnp.where(first, kv_m[1], kv_o[1]), jnp.where(first, kv_o[1], kv_m[1])
    v_o1 = with_ones(v_o)
    *low, weight, out_a, out_b = refs
    lows = stacked(low)
    rows_a, rows_b = ([], []), ([], [])
    for index in range(cols // block):
        a, b = index * block, (index + 1) * block
        mine = slice(a, b)
        m_k, m_v, o_k, o_v = (part[mine].astype(F32) for part in lows)
        ce = (k_e[mine].astype(F32), v_e[mine].astype(F32), None)
        co = (k_o[mine].astype(F32), v_o[mine].astype(F32), None)
        low = [(m_k, m_v, below), (o_k, o_v, below)]
        for q, out, rows, dense, singles in (
            (qa, out_a, rows_a, [(k_o, v_o1, None)], [ce]),
            (qb, out_b, rows_b, [], [ce, co]),
        ):
            o1, l1 = attend(q[0, mine], dense, singles + low, coef)
            o2, l2 = attend(q[1, mine], [], [ce, co] + low, coef)
            o1, o2 = o1.astype(BF16), o2.astype(BF16)
            other = slice(cols + a, cols + b)
            if out is out_b:
                o1, o2 = jnp.where(below, o1, weight[mine]), jnp.where(below, o2, weight[other])
            out[mine] = o1
            out[other] = o2
            e, o = lse_rows(l1, l2)
            rows[0].extend(e)
            rows[1].extend(o)
    put_lse(out_a, 2 * cols, *rows_a)
    put_lse(out_b, 2 * cols, *rows_b)


def merge_kernel(cols, at, own, oa, ob, out):
    z = at[1]
    own_l, a_l, b_l = (get_lse(ref, 2 * cols, cols) for ref in (own, oa, ob))
    for row in range(2):
        tokens = slice(row * cols, (row + 1) * cols)
        l0 = own_l[row]
        l1 = jnp.where(z >= 2, a_l[row], NEG)
        l2 = jnp.where(z >= 3, b_l[row], NEG)
        top = jnp.maximum(l0, jnp.maximum(l1, l2))
        w0, w1, w2 = jnp.exp2(l0 - top), jnp.exp2(l1 - top), jnp.exp2(l2 - top)
        mixed = w0 * own[tokens].astype(F32) + w1 * oa[tokens].astype(F32) + w2 * ob[tokens].astype(F32)
        out[row] = (mixed / (w0 + w1 + w2)).astype(BF16)


def cost(us):
    return pl.CostEstimate(flops=int(us * 1e9), bytes_accessed=1024, transcendentals=0)


def head_call(kernel, at, args, outs, heads, name, us):
    def spec(shape, start=0):
        lead = len(shape) - 1
        return pl.BlockSpec(tuple(shape[:-1]) + (HEAD,), lambda h, at: (0,) * lead + (start + h,))

    return pl.pallas_call(
        kernel,
        out_shape=outs,
        grid_spec=pltpu.PrefetchScalarGridSpec(
            num_scalar_prefetch=1,
            grid=(heads,),
            in_specs=[spec(a.shape, start) for a, start in args],
            out_specs=[spec(o.shape) for o in outs],
        ),
        compiler_params=pltpu.CompilerParams(vmem_limit_bytes=VMEM),
        cost_estimate=cost(us),
        name=name,
    )(at, *(a for a, _ in args))


def project_kernel(chunks, at, *refs):
    x, core = at[0], at[2]
    near, far = refs[:chunks], refs[chunks : 2 * chunks]
    weights, send, keep = refs[2 * chunks : -2], refs[-2], refs[-1]
    tokens = near[0].shape[3]
    half = sum(ref.shape[4] for ref in near)
    for who, out in ((1 - core, send), (core, keep)):

        def rows(ref):
            return jnp.concatenate([ref[r, y, who] for y in range(2) for r in range(2)], axis=0)

        left = jnp.concatenate([rows(ref) for ref in near], axis=1)
        right = jnp.concatenate([rows(ref) for ref in far], axis=1)
        base = 0
        for weight in weights:
            top = weight[pl.ds(pl.multiple_of(x * half, half), half)]
            bottom = weight[pl.ds(pl.multiple_of((1 - x) * half, half), half)]
            c = jnp.dot(left, top, preferred_element_type=F32) + jnp.dot(right, bottom, preferred_element_type=F32)
            width = weight.shape[1]
            s, lane = base // out.shape[4], base % out.shape[4]
            out[s, :, :, :, lane : lane + width] = c.astype(BF16).reshape(2, 2, tokens, width)
            base += width


def project(at, near, far, weights, out_width):
    cols = near[0].shape[1]
    args = [a.reshape(2, 2, 2, cols // 4, a.shape[2]) for a in near + far] + weights
    layers = sum(w.shape[1] for w in weights) // out_width
    out = jax.ShapeDtypeStruct((layers, 2, 2, cols // 4, out_width), BF16)
    return whole_call(
        functools.partial(project_kernel, len(near)), at, args, [out, out], "project", 2 * layers)


def whole_call(kernel, at, args, outs, name, us):
    return pl.pallas_call(
        kernel,
        out_shape=outs,
        in_specs=[pl.BlockSpec(memory_space=pltpu.SMEM)] + [pl.BlockSpec(memory_space=pltpu.VMEM)] * len(args),
        out_specs=[pl.BlockSpec(memory_space=pltpu.VMEM)] * len(outs),
        compiler_params=pltpu.CompilerParams(vmem_limit_bytes=VMEM),
        cost_estimate=cost(us),
        name=name,
    )(at, *args)


def total(a, b):
    return (a.astype(F32) + b.astype(F32)).astype(BF16)


def split_kernel(at, kept, got, stay, to_y, to_x, to_xy):
    x, y = at[0], at[3]
    for s in range(kept.shape[0]):
        for out, yy, xx in ((to_xy, 1 - y, 1 - x), (to_y, 1 - y, x), (to_x, y, 1 - x), (stay, y, x)):
            out[s] = total(kept[s, yy, xx], got[s, yy, xx])


def place_kernel(at, *refs):
    x, z, out = at[0], at[1], refs[-1]
    layers = [z, z + 1 - 2 * (z % 2), (z + 2) % 4, 3 - z]
    for stay, from_y, from_x, from_xy in zip(*(refs[i:-1:4] for i in range(4))):
        width = stay.shape[-1]
        for s in range(stay.shape[0]):
            base = 2 * layers.pop(0)
            mine = pl.ds(pl.multiple_of((base + x) * width, width), width)
            theirs = pl.ds(pl.multiple_of((base + 1 - x) * width, width), width)
            out[:, mine] = total(stay[s], from_y[s])
            out[:, theirs] = total(from_x[s], from_xy[s])


def after(value, *earlier):
    return lax.optimization_barrier((value, earlier))[0]


def body_eight(qkv, out_weight):
    _, _, cols, features = qkv.shape
    half = features // 2
    chunks = 2
    width = half // chunks
    heads = width // HEAD
    coef = HEAD ** (-0.5) * LOG2E
    me = lax.axis_index("seq")
    who = lax.axis_index("head")
    z, x, core, y = me // 2, me % 2, who % 2, who // 2
    at = jnp.stack([x, z, core, y]).astype(jnp.int32)
    local = qkv.reshape(3, cols, features)
    first = x == 0

    def seq_perm(array, *layers, cross=False):
        pairs = [(2 * a + i, 2 * b + (1 - i if cross else i)) for a, b in layers for i in range(2)]
        return lax.ppermute(array, "seq", pairs)

    def swap(array):
        return seq_perm(array, (0, 0), (1, 1), (2, 2), (3, 3), cross=True)

    def head_perm(array, flip):
        return lax.ppermute(array, "head", [(i, i ^ flip) for i in range(4)])

    def lanes(lo, hi, part, source=local):
        return lax.dynamic_slice(source, (lo, 0, part * half), (hi - lo, cols, half))

    def lanes(lo, hi, half_of):
        return lax.dynamic_slice(local, (lo, 0, half_of * half), (hi - lo, cols, half))

    def pieces(array, c):
        return array[..., c * width : (c + 1) * width]

    q_m, q_o = lanes(0, 1, x), swap(lanes(0, 1, 1 - x))
    kv_m, kv_give = lanes(1, 3, x), lanes(1, 3, 1 - x)
    q, qs, low = [], [], []
    for c in range(chunks):
        a, b = pieces(q_m, c), pieces(q_o, c)
        q.append(jnp.concatenate([jnp.where(first, a, b), jnp.where(first, b, a)]))
        block = pieces(out_weight, c).reshape(q[c].shape)
        going = [q[c], jnp.where(z == 3, q[c], block)]
        if c:
            going = after(going, *qs[0])
        else:
            kv_o = swap(after(kv_give, q[0]))
        qs.append([seq_perm(going[0], (2, 1), (3, 2)), seq_perm(going[1], (3, 1), (1, 0), (2, 3))])
        mine = jnp.where(z == 0, pieces(kv_m, c), block)
        if c:
            low.append([seq_perm(after(jnp.concatenate([mine, pieces(kv_o, c)]), *low[0]), (0, 1), (1, 3))])
        else:
            low.append([seq_perm(mine, (0, 1), (1, 3)), seq_perm(pieces(kv_give, c), (0, 1), cross=True)])

    struct = jax.ShapeDtypeStruct
    partial = struct((2 * cols + lse_height(cols), width), BF16)
    oa, ob, own, sent = [], [], [], []
    turn = at
    for c in range(chunks):
        kvs = [(a, c * heads) for a in (kv_m, kv_o)]
        a, b = head_call(
            functools.partial(upper_kernel, coef, cols), turn,
            [(a, 0) for a in qs[c]] + kvs + [(a, 0) for a in low[c]] + [(out_weight, c * heads)], [partial] * 2, heads, "upper_rows", 7)
        sent.append(a)
        oa.append(seq_perm(a, (1, 2), (2, 3)))
        ob.append(seq_perm(b, (1, 3), (0, 1), (3, 2)))
        (mine,) = head_call(
            functools.partial(own_kernel, coef, cols), after(at, a), [(q[c], 0)] + kvs + [(a, 0) for a in low[c]],
            [partial], heads, "own_rows", 6)
        own.append(mine)
        turn = after(at, mine, oa[c], ob[c])

    w_second = seq_perm(after(out_weight, own[0], *qs[1]), (0, 2))
    depth = out_weight.shape[0]
    w_down = seq_perm(after(out_weight, own[0], *qs[1]), (2, 0), (3, 1))
    w_near = [
        jnp.where((z == 0) | (z == 3), qs[c][1].reshape(depth, width), ob[c][:depth]) for c in range(chunks)
    ]

    def merged(c, earlier):
        (a,) = head_call(
            functools.partial(merge_kernel, cols), after(at, earlier), [(a[c], 0) for a in (own, oa, ob)],
            [struct((2, cols, width), BF16)], heads, "merge", 2)
        return a, swap(a)

    first_half = merged(0, own[1])
    w_ridden = jnp.concatenate([low[c][0][:2].reshape(depth, width) for c in range(chunks)], axis=1)
    w_far = jnp.where(
        z >= 2, jnp.where(z == 2, w_second, w_ridden), after(w_down, first_half[0], own[1]))
    near, far = map(list, zip(first_half, merged(1, (w_far, first_half[1]))))
    w_other = seq_perm(w_far, (0, 1), (1, 0), (2, 3), (3, 2))

    parts = []
    turn = after(at, w_other)
    for weights in (
        [out_weight] + w_near,
        [w_far, w_other],
    ):
        send, kept = project(turn, near, far, weights, out_weight.shape[1])
        got = head_perm(send, 1)
        piece = struct(send.shape[:1] + send.shape[3:], BF16)
        stay, to_y, to_x, to_xy = whole_call(split_kernel, at, [kept, got], [piece] * 4, "split", 2)
        turn = after(at, stay)
        diagonal = [((2 * i + j) * 4 + h, (2 * i + 1 - j) * 4 + (h ^ 2)) for i in range(4) for j in range(2) for h in range(4)]
        from_xy = lax.ppermute(to_xy, ("seq", "head"), diagonal)
        parts += [stay, head_perm(to_y, 2), swap(to_x), from_xy]
    (out,) = whole_call(
        place_kernel, at, parts, [struct((cols // 4, 8 * out_weight.shape[1]), BF16)], "place", 2)
    return out.reshape(cols // 4, 1, 8 * out_weight.shape[1])


def solution(mesh):
    in_specs = (P(None, "seq", None, "head"), P("head", "seq"))
    out_specs = P("head", "seq", None)
    small = mesh.shape["seq"] == 8 and mesh.shape["head"] == 4

    def body(qkv, out_weight):
        if small and qkv.shape[1] == 1:
            return body_eight(qkv, out_weight)
        return body_any(qkv, out_weight)

    return jax.shard_map(body, mesh=mesh, in_specs=in_specs, out_specs=out_specs, check_vma=False)
```

```python
import functools
import jax
import jax.numpy as jnp
from jax import lax
from jax.experimental import pallas as pl
from jax.experimental.pallas import tpu as pltpu
from jax.sharding import PartitionSpec as P

HEAD = 128
LOG2E = 1.4426950408889634
NEG = -1e30
QB = 128
VMEM = 24 * 1024 * 1024
F32, BF16 = jnp.float32, jnp.bfloat16


def shifted(shard, axis, by):
    size = lax.axis_size(axis)
    pairs = [(i, i + by) for i in range(size) if 0 <= i + by < size]
    return lax.ppermute(shard, axis, pairs)


def column_part(part):
    queries, keys_part, values = (part[0], part[1], part[2])
    rows = queries.shape[0]
    scale = queries.shape[-1] ** (-0.5)
    scores = (
        jnp.einsum("rchd,schd->chrs", queries, keys_part, preferred_element_type=jnp.float32)
        * scale
    )
    r_idx = lax.broadcasted_iota(jnp.int32, (rows, rows), 0)
    s_idx = lax.broadcasted_iota(jnp.int32, (rows, rows), 1)
    allowed = s_idx <= r_idx - 2
    masked = jnp.where(allowed, scores, jnp.float32(-1e30))
    peak = jnp.max(masked, axis=-1)
    weights = jnp.where(allowed, jnp.exp(masked - peak[..., None]), jnp.float32(0.0))
    total = jnp.maximum(jnp.sum(weights, axis=-1), jnp.float32(1.0))
    rounded = weights.astype(jnp.bfloat16)
    mixed = jnp.einsum("chrs,schd->rchd", rounded, values, preferred_element_type=jnp.float32)
    col_out = (mixed / jnp.transpose(total, (2, 0, 1))[..., None]).astype(jnp.bfloat16)
    col_lse = jnp.transpose(peak + jnp.log(total), (2, 0, 1))
    return (col_out, col_lse)


def row_part(local, previous, first_row):
    rows_dev, cols, heads_local, head_size = (
        local.shape[1],
        local.shape[2],
        local.shape[3],
        local.shape[4],
    )
    scale = head_size ** (-0.5)
    keys_ext = jnp.concatenate([previous, local[1:3]], axis=1)
    key_idx = lax.broadcasted_iota(jnp.int32, (cols, 2 * cols), 1)
    query_idx = lax.broadcasted_iota(jnp.int32, (cols, 2 * cols), 0)

    def one_row(index):
        queries = lax.dynamic_index_in_dim(local[0], index, 0, keepdims=False)
        pair = keys_ext.reshape(2, 2 * cols, heads_local, head_size)
        scores = (
            jnp.einsum("qhd,khd->hqk", queries, pair[0], preferred_element_type=jnp.float32) * scale
        )
        allowed = (key_idx < cols) & (first_row + index > 0) | (key_idx >= cols) & (
            key_idx - cols <= query_idx
        )
        masked = jnp.where(allowed[None], scores, jnp.float32(-1e30))
        peak = jnp.max(masked, axis=-1)
        weights = jnp.where(allowed[None], jnp.exp(masked - peak[..., None]), jnp.float32(0.0))
        total = jnp.sum(weights, axis=-1)
        rounded = weights.astype(jnp.bfloat16)
        mixed = jnp.einsum("hqk,khd->qhd", rounded, pair[1], preferred_element_type=jnp.float32)
        return (mixed / jnp.transpose(total)[..., None], jnp.transpose(peak + jnp.log(total)))

    return lax.map(one_row, jnp.arange(rows_dev, dtype=jnp.int32))


def body_any(qkv, out_weight):
    rows_dev, cols, features = (qkv.shape[1], qkv.shape[2], qkv.shape[3])
    head_size = HEAD
    heads_local = features // head_size
    local = qkv.reshape(3, rows_dev, cols, heads_local, head_size)
    previous = shifted(local[1:3, rows_dev - 1 : rows_dev], "seq", 1)
    first_row = lax.axis_index("seq") * rows_dev
    row_out, row_lse = row_part(local, previous, first_row)
    columns = lax.all_to_all(local, "seq", split_axis=2, concat_axis=1, tiled=True)
    col_part_out, col_part_lse = column_part(columns)
    col_out, col_lse = (
        lax.all_to_all(col_part_out, "seq", split_axis=0, concat_axis=1, tiled=True),
        lax.all_to_all(
            col_part_lse.astype(jnp.bfloat16), "seq", split_axis=0, concat_axis=1, tiled=True
        ).astype(col_part_lse.dtype),
    )
    top = jnp.maximum(row_lse, col_lse)
    left = jnp.exp(row_lse - top)
    right = jnp.exp(col_lse - top)
    attended = (left[..., None] * row_out + right[..., None] * col_out.astype(jnp.float32)) / (
        left + right
    )[..., None]
    attended = attended.astype(jnp.bfloat16).reshape(rows_dev, cols, features)
    terms = jnp.einsum(
        "rcf,fd->crd",
        attended,
        lax.all_gather(out_weight, "seq", axis=1, tiled=True),
        preferred_element_type=jnp.float32,
    )
    summed = lax.psum_scatter(terms.astype(jnp.bfloat16), "head", scatter_dimension=0, tiled=True)
    return summed


def dense_scores(q, k):
    return lax.dot_general(q, k, (((1,), (1,)), ((), ())), preferred_element_type=F32)


def col_scores(q, k):
    prod = q * k
    high = prod.astype(BF16)
    low = (prod - high.astype(F32)).astype(BF16)
    ones = jnp.ones((2 * HEAD, HEAD), BF16)
    return jnp.dot(jnp.concatenate([high, low], axis=1), ones, preferred_element_type=F32)


def with_ones(v):
    return jnp.concatenate([v, jnp.ones_like(v)], axis=1)


def attend(q, dense, cols, coef):
    rows = q.shape[0]
    scores = []
    for k, _, allowed in dense:
        s = dense_scores(q, k)
        scores.append(s if allowed is None else jnp.where(allowed, s, NEG))
    singles = []
    if cols:
        wide = q.astype(F32)
    for k, _, allowed in cols:
        c = col_scores(wide, k)
        singles.append(c if allowed is None else jnp.where(allowed, c, NEG))
    peak = None
    for s in scores:
        for j in range(s.shape[1] // HEAD):
            part = s[:, j * HEAD : (j + 1) * HEAD]
            peak = part if peak is None else jnp.maximum(peak, part)
    if peak is not None:
        peak = jnp.broadcast_to(jnp.max(peak, axis=1, keepdims=True), (rows, HEAD))
    for c in singles:
        peak = c if peak is None else jnp.maximum(peak, c)
    peak = peak * coef
    both = None
    for s, (_, v, _) in zip(scores, dense):
        tiled = jnp.concatenate([peak] * (s.shape[1] // HEAD), axis=1)
        p = jnp.exp2(s * coef - tiled).astype(BF16)
        term = jnp.dot(p, v, preferred_element_type=F32)
        both = term if both is None else both + term
    out = None if both is None else both[:, :HEAD]
    total = None if both is None else both[:, HEAD:]
    for c, (_, v, _) in zip(singles, cols):
        w = jnp.exp2(c * coef - peak)
        total = w if total is None else total + w
        out = w * v if out is None else out + w * v
    return out / total, peak + jnp.log2(total)


def lse_rows(even, odd):
    lane = lax.broadcasted_iota(jnp.int32, (HEAD, HEAD), 1)
    evens, odds = [], []
    for t in range(even.shape[0] // HEAD):
        block = slice(t * HEAD, (t + 1) * HEAD)
        turned = jnp.transpose(jnp.where(lane == 0, even[block], odd[block]))
        evens.append(turned[0:1])
        odds.append(turned[1:2])
    return evens, odds


def put_lse(ref, base, evens, odds):
    rows = jnp.concatenate(evens + odds, axis=0)
    pad = (-rows.shape[0]) % 16
    if pad:
        rows = jnp.concatenate([rows, jnp.zeros((pad, HEAD), F32)], axis=0)
    count = rows.shape[0]
    for piece in range(3):
        part = rows.astype(BF16)
        ref[pl.ds(base + piece * count, count), :] = part
        rows = rows - part.astype(F32)


def get_lse(ref, base, cols):
    blocks = cols // HEAD
    count = -(-2 * blocks // 16) * 16
    rows = sum(ref[pl.ds(base + piece * count, count), :].astype(F32) for piece in range(3))
    turned = [
        jnp.transpose(jnp.broadcast_to(rows[t : t + 1], (HEAD, HEAD))) for t in range(2 * blocks)
    ]
    return jnp.concatenate(turned[:blocks], axis=0), jnp.concatenate(turned[blocks:], axis=0)


def lse_height(cols):
    return 3 * (-(-2 * (cols // HEAD) // 16) * 16)


def stacked(refs):
    return [ref[i] for ref in refs for i in range(ref.shape[0])]


def own_kernel(coef, cols, at, q, kv_m, kv_o, *refs):
    x, z = at[0], at[1]
    below = z == 1
    block = 256
    tri = lax.broadcasted_iota(jnp.int32, (block, block), 1) <= lax.broadcasted_iota(
        jnp.int32, (block, block), 0
    )
    first = x == 0
    k_e, k_o = jnp.where(first, kv_m[0], kv_o[0]), jnp.where(first, kv_o[0], kv_m[0])
    v_e, v_o = jnp.where(first, kv_m[1], kv_o[1]), jnp.where(first, kv_o[1], kv_m[1])
    v_e, v_o = with_ones(v_e), with_ones(v_o)
    *low, out = refs
    m_k, m_v, o_k, o_v = stacked(low)
    lk_e, lk_o = jnp.where(first, m_k, o_k), jnp.where(first, o_k, m_k)
    lv_e, lv_o = jnp.where(first, m_v, o_v), jnp.where(first, o_v, m_v)
    lv_o1 = with_ones(lv_o)
    evens, odds = [], []
    for part in range(cols // block):
        a, b = part * block, (part + 1) * block
        mine = slice(a, b)
        col_e = (lk_e[mine].astype(F32), lv_e[mine].astype(F32), below)
        col_o = (lk_o[mine].astype(F32), lv_o[mine].astype(F32), below)

        def causal(k, v):
            blocks = [(k[a:b], v[a:b], tri)]
            return blocks if part == 0 else [(k[:a], v[:a], None)] + blocks

        o1, l1 = attend(q[0, mine], causal(k_e, v_e) + [(lk_o, lv_o1, below)], [col_e], coef)
        o2, l2 = attend(q[1, mine], causal(k_o, v_o) + [(k_e, v_e, None)], [col_e, col_o], coef)
        out[mine] = o1.astype(BF16)
        out[cols + a : cols + b] = o2.astype(BF16)
        e, o = lse_rows(l1, l2)
        evens, odds = evens + e, odds + o
    put_lse(out, 2 * cols, evens, odds)


def upper_kernel(coef, cols, at, qa, qb, kv_m, kv_o, *refs):
    x, z = at[0], at[1]
    below = z == 1
    first = x == 0
    block = 256
    k_e, k_o = jnp.where(first, kv_m[0], kv_o[0]), jnp.where(first, kv_o[0], kv_m[0])
    v_e, v_o = jnp.where(first, kv_m[1], kv_o[1]), jnp.where(first, kv_o[1], kv_m[1])
    v_o1 = with_ones(v_o)
    *low, weight, out_a, out_b = refs
    lows = stacked(low)
    rows_a, rows_b = ([], []), ([], [])
    for index in range(cols // block):
        a, b = index * block, (index + 1) * block
        mine = slice(a, b)
        m_k, m_v, o_k, o_v = (part[mine].astype(F32) for part in lows)
        ce = (k_e[mine].astype(F32), v_e[mine].astype(F32), None)
        co = (k_o[mine].astype(F32), v_o[mine].astype(F32), None)
        low = [(m_k, m_v, below), (o_k, o_v, below)]
        for q, out, rows, dense, singles in (
            (qa, out_a, rows_a, [(k_o, v_o1, None)], [ce]),
            (qb, out_b, rows_b, [], [ce, co]),
        ):
            o1, l1 = attend(q[0, mine], dense, singles + low, coef)
            o2, l2 = attend(q[1, mine], [], [ce, co] + low, coef)
            o1, o2 = o1.astype(BF16), o2.astype(BF16)
            other = slice(cols + a, cols + b)
            if out is out_b:
                o1, o2 = jnp.where(below, o1, weight[mine]), jnp.where(below, o2, weight[other])
            out[mine] = o1
            out[other] = o2
            e, o = lse_rows(l1, l2)
            rows[0].extend(e)
            rows[1].extend(o)
    put_lse(out_a, 2 * cols, *rows_a)
    put_lse(out_b, 2 * cols, *rows_b)


def merge_kernel(cols, at, own, oa, ob, out):
    z = at[1]
    own_l, a_l, b_l = (get_lse(ref, 2 * cols, cols) for ref in (own, oa, ob))
    for row in range(2):
        tokens = slice(row * cols, (row + 1) * cols)
        l0 = own_l[row]
        l1 = jnp.where(z >= 2, a_l[row], NEG)
        l2 = jnp.where(z >= 3, b_l[row], NEG)
        top = jnp.maximum(l0, jnp.maximum(l1, l2))
        w0, w1, w2 = jnp.exp2(l0 - top), jnp.exp2(l1 - top), jnp.exp2(l2 - top)
        mixed = w0 * own[tokens].astype(F32) + w1 * oa[tokens].astype(F32) + w2 * ob[tokens].astype(F32)
        out[row] = (mixed / (w0 + w1 + w2)).astype(BF16)


def cost(us):
    return pl.CostEstimate(flops=int(us * 1e9), bytes_accessed=1024, transcendentals=0)


def head_call(kernel, at, args, outs, heads, name, us):
    def spec(shape, start=0):
        lead = len(shape) - 1
        return pl.BlockSpec(tuple(shape[:-1]) + (HEAD,), lambda h, at: (0,) * lead + (start + h,))

    return pl.pallas_call(
        kernel,
        out_shape=outs,
        grid_spec=pltpu.PrefetchScalarGridSpec(
            num_scalar_prefetch=1,
            grid=(heads,),
            in_specs=[spec(a.shape, start) for a, start in args],
            out_specs=[spec(o.shape) for o in outs],
        ),
        compiler_params=pltpu.CompilerParams(vmem_limit_bytes=VMEM),
        cost_estimate=cost(us),
        name=name,
    )(at, *(a for a, _ in args))


def project_kernel(chunks, at, *refs):
    x, core = at[0], at[2]
    near, far = refs[:chunks], refs[chunks : 2 * chunks]
    weights, send, keep = refs[2 * chunks : -2], refs[-2], refs[-1]
    tokens = near[0].shape[3]
    half = sum(ref.shape[4] for ref in near)
    for who, out in ((1 - core, send), (core, keep)):

        def rows(ref):
            return jnp.concatenate([ref[r, y, who] for y in range(2) for r in range(2)], axis=0)

        left = jnp.concatenate([rows(ref) for ref in near], axis=1)
        right = jnp.concatenate([rows(ref) for ref in far], axis=1)
        base = 0
        for weight in weights:
            top = weight[pl.ds(pl.multiple_of(x * half, half), half)]
            bottom = weight[pl.ds(pl.multiple_of((1 - x) * half, half), half)]
            c = jnp.dot(left, top, preferred_element_type=F32) + jnp.dot(right, bottom, preferred_element_type=F32)
            width = weight.shape[1]
            s, lane = base // out.shape[4], base % out.shape[4]
            out[s, :, :, :, lane : lane + width] = c.astype(BF16).reshape(2, 2, tokens, width)
            base += width


def project(at, near, far, weights, out_width):
    cols = near[0].shape[1]
    args = [a.reshape(2, 2, 2, cols // 4, a.shape[2]) for a in near + far] + weights
    layers = sum(w.shape[1] for w in weights) // out_width
    out = jax.ShapeDtypeStruct((layers, 2, 2, cols // 4, out_width), BF16)
    return whole_call(
        functools.partial(project_kernel, len(near)), at, args, [out, out], "project", 2 * layers)


def whole_call(kernel, at, args, outs, name, us):
    return pl.pallas_call(
        kernel,
        out_shape=outs,
        in_specs=[pl.BlockSpec(memory_space=pltpu.SMEM)] + [pl.BlockSpec(memory_space=pltpu.VMEM)] * len(args),
        out_specs=[pl.BlockSpec(memory_space=pltpu.VMEM)] * len(outs),
        compiler_params=pltpu.CompilerParams(vmem_limit_bytes=VMEM),
        cost_estimate=cost(us),
        name=name,
    )(at, *args)


def total(a, b):
    return (a.astype(F32) + b.astype(F32)).astype(BF16)


def split_kernel(at, kept, got, stay, to_y, to_x, to_xy):
    x, y = at[0], at[3]
    for s in range(kept.shape[0]):
        for out, yy, xx in ((to_xy, 1 - y, 1 - x), (to_y, 1 - y, x), (to_x, y, 1 - x), (stay, y, x)):
            out[s] = total(kept[s, yy, xx], got[s, yy, xx])


def place_kernel(at, *refs):
    x, z, out = at[0], at[1], refs[-1]
    layers = [z, z + 1 - 2 * (z % 2), (z + 2) % 4, 3 - z]
    for stay, from_y, from_x, from_xy in zip(*(refs[i:-1:4] for i in range(4))):
        width = stay.shape[-1]
        for s in range(stay.shape[0]):
            base = 2 * layers.pop(0)
            mine = pl.ds(pl.multiple_of((base + x) * width, width), width)
            theirs = pl.ds(pl.multiple_of((base + 1 - x) * width, width), width)
            out[:, mine] = total(stay[s], from_y[s])
            out[:, theirs] = total(from_x[s], from_xy[s])


def after(value, *earlier):
    return lax.optimization_barrier((value, earlier))[0]


def body_eight(qkv, out_weight):
    _, _, cols, features = qkv.shape
    half = features // 2
    chunks = 2
    width = half // chunks
    heads = width // HEAD
    coef = HEAD ** (-0.5) * LOG2E
    me = lax.axis_index("seq")
    who = lax.axis_index("head")
    z, x, core, y = me // 2, me % 2, who % 2, who // 2
    at = jnp.stack([x, z, core, y]).astype(jnp.int32)
    local = qkv.reshape(3, cols, features)
    first = x == 0

    def seq_perm(array, *layers, cross=False):
        pairs = [(2 * a + i, 2 * b + (1 - i if cross else i)) for a, b in layers for i in range(2)]
        return lax.ppermute(array, "seq", pairs)

    def swap(array):
        return seq_perm(array, (0, 0), (1, 1), (2, 2), (3, 3), cross=True)

    def head_perm(array, flip):
        return lax.ppermute(array, "head", [(i, i ^ flip) for i in range(4)])

    def lanes(lo, hi, part, source=local):
        return lax.dynamic_slice(source, (lo, 0, part * half), (hi - lo, cols, half))

    def lanes(lo, hi, half_of):
        return lax.dynamic_slice(local, (lo, 0, half_of * half), (hi - lo, cols, half))

    def pieces(array, c):
        return array[..., c * width : (c + 1) * width]

    q_m, q_o = lanes(0, 1, x), swap(lanes(0, 1, 1 - x))
    w_second = seq_perm(out_weight, (0, 2))
    kv_m, kv_give = lanes(1, 3, x), lanes(1, 3, 1 - x)
    q, qs, low = [], [], []
    for c in range(chunks):
        a, b = pieces(q_m, c), pieces(q_o, c)
        q.append(jnp.concatenate([jnp.where(first, a, b), jnp.where(first, b, a)]))
        block = pieces(out_weight, c).reshape(q[c].shape)
        going = [jnp.where(z == 1, block, q[c]), jnp.where(z == 3, q[c], block)]
        if c:
            going = after(going, *qs[0])
        qs.append([seq_perm(going[0], (2, 1), (3, 2), (1, 3)), seq_perm(going[1], (3, 1), (1, 0), (2, 3))])
        if c == 0:
            kv_o = swap(after(kv_give, q[0]))
            ups = after([pieces(kv_m, c), pieces(kv_give, c)], w_second)
            low.append([seq_perm(ups[0], (0, 1)), seq_perm(ups[1], (0, 1), cross=True)])
        else:
            up = jnp.concatenate([pieces(kv_m, c), pieces(kv_o, c)])
            low.append([seq_perm(after(up, *low[0]), (0, 1))])

    struct = jax.ShapeDtypeStruct
    partial = struct((2 * cols + lse_height(cols), width), BF16)
    oa, ob, own, sent = [], [], [], []
    turn = at
    for c in range(chunks):
        pair = [(kv_m, c * heads), (kv_o, c * heads)]
        a, b = head_call(
            functools.partial(upper_kernel, coef, cols), turn,
            [(a, 0) for a in qs[c]] + pair + [(a, 0) for a in low[c]] + [(out_weight, c * heads)], [partial] * 2, heads, "upper_rows", 7)
        sent.append(a)
        oa.append(seq_perm(a, (1, 2), (2, 3)))
        ob.append(seq_perm(b, (1, 3), (0, 1), (3, 2)))
        (mine,) = head_call(
            functools.partial(own_kernel, coef, cols), after(at, a), [(q[c], 0)] + pair + [(a, 0) for a in low[c]],
            [partial], heads, "own_rows", 6)
        own.append(mine)
        turn = after(at, mine)

    depth = out_weight.shape[0]
    w_down = seq_perm(after(out_weight, own[0], *qs[1]), (2, 0), (3, 1))
    w_near = [
        jnp.where((z == 0) | (z == 3), qs[c][1].reshape(depth, width), ob[c][:depth]) for c in range(chunks)
    ]

    def merged(c, earlier):
        (a,) = head_call(
            functools.partial(merge_kernel, cols), after(at, earlier), [(a[c], 0) for a in (own, oa, ob)],
            [struct((2, cols, width), BF16)], heads, "merge", 2)
        return a, swap(a)

    first_half = merged(0, own[1])
    w_ridden = jnp.concatenate([qs[c][0].reshape(depth, width) for c in range(chunks)], axis=1)
    w_far = jnp.where(
        z >= 2, jnp.where(z == 2, w_second, w_ridden), after(w_down, first_half[0], own[1]))
    near, far = map(list, zip(first_half, merged(1, (w_far, first_half[1]))))
    w_other = seq_perm(w_far, (0, 1), (1, 0), (2, 3), (3, 2))

    parts = []
    turn = after(at, w_other)
    for weights in (
        [out_weight] + w_near,
        [w_far, w_other],
    ):
        send, kept = project(turn, near, far, weights, out_weight.shape[1])
        got = head_perm(send, 1)
        piece = struct(send.shape[:1] + send.shape[3:], BF16)
        stay, to_y, to_x, to_xy = whole_call(
            split_kernel, after(at, parts[1:2]), [kept, got], [piece] * 4, "split", 2)
        turn = after(at, stay)
        diagonal = [((2 * i + j) * 4 + h, (2 * i + 1 - j) * 4 + (h ^ 2)) for i in range(4) for j in range(2) for h in range(4)]
        from_xy = lax.ppermute(to_xy, ("seq", "head"), diagonal)
        parts += [stay, head_perm(to_y, 2), swap(to_x), from_xy]
    (out,) = whole_call(
        place_kernel, at, parts, [struct((cols // 4, 8 * out_weight.shape[1]), BF16)], "place", 2)
    return out.reshape(cols // 4, 1, 8 * out_weight.shape[1])


def solution(mesh):
    in_specs = (P(None, "seq", None, "head"), P("head", "seq"))
    out_specs = P("head", "seq", None)
    small = mesh.shape["seq"] == 8 and mesh.shape["head"] == 4

    def body(qkv, out_weight):
        if small and qkv.shape[1] == 1:
            return body_eight(qkv, out_weight)
        return body_any(qkv, out_weight)

    return jax.shard_map(body, mesh=mesh, in_specs=in_specs, out_specs=out_specs, check_vma=False)
```

```python
import functools
import jax
import jax.numpy as jnp
from jax import lax
from jax.experimental import pallas as pl
from jax.experimental.pallas import tpu as pltpu
from jax.sharding import PartitionSpec as P

HEAD = 128
LOG2E = 1.4426950408889634
NEG = -1e30
QB = 128
VMEM = 24 * 1024 * 1024
F32, BF16 = jnp.float32, jnp.bfloat16


def shifted(shard, axis, by):
    size = lax.axis_size(axis)
    pairs = [(i, i + by) for i in range(size) if 0 <= i + by < size]
    return lax.ppermute(shard, axis, pairs)


def column_part(part):
    queries, keys_part, values = (part[0], part[1], part[2])
    rows = queries.shape[0]
    scale = queries.shape[-1] ** (-0.5)
    scores = (
        jnp.einsum("rchd,schd->chrs", queries, keys_part, preferred_element_type=jnp.float32)
        * scale
    )
    r_idx = lax.broadcasted_iota(jnp.int32, (rows, rows), 0)
    s_idx = lax.broadcasted_iota(jnp.int32, (rows, rows), 1)
    allowed = s_idx <= r_idx - 2
    masked = jnp.where(allowed, scores, jnp.float32(-1e30))
    peak = jnp.max(masked, axis=-1)
    weights = jnp.where(allowed, jnp.exp(masked - peak[..., None]), jnp.float32(0.0))
    total = jnp.maximum(jnp.sum(weights, axis=-1), jnp.float32(1.0))
    rounded = weights.astype(jnp.bfloat16)
    mixed = jnp.einsum("chrs,schd->rchd", rounded, values, preferred_element_type=jnp.float32)
    col_out = (mixed / jnp.transpose(total, (2, 0, 1))[..., None]).astype(jnp.bfloat16)
    col_lse = jnp.transpose(peak + jnp.log(total), (2, 0, 1))
    return (col_out, col_lse)


def row_part(local, previous, first_row):
    rows_dev, cols, heads_local, head_size = (
        local.shape[1],
        local.shape[2],
        local.shape[3],
        local.shape[4],
    )
    scale = head_size ** (-0.5)
    keys_ext = jnp.concatenate([previous, local[1:3]], axis=1)
    key_idx = lax.broadcasted_iota(jnp.int32, (cols, 2 * cols), 1)
    query_idx = lax.broadcasted_iota(jnp.int32, (cols, 2 * cols), 0)

    def one_row(index):
        queries = lax.dynamic_index_in_dim(local[0], index, 0, keepdims=False)
        pair = keys_ext.reshape(2, 2 * cols, heads_local, head_size)
        scores = (
            jnp.einsum("qhd,khd->hqk", queries, pair[0], preferred_element_type=jnp.float32) * scale
        )
        allowed = (key_idx < cols) & (first_row + index > 0) | (key_idx >= cols) & (
            key_idx - cols <= query_idx
        )
        masked = jnp.where(allowed[None], scores, jnp.float32(-1e30))
        peak = jnp.max(masked, axis=-1)
        weights = jnp.where(allowed[None], jnp.exp(masked - peak[..., None]), jnp.float32(0.0))
        total = jnp.sum(weights, axis=-1)
        rounded = weights.astype(jnp.bfloat16)
        mixed = jnp.einsum("hqk,khd->qhd", rounded, pair[1], preferred_element_type=jnp.float32)
        return (mixed / jnp.transpose(total)[..., None], jnp.transpose(peak + jnp.log(total)))

    return lax.map(one_row, jnp.arange(rows_dev, dtype=jnp.int32))


def body_any(qkv, out_weight):
    rows_dev, cols, features = (qkv.shape[1], qkv.shape[2], qkv.shape[3])
    head_size = HEAD
    heads_local = features // head_size
    local = qkv.reshape(3, rows_dev, cols, heads_local, head_size)
    previous = shifted(local[1:3, rows_dev - 1 : rows_dev], "seq", 1)
    first_row = lax.axis_index("seq") * rows_dev
    row_out, row_lse = row_part(local, previous, first_row)
    columns = lax.all_to_all(local, "seq", split_axis=2, concat_axis=1, tiled=True)
    col_part_out, col_part_lse = column_part(columns)
    col_out, col_lse = (
        lax.all_to_all(col_part_out, "seq", split_axis=0, concat_axis=1, tiled=True),
        lax.all_to_all(
            col_part_lse.astype(jnp.bfloat16), "seq", split_axis=0, concat_axis=1, tiled=True
        ).astype(col_part_lse.dtype),
    )
    top = jnp.maximum(row_lse, col_lse)
    left = jnp.exp(row_lse - top)
    right = jnp.exp(col_lse - top)
    attended = (left[..., None] * row_out + right[..., None] * col_out.astype(jnp.float32)) / (
        left + right
    )[..., None]
    attended = attended.astype(jnp.bfloat16).reshape(rows_dev, cols, features)
    terms = jnp.einsum(
        "rcf,fd->crd",
        attended,
        lax.all_gather(out_weight, "seq", axis=1, tiled=True),
        preferred_element_type=jnp.float32,
    )
    summed = lax.psum_scatter(terms.astype(jnp.bfloat16), "head", scatter_dimension=0, tiled=True)
    return summed


def dense_scores(q, k):
    return lax.dot_general(q, k, (((1,), (1,)), ((), ())), preferred_element_type=F32)


def col_scores(q, k):
    prod = q * k
    high = prod.astype(BF16)
    low = (prod - high.astype(F32)).astype(BF16)
    ones = jnp.ones((2 * HEAD, HEAD), BF16)
    return jnp.dot(jnp.concatenate([high, low], axis=1), ones, preferred_element_type=F32)


def with_ones(v):
    return jnp.concatenate([v, jnp.ones_like(v)], axis=1)


def attend(q, dense, cols, coef):
    rows = q.shape[0]
    scores = []
    for k, _, allowed in dense:
        s = dense_scores(q, k)
        scores.append(s if allowed is None else jnp.where(allowed, s, NEG))
    singles = []
    if cols:
        wide = q.astype(F32)
    for k, _, allowed in cols:
        c = col_scores(wide, k)
        singles.append(c if allowed is None else jnp.where(allowed, c, NEG))
    peak = None
    for s in scores:
        for j in range(s.shape[1] // HEAD):
            part = s[:, j * HEAD : (j + 1) * HEAD]
            peak = part if peak is None else jnp.maximum(peak, part)
    if peak is not None:
        peak = jnp.broadcast_to(jnp.max(peak, axis=1, keepdims=True), (rows, HEAD))
    for c in singles:
        peak = c if peak is None else jnp.maximum(peak, c)
    peak = peak * coef
    both = None
    for s, (_, v, _) in zip(scores, dense):
        tiled = jnp.concatenate([peak] * (s.shape[1] // HEAD), axis=1)
        p = jnp.exp2(s * coef - tiled).astype(BF16)
        term = jnp.dot(p, v, preferred_element_type=F32)
        both = term if both is None else both + term
    out = None if both is None else both[:, :HEAD]
    total = None if both is None else both[:, HEAD:]
    for c, (_, v, _) in zip(singles, cols):
        w = jnp.exp2(c * coef - peak)
        total = w if total is None else total + w
        out = w * v if out is None else out + w * v
    return out / total, peak + jnp.log2(total)


def lse_rows(even, odd):
    lane = lax.broadcasted_iota(jnp.int32, (HEAD, HEAD), 1)
    evens, odds = [], []
    for t in range(even.shape[0] // HEAD):
        block = slice(t * HEAD, (t + 1) * HEAD)
        turned = jnp.transpose(jnp.where(lane == 0, even[block], odd[block]))
        evens.append(turned[0:1])
        odds.append(turned[1:2])
    return evens, odds


def put_lse(ref, base, evens, odds):
    rows = jnp.concatenate(evens + odds, axis=0)
    pad = (-rows.shape[0]) % 16
    if pad:
        rows = jnp.concatenate([rows, jnp.zeros((pad, HEAD), F32)], axis=0)
    count = rows.shape[0]
    for piece in range(3):
        part = rows.astype(BF16)
        ref[pl.ds(base + piece * count, count), :] = part
        rows = rows - part.astype(F32)


def get_lse(ref, base, cols):
    blocks = cols // HEAD
    count = -(-2 * blocks // 16) * 16
    rows = sum(ref[pl.ds(base + piece * count, count), :].astype(F32) for piece in range(3))
    turned = [
        jnp.transpose(jnp.broadcast_to(rows[t : t + 1], (HEAD, HEAD))) for t in range(2 * blocks)
    ]
    return jnp.concatenate(turned[:blocks], axis=0), jnp.concatenate(turned[blocks:], axis=0)


def lse_height(cols):
    return 3 * (-(-2 * (cols // HEAD) // 16) * 16)


def stacked(refs):
    return [ref[i] for ref in refs for i in range(ref.shape[0])]


def own_kernel(coef, cols, at, q, kv_m, kv_o, *refs):
    x, z = at[0], at[1]
    below = z == 1
    block = 256
    tri = lax.broadcasted_iota(jnp.int32, (block, block), 1) <= lax.broadcasted_iota(
        jnp.int32, (block, block), 0
    )
    first = x == 0
    k_e, k_o = jnp.where(first, kv_m[0], kv_o[0]), jnp.where(first, kv_o[0], kv_m[0])
    v_e, v_o = jnp.where(first, kv_m[1], kv_o[1]), jnp.where(first, kv_o[1], kv_m[1])
    v_e, v_o = with_ones(v_e), with_ones(v_o)
    *low, out = refs
    m_k, m_v, o_k, o_v = stacked(low)
    lk_e, lk_o = jnp.where(first, m_k, o_k), jnp.where(first, o_k, m_k)
    lv_e, lv_o = jnp.where(first, m_v, o_v), jnp.where(first, o_v, m_v)
    lv_o1 = with_ones(lv_o)
    evens, odds = [], []
    for part in range(cols // block):
        a, b = part * block, (part + 1) * block
        mine = slice(a, b)
        col_e = (lk_e[mine].astype(F32), lv_e[mine].astype(F32), below)
        col_o = (lk_o[mine].astype(F32), lv_o[mine].astype(F32), below)

        def causal(k, v):
            blocks = [(k[a:b], v[a:b], tri)]
            return blocks if part == 0 else [(k[:a], v[:a], None)] + blocks

        o1, l1 = attend(q[0, mine], causal(k_e, v_e) + [(lk_o, lv_o1, below)], [col_e], coef)
        o2, l2 = attend(q[1, mine], causal(k_o, v_o) + [(k_e, v_e, None)], [col_e, col_o], coef)
        out[mine] = o1.astype(BF16)
        out[cols + a : cols + b] = o2.astype(BF16)
        e, o = lse_rows(l1, l2)
        evens, odds = evens + e, odds + o
    put_lse(out, 2 * cols, evens, odds)


def upper_kernel(coef, cols, at, qa, qb, kv_m, kv_o, *refs):
    x, z = at[0], at[1]
    below = z == 1
    first = x == 0
    block = 256
    k_e, k_o = jnp.where(first, kv_m[0], kv_o[0]), jnp.where(first, kv_o[0], kv_m[0])
    v_e, v_o = jnp.where(first, kv_m[1], kv_o[1]), jnp.where(first, kv_o[1], kv_m[1])
    v_o1 = with_ones(v_o)
    *low, weight, out_a, out_b = refs
    lows = stacked(low)
    rows_a, rows_b = ([], []), ([], [])
    for index in range(cols // block):
        a, b = index * block, (index + 1) * block
        mine = slice(a, b)
        m_k, m_v, o_k, o_v = (part[mine].astype(F32) for part in lows)
        ce = (k_e[mine].astype(F32), v_e[mine].astype(F32), None)
        co = (k_o[mine].astype(F32), v_o[mine].astype(F32), None)
        low = [(m_k, m_v, below), (o_k, o_v, below)]
        for q, out, rows, dense, singles in (
            (qa, out_a, rows_a, [(k_o, v_o1, None)], [ce]),
            (qb, out_b, rows_b, [], [ce, co]),
        ):
            o1, l1 = attend(q[0, mine], dense, singles + low, coef)
            o2, l2 = attend(q[1, mine], [], [ce, co] + low, coef)
            o1, o2 = o1.astype(BF16), o2.astype(BF16)
            other = slice(cols + a, cols + b)
            if out is out_b:
                o1, o2 = jnp.where(below, o1, weight[mine]), jnp.where(below, o2, weight[other])
            out[mine] = o1
            out[other] = o2
            e, o = lse_rows(l1, l2)
            rows[0].extend(e)
            rows[1].extend(o)
    put_lse(out_a, 2 * cols, *rows_a)
    put_lse(out_b, 2 * cols, *rows_b)


def merge_kernel(cols, at, own, oa, ob, out):
    z = at[1]
    own_l, a_l, b_l = (get_lse(ref, 2 * cols, cols) for ref in (own, oa, ob))
    for row in range(2):
        tokens = slice(row * cols, (row + 1) * cols)
        l0 = own_l[row]
        l1 = jnp.where(z >= 2, a_l[row], NEG)
        l2 = jnp.where(z >= 3, b_l[row], NEG)
        top = jnp.maximum(l0, jnp.maximum(l1, l2))
        w0, w1, w2 = jnp.exp2(l0 - top), jnp.exp2(l1 - top), jnp.exp2(l2 - top)
        mixed = w0 * own[tokens].astype(F32) + w1 * oa[tokens].astype(F32) + w2 * ob[tokens].astype(F32)
        out[row] = (mixed / (w0 + w1 + w2)).astype(BF16)


def cost(us):
    return pl.CostEstimate(flops=int(us * 1e9), bytes_accessed=1024, transcendentals=0)


def head_call(kernel, at, args, outs, heads, name, us):
    def spec(shape, start=0):
        lead = len(shape) - 1
        return pl.BlockSpec(tuple(shape[:-1]) + (HEAD,), lambda h, at: (0,) * lead + (start + h,))

    return pl.pallas_call(
        kernel,
        out_shape=outs,
        grid_spec=pltpu.PrefetchScalarGridSpec(
            num_scalar_prefetch=1,
            grid=(heads,),
            in_specs=[spec(a.shape, start) for a, start in args],
            out_specs=[spec(o.shape) for o in outs],
        ),
        compiler_params=pltpu.CompilerParams(vmem_limit_bytes=VMEM),
        cost_estimate=cost(us),
        name=name,
    )(at, *(a for a, _ in args))


def project_kernel(chunks, at, *refs):
    x, core = at[0], at[2]
    near, far = refs[:chunks], refs[chunks : 2 * chunks]
    weights, send, keep = refs[2 * chunks : -2], refs[-2], refs[-1]
    tokens = near[0].shape[3]
    half = sum(ref.shape[4] for ref in near)
    for who, out in ((1 - core, send), (core, keep)):

        def rows(ref):
            return jnp.concatenate([ref[r, y, who] for y in range(2) for r in range(2)], axis=0)

        left = jnp.concatenate([rows(ref) for ref in near], axis=1)
        right = jnp.concatenate([rows(ref) for ref in far], axis=1)
        base = 0
        for weight in weights:
            top = weight[pl.ds(pl.multiple_of(x * half, half), half)]
            bottom = weight[pl.ds(pl.multiple_of((1 - x) * half, half), half)]
            c = jnp.dot(left, top, preferred_element_type=F32) + jnp.dot(right, bottom, preferred_element_type=F32)
            width = weight.shape[1]
            s, lane = base // out.shape[4], base % out.shape[4]
            out[s, :, :, :, lane : lane + width] = c.astype(BF16).reshape(2, 2, tokens, width)
            base += width


def project(at, near, far, weights, out_width):
    cols = near[0].shape[1]
    args = [a.reshape(2, 2, 2, cols // 4, a.shape[2]) for a in near + far] + weights
    layers = sum(w.shape[1] for w in weights) // out_width
    out = jax.ShapeDtypeStruct((layers, 2, 2, cols // 4, out_width), BF16)
    return whole_call(
        functools.partial(project_kernel, len(near)), at, args, [out, out], "project", 2 * layers)


def whole_call(kernel, at, args, outs, name, us):
    return pl.pallas_call(
        kernel,
        out_shape=outs,
        in_specs=[pl.BlockSpec(memory_space=pltpu.SMEM)] + [pl.BlockSpec(memory_space=pltpu.VMEM)] * len(args),
        out_specs=[pl.BlockSpec(memory_space=pltpu.VMEM)] * len(outs),
        compiler_params=pltpu.CompilerParams(vmem_limit_bytes=VMEM),
        cost_estimate=cost(us),
        name=name,
    )(at, *args)


def total(a, b):
    return (a.astype(F32) + b.astype(F32)).astype(BF16)


def split_kernel(at, kept, got, stay, to_y, to_x, to_xy):
    x, y = at[0], at[3]
    for s in range(kept.shape[0]):
        for out, yy, xx in ((to_xy, 1 - y, 1 - x), (to_y, 1 - y, x), (to_x, y, 1 - x), (stay, y, x)):
            out[s] = total(kept[s, yy, xx], got[s, yy, xx])


def place_kernel(at, *refs):
    x, z, out = at[0], at[1], refs[-1]
    layers = [z, z + 1 - 2 * (z % 2), (z + 2) % 4, 3 - z]
    for stay, from_y, from_x, from_xy in zip(*(refs[i:-1:4] for i in range(4))):
        width = stay.shape[-1]
        for s in range(stay.shape[0]):
            base = 2 * layers.pop(0)
            mine = pl.ds(pl.multiple_of((base + x) * width, width), width)
            theirs = pl.ds(pl.multiple_of((base + 1 - x) * width, width), width)
            out[:, mine] = total(stay[s], from_y[s])
            out[:, theirs] = total(from_x[s], from_xy[s])


def after(value, *earlier):
    return lax.optimization_barrier((value, earlier))[0]


def body_eight(qkv, out_weight):
    _, _, cols, features = qkv.shape
    half = features // 2
    chunks = 2
    width = half // chunks
    heads = width // HEAD
    coef = HEAD ** (-0.5) * LOG2E
    me = lax.axis_index("seq")
    who = lax.axis_index("head")
    z, x, core, y = me // 2, me % 2, who % 2, who // 2
    at = jnp.stack([x, z, core, y]).astype(jnp.int32)
    local = qkv.reshape(3, cols, features)
    first = x == 0

    def seq_perm(array, *layers, cross=False):
        pairs = [(2 * a + i, 2 * b + (1 - i if cross else i)) for a, b in layers for i in range(2)]
        return lax.ppermute(array, "seq", pairs)

    def swap(array):
        return seq_perm(array, (0, 0), (1, 1), (2, 2), (3, 3), cross=True)

    def head_perm(array, flip):
        return lax.ppermute(array, "head", [(i, i ^ flip) for i in range(4)])

    def lanes(lo, hi, part, source=local):
        return lax.dynamic_slice(source, (lo, 0, part * half), (hi - lo, cols, half))

    def lanes(lo, hi, half_of):
        return lax.dynamic_slice(local, (lo, 0, half_of * half), (hi - lo, cols, half))

    def pieces(array, c):
        return array[..., c * width : (c + 1) * width]

    w_halves = [pieces(out_weight, c) for c in range(chunks)]
    w_first = seq_perm(w_halves[0], (0, 2), (1, 3), (2, 0), (3, 1))
    q_m, q_o = lanes(0, 1, x), swap(lanes(0, 1, 1 - x))
    kv_m, kv_give = lanes(1, 3, x), lanes(1, 3, 1 - x)
    q, qs, low = [], [], []
    for c in range(chunks):
        a, b = pieces(q_m, c), pieces(q_o, c)
        q.append(jnp.concatenate([jnp.where(first, a, b), jnp.where(first, b, a)]))
        block, last = (w.reshape(q[c].shape) for w in (w_halves[c], w_halves[1]))
        if c == 0:
            going = [jnp.where(z == 1, last, q[c]), jnp.where(z == 3, q[c], jnp.where(z == 0, last, block))]
        else:
            going = after([q[c], jnp.where(z == 3, q[c], block)], *qs[0])
        qs.append([
            seq_perm(going[0], (2, 1), (3, 2), *([(1, 3)] if c == 0 else [])),
            seq_perm(going[1], (3, 1), (1, 0), (2, 3), *([(0, 2)] if c == 0 else [])),
        ])
        if c == 0:
            kv_o = swap(after(kv_give, q[0], w_first))
            low.append([seq_perm(pieces(kv_m, c), (0, 1)), seq_perm(pieces(kv_give, c), (0, 1), cross=True)])
        else:
            up = jnp.concatenate([pieces(kv_m, c), pieces(kv_o, c)])
            low.append([seq_perm(after(up, *low[0]), (0, 1))])

    struct = jax.ShapeDtypeStruct
    partial = struct((2 * cols + lse_height(cols), width), BF16)
    oa, ob, own, sent = [], [], [], []
    turn = at
    for c in range(chunks):
        pair = [(kv_m, c * heads), (kv_o, c * heads)]
        a, b = head_call(
            functools.partial(upper_kernel, coef, cols), turn,
            [(a, 0) for a in qs[c]] + pair + [(a, 0) for a in low[c]] + [(out_weight, c * heads)], [partial] * 2, heads, "upper_rows", 7)
        sent.append(a)
        oa.append(seq_perm(a, (1, 2), (2, 3)))
        ob.append(seq_perm(b, (1, 3), (0, 1), (3, 2)))
        (mine,) = head_call(
            functools.partial(own_kernel, coef, cols), after(at, a), [(q[c], 0)] + pair + [(a, 0) for a in low[c]],
            [partial], heads, "own_rows", 6)
        own.append(mine)
        turn = after(at, mine)

    depth = out_weight.shape[0]

    def block(array):
        return array.reshape(depth, width)

    def pair_swap(half):
        return seq_perm(half, (0, 1), (1, 0), (2, 3), (3, 2))

    w_near = [jnp.where((z == 0) | (z == 3), block(qs[c][1]), ob[c][:depth]) for c in range(chunks)]
    w_last = seq_perm(after(w_halves[1], own[0], *qs[1]), (2, 0), (3, 1))
    w_other = [pair_swap(after(w_first, oa[0], ob[0]))]

    def merged(c, earlier):
        (a,) = head_call(
            functools.partial(merge_kernel, cols), after(at, earlier), [(a[c], 0) for a in (own, oa, ob)],
            [struct((2, cols, width), BF16)], heads, "merge", 2)
        return a, swap(a)

    first_half = merged(0, (own[1], w_last))
    up_last = jnp.where(z == 2, block(qs[0][1]), block(qs[0][0]))
    w_far = [w_first, jnp.where(z >= 2, up_last, after(w_last, own[1]))]
    w_other.append(pair_swap(w_far[1]))
    near, far = map(list, zip(first_half, merged(1, (first_half[1], w_other))))

    parts = []
    for weights in (
        [out_weight] + w_near,
        w_far + w_other,
    ):
        send, kept = project(at, near, far, weights, out_weight.shape[1])
        got = head_perm(send, 1)
        piece = struct(send.shape[:1] + send.shape[3:], BF16)
        stay, to_y, to_x, to_xy = whole_call(
            split_kernel, at, [kept, got], [piece] * 4, "split", 2)
        diagonal = [((2 * i + j) * 4 + h, (2 * i + 1 - j) * 4 + (h ^ 2)) for i in range(4) for j in range(2) for h in range(4)]
        from_xy = lax.ppermute(to_xy, ("seq", "head"), diagonal)
        parts += [stay, head_perm(to_y, 2), swap(to_x), from_xy]
    (out,) = whole_call(
        place_kernel, at, parts, [struct((cols // 4, 8 * out_weight.shape[1]), BF16)], "place", 2)
    return out.reshape(cols // 4, 1, 8 * out_weight.shape[1])


def solution(mesh):
    in_specs = (P(None, "seq", None, "head"), P("head", "seq"))
    out_specs = P("head", "seq", None)
    small = mesh.shape["seq"] == 8 and mesh.shape["head"] == 4

    def body(qkv, out_weight):
        if small and qkv.shape[1] == 1:
            return body_eight(qkv, out_weight)
        return body_any(qkv, out_weight)

    return jax.shard_map(body, mesh=mesh, in_specs=in_specs, out_specs=out_specs, check_vma=False)
```

```python
import functools
import jax
import jax.numpy as jnp
from jax import lax
from jax.experimental import pallas as pl
from jax.experimental.pallas import tpu as pltpu
from jax.sharding import PartitionSpec as P

HEAD = 128
LOG2E = 1.4426950408889634
NEG = -1e30
QB = 128
VMEM = 24 * 1024 * 1024
F32, BF16 = jnp.float32, jnp.bfloat16


def shifted(shard, axis, by):
    size = lax.axis_size(axis)
    pairs = [(i, i + by) for i in range(size) if 0 <= i + by < size]
    return lax.ppermute(shard, axis, pairs)


def column_part(part):
    queries, keys_part, values = (part[0], part[1], part[2])
    rows = queries.shape[0]
    scale = queries.shape[-1] ** (-0.5)
    scores = (
        jnp.einsum("rchd,schd->chrs", queries, keys_part, preferred_element_type=jnp.float32)
        * scale
    )
    r_idx = lax.broadcasted_iota(jnp.int32, (rows, rows), 0)
    s_idx = lax.broadcasted_iota(jnp.int32, (rows, rows), 1)
    allowed = s_idx <= r_idx - 2
    masked = jnp.where(allowed, scores, jnp.float32(-1e30))
    peak = jnp.max(masked, axis=-1)
    weights = jnp.where(allowed, jnp.exp(masked - peak[..., None]), jnp.float32(0.0))
    total = jnp.maximum(jnp.sum(weights, axis=-1), jnp.float32(1.0))
    rounded = weights.astype(jnp.bfloat16)
    mixed = jnp.einsum("chrs,schd->rchd", rounded, values, preferred_element_type=jnp.float32)
    col_out = (mixed / jnp.transpose(total, (2, 0, 1))[..., None]).astype(jnp.bfloat16)
    col_lse = jnp.transpose(peak + jnp.log(total), (2, 0, 1))
    return (col_out, col_lse)


def row_part(local, previous, first_row):
    rows_dev, cols, heads_local, head_size = (
        local.shape[1],
        local.shape[2],
        local.shape[3],
        local.shape[4],
    )
    scale = head_size ** (-0.5)
    keys_ext = jnp.concatenate([previous, local[1:3]], axis=1)
    key_idx = lax.broadcasted_iota(jnp.int32, (cols, 2 * cols), 1)
    query_idx = lax.broadcasted_iota(jnp.int32, (cols, 2 * cols), 0)

    def one_row(index):
        queries = lax.dynamic_index_in_dim(local[0], index, 0, keepdims=False)
        pair = keys_ext.reshape(2, 2 * cols, heads_local, head_size)
        scores = (
            jnp.einsum("qhd,khd->hqk", queries, pair[0], preferred_element_type=jnp.float32) * scale
        )
        allowed = (key_idx < cols) & (first_row + index > 0) | (key_idx >= cols) & (
            key_idx - cols <= query_idx
        )
        masked = jnp.where(allowed[None], scores, jnp.float32(-1e30))
        peak = jnp.max(masked, axis=-1)
        weights = jnp.where(allowed[None], jnp.exp(masked - peak[..., None]), jnp.float32(0.0))
        total = jnp.sum(weights, axis=-1)
        rounded = weights.astype(jnp.bfloat16)
        mixed = jnp.einsum("hqk,khd->qhd", rounded, pair[1], preferred_element_type=jnp.float32)
        return (mixed / jnp.transpose(total)[..., None], jnp.transpose(peak + jnp.log(total)))

    return lax.map(one_row, jnp.arange(rows_dev, dtype=jnp.int32))


def body_any(qkv, out_weight):
    rows_dev, cols, features = (qkv.shape[1], qkv.shape[2], qkv.shape[3])
    head_size = HEAD
    heads_local = features // head_size
    local = qkv.reshape(3, rows_dev, cols, heads_local, head_size)
    previous = shifted(local[1:3, rows_dev - 1 : rows_dev], "seq", 1)
    first_row = lax.axis_index("seq") * rows_dev
    row_out, row_lse = row_part(local, previous, first_row)
    columns = lax.all_to_all(local, "seq", split_axis=2, concat_axis=1, tiled=True)
    col_part_out, col_part_lse = column_part(columns)
    col_out, col_lse = (
        lax.all_to_all(col_part_out, "seq", split_axis=0, concat_axis=1, tiled=True),
        lax.all_to_all(
            col_part_lse.astype(jnp.bfloat16), "seq", split_axis=0, concat_axis=1, tiled=True
        ).astype(col_part_lse.dtype),
    )
    top = jnp.maximum(row_lse, col_lse)
    left = jnp.exp(row_lse - top)
    right = jnp.exp(col_lse - top)
    attended = (left[..., None] * row_out + right[..., None] * col_out.astype(jnp.float32)) / (
        left + right
    )[..., None]
    attended = attended.astype(jnp.bfloat16).reshape(rows_dev, cols, features)
    terms = jnp.einsum(
        "rcf,fd->crd",
        attended,
        lax.all_gather(out_weight, "seq", axis=1, tiled=True),
        preferred_element_type=jnp.float32,
    )
    summed = lax.psum_scatter(terms.astype(jnp.bfloat16), "head", scatter_dimension=0, tiled=True)
    return summed


def dense_scores(q, k):
    return lax.dot_general(q, k, (((1,), (1,)), ((), ())), preferred_element_type=F32)


def col_scores(q, k):
    prod = q * k
    high = prod.astype(BF16)
    low = (prod - high.astype(F32)).astype(BF16)
    ones = jnp.ones((2 * HEAD, HEAD), BF16)
    return jnp.dot(jnp.concatenate([high, low], axis=1), ones, preferred_element_type=F32)


def with_ones(v):
    return jnp.concatenate([v, jnp.ones_like(v)], axis=1)


def attend(q, dense, cols, coef):
    rows = q.shape[0]
    scores = []
    for k, _, allowed in dense:
        s = dense_scores(q, k)
        scores.append(s if allowed is None else jnp.where(allowed, s, NEG))
    singles = []
    if cols:
        wide = q.astype(F32)
    for k, _, allowed in cols:
        c = col_scores(wide, k)
        singles.append(c if allowed is None else jnp.where(allowed, c, NEG))
    peak = None
    for s in scores:
        for j in range(s.shape[1] // HEAD):
            part = s[:, j * HEAD : (j + 1) * HEAD]
            peak = part if peak is None else jnp.maximum(peak, part)
    if peak is not None:
        peak = jnp.broadcast_to(jnp.max(peak, axis=1, keepdims=True), (rows, HEAD))
    for c in singles:
        peak = c if peak is None else jnp.maximum(peak, c)
    peak = peak * coef
    both = None
    for s, (_, v, _) in zip(scores, dense):
        tiled = jnp.concatenate([peak] * (s.shape[1] // HEAD), axis=1)
        p = jnp.exp2(s * coef - tiled).astype(BF16)
        term = jnp.dot(p, v, preferred_element_type=F32)
        both = term if both is None else both + term
    out = None if both is None else both[:, :HEAD]
    total = None if both is None else both[:, HEAD:]
    for c, (_, v, _) in zip(singles, cols):
        w = jnp.exp2(c * coef - peak)
        total = w if total is None else total + w
        out = w * v if out is None else out + w * v
    return out / total, peak + jnp.log2(total)


def lse_rows(even, odd):
    lane = lax.broadcasted_iota(jnp.int32, (HEAD, HEAD), 1)
    evens, odds = [], []
    for t in range(even.shape[0] // HEAD):
        block = slice(t * HEAD, (t + 1) * HEAD)
        turned = jnp.transpose(jnp.where(lane == 0, even[block], odd[block]))
        evens.append(turned[0:1])
        odds.append(turned[1:2])
    return evens, odds


def put_lse(ref, base, evens, odds):
    rows = jnp.concatenate(evens + odds, axis=0)
    pad = (-rows.shape[0]) % 16
    if pad:
        rows = jnp.concatenate([rows, jnp.zeros((pad, HEAD), F32)], axis=0)
    count = rows.shape[0]
    for piece in range(3):
        part = rows.astype(BF16)
        ref[pl.ds(base + piece * count, count), :] = part
        rows = rows - part.astype(F32)


def get_lse(ref, base, cols):
    blocks = cols // HEAD
    count = -(-2 * blocks // 16) * 16
    rows = sum(ref[pl.ds(base + piece * count, count), :].astype(F32) for piece in range(3))
    turned = [
        jnp.transpose(jnp.broadcast_to(rows[t : t + 1], (HEAD, HEAD))) for t in range(2 * blocks)
    ]
    return jnp.concatenate(turned[:blocks], axis=0), jnp.concatenate(turned[blocks:], axis=0)


def lse_height(cols):
    return 3 * (-(-2 * (cols // HEAD) // 16) * 16)


def stacked(refs):
    return [ref[i] for ref in refs for i in range(ref.shape[0])]


def own_kernel(coef, cols, at, q, kv_m, kv_o, *refs):
    x, z = at[0], at[1]
    below = z == 1
    block = 256
    tri = lax.broadcasted_iota(jnp.int32, (block, block), 1) <= lax.broadcasted_iota(
        jnp.int32, (block, block), 0
    )
    first = x == 0
    k_e, k_o = jnp.where(first, kv_m[0], kv_o[0]), jnp.where(first, kv_o[0], kv_m[0])
    v_e, v_o = jnp.where(first, kv_m[1], kv_o[1]), jnp.where(first, kv_o[1], kv_m[1])
    v_e, v_o = with_ones(v_e), with_ones(v_o)
    *low, out = refs
    m_k, m_v, o_k, o_v = stacked(low)
    lk_e, lk_o = jnp.where(first, m_k, o_k), jnp.where(first, o_k, m_k)
    lv_e, lv_o = jnp.where(first, m_v, o_v), jnp.where(first, o_v, m_v)
    lv_o1 = with_ones(lv_o)
    evens, odds = [], []
    for part in range(cols // block):
        a, b = part * block, (part + 1) * block
        mine = slice(a, b)
        col_e = (lk_e[mine].astype(F32), lv_e[mine].astype(F32), below)
        col_o = (lk_o[mine].astype(F32), lv_o[mine].astype(F32), below)

        def causal(k, v):
            blocks = [(k[a:b], v[a:b], tri)]
            return blocks if part == 0 else [(k[:a], v[:a], None)] + blocks

        o1, l1 = attend(q[0, mine], causal(k_e, v_e) + [(lk_o, lv_o1, below)], [col_e], coef)
        o2, l2 = attend(q[1, mine], causal(k_o, v_o) + [(k_e, v_e, None)], [col_e, col_o], coef)
        out[mine] = o1.astype(BF16)
        out[cols + a : cols + b] = o2.astype(BF16)
        e, o = lse_rows(l1, l2)
        evens, odds = evens + e, odds + o
    put_lse(out, 2 * cols, evens, odds)


def upper_kernel(coef, cols, at, qa, qb, kv_m, kv_o, *refs):
    x, z = at[0], at[1]
    below = z == 1
    first = x == 0
    block = 256
    k_e, k_o = jnp.where(first, kv_m[0], kv_o[0]), jnp.where(first, kv_o[0], kv_m[0])
    v_e, v_o = jnp.where(first, kv_m[1], kv_o[1]), jnp.where(first, kv_o[1], kv_m[1])
    v_o1 = with_ones(v_o)
    *low, weight, out_a, out_b = refs
    lows = stacked(low)
    rows_a, rows_b = ([], []), ([], [])
    for index in range(cols // block):
        a, b = index * block, (index + 1) * block
        mine = slice(a, b)
        m_k, m_v, o_k, o_v = (part[mine].astype(F32) for part in lows)
        ce = (k_e[mine].astype(F32), v_e[mine].astype(F32), None)
        co = (k_o[mine].astype(F32), v_o[mine].astype(F32), None)
        low = [(m_k, m_v, below), (o_k, o_v, below)]
        for q, out, rows, dense, singles in (
            (qa, out_a, rows_a, [(k_o, v_o1, None)], [ce]),
            (qb, out_b, rows_b, [], [ce, co]),
        ):
            o1, l1 = attend(q[0, mine], dense, singles + low, coef)
            o2, l2 = attend(q[1, mine], [], [ce, co] + low, coef)
            o1, o2 = o1.astype(BF16), o2.astype(BF16)
            other = slice(cols + a, cols + b)
            if out is out_b:
                o1, o2 = jnp.where(below, o1, weight[mine]), jnp.where(below, o2, weight[other])
            out[mine] = o1
            out[other] = o2
            e, o = lse_rows(l1, l2)
            rows[0].extend(e)
            rows[1].extend(o)
    put_lse(out_a, 2 * cols, *rows_a)
    put_lse(out_b, 2 * cols, *rows_b)


def merge_kernel(cols, at, own, oa, ob, out):
    z = at[1]
    own_l, a_l, b_l = (get_lse(ref, 2 * cols, cols) for ref in (own, oa, ob))
    for row in range(2):
        tokens = slice(row * cols, (row + 1) * cols)
        l0 = own_l[row]
        l1 = jnp.where(z >= 2, a_l[row], NEG)
        l2 = jnp.where(z >= 3, b_l[row], NEG)
        top = jnp.maximum(l0, jnp.maximum(l1, l2))
        w0, w1, w2 = jnp.exp2(l0 - top), jnp.exp2(l1 - top), jnp.exp2(l2 - top)
        mixed = w0 * own[tokens].astype(F32) + w1 * oa[tokens].astype(F32) + w2 * ob[tokens].astype(F32)
        out[row] = (mixed / (w0 + w1 + w2)).astype(BF16)


def cost(us):
    return pl.CostEstimate(flops=int(us * 1e9), bytes_accessed=1024, transcendentals=0)


def head_call(kernel, at, args, outs, heads, name, us):
    def spec(shape, start=0):
        lead = len(shape) - 1
        return pl.BlockSpec(tuple(shape[:-1]) + (HEAD,), lambda h, at: (0,) * lead + (start + h,))

    return pl.pallas_call(
        kernel,
        out_shape=outs,
        grid_spec=pltpu.PrefetchScalarGridSpec(
            num_scalar_prefetch=1,
            grid=(heads,),
            in_specs=[spec(a.shape, start) for a, start in args],
            out_specs=[spec(o.shape) for o in outs],
        ),
        compiler_params=pltpu.CompilerParams(vmem_limit_bytes=VMEM),
        cost_estimate=cost(us),
        name=name,
    )(at, *(a for a, _ in args))


def project_kernel(chunks, at, *refs):
    x, core = at[0], at[2]
    near, far = refs[:chunks], refs[chunks : 2 * chunks]
    weights, send, keep = refs[2 * chunks : -2], refs[-2], refs[-1]
    tokens = near[0].shape[3]
    half = sum(ref.shape[4] for ref in near)
    for who, out in ((1 - core, send), (core, keep)):

        def rows(ref):
            return jnp.concatenate([ref[r, y, who] for y in range(2) for r in range(2)], axis=0)

        left = jnp.concatenate([rows(ref) for ref in near], axis=1)
        right = jnp.concatenate([rows(ref) for ref in far], axis=1)
        base = 0
        for weight in weights:
            top = weight[pl.ds(pl.multiple_of(x * half, half), half)]
            bottom = weight[pl.ds(pl.multiple_of((1 - x) * half, half), half)]
            c = jnp.dot(left, top, preferred_element_type=F32) + jnp.dot(right, bottom, preferred_element_type=F32)
            width = weight.shape[1]
            s, lane = base // out.shape[4], base % out.shape[4]
            out[s, :, :, :, lane : lane + width] = c.astype(BF16).reshape(2, 2, tokens, width)
            base += width


def project(at, near, far, weights, out_width):
    cols = near[0].shape[1]
    args = [a.reshape(2, 2, 2, cols // 4, a.shape[2]) for a in near + far] + weights
    layers = sum(w.shape[1] for w in weights) // out_width
    out = jax.ShapeDtypeStruct((layers, 2, 2, cols // 4, out_width), BF16)
    return whole_call(
        functools.partial(project_kernel, len(near)), at, args, [out, out], "project", 2 * layers)


def whole_call(kernel, at, args, outs, name, us):
    return pl.pallas_call(
        kernel,
        out_shape=outs,
        in_specs=[pl.BlockSpec(memory_space=pltpu.SMEM)] + [pl.BlockSpec(memory_space=pltpu.VMEM)] * len(args),
        out_specs=[pl.BlockSpec(memory_space=pltpu.VMEM)] * len(outs),
        compiler_params=pltpu.CompilerParams(vmem_limit_bytes=VMEM),
        cost_estimate=cost(us),
        name=name,
    )(at, *args)


def total(a, b):
    return (a.astype(F32) + b.astype(F32)).astype(BF16)


def split_kernel(at, kept, got, stay, to_y, to_x, to_xy):
    x, y = at[0], at[3]
    for s in range(kept.shape[0]):
        for out, yy, xx in ((to_xy, 1 - y, 1 - x), (to_y, 1 - y, x), (to_x, y, 1 - x), (stay, y, x)):
            out[s] = total(kept[s, yy, xx], got[s, yy, xx])


def place_kernel(at, *refs):
    x, z, out = at[0], at[1], refs[-1]
    layers = [z, z + 1 - 2 * (z % 2), (z + 2) % 4, 3 - z]
    for stay, from_y, from_x, from_xy in zip(*(refs[i:-1:4] for i in range(4))):
        width = stay.shape[-1]
        for s in range(stay.shape[0]):
            base = 2 * layers.pop(0)
            mine = pl.ds(pl.multiple_of((base + x) * width, width), width)
            theirs = pl.ds(pl.multiple_of((base + 1 - x) * width, width), width)
            out[:, mine] = total(stay[s], from_y[s])
            out[:, theirs] = total(from_x[s], from_xy[s])


def after(value, *earlier):
    return lax.optimization_barrier((value, earlier))[0]


def body_eight(qkv, out_weight):
    _, _, cols, features = qkv.shape
    half = features // 2
    chunks = 2
    width = half // chunks
    heads = width // HEAD
    coef = HEAD ** (-0.5) * LOG2E
    me = lax.axis_index("seq")
    who = lax.axis_index("head")
    z, x, core, y = me // 2, me % 2, who % 2, who // 2
    at = jnp.stack([x, z, core, y]).astype(jnp.int32)
    local = qkv.reshape(3, cols, features)
    first = x == 0

    def seq_perm(array, *layers, cross=False):
        pairs = [(2 * a + i, 2 * b + (1 - i if cross else i)) for a, b in layers for i in range(2)]
        return lax.ppermute(array, "seq", pairs)

    def swap(array):
        return seq_perm(array, (0, 0), (1, 1), (2, 2), (3, 3), cross=True)

    def head_perm(array, flip):
        return lax.ppermute(array, "head", [(i, i ^ flip) for i in range(4)])

    def lanes(lo, hi, part, source=local):
        return lax.dynamic_slice(source, (lo, 0, part * half), (hi - lo, cols, half))

    def lanes(lo, hi, half_of):
        return lax.dynamic_slice(local, (lo, 0, half_of * half), (hi - lo, cols, half))

    def pieces(array, c):
        return array[..., c * width : (c + 1) * width]

    q_m, q_o = lanes(0, 1, x), swap(lanes(0, 1, 1 - x))
    w_second = seq_perm(out_weight, (0, 2))
    w_halves = [pieces(out_weight, c) for c in range(chunks)]
    kv_m, kv_give = lanes(1, 3, x), lanes(1, 3, 1 - x)
    q, qs, low = [], [], []
    for c in range(chunks):
        a, b = pieces(q_m, c), pieces(q_o, c)
        q.append(jnp.concatenate([jnp.where(first, a, b), jnp.where(first, b, a)]))
        block = w_halves[c].reshape(q[c].shape)
        going = [jnp.where(z == 1, block, q[c]), jnp.where(z == 3, q[c], block)]
        if c:
            going = [after(a, b) for a, b in zip(going, qs[0])]
        qs.append([seq_perm(going[0], (2, 1), (3, 2), (1, 3)), seq_perm(going[1], (3, 1), (1, 0), (2, 3))])
        if c == 0:
            kv_o = swap(after(kv_give, q[0]))
            ups = after([pieces(kv_m, c), pieces(kv_give, c)], w_second)
            low.append([seq_perm(ups[0], (0, 1)), seq_perm(ups[1], (0, 1), cross=True)])
        else:
            up = jnp.concatenate([pieces(kv_m, c), pieces(kv_o, c)])
            low.append([seq_perm(after(up, *low[0]), (0, 1))])

    struct = jax.ShapeDtypeStruct
    partial = struct((2 * cols + lse_height(cols), width), BF16)
    oa, ob, own, sent = [], [], [], []
    turn = at
    for c in range(chunks):
        pair = [(kv_m, c * heads), (kv_o, c * heads)]
        a, b = head_call(
            functools.partial(upper_kernel, coef, cols), turn,
            [(a, 0) for a in qs[c]] + pair + [(a, 0) for a in low[c]] + [(out_weight, c * heads)], [partial] * 2, heads, "upper_rows", 7)
        sent.append(a)
        oa.append(seq_perm(a, (1, 2), (2, 3)))
        ob.append(seq_perm(b, (1, 3), (0, 1), (3, 2)))
        (mine,) = head_call(
            functools.partial(own_kernel, coef, cols), after(at, a), [(q[c], 0)] + pair + [(a, 0) for a in low[c]],
            [partial], heads, "own_rows", 6)
        own.append(mine)
        turn = after(at, mine)

    depth = out_weight.shape[0]
    w_near = [
        jnp.where((z == 0) | (z == 3), qs[c][1].reshape(depth, width), ob[c][:depth]) for c in range(chunks)
    ]
    w_down = [seq_perm(after(w_halves[0], own[0], *qs[1]), (2, 0), (3, 1))]
    w_down.append(seq_perm(after(w_halves[1], w_down[0], sent[1]), (2, 0), (3, 1)))

    def far_half(c, earlier):
        up = jnp.where(z == 2, pieces(w_second, c), qs[c][0].reshape(depth, width))
        half = jnp.where(z >= 2, up, after(w_down[c], earlier))
        return half, seq_perm(half, (0, 1), (1, 0), (2, 3), (3, 2))

    def merged(c, earlier):
        (a,) = head_call(
            functools.partial(merge_kernel, cols), after(at, earlier), [(a[c], 0) for a in (own, oa, ob)],
            [struct((2, cols, width), BF16)], heads, "merge", 2)
        return a, swap(a)

    far_0 = far_half(0, own[1])
    first_half = merged(0, own[1])
    near, far = map(list, zip(first_half, merged(1, (first_half[1], far_0[1]))))
    w_far, w_other = map(list, zip(far_0, far_half(1, near[1])))

    parts = []
    turn = at
    for weights in (
        [out_weight] + w_near,
        w_far + w_other,
    ):
        send, kept = project(turn, near, far, weights, out_weight.shape[1])
        turn = after(at, send)
        got = head_perm(send, 1)
        piece = struct(send.shape[:1] + send.shape[3:], BF16)
        stay, to_y, to_x, to_xy = whole_call(
            split_kernel, at, [kept, got], [piece] * 4, "split", 2)
        diagonal = [((2 * i + j) * 4 + h, (2 * i + 1 - j) * 4 + (h ^ 2)) for i in range(4) for j in range(2) for h in range(4)]
        from_xy = lax.ppermute(to_xy, ("seq", "head"), diagonal)
        parts += [stay, head_perm(to_y, 2), swap(to_x), from_xy]
    (out,) = whole_call(
        place_kernel, at, parts, [struct((cols // 4, 8 * out_weight.shape[1]), BF16)], "place", 2)
    return out.reshape(cols // 4, 1, 8 * out_weight.shape[1])


def solution(mesh):
    in_specs = (P(None, "seq", None, "head"), P("head", "seq"))
    out_specs = P("head", "seq", None)
    small = mesh.shape["seq"] == 8 and mesh.shape["head"] == 4

    def body(qkv, out_weight):
        if small and qkv.shape[1] == 1:
            return body_eight(qkv, out_weight)
        return body_any(qkv, out_weight)

    return jax.shard_map(body, mesh=mesh, in_specs=in_specs, out_specs=out_specs, check_vma=False)
```

```python
import functools
import jax
import jax.numpy as jnp
from jax import lax
from jax.experimental import pallas as pl
from jax.experimental.pallas import tpu as pltpu
from jax.sharding import PartitionSpec as P

HEAD = 128
LOG2E = 1.4426950408889634
NEG = -1e30
QB = 128
VMEM = 24 * 1024 * 1024
F32, BF16 = jnp.float32, jnp.bfloat16


def shifted(shard, axis, by):
    size = lax.axis_size(axis)
    pairs = [(i, i + by) for i in range(size) if 0 <= i + by < size]
    return lax.ppermute(shard, axis, pairs)


def column_part(part):
    queries, keys_part, values = (part[0], part[1], part[2])
    rows = queries.shape[0]
    scale = queries.shape[-1] ** (-0.5)
    scores = (
        jnp.einsum("rchd,schd->chrs", queries, keys_part, preferred_element_type=jnp.float32)
        * scale
    )
    r_idx = lax.broadcasted_iota(jnp.int32, (rows, rows), 0)
    s_idx = lax.broadcasted_iota(jnp.int32, (rows, rows), 1)
    allowed = s_idx <= r_idx - 2
    masked = jnp.where(allowed, scores, jnp.float32(-1e30))
    peak = jnp.max(masked, axis=-1)
    weights = jnp.where(allowed, jnp.exp(masked - peak[..., None]), jnp.float32(0.0))
    total = jnp.maximum(jnp.sum(weights, axis=-1), jnp.float32(1.0))
    rounded = weights.astype(jnp.bfloat16)
    mixed = jnp.einsum("chrs,schd->rchd", rounded, values, preferred_element_type=jnp.float32)
    col_out = (mixed / jnp.transpose(total, (2, 0, 1))[..., None]).astype(jnp.bfloat16)
    col_lse = jnp.transpose(peak + jnp.log(total), (2, 0, 1))
    return (col_out, col_lse)


def row_part(local, previous, first_row):
    rows_dev, cols, heads_local, head_size = (
        local.shape[1],
        local.shape[2],
        local.shape[3],
        local.shape[4],
    )
    scale = head_size ** (-0.5)
    keys_ext = jnp.concatenate([previous, local[1:3]], axis=1)
    key_idx = lax.broadcasted_iota(jnp.int32, (cols, 2 * cols), 1)
    query_idx = lax.broadcasted_iota(jnp.int32, (cols, 2 * cols), 0)

    def one_row(index):
        queries = lax.dynamic_index_in_dim(local[0], index, 0, keepdims=False)
        pair = keys_ext.reshape(2, 2 * cols, heads_local, head_size)
        scores = (
            jnp.einsum("qhd,khd->hqk", queries, pair[0], preferred_element_type=jnp.float32) * scale
        )
        allowed = (key_idx < cols) & (first_row + index > 0) | (key_idx >= cols) & (
            key_idx - cols <= query_idx
        )
        masked = jnp.where(allowed[None], scores, jnp.float32(-1e30))
        peak = jnp.max(masked, axis=-1)
        weights = jnp.where(allowed[None], jnp.exp(masked - peak[..., None]), jnp.float32(0.0))
        total = jnp.sum(weights, axis=-1)
        rounded = weights.astype(jnp.bfloat16)
        mixed = jnp.einsum("hqk,khd->qhd", rounded, pair[1], preferred_element_type=jnp.float32)
        return (mixed / jnp.transpose(total)[..., None], jnp.transpose(peak + jnp.log(total)))

    return lax.map(one_row, jnp.arange(rows_dev, dtype=jnp.int32))


def body_any(qkv, out_weight):
    rows_dev, cols, features = (qkv.shape[1], qkv.shape[2], qkv.shape[3])
    head_size = HEAD
    heads_local = features // head_size
    local = qkv.reshape(3, rows_dev, cols, heads_local, head_size)
    previous = shifted(local[1:3, rows_dev - 1 : rows_dev], "seq", 1)
    first_row = lax.axis_index("seq") * rows_dev
    row_out, row_lse = row_part(local, previous, first_row)
    columns = lax.all_to_all(local, "seq", split_axis=2, concat_axis=1, tiled=True)
    col_part_out, col_part_lse = column_part(columns)
    col_out, col_lse = (
        lax.all_to_all(col_part_out, "seq", split_axis=0, concat_axis=1, tiled=True),
        lax.all_to_all(
            col_part_lse.astype(jnp.bfloat16), "seq", split_axis=0, concat_axis=1, tiled=True
        ).astype(col_part_lse.dtype),
    )
    top = jnp.maximum(row_lse, col_lse)
    left = jnp.exp(row_lse - top)
    right = jnp.exp(col_lse - top)
    attended = (left[..., None] * row_out + right[..., None] * col_out.astype(jnp.float32)) / (
        left + right
    )[..., None]
    attended = attended.astype(jnp.bfloat16).reshape(rows_dev, cols, features)
    terms = jnp.einsum(
        "rcf,fd->crd",
        attended,
        lax.all_gather(out_weight, "seq", axis=1, tiled=True),
        preferred_element_type=jnp.float32,
    )
    summed = lax.psum_scatter(terms.astype(jnp.bfloat16), "head", scatter_dimension=0, tiled=True)
    return summed


def dense_scores(q, k):
    return lax.dot_general(q, k, (((1,), (1,)), ((), ())), preferred_element_type=F32)


def col_scores(q, k):
    prod = q * k
    high = prod.astype(BF16)
    low = (prod - high.astype(F32)).astype(BF16)
    ones = jnp.ones((2 * HEAD, HEAD), BF16)
    return jnp.dot(jnp.concatenate([high, low], axis=1), ones, preferred_element_type=F32)


def with_ones(v):
    return jnp.concatenate([v, jnp.ones_like(v)], axis=1)


def attend(q, dense, cols, coef):
    rows = q.shape[0]
    scores = []
    for k, _, allowed in dense:
        s = dense_scores(q, k)
        scores.append(s if allowed is None else jnp.where(allowed, s, NEG))
    singles = []
    if cols:
        wide = q.astype(F32)
    for k, _, allowed in cols:
        c = col_scores(wide, k)
        singles.append(c if allowed is None else jnp.where(allowed, c, NEG))
    peak = None
    for s in scores:
        for j in range(s.shape[1] // HEAD):
            part = s[:, j * HEAD : (j + 1) * HEAD]
            peak = part if peak is None else jnp.maximum(peak, part)
    if peak is not None:
        peak = jnp.broadcast_to(jnp.max(peak, axis=1, keepdims=True), (rows, HEAD))
    for c in singles:
        peak = c if peak is None else jnp.maximum(peak, c)
    peak = peak * coef
    both = None
    for s, (_, v, _) in zip(scores, dense):
        tiled = jnp.concatenate([peak] * (s.shape[1] // HEAD), axis=1)
        p = jnp.exp2(s * coef - tiled).astype(BF16)
        term = jnp.dot(p, v, preferred_element_type=F32)
        both = term if both is None else both + term
    out = None if both is None else both[:, :HEAD]
    total = None if both is None else both[:, HEAD:]
    for c, (_, v, _) in zip(singles, cols):
        w = jnp.exp2(c * coef - peak)
        total = w if total is None else total + w
        out = w * v if out is None else out + w * v
    return out / total, peak + jnp.log2(total)


def lse_rows(even, odd):
    lane = lax.broadcasted_iota(jnp.int32, (HEAD, HEAD), 1)
    evens, odds = [], []
    for t in range(even.shape[0] // HEAD):
        block = slice(t * HEAD, (t + 1) * HEAD)
        turned = jnp.transpose(jnp.where(lane == 0, even[block], odd[block]))
        evens.append(turned[0:1])
        odds.append(turned[1:2])
    return evens, odds


def put_lse(ref, base, evens, odds):
    rows = jnp.concatenate(evens + odds, axis=0)
    pad = (-rows.shape[0]) % 16
    if pad:
        rows = jnp.concatenate([rows, jnp.zeros((pad, HEAD), F32)], axis=0)
    count = rows.shape[0]
    for piece in range(3):
        part = rows.astype(BF16)
        ref[pl.ds(base + piece * count, count), :] = part
        rows = rows - part.astype(F32)


def get_lse(ref, base, cols):
    blocks = cols // HEAD
    count = -(-2 * blocks // 16) * 16
    rows = sum(ref[pl.ds(base + piece * count, count), :].astype(F32) for piece in range(3))
    turned = [
        jnp.transpose(jnp.broadcast_to(rows[t : t + 1], (HEAD, HEAD))) for t in range(2 * blocks)
    ]
    return jnp.concatenate(turned[:blocks], axis=0), jnp.concatenate(turned[blocks:], axis=0)


def lse_height(cols):
    return 3 * (-(-2 * (cols // HEAD) // 16) * 16)


def stacked(refs):
    return [ref[i] for ref in refs for i in range(ref.shape[0])]


def own_kernel(coef, cols, at, q, kv_m, kv_o, *refs):
    x, z = at[0], at[1]
    below = z == 1
    block = 256
    tri = lax.broadcasted_iota(jnp.int32, (block, block), 1) <= lax.broadcasted_iota(
        jnp.int32, (block, block), 0
    )
    first = x == 0
    k_e, k_o = jnp.where(first, kv_m[0], kv_o[0]), jnp.where(first, kv_o[0], kv_m[0])
    v_e, v_o = jnp.where(first, kv_m[1], kv_o[1]), jnp.where(first, kv_o[1], kv_m[1])
    v_e, v_o = with_ones(v_e), with_ones(v_o)
    *low, out = refs
    m_k, m_v, o_k, o_v = stacked(low)
    lk_e, lk_o = jnp.where(first, m_k, o_k), jnp.where(first, o_k, m_k)
    lv_e, lv_o = jnp.where(first, m_v, o_v), jnp.where(first, o_v, m_v)
    lv_o1 = with_ones(lv_o)
    evens, odds = [], []
    for part in range(cols // block):
        a, b = part * block, (part + 1) * block
        mine = slice(a, b)
        col_e = (lk_e[mine].astype(F32), lv_e[mine].astype(F32), below)
        col_o = (lk_o[mine].astype(F32), lv_o[mine].astype(F32), below)

        def causal(k, v):
            blocks = [(k[a:b], v[a:b], tri)]
            return blocks if part == 0 else [(k[:a], v[:a], None)] + blocks

        o1, l1 = attend(q[0, mine], causal(k_e, v_e) + [(lk_o, lv_o1, below)], [col_e], coef)
        o2, l2 = attend(q[1, mine], causal(k_o, v_o) + [(k_e, v_e, None)], [col_e, col_o], coef)
        out[mine] = o1.astype(BF16)
        out[cols + a : cols + b] = o2.astype(BF16)
        e, o = lse_rows(l1, l2)
        evens, odds = evens + e, odds + o
    put_lse(out, 2 * cols, evens, odds)


def upper_kernel(coef, cols, at, qa, qb, kv_m, kv_o, *refs):
    x, z = at[0], at[1]
    below = z == 1
    first = x == 0
    block = 256
    k_e, k_o = jnp.where(first, kv_m[0], kv_o[0]), jnp.where(first, kv_o[0], kv_m[0])
    v_e, v_o = jnp.where(first, kv_m[1], kv_o[1]), jnp.where(first, kv_o[1], kv_m[1])
    v_o1 = with_ones(v_o)
    *low, weight, out_a, out_b = refs
    lows = stacked(low)
    rows_a, rows_b = ([], []), ([], [])
    for index in range(cols // block):
        a, b = index * block, (index + 1) * block
        mine = slice(a, b)
        m_k, m_v, o_k, o_v = (part[mine].astype(F32) for part in lows)
        ce = (k_e[mine].astype(F32), v_e[mine].astype(F32), None)
        co = (k_o[mine].astype(F32), v_o[mine].astype(F32), None)
        low = [(m_k, m_v, below), (o_k, o_v, below)]
        for q, out, rows, dense, singles in (
            (qa, out_a, rows_a, [(k_o, v_o1, None)], [ce]),
            (qb, out_b, rows_b, [], [ce, co]),
        ):
            o1, l1 = attend(q[0, mine], dense, singles + low, coef)
            o2, l2 = attend(q[1, mine], [], [ce, co] + low, coef)
            o1, o2 = o1.astype(BF16), o2.astype(BF16)
            other = slice(cols + a, cols + b)
            useful = below if out is out_b else z < 3
            o1, o2 = jnp.where(useful, o1, weight[mine]), jnp.where(useful, o2, weight[other])
            out[mine] = o1
            out[other] = o2
            e, o = lse_rows(l1, l2)
            rows[0].extend(e)
            rows[1].extend(o)
    put_lse(out_a, 2 * cols, *rows_a)
    put_lse(out_b, 2 * cols, *rows_b)


def merge_kernel(cols, at, own, oa, ob, out):
    z = at[1]
    own_l, a_l, b_l = (get_lse(ref, 2 * cols, cols) for ref in (own, oa, ob))
    for row in range(2):
        tokens = slice(row * cols, (row + 1) * cols)
        l0 = own_l[row]
        l1 = jnp.where(z >= 2, a_l[row], NEG)
        l2 = jnp.where(z >= 3, b_l[row], NEG)
        top = jnp.maximum(l0, jnp.maximum(l1, l2))
        w0, w1, w2 = jnp.exp2(l0 - top), jnp.exp2(l1 - top), jnp.exp2(l2 - top)
        mixed = w0 * own[tokens].astype(F32) + w1 * oa[tokens].astype(F32) + w2 * ob[tokens].astype(F32)
        out[row] = (mixed / (w0 + w1 + w2)).astype(BF16)


def cost(us):
    return pl.CostEstimate(flops=int(us * 1e9), bytes_accessed=1024, transcendentals=0)


def head_call(kernel, at, args, outs, heads, name, us):
    def spec(shape, start=0):
        lead = len(shape) - 1
        return pl.BlockSpec(tuple(shape[:-1]) + (HEAD,), lambda h, at: (0,) * lead + (start + h,))

    return pl.pallas_call(
        kernel,
        out_shape=outs,
        grid_spec=pltpu.PrefetchScalarGridSpec(
            num_scalar_prefetch=1,
            grid=(heads,),
            in_specs=[spec(a.shape, start) for a, start in args],
            out_specs=[spec(o.shape) for o in outs],
        ),
        compiler_params=pltpu.CompilerParams(vmem_limit_bytes=VMEM),
        cost_estimate=cost(us),
        name=name,
    )(at, *(a for a, _ in args))


def project_kernel(chunks, at, *refs):
    x, core = at[0], at[2]
    near, far = refs[:chunks], refs[chunks : 2 * chunks]
    weights, send, keep = refs[2 * chunks : -2], refs[-2], refs[-1]
    tokens = near[0].shape[3]
    half = sum(ref.shape[4] for ref in near)
    for who, out in ((1 - core, send), (core, keep)):

        def rows(ref):
            return jnp.concatenate([ref[r, y, who] for y in range(2) for r in range(2)], axis=0)

        left = jnp.concatenate([rows(ref) for ref in near], axis=1)
        right = jnp.concatenate([rows(ref) for ref in far], axis=1)
        base = 0
        for weight in weights:
            top = weight[pl.ds(pl.multiple_of(x * half, half), half)]
            bottom = weight[pl.ds(pl.multiple_of((1 - x) * half, half), half)]
            c = jnp.dot(left, top, preferred_element_type=F32) + jnp.dot(right, bottom, preferred_element_type=F32)
            width = weight.shape[1]
            s, lane = base // out.shape[4], base % out.shape[4]
            out[s, :, :, :, lane : lane + width] = c.astype(BF16).reshape(2, 2, tokens, width)
            base += width


def project(at, near, far, weights, out_width):
    cols = near[0].shape[1]
    args = [a.reshape(2, 2, 2, cols // 4, a.shape[2]) for a in near + far] + weights
    layers = sum(w.shape[1] for w in weights) // out_width
    out = jax.ShapeDtypeStruct((layers, 2, 2, cols // 4, out_width), BF16)
    return whole_call(
        functools.partial(project_kernel, len(near)), at, args, [out, out], "project", 2 * layers)


def whole_call(kernel, at, args, outs, name, us):
    return pl.pallas_call(
        kernel,
        out_shape=outs,
        in_specs=[pl.BlockSpec(memory_space=pltpu.SMEM)] + [pl.BlockSpec(memory_space=pltpu.VMEM)] * len(args),
        out_specs=[pl.BlockSpec(memory_space=pltpu.VMEM)] * len(outs),
        compiler_params=pltpu.CompilerParams(vmem_limit_bytes=VMEM),
        cost_estimate=cost(us),
        name=name,
    )(at, *args)


def total(a, b):
    return (a.astype(F32) + b.astype(F32)).astype(BF16)


def split_kernel(at, kept, got, stay, to_y, to_x, to_xy):
    x, y = at[0], at[3]
    for s in range(kept.shape[0]):
        for out, yy, xx in ((to_xy, 1 - y, 1 - x), (to_y, 1 - y, x), (to_x, y, 1 - x), (stay, y, x)):
            out[s] = total(kept[s, yy, xx], got[s, yy, xx])


def place_kernel(at, *refs):
    x, z, out = at[0], at[1], refs[-1]
    layers = [z, z + 1 - 2 * (z % 2), (z + 2) % 4, 3 - z]
    for stay, from_y, from_x, from_xy in zip(*(refs[i:-1:4] for i in range(4))):
        width = stay.shape[-1]
        for s in range(stay.shape[0]):
            base = 2 * layers.pop(0)
            mine = pl.ds(pl.multiple_of((base + x) * width, width), width)
            theirs = pl.ds(pl.multiple_of((base + 1 - x) * width, width), width)
            out[:, mine] = total(stay[s], from_y[s])
            out[:, theirs] = total(from_x[s], from_xy[s])


def after(value, *earlier):
    return lax.optimization_barrier((value, earlier))[0]


def body_eight(qkv, out_weight):
    _, _, cols, features = qkv.shape
    half = features // 2
    chunks = 2
    width = half // chunks
    heads = width // HEAD
    coef = HEAD ** (-0.5) * LOG2E
    me = lax.axis_index("seq")
    who = lax.axis_index("head")
    z, x, core, y = me // 2, me % 2, who % 2, who // 2
    at = jnp.stack([x, z, core, y]).astype(jnp.int32)
    local = qkv.reshape(3, cols, features)
    first = x == 0

    def seq_perm(array, *layers, cross=False):
        pairs = [(2 * a + i, 2 * b + (1 - i if cross else i)) for a, b in layers for i in range(2)]
        return lax.ppermute(array, "seq", pairs)

    def swap(array):
        return seq_perm(array, (0, 0), (1, 1), (2, 2), (3, 3), cross=True)

    def head_perm(array, flip):
        return lax.ppermute(array, "head", [(i, i ^ flip) for i in range(4)])

    def lanes(lo, hi, part, source=local):
        return lax.dynamic_slice(source, (lo, 0, part * half), (hi - lo, cols, half))

    def lanes(lo, hi, half_of):
        return lax.dynamic_slice(local, (lo, 0, half_of * half), (hi - lo, cols, half))

    def pieces(array, c):
        return array[..., c * width : (c + 1) * width]

    q_m, q_o = lanes(0, 1, x), swap(lanes(0, 1, 1 - x))
    w_second = seq_perm(out_weight, (0, 2))
    w_halves = [pieces(out_weight, c) for c in range(chunks)]
    kv_m, kv_give = lanes(1, 3, x), lanes(1, 3, 1 - x)
    q, qs, low = [], [], []
    for c in range(chunks):
        a, b = pieces(q_m, c), pieces(q_o, c)
        q.append(jnp.concatenate([jnp.where(first, a, b), jnp.where(first, b, a)]))
        block = w_halves[c].reshape(q[c].shape)
        going = [jnp.where(z == 1, block, q[c]), jnp.where(z == 3, q[c], block)]
        if c:
            going = after(going, *qs[0])
        qs.append([seq_perm(going[0], (2, 1), (3, 2), (1, 3)), seq_perm(going[1], (3, 1), (1, 0), (2, 3))])
        if c == 0:
            kv_o = swap(after(kv_give, q[0]))
            ups = after([pieces(kv_m, c), pieces(kv_give, c)], w_second)
            low.append([seq_perm(ups[0], (0, 1)), seq_perm(ups[1], (0, 1), cross=True)])
        else:
            up = jnp.concatenate([pieces(kv_m, c), pieces(kv_o, c)])
            low.append([seq_perm(after(up, *low[0]), (0, 1))])

    struct = jax.ShapeDtypeStruct
    partial = struct((2 * cols + lse_height(cols), width), BF16)
    oa, ob, own, sent = [], [], [], []
    turn = at
    for c in range(chunks):
        pair = [(kv_m, c * heads), (kv_o, c * heads)]
        a, b = head_call(
            functools.partial(upper_kernel, coef, cols), turn,
            [(a, 0) for a in qs[c]] + pair + [(a, 0) for a in low[c]] + [(out_weight, c * heads)], [partial] * 2, heads, "upper_rows", 7)
        sent.append(a)
        oa.append(seq_perm(a, (1, 2), (2, 3), (3, 1)))
        ob.append(seq_perm(b, (1, 3), (0, 1), (3, 2), (2, 0)))
        (mine,) = head_call(
            functools.partial(own_kernel, coef, cols), after(at, a), [(q[c], 0)] + pair + [(a, 0) for a in low[c]],
            [partial], heads, "own_rows", 6)
        own.append(mine)
        turn = after(at, mine)

    depth = out_weight.shape[0]

    def block(array):
        return array[:depth] if array.ndim == 2 else array.reshape(depth, width)

    def far_half(c, earlier):
        down = jnp.where(z == 0, block(ob[c]), after(block(oa[c]), earlier))
        half = jnp.where(z >= 2, jnp.where(z == 2, pieces(w_second, c), block(qs[c][0])), down)
        return half, seq_perm(half, (0, 1), (1, 0), (2, 3), (3, 2))

    w_near = [jnp.where((z == 0) | (z == 3), block(qs[c][1]), block(ob[c])) for c in range(chunks)]

    def merged(c, earlier):
        (a,) = head_call(
            functools.partial(merge_kernel, cols), after(at, earlier), [(a[c], 0) for a in (own, oa, ob)],
            [struct((2, cols, width), BF16)], heads, "merge", 2)
        return a, swap(a)

    first_half = merged(0, own[1])
    far_0 = far_half(0, first_half[0])
    near, far = map(list, zip(first_half, merged(1, (first_half[1], far_0[1]))))
    w_far, w_other = map(list, zip(far_0, far_half(1, near[1])))

    parts = []
    turn = at
    for weights in (
        [out_weight] + w_near,
        w_far + w_other,
    ):
        send, kept = project(turn, near, far, weights, out_weight.shape[1])
        got = head_perm(send, 1)
        piece = struct(send.shape[:1] + send.shape[3:], BF16)
        stay, to_y, to_x, to_xy = whole_call(
            split_kernel, at, [kept, got], [piece] * 4, "split", 2)
        turn = after(at, send)
        diagonal = [((2 * i + j) * 4 + h, (2 * i + 1 - j) * 4 + (h ^ 2)) for i in range(4) for j in range(2) for h in range(4)]
        from_xy = lax.ppermute(to_xy, ("seq", "head"), diagonal)
        parts += [stay, head_perm(to_y, 2), swap(to_x), from_xy]
    (out,) = whole_call(
        place_kernel, at, parts, [struct((cols // 4, 8 * out_weight.shape[1]), BF16)], "place", 2)
    return out.reshape(cols // 4, 1, 8 * out_weight.shape[1])


def solution(mesh):
    in_specs = (P(None, "seq", None, "head"), P("head", "seq"))
    out_specs = P("head", "seq", None)
    small = mesh.shape["seq"] == 8 and mesh.shape["head"] == 4

    def body(qkv, out_weight):
        if small and qkv.shape[1] == 1:
            return body_eight(qkv, out_weight)
        return body_any(qkv, out_weight)

    return jax.shard_map(body, mesh=mesh, in_specs=in_specs, out_specs=out_specs, check_vma=False)
```

```python
import functools
import jax
import jax.numpy as jnp
from jax import lax
from jax.experimental import pallas as pl
from jax.experimental.pallas import tpu as pltpu
from jax.sharding import PartitionSpec as P

HEAD = 128
LOG2E = 1.4426950408889634
NEG = -1e30
QB = 128
VMEM = 24 * 1024 * 1024
F32, BF16 = jnp.float32, jnp.bfloat16


def shifted(shard, axis, by):
    size = lax.axis_size(axis)
    pairs = [(i, i + by) for i in range(size) if 0 <= i + by < size]
    return lax.ppermute(shard, axis, pairs)


def column_part(part):
    queries, keys_part, values = (part[0], part[1], part[2])
    rows = queries.shape[0]
    scale = queries.shape[-1] ** (-0.5)
    scores = (
        jnp.einsum("rchd,schd->chrs", queries, keys_part, preferred_element_type=jnp.float32)
        * scale
    )
    r_idx = lax.broadcasted_iota(jnp.int32, (rows, rows), 0)
    s_idx = lax.broadcasted_iota(jnp.int32, (rows, rows), 1)
    allowed = s_idx <= r_idx - 2
    masked = jnp.where(allowed, scores, jnp.float32(-1e30))
    peak = jnp.max(masked, axis=-1)
    weights = jnp.where(allowed, jnp.exp(masked - peak[..., None]), jnp.float32(0.0))
    total = jnp.maximum(jnp.sum(weights, axis=-1), jnp.float32(1.0))
    rounded = weights.astype(jnp.bfloat16)
    mixed = jnp.einsum("chrs,schd->rchd", rounded, values, preferred_element_type=jnp.float32)
    col_out = (mixed / jnp.transpose(total, (2, 0, 1))[..., None]).astype(jnp.bfloat16)
    col_lse = jnp.transpose(peak + jnp.log(total), (2, 0, 1))
    return (col_out, col_lse)


def row_part(local, previous, first_row):
    rows_dev, cols, heads_local, head_size = (
        local.shape[1],
        local.shape[2],
        local.shape[3],
        local.shape[4],
    )
    scale = head_size ** (-0.5)
    keys_ext = jnp.concatenate([previous, local[1:3]], axis=1)
    key_idx = lax.broadcasted_iota(jnp.int32, (cols, 2 * cols), 1)
    query_idx = lax.broadcasted_iota(jnp.int32, (cols, 2 * cols), 0)

    def one_row(index):
        queries = lax.dynamic_index_in_dim(local[0], index, 0, keepdims=False)
        pair = keys_ext.reshape(2, 2 * cols, heads_local, head_size)
        scores = (
            jnp.einsum("qhd,khd->hqk", queries, pair[0], preferred_element_type=jnp.float32) * scale
        )
        allowed = (key_idx < cols) & (first_row + index > 0) | (key_idx >= cols) & (
            key_idx - cols <= query_idx
        )
        masked = jnp.where(allowed[None], scores, jnp.float32(-1e30))
        peak = jnp.max(masked, axis=-1)
        weights = jnp.where(allowed[None], jnp.exp(masked - peak[..., None]), jnp.float32(0.0))
        total = jnp.sum(weights, axis=-1)
        rounded = weights.astype(jnp.bfloat16)
        mixed = jnp.einsum("hqk,khd->qhd", rounded, pair[1], preferred_element_type=jnp.float32)
        return (mixed / jnp.transpose(total)[..., None], jnp.transpose(peak + jnp.log(total)))

    return lax.map(one_row, jnp.arange(rows_dev, dtype=jnp.int32))


def body_any(qkv, out_weight):
    rows_dev, cols, features = (qkv.shape[1], qkv.shape[2], qkv.shape[3])
    head_size = HEAD
    heads_local = features // head_size
    local = qkv.reshape(3, rows_dev, cols, heads_local, head_size)
    previous = shifted(local[1:3, rows_dev - 1 : rows_dev], "seq", 1)
    first_row = lax.axis_index("seq") * rows_dev
    row_out, row_lse = row_part(local, previous, first_row)
    columns = lax.all_to_all(local, "seq", split_axis=2, concat_axis=1, tiled=True)
    col_part_out, col_part_lse = column_part(columns)
    col_out, col_lse = (
        lax.all_to_all(col_part_out, "seq", split_axis=0, concat_axis=1, tiled=True),
        lax.all_to_all(
            col_part_lse.astype(jnp.bfloat16), "seq", split_axis=0, concat_axis=1, tiled=True
        ).astype(col_part_lse.dtype),
    )
    top = jnp.maximum(row_lse, col_lse)
    left = jnp.exp(row_lse - top)
    right = jnp.exp(col_lse - top)
    attended = (left[..., None] * row_out + right[..., None] * col_out.astype(jnp.float32)) / (
        left + right
    )[..., None]
    attended = attended.astype(jnp.bfloat16).reshape(rows_dev, cols, features)
    terms = jnp.einsum(
        "rcf,fd->crd",
        attended,
        lax.all_gather(out_weight, "seq", axis=1, tiled=True),
        preferred_element_type=jnp.float32,
    )
    summed = lax.psum_scatter(terms.astype(jnp.bfloat16), "head", scatter_dimension=0, tiled=True)
    return summed


def dense_scores(q, k):
    return lax.dot_general(q, k, (((1,), (1,)), ((), ())), preferred_element_type=F32)


def col_scores(q, k):
    prod = q * k
    high = prod.astype(BF16)
    low = (prod - high.astype(F32)).astype(BF16)
    ones = jnp.ones((2 * HEAD, HEAD), BF16)
    return jnp.dot(jnp.concatenate([high, low], axis=1), ones, preferred_element_type=F32)


def with_ones(v):
    return jnp.concatenate([v, jnp.ones_like(v)], axis=1)


def attend(q, dense, cols, coef):
    rows = q.shape[0]
    scores = []
    for k, _, allowed in dense:
        s = dense_scores(q, k)
        scores.append(s if allowed is None else jnp.where(allowed, s, NEG))
    singles = []
    if cols:
        wide = q.astype(F32)
    for k, _, allowed in cols:
        c = col_scores(wide, k)
        singles.append(c if allowed is None else jnp.where(allowed, c, NEG))
    peak = None
    for s in scores:
        for j in range(s.shape[1] // HEAD):
            part = s[:, j * HEAD : (j + 1) * HEAD]
            peak = part if peak is None else jnp.maximum(peak, part)
    if peak is not None:
        peak = jnp.broadcast_to(jnp.max(peak, axis=1, keepdims=True), (rows, HEAD))
    for c in singles:
        peak = c if peak is None else jnp.maximum(peak, c)
    peak = peak * coef
    both = None
    for s, (_, v, _) in zip(scores, dense):
        tiled = jnp.concatenate([peak] * (s.shape[1] // HEAD), axis=1)
        p = jnp.exp2(s * coef - tiled).astype(BF16)
        term = jnp.dot(p, v, preferred_element_type=F32)
        both = term if both is None else both + term
    out = None if both is None else both[:, :HEAD]
    total = None if both is None else both[:, HEAD:]
    for c, (_, v, _) in zip(singles, cols):
        w = jnp.exp2(c * coef - peak)
        total = w if total is None else total + w
        out = w * v if out is None else out + w * v
    return out / total, peak + jnp.log2(total)


def lse_rows(even, odd):
    lane = lax.broadcasted_iota(jnp.int32, (HEAD, HEAD), 1)
    evens, odds = [], []
    for t in range(even.shape[0] // HEAD):
        block = slice(t * HEAD, (t + 1) * HEAD)
        turned = jnp.transpose(jnp.where(lane == 0, even[block], odd[block]))
        evens.append(turned[0:1])
        odds.append(turned[1:2])
    return evens, odds


def put_lse(ref, base, evens, odds):
    rows = jnp.concatenate(evens + odds, axis=0)
    pad = (-rows.shape[0]) % 16
    if pad:
        rows = jnp.concatenate([rows, jnp.zeros((pad, HEAD), F32)], axis=0)
    count = rows.shape[0]
    for piece in range(3):
        part = rows.astype(BF16)
        ref[pl.ds(base + piece * count, count), :] = part
        rows = rows - part.astype(F32)


def get_lse(ref, base, cols):
    blocks = cols // HEAD
    count = -(-2 * blocks // 16) * 16
    rows = sum(ref[pl.ds(base + piece * count, count), :].astype(F32) for piece in range(3))
    turned = [
        jnp.transpose(jnp.broadcast_to(rows[t : t + 1], (HEAD, HEAD))) for t in range(2 * blocks)
    ]
    return jnp.concatenate(turned[:blocks], axis=0), jnp.concatenate(turned[blocks:], axis=0)


def lse_height(cols):
    return 3 * (-(-2 * (cols // HEAD) // 16) * 16)


def stacked(refs):
    return [ref[i] for ref in refs for i in range(ref.shape[0])]


def own_kernel(coef, cols, at, q, kv_m, kv_o, *refs):
    x, z = at[0], at[1]
    below = z == 1
    block = 256
    tri = lax.broadcasted_iota(jnp.int32, (block, block), 1) <= lax.broadcasted_iota(
        jnp.int32, (block, block), 0
    )
    first = x == 0
    k_e, k_o = jnp.where(first, kv_m[0], kv_o[0]), jnp.where(first, kv_o[0], kv_m[0])
    v_e, v_o = jnp.where(first, kv_m[1], kv_o[1]), jnp.where(first, kv_o[1], kv_m[1])
    v_e, v_o = with_ones(v_e), with_ones(v_o)
    *low, out = refs
    m_k, m_v, o_k, o_v = stacked(low)
    lk_e, lk_o = jnp.where(first, m_k, o_k), jnp.where(first, o_k, m_k)
    lv_e, lv_o = jnp.where(first, m_v, o_v), jnp.where(first, o_v, m_v)
    lv_o1 = with_ones(lv_o)
    evens, odds = [], []
    for part in range(cols // block):
        a, b = part * block, (part + 1) * block
        mine = slice(a, b)
        col_e = (lk_e[mine].astype(F32), lv_e[mine].astype(F32), below)
        col_o = (lk_o[mine].astype(F32), lv_o[mine].astype(F32), below)

        def causal(k, v):
            blocks = [(k[a:b], v[a:b], tri)]
            return blocks if part == 0 else [(k[:a], v[:a], None)] + blocks

        o1, l1 = attend(q[0, mine], causal(k_e, v_e) + [(lk_o, lv_o1, below)], [col_e], coef)
        o2, l2 = attend(q[1, mine], causal(k_o, v_o) + [(k_e, v_e, None)], [col_e, col_o], coef)
        out[mine] = o1.astype(BF16)
        out[cols + a : cols + b] = o2.astype(BF16)
        e, o = lse_rows(l1, l2)
        evens, odds = evens + e, odds + o
    put_lse(out, 2 * cols, evens, odds)


def upper_kernel(coef, cols, at, qa, qb, kv_m, kv_o, *refs):
    x, z = at[0], at[1]
    below = z == 1
    first = x == 0
    block = 256
    k_e, k_o = jnp.where(first, kv_m[0], kv_o[0]), jnp.where(first, kv_o[0], kv_m[0])
    v_e, v_o = jnp.where(first, kv_m[1], kv_o[1]), jnp.where(first, kv_o[1], kv_m[1])
    v_o1 = with_ones(v_o)
    *low, weight, out_a, out_b = refs
    lows = stacked(low)
    rows_a, rows_b = ([], []), ([], [])
    for index in range(cols // block):
        a, b = index * block, (index + 1) * block
        mine = slice(a, b)
        m_k, m_v, o_k, o_v = (part[mine].astype(F32) for part in lows)
        ce = (k_e[mine].astype(F32), v_e[mine].astype(F32), None)
        co = (k_o[mine].astype(F32), v_o[mine].astype(F32), None)
        low = [(m_k, m_v, below), (o_k, o_v, below)]
        for q, out, rows, dense, singles in (
            (qa, out_a, rows_a, [(k_o, v_o1, None)], [ce]),
            (qb, out_b, rows_b, [], [ce, co]),
        ):
            o1, l1 = attend(q[0, mine], dense, singles + low, coef)
            o2, l2 = attend(q[1, mine], [], [ce, co] + low, coef)
            o1, o2 = o1.astype(BF16), o2.astype(BF16)
            other = slice(cols + a, cols + b)
            if out is out_b:
                o1, o2 = jnp.where(below, o1, weight[mine]), jnp.where(below, o2, weight[other])
            out[mine] = o1
            out[other] = o2
            e, o = lse_rows(l1, l2)
            rows[0].extend(e)
            rows[1].extend(o)
    put_lse(out_a, 2 * cols, *rows_a)
    put_lse(out_b, 2 * cols, *rows_b)


def merge_kernel(cols, at, own, oa, ob, out):
    z = at[1]
    own_l, a_l, b_l = (get_lse(ref, 2 * cols, cols) for ref in (own, oa, ob))
    for row in range(2):
        tokens = slice(row * cols, (row + 1) * cols)
        l0 = own_l[row]
        l1 = jnp.where(z >= 2, a_l[row], NEG)
        l2 = jnp.where(z >= 3, b_l[row], NEG)
        top = jnp.maximum(l0, jnp.maximum(l1, l2))
        w0, w1, w2 = jnp.exp2(l0 - top), jnp.exp2(l1 - top), jnp.exp2(l2 - top)
        mixed = w0 * own[tokens].astype(F32) + w1 * oa[tokens].astype(F32) + w2 * ob[tokens].astype(F32)
        out[row] = (mixed / (w0 + w1 + w2)).astype(BF16)


def cost(us):
    return pl.CostEstimate(flops=int(us * 1e9), bytes_accessed=1024, transcendentals=0)


def head_call(kernel, at, args, outs, heads, name, us):
    def spec(shape, start=0):
        lead = len(shape) - 1
        return pl.BlockSpec(tuple(shape[:-1]) + (HEAD,), lambda h, at: (0,) * lead + (start + h,))

    return pl.pallas_call(
        kernel,
        out_shape=outs,
        grid_spec=pltpu.PrefetchScalarGridSpec(
            num_scalar_prefetch=1,
            grid=(heads,),
            in_specs=[spec(a.shape, start) for a, start in args],
            out_specs=[spec(o.shape) for o in outs],
        ),
        compiler_params=pltpu.CompilerParams(vmem_limit_bytes=VMEM),
        cost_estimate=cost(us),
        name=name,
    )(at, *(a for a, _ in args))


def project_kernel(chunks, at, *refs):
    x, core = at[0], at[2]
    near, far = refs[:chunks], refs[chunks : 2 * chunks]
    weights, send, keep = refs[2 * chunks : -2], refs[-2], refs[-1]
    tokens = near[0].shape[3]
    half = sum(ref.shape[4] for ref in near)
    for who, out in ((1 - core, send), (core, keep)):

        def rows(ref):
            return jnp.concatenate([ref[r, y, who] for y in range(2) for r in range(2)], axis=0)

        left = jnp.concatenate([rows(ref) for ref in near], axis=1)
        right = jnp.concatenate([rows(ref) for ref in far], axis=1)
        base = 0
        for weight in weights:
            top = weight[pl.ds(pl.multiple_of(x * half, half), half)]
            bottom = weight[pl.ds(pl.multiple_of((1 - x) * half, half), half)]
            c = jnp.dot(left, top, preferred_element_type=F32) + jnp.dot(right, bottom, preferred_element_type=F32)
            width = weight.shape[1]
            s, lane = base // out.shape[4], base % out.shape[4]
            out[s, :, :, :, lane : lane + width] = c.astype(BF16).reshape(2, 2, tokens, width)
            base += width


def project(at, near, far, weights, out_width):
    cols = near[0].shape[1]
    args = [a.reshape(2, 2, 2, cols // 4, a.shape[2]) for a in near + far] + weights
    layers = sum(w.shape[1] for w in weights) // out_width
    out = jax.ShapeDtypeStruct((layers, 2, 2, cols // 4, out_width), BF16)
    return whole_call(
        functools.partial(project_kernel, len(near)), at, args, [out, out], "project", 2 * layers)


def whole_call(kernel, at, args, outs, name, us):
    return pl.pallas_call(
        kernel,
        out_shape=outs,
        in_specs=[pl.BlockSpec(memory_space=pltpu.SMEM)] + [pl.BlockSpec(memory_space=pltpu.VMEM)] * len(args),
        out_specs=[pl.BlockSpec(memory_space=pltpu.VMEM)] * len(outs),
        compiler_params=pltpu.CompilerParams(vmem_limit_bytes=VMEM),
        cost_estimate=cost(us),
        name=name,
    )(at, *args)


def total(a, b):
    return (a.astype(F32) + b.astype(F32)).astype(BF16)


def split_kernel(at, kept, got, stay, to_y, to_x, to_xy):
    x, y = at[0], at[3]
    for s in range(kept.shape[0]):
        for out, yy, xx in ((to_xy, 1 - y, 1 - x), (to_y, 1 - y, x), (to_x, y, 1 - x), (stay, y, x)):
            out[s] = total(kept[s, yy, xx], got[s, yy, xx])


def place_kernel(at, *refs):
    x, z, out = at[0], at[1], refs[-1]
    layers = [z, z + 1 - 2 * (z % 2), (z + 2) % 4, 3 - z]
    for stay, from_y, from_x, from_xy in zip(*(refs[i:-1:4] for i in range(4))):
        width = stay.shape[-1]
        for s in range(stay.shape[0]):
            base = 2 * layers.pop(0)
            mine = pl.ds(pl.multiple_of((base + x) * width, width), width)
            theirs = pl.ds(pl.multiple_of((base + 1 - x) * width, width), width)
            out[:, mine] = total(stay[s], from_y[s])
            out[:, theirs] = total(from_x[s], from_xy[s])


def after(value, *earlier):
    return lax.optimization_barrier((value, earlier))[0]


def body_eight(qkv, out_weight):
    _, _, cols, features = qkv.shape
    half = features // 2
    chunks = 2
    width = half // chunks
    heads = width // HEAD
    coef = HEAD ** (-0.5) * LOG2E
    me = lax.axis_index("seq")
    who = lax.axis_index("head")
    z, x, core, y = me // 2, me % 2, who % 2, who // 2
    at = jnp.stack([x, z, core, y]).astype(jnp.int32)
    local = qkv.reshape(3, cols, features)
    first = x == 0

    def seq_perm(array, *layers, cross=False):
        pairs = [(2 * a + i, 2 * b + (1 - i if cross else i)) for a, b in layers for i in range(2)]
        return lax.ppermute(array, "seq", pairs)

    def swap(array):
        return seq_perm(array, (0, 0), (1, 1), (2, 2), (3, 3), cross=True)

    def head_perm(array, flip):
        return lax.ppermute(array, "head", [(i, i ^ flip) for i in range(4)])

    def lanes(lo, hi, part, source=local):
        return lax.dynamic_slice(source, (lo, 0, part * half), (hi - lo, cols, half))

    def lanes(lo, hi, half_of):
        return lax.dynamic_slice(local, (lo, 0, half_of * half), (hi - lo, cols, half))

    def pieces(array, c):
        return array[..., c * width : (c + 1) * width]

    w_halves = [pieces(out_weight, c) for c in range(chunks)]
    w_first = seq_perm(w_halves[0], (0, 2), (1, 3), (2, 0), (3, 1))
    q_m, q_o = lanes(0, 1, x), swap(lanes(0, 1, 1 - x))
    kv_m, kv_give = lanes(1, 3, x), lanes(1, 3, 1 - x)
    q, qs, low = [], [], []
    for c in range(chunks):
        a, b = pieces(q_m, c), pieces(q_o, c)
        q.append(jnp.concatenate([jnp.where(first, a, b), jnp.where(first, b, a)]))
        block, last = (w.reshape(q[c].shape) for w in (w_halves[c], w_halves[1]))
        if c == 0:
            going = [jnp.where(z == 1, last, q[c]), jnp.where(z == 3, q[c], jnp.where(z == 0, last, block))]
        else:
            going = after([q[c], jnp.where(z == 3, q[c], block)], *qs[0])
        qs.append([
            seq_perm(going[0], (2, 1), (3, 2), *([(1, 3)] if c == 0 else [])),
            seq_perm(going[1], (3, 1), (1, 0), (2, 3), *([(0, 2)] if c == 0 else [])),
        ])
        if c == 0:
            kv_o = swap(after(kv_give, q[0]))
            low_m = seq_perm(after(pieces(kv_m, c), w_first), (0, 1))
            low.append([low_m, seq_perm(after(pieces(kv_give, c), low_m), (0, 1), cross=True)])
        else:
            up = jnp.concatenate([pieces(kv_m, c), pieces(kv_o, c)])
            low.append([seq_perm(after(up, *low[0]), (0, 1))])

    struct = jax.ShapeDtypeStruct
    partial = struct((2 * cols + lse_height(cols), width), BF16)
    oa, ob, own, sent = [], [], [], []
    turn = at
    for c in range(chunks):
        pair = [(kv_m, c * heads), (kv_o, c * heads)]
        a, b = head_call(
            functools.partial(upper_kernel, coef, cols), turn,
            [(a, 0) for a in qs[c]] + pair + [(a, 0) for a in low[c]] + [(out_weight, c * heads)], [partial] * 2, heads, "upper_rows", 7)
        sent.append(a)
        oa.append(seq_perm(a, (1, 2), (2, 3)))
        ob.append(seq_perm(b, (1, 3), (0, 1), (3, 2)))
        (mine,) = head_call(
            functools.partial(own_kernel, coef, cols), after(at, a), [(q[c], 0)] + pair + [(a, 0) for a in low[c]],
            [partial], heads, "own_rows", 6)
        own.append(mine)
        turn = after(at, mine)

    depth = out_weight.shape[0]

    def block(array):
        return array.reshape(depth, width)

    w_near = [jnp.where((z == 0) | (z == 3), block(qs[c][1]), ob[c][:depth]) for c in range(chunks)]
    w_down = seq_perm(after(w_halves[1], own[0], *qs[1]), (2, 0), (3, 1))

    def merged(c, earlier):
        (a,) = head_call(
            functools.partial(merge_kernel, cols), after(at, earlier), [(a[c], 0) for a in (own, oa, ob)],
            [struct((2, cols, width), BF16)], heads, "merge", 2)
        return a, swap(a)

    first_half = merged(0, own[1])
    up = jnp.where(z == 2, block(qs[0][1]), block(qs[0][0]))
    w_far = [w_first, jnp.where(z >= 2, up, after(w_down, first_half[0], own[1]))]
    near, far = map(list, zip(first_half, merged(1, (w_far, first_half[1]))))
    w_other = seq_perm(jnp.concatenate(w_far, axis=1), (0, 1), (1, 0), (2, 3), (3, 2))

    parts = []
    turn = after(at, w_other)
    for weights in (
        [out_weight] + w_near,
        w_far + [w_other],
    ):
        send, kept = project(turn, near, far, weights, out_weight.shape[1])
        got = head_perm(send, 1)
        piece = struct(send.shape[:1] + send.shape[3:], BF16)
        stay, to_y, to_x, to_xy = whole_call(
            split_kernel, at, [kept, got], [piece] * 4, "split", 2)
        turn = after(at, send)
        diagonal = [((2 * i + j) * 4 + h, (2 * i + 1 - j) * 4 + (h ^ 2)) for i in range(4) for j in range(2) for h in range(4)]
        from_xy = lax.ppermute(to_xy, ("seq", "head"), diagonal)
        parts += [stay, head_perm(to_y, 2), swap(to_x), from_xy]
    (out,) = whole_call(
        place_kernel, at, parts, [struct((cols // 4, 8 * out_weight.shape[1]), BF16)], "place", 2)
    return out.reshape(cols // 4, 1, 8 * out_weight.shape[1])


def solution(mesh):
    in_specs = (P(None, "seq", None, "head"), P("head", "seq"))
    out_specs = P("head", "seq", None)
    small = mesh.shape["seq"] == 8 and mesh.shape["head"] == 4

    def body(qkv, out_weight):
        if small and qkv.shape[1] == 1:
            return body_eight(qkv, out_weight)
        return body_any(qkv, out_weight)

    return jax.shard_map(body, mesh=mesh, in_specs=in_specs, out_specs=out_specs, check_vma=False)
```

```python
import functools
import jax
import jax.numpy as jnp
from jax import lax
from jax.experimental import pallas as pl
from jax.experimental.pallas import tpu as pltpu
from jax.sharding import PartitionSpec as P

HEAD = 128
LOG2E = 1.4426950408889634
NEG = -1e30
QB = 128
VMEM = 24 * 1024 * 1024
F32, BF16 = jnp.float32, jnp.bfloat16


def shifted(shard, axis, by):
    size = lax.axis_size(axis)
    pairs = [(i, i + by) for i in range(size) if 0 <= i + by < size]
    return lax.ppermute(shard, axis, pairs)


def column_part(part):
    queries, keys_part, values = (part[0], part[1], part[2])
    rows = queries.shape[0]
    scale = queries.shape[-1] ** (-0.5)
    scores = (
        jnp.einsum("rchd,schd->chrs", queries, keys_part, preferred_element_type=jnp.float32)
        * scale
    )
    r_idx = lax.broadcasted_iota(jnp.int32, (rows, rows), 0)
    s_idx = lax.broadcasted_iota(jnp.int32, (rows, rows), 1)
    allowed = s_idx <= r_idx - 2
    masked = jnp.where(allowed, scores, jnp.float32(-1e30))
    peak = jnp.max(masked, axis=-1)
    weights = jnp.where(allowed, jnp.exp(masked - peak[..., None]), jnp.float32(0.0))
    total = jnp.maximum(jnp.sum(weights, axis=-1), jnp.float32(1.0))
    rounded = weights.astype(jnp.bfloat16)
    mixed = jnp.einsum("chrs,schd->rchd", rounded, values, preferred_element_type=jnp.float32)
    col_out = (mixed / jnp.transpose(total, (2, 0, 1))[..., None]).astype(jnp.bfloat16)
    col_lse = jnp.transpose(peak + jnp.log(total), (2, 0, 1))
    return (col_out, col_lse)


def row_part(local, previous, first_row):
    rows_dev, cols, heads_local, head_size = (
        local.shape[1],
        local.shape[2],
        local.shape[3],
        local.shape[4],
    )
    scale = head_size ** (-0.5)
    keys_ext = jnp.concatenate([previous, local[1:3]], axis=1)
    key_idx = lax.broadcasted_iota(jnp.int32, (cols, 2 * cols), 1)
    query_idx = lax.broadcasted_iota(jnp.int32, (cols, 2 * cols), 0)

    def one_row(index):
        queries = lax.dynamic_index_in_dim(local[0], index, 0, keepdims=False)
        pair = keys_ext.reshape(2, 2 * cols, heads_local, head_size)
        scores = (
            jnp.einsum("qhd,khd->hqk", queries, pair[0], preferred_element_type=jnp.float32) * scale
        )
        allowed = (key_idx < cols) & (first_row + index > 0) | (key_idx >= cols) & (
            key_idx - cols <= query_idx
        )
        masked = jnp.where(allowed[None], scores, jnp.float32(-1e30))
        peak = jnp.max(masked, axis=-1)
        weights = jnp.where(allowed[None], jnp.exp(masked - peak[..., None]), jnp.float32(0.0))
        total = jnp.sum(weights, axis=-1)
        rounded = weights.astype(jnp.bfloat16)
        mixed = jnp.einsum("hqk,khd->qhd", rounded, pair[1], preferred_element_type=jnp.float32)
        return (mixed / jnp.transpose(total)[..., None], jnp.transpose(peak + jnp.log(total)))

    return lax.map(one_row, jnp.arange(rows_dev, dtype=jnp.int32))


def body_any(qkv, out_weight):
    rows_dev, cols, features = (qkv.shape[1], qkv.shape[2], qkv.shape[3])
    head_size = HEAD
    heads_local = features // head_size
    local = qkv.reshape(3, rows_dev, cols, heads_local, head_size)
    previous = shifted(local[1:3, rows_dev - 1 : rows_dev], "seq", 1)
    first_row = lax.axis_index("seq") * rows_dev
    row_out, row_lse = row_part(local, previous, first_row)
    columns = lax.all_to_all(local, "seq", split_axis=2, concat_axis=1, tiled=True)
    col_part_out, col_part_lse = column_part(columns)
    col_out, col_lse = (
        lax.all_to_all(col_part_out, "seq", split_axis=0, concat_axis=1, tiled=True),
        lax.all_to_all(
            col_part_lse.astype(jnp.bfloat16), "seq", split_axis=0, concat_axis=1, tiled=True
        ).astype(col_part_lse.dtype),
    )
    top = jnp.maximum(row_lse, col_lse)
    left = jnp.exp(row_lse - top)
    right = jnp.exp(col_lse - top)
    attended = (left[..., None] * row_out + right[..., None] * col_out.astype(jnp.float32)) / (
        left + right
    )[..., None]
    attended = attended.astype(jnp.bfloat16).reshape(rows_dev, cols, features)
    terms = jnp.einsum(
        "rcf,fd->crd",
        attended,
        lax.all_gather(out_weight, "seq", axis=1, tiled=True),
        preferred_element_type=jnp.float32,
    )
    summed = lax.psum_scatter(terms.astype(jnp.bfloat16), "head", scatter_dimension=0, tiled=True)
    return summed


def dense_scores(q, k):
    return lax.dot_general(q, k, (((1,), (1,)), ((), ())), preferred_element_type=F32)


def col_scores(q, k):
    prod = q * k
    high = prod.astype(BF16)
    low = (prod - high.astype(F32)).astype(BF16)
    ones = jnp.ones((2 * HEAD, HEAD), BF16)
    return jnp.dot(jnp.concatenate([high, low], axis=1), ones, preferred_element_type=F32)


def with_ones(v):
    return jnp.concatenate([v, jnp.ones_like(v)], axis=1)


def attend(q, dense, cols, coef):
    rows = q.shape[0]
    scores = []
    for k, _, allowed in dense:
        s = dense_scores(q, k)
        scores.append(s if allowed is None else jnp.where(allowed, s, NEG))
    singles = []
    if cols:
        wide = q.astype(F32)
    for k, _, allowed in cols:
        c = col_scores(wide, k)
        singles.append(c if allowed is None else jnp.where(allowed, c, NEG))
    peak = None
    for s in scores:
        for j in range(s.shape[1] // HEAD):
            part = s[:, j * HEAD : (j + 1) * HEAD]
            peak = part if peak is None else jnp.maximum(peak, part)
    if peak is not None:
        peak = jnp.broadcast_to(jnp.max(peak, axis=1, keepdims=True), (rows, HEAD))
    for c in singles:
        peak = c if peak is None else jnp.maximum(peak, c)
    peak = peak * coef
    both = None
    for s, (_, v, _) in zip(scores, dense):
        tiled = jnp.concatenate([peak] * (s.shape[1] // HEAD), axis=1)
        p = jnp.exp2(s * coef - tiled).astype(BF16)
        term = jnp.dot(p, v, preferred_element_type=F32)
        both = term if both is None else both + term
    out = None if both is None else both[:, :HEAD]
    total = None if both is None else both[:, HEAD:]
    for c, (_, v, _) in zip(singles, cols):
        w = jnp.exp2(c * coef - peak)
        total = w if total is None else total + w
        out = w * v if out is None else out + w * v
    return out / total, peak + jnp.log2(total)


def lse_rows(even, odd):
    lane = lax.broadcasted_iota(jnp.int32, (HEAD, HEAD), 1)
    evens, odds = [], []
    for t in range(even.shape[0] // HEAD):
        block = slice(t * HEAD, (t + 1) * HEAD)
        turned = jnp.transpose(jnp.where(lane == 0, even[block], odd[block]))
        evens.append(turned[0:1])
        odds.append(turned[1:2])
    return evens, odds


def put_lse(ref, base, evens, odds):
    rows = jnp.concatenate(evens + odds, axis=0)
    pad = (-rows.shape[0]) % 16
    if pad:
        rows = jnp.concatenate([rows, jnp.zeros((pad, HEAD), F32)], axis=0)
    count = rows.shape[0]
    for piece in range(3):
        part = rows.astype(BF16)
        ref[pl.ds(base + piece * count, count), :] = part
        rows = rows - part.astype(F32)


def get_lse(ref, base, cols):
    blocks = cols // HEAD
    count = -(-2 * blocks // 16) * 16
    rows = sum(ref[pl.ds(base + piece * count, count), :].astype(F32) for piece in range(3))
    turned = [
        jnp.transpose(jnp.broadcast_to(rows[t : t + 1], (HEAD, HEAD))) for t in range(2 * blocks)
    ]
    return jnp.concatenate(turned[:blocks], axis=0), jnp.concatenate(turned[blocks:], axis=0)


def lse_height(cols):
    return 3 * (-(-2 * (cols // HEAD) // 16) * 16)


def stacked(refs):
    return [ref[i] for ref in refs for i in range(ref.shape[0])]


def own_kernel(coef, cols, at, q_m, q_o, kv_m, kv_o, *refs):
    x, z = at[0], at[1]
    below = z == 1
    block = 256
    tri = lax.broadcasted_iota(jnp.int32, (block, block), 1) <= lax.broadcasted_iota(
        jnp.int32, (block, block), 0
    )
    first = x == 0
    k_e, k_o = jnp.where(first, kv_m[0], kv_o[0]), jnp.where(first, kv_o[0], kv_m[0])
    v_e, v_o = jnp.where(first, kv_m[1], kv_o[1]), jnp.where(first, kv_o[1], kv_m[1])
    v_e, v_o = with_ones(v_e), with_ones(v_o)
    *low, out = refs
    m_k, m_v, o_k, o_v = stacked(low)
    lk_e, lk_o = jnp.where(first, m_k, o_k), jnp.where(first, o_k, m_k)
    lv_e, lv_o = jnp.where(first, m_v, o_v), jnp.where(first, o_v, m_v)
    lv_o1 = with_ones(lv_o)
    q_e, q_o = jnp.where(first, q_m[0], q_o[0]), jnp.where(first, q_o[0], q_m[0])
    evens, odds = [], []
    for part in range(cols // block):
        a, b = part * block, (part + 1) * block
        mine = slice(a, b)
        col_e = (lk_e[mine].astype(F32), lv_e[mine].astype(F32), below)
        col_o = (lk_o[mine].astype(F32), lv_o[mine].astype(F32), below)

        def causal(k, v):
            blocks = [(k[a:b], v[a:b], tri)]
            return blocks if part == 0 else [(k[:a], v[:a], None)] + blocks

        o1, l1 = attend(q_e[mine], causal(k_e, v_e) + [(lk_o, lv_o1, below)], [col_e], coef)
        o2, l2 = attend(q_o[mine], causal(k_o, v_o) + [(k_e, v_e, None)], [col_e, col_o], coef)
        out[mine] = o1.astype(BF16)
        out[cols + a : cols + b] = o2.astype(BF16)
        e, o = lse_rows(l1, l2)
        evens, odds = evens + e, odds + o
    put_lse(out, 2 * cols, evens, odds)


def upper_kernel(coef, cols, at, qa_m, qa_o, qb_m, qb_o, kv_m, kv_o, *refs):
    x, z = at[0], at[1]
    below = z == 1
    first = x == 0
    block = 256
    k_e, k_o = jnp.where(first, kv_m[0], kv_o[0]), jnp.where(first, kv_o[0], kv_m[0])
    v_e, v_o = jnp.where(first, kv_m[1], kv_o[1]), jnp.where(first, kv_o[1], kv_m[1])
    v_o1 = with_ones(v_o)
    *low, weight, out_a, out_b = refs
    lows = stacked(low)
    qa = jnp.where(first, qa_m[0], qa_o[0]), jnp.where(first, qa_o[0], qa_m[0])
    qb = jnp.where(first, qb_m[0], qb_o[0]), jnp.where(first, qb_o[0], qb_m[0])
    rows_a, rows_b = ([], []), ([], [])
    for index in range(cols // block):
        a, b = index * block, (index + 1) * block
        mine = slice(a, b)
        m_k, m_v, o_k, o_v = (part[mine].astype(F32) for part in lows)
        ce = (k_e[mine].astype(F32), v_e[mine].astype(F32), None)
        co = (k_o[mine].astype(F32), v_o[mine].astype(F32), None)
        low = [(m_k, m_v, below), (o_k, o_v, below)]
        for q, out, rows, dense, singles in (
            (qa, out_a, rows_a, [(k_o, v_o1, None)], [ce]),
            (qb, out_b, rows_b, [], [ce, co]),
        ):
            o1, l1 = attend(q[0][mine], dense, singles + low, coef)
            o2, l2 = attend(q[1][mine], [], [ce, co] + low, coef)
            o1, o2 = o1.astype(BF16), o2.astype(BF16)
            other = slice(cols + a, cols + b)
            if out is out_b:
                o1, o2 = jnp.where(below, o1, weight[mine]), jnp.where(below, o2, weight[other])
            out[mine] = o1
            out[other] = o2
            e, o = lse_rows(l1, l2)
            rows[0].extend(e)
            rows[1].extend(o)
    put_lse(out_a, 2 * cols, *rows_a)
    put_lse(out_b, 2 * cols, *rows_b)


def merge_kernel(cols, at, own, oa, ob, out):
    z = at[1]
    own_l, a_l, b_l = (get_lse(ref, 2 * cols, cols) for ref in (own, oa, ob))
    for row in range(2):
        tokens = slice(row * cols, (row + 1) * cols)
        l0 = own_l[row]
        l1 = jnp.where(z >= 2, a_l[row], NEG)
        l2 = jnp.where(z >= 3, b_l[row], NEG)
        top = jnp.maximum(l0, jnp.maximum(l1, l2))
        w0, w1, w2 = jnp.exp2(l0 - top), jnp.exp2(l1 - top), jnp.exp2(l2 - top)
        mixed = w0 * own[tokens].astype(F32) + w1 * oa[tokens].astype(F32) + w2 * ob[tokens].astype(F32)
        out[row] = (mixed / (w0 + w1 + w2)).astype(BF16)


def cost(us):
    return pl.CostEstimate(flops=int(us * 1e8), bytes_accessed=1024, transcendentals=0)


def head_call(kernel, at, args, outs, heads, name, us):
    def spec(shape, start=0):
        lead = len(shape) - 1
        return pl.BlockSpec(tuple(shape[:-1]) + (HEAD,), lambda h, at: (0,) * lead + (start + h,))

    return pl.pallas_call(
        kernel,
        out_shape=outs,
        grid_spec=pltpu.PrefetchScalarGridSpec(
            num_scalar_prefetch=1,
            grid=(heads,),
            in_specs=[spec(a.shape, start) for a, start in args],
            out_specs=[spec(o.shape) for o in outs],
        ),
        compiler_params=pltpu.CompilerParams(vmem_limit_bytes=VMEM),
        cost_estimate=cost(us),
        name=name,
    )(at, *(a for a, _ in args))


def project_kernel(chunks, at, *refs):
    x, core = at[0], at[2]
    near, far = refs[:chunks], refs[chunks : 2 * chunks]
    weights, send, keep = refs[2 * chunks : -2], refs[-2], refs[-1]
    tokens = near[0].shape[3]
    half = sum(ref.shape[4] for ref in near)
    for who, out in ((1 - core, send), (core, keep)):

        def rows(ref):
            return jnp.concatenate([ref[r, y, who] for y in range(2) for r in range(2)], axis=0)

        left = jnp.concatenate([rows(ref) for ref in near], axis=1)
        right = jnp.concatenate([rows(ref) for ref in far], axis=1)
        base = 0
        for weight in weights:
            top = weight[pl.ds(pl.multiple_of(x * half, half), half)]
            bottom = weight[pl.ds(pl.multiple_of((1 - x) * half, half), half)]
            c = jnp.dot(left, top, preferred_element_type=F32) + jnp.dot(right, bottom, preferred_element_type=F32)
            width = weight.shape[1]
            s, lane = base // out.shape[4], base % out.shape[4]
            out[s, :, :, :, lane : lane + width] = c.astype(BF16).reshape(2, 2, tokens, width)
            base += width


def project(at, near, far, weights, out_width):
    cols = near[0].shape[1]
    args = [a.reshape(2, 2, 2, cols // 4, a.shape[2]) for a in near + far] + weights
    layers = sum(w.shape[1] for w in weights) // out_width
    out = jax.ShapeDtypeStruct((layers, 2, 2, cols // 4, out_width), BF16)
    return whole_call(
        functools.partial(project_kernel, len(near)), at, args, [out, out], "project", 2 * layers)


def whole_call(kernel, at, args, outs, name, us):
    return pl.pallas_call(
        kernel,
        out_shape=outs,
        in_specs=[pl.BlockSpec(memory_space=pltpu.SMEM)] + [pl.BlockSpec(memory_space=pltpu.VMEM)] * len(args),
        out_specs=[pl.BlockSpec(memory_space=pltpu.VMEM)] * len(outs),
        compiler_params=pltpu.CompilerParams(vmem_limit_bytes=VMEM),
        cost_estimate=cost(us),
        name=name,
    )(at, *args)


def total(a, b):
    return (a.astype(F32) + b.astype(F32)).astype(BF16)


def split_kernel(at, kept, got, stay, to_y, to_x, to_xy):
    x, y = at[0], at[3]
    for s in range(kept.shape[0]):
        for out, yy, xx in ((to_xy, 1 - y, 1 - x), (to_y, 1 - y, x), (to_x, y, 1 - x), (stay, y, x)):
            out[s] = total(kept[s, yy, xx], got[s, yy, xx])


def place_kernel(at, *refs):
    x, z, out = at[0], at[1], refs[-1]
    layers = [z, z + 1 - 2 * (z % 2), (z + 2) % 4, 3 - z]
    for stay, from_y, from_x, from_xy in zip(*(refs[i:-1:4] for i in range(4))):
        width = stay.shape[-1]
        for s in range(stay.shape[0]):
            base = 2 * layers.pop(0)
            mine = pl.ds(pl.multiple_of((base + x) * width, width), width)
            theirs = pl.ds(pl.multiple_of((base + 1 - x) * width, width), width)
            out[:, mine] = total(stay[s], from_y[s])
            out[:, theirs] = total(from_x[s], from_xy[s])


def after(value, *earlier):
    return lax.optimization_barrier((value, earlier))[0]


def body_eight(qkv, out_weight):
    _, _, cols, features = qkv.shape
    half = features // 2
    chunks = 2
    width = half // chunks
    heads = width // HEAD
    coef = HEAD ** (-0.5) * LOG2E
    me = lax.axis_index("seq")
    who = lax.axis_index("head")
    z, x, core, y = me // 2, me % 2, who % 2, who // 2
    at = jnp.stack([x, z, core, y]).astype(jnp.int32)
    local = qkv.reshape(3, cols, features)
    first = x == 0

    def seq_perm(array, *layers, cross=False):
        pairs = [(2 * a + i, 2 * b + (1 - i if cross else i)) for a, b in layers for i in range(2)]
        return lax.ppermute(array, "seq", pairs)

    def swap(array):
        return seq_perm(array, (0, 0), (1, 1), (2, 2), (3, 3), cross=True)

    def head_perm(array, flip):
        return lax.ppermute(array, "head", [(i, i ^ flip) for i in range(4)])

    def lanes(lo, hi, part, source=local):
        return lax.dynamic_slice(source, (lo, 0, part * half), (hi - lo, cols, half))

    def with_weight(array, part):
        return jnp.where(z == 3, array, out_weight[part * cols : (part + 1) * cols].reshape(array.shape))

    down, two_down = [(2, 1), (3, 2)], [(3, 1), (0, 2), (1, 0), (2, 3)]
    q_m = lanes(0, 1, x)
    q_o = swap(lanes(0, 1, 1 - x))
    qs = [seq_perm(q_m, *down), None, seq_perm(with_weight(q_m, 0), *two_down), None]
    kv_m, kv_give = lanes(1, 3, x), lanes(1, 3, 1 - x)
    low_m = seq_perm(jnp.where(z == 0, kv_m, out_weight.reshape(kv_m.shape)), (0, 1), (1, 3))
    low_o = seq_perm(kv_give, (0, 1), cross=True)
    kv_o = swap(after(kv_give, q_o, qs[0]))
    qs[1], qs[3] = seq_perm(q_o, *down), seq_perm(with_weight(q_o, 1), *two_down)

    struct = jax.ShapeDtypeStruct
    partial = struct((2 * cols + lse_height(cols), width), BF16)
    oa, ob, own = [], [], []
    turn = at
    kvs = [kv_m, kv_o, low_m, low_o]
    for c in range(chunks):
        a, b = head_call(
            functools.partial(upper_kernel, coef, cols), turn, [(a, c * heads) for a in qs + kvs + [out_weight]],
            [partial] * 2, heads, "upper_rows", 7)
        turn = after(at, a)
        oa.append(seq_perm(a, (1, 2), (2, 3)))
        ob.append(seq_perm(b, (1, 3), (0, 1), (3, 2)))
    for c in range(chunks):
        (mine,) = head_call(
            functools.partial(own_kernel, coef, cols), turn, [(a, c * heads) for a in [q_m, q_o] + kvs],
            [partial], heads, "own_rows", 6)
        own.append(mine)
        turn = after(at, mine)

    w_down = seq_perm(after(out_weight, *qs), (2, 0), (3, 1))
    depth = out_weight.shape[0]
    ridden = jnp.concatenate([qs[2], qs[3]], axis=1).reshape(out_weight.shape)
    w_near = jnp.where((z == 0) | (z == 3), ridden, jnp.concatenate([o[:depth] for o in ob], axis=1))

    def merged(c, earlier):
        (a,) = head_call(
            functools.partial(merge_kernel, cols), after(at, earlier), [(a[c], 0) for a in (own, oa, ob)],
            [struct((2, cols, width), BF16)], heads, "merge", 2)
        return a, swap(a)

    first_half = merged(0, own[1])
    w_far = jnp.where(
        z >= 2, jnp.where(z == 2, ridden, low_m.reshape(out_weight.shape)), after(w_down, first_half[0], own[1]))
    near, far = map(list, zip(first_half, merged(1, (w_far, first_half[1]))))
    w_other = seq_perm(w_far, (0, 1), (1, 0), (2, 3), (3, 2))

    parts = []
    turn = after(at, w_other)
    for weights in (
        [out_weight, w_near],
        [w_far, w_other],
    ):
        send, kept = project(turn, near, far, weights, out_weight.shape[1])
        got = head_perm(send, 1)
        piece = struct(send.shape[:1] + send.shape[3:], BF16)
        stay, to_y, to_x, to_xy = whole_call(split_kernel, at, [kept, got], [piece] * 4, "split", 2)
        turn = after(at, send)
        diagonal = [((2 * i + j) * 4 + h, (2 * i + 1 - j) * 4 + (h ^ 2)) for i in range(4) for j in range(2) for h in range(4)]
        from_xy = lax.ppermute(to_xy, ("seq", "head"), diagonal)
        parts += [stay, head_perm(to_y, 2), swap(to_x), from_xy]
    (out,) = whole_call(
        place_kernel, at, parts, [struct((cols // 4, 8 * out_weight.shape[1]), BF16)], "place", 2)
    return out.reshape(cols // 4, 1, 8 * out_weight.shape[1])


def solution(mesh):
    in_specs = (P(None, "seq", None, "head"), P("head", "seq"))
    out_specs = P("head", "seq", None)
    small = mesh.shape["seq"] == 8 and mesh.shape["head"] == 4

    def body(qkv, out_weight):
        if small and qkv.shape[1] == 1:
            return body_eight(qkv, out_weight)
        return body_any(qkv, out_weight)

    return jax.shard_map(body, mesh=mesh, in_specs=in_specs, out_specs=out_specs, check_vma=False)
```

```python
import functools
import jax
import jax.numpy as jnp
from jax import lax
from jax.experimental import pallas as pl
from jax.experimental.pallas import tpu as pltpu
from jax.sharding import PartitionSpec as P

HEAD = 128
LOG2E = 1.4426950408889634
NEG = -1e30
QB = 128
VMEM = 24 * 1024 * 1024
F32, BF16 = jnp.float32, jnp.bfloat16


def shifted(shard, axis, by):
    size = lax.axis_size(axis)
    pairs = [(i, i + by) for i in range(size) if 0 <= i + by < size]
    return lax.ppermute(shard, axis, pairs)


def column_part(part):
    queries, keys_part, values = (part[0], part[1], part[2])
    rows = queries.shape[0]
    scale = queries.shape[-1] ** (-0.5)
    scores = (
        jnp.einsum("rchd,schd->chrs", queries, keys_part, preferred_element_type=jnp.float32)
        * scale
    )
    r_idx = lax.broadcasted_iota(jnp.int32, (rows, rows), 0)
    s_idx = lax.broadcasted_iota(jnp.int32, (rows, rows), 1)
    allowed = s_idx <= r_idx - 2
    masked = jnp.where(allowed, scores, jnp.float32(-1e30))
    peak = jnp.max(masked, axis=-1)
    weights = jnp.where(allowed, jnp.exp(masked - peak[..., None]), jnp.float32(0.0))
    total = jnp.maximum(jnp.sum(weights, axis=-1), jnp.float32(1.0))
    rounded = weights.astype(jnp.bfloat16)
    mixed = jnp.einsum("chrs,schd->rchd", rounded, values, preferred_element_type=jnp.float32)
    col_out = (mixed / jnp.transpose(total, (2, 0, 1))[..., None]).astype(jnp.bfloat16)
    col_lse = jnp.transpose(peak + jnp.log(total), (2, 0, 1))
    return (col_out, col_lse)


def row_part(local, previous, first_row):
    rows_dev, cols, heads_local, head_size = (
        local.shape[1],
        local.shape[2],
        local.shape[3],
        local.shape[4],
    )
    scale = head_size ** (-0.5)
    keys_ext = jnp.concatenate([previous, local[1:3]], axis=1)
    key_idx = lax.broadcasted_iota(jnp.int32, (cols, 2 * cols), 1)
    query_idx = lax.broadcasted_iota(jnp.int32, (cols, 2 * cols), 0)

    def one_row(index):
        queries = lax.dynamic_index_in_dim(local[0], index, 0, keepdims=False)
        pair = keys_ext.reshape(2, 2 * cols, heads_local, head_size)
        scores = (
            jnp.einsum("qhd,khd->hqk", queries, pair[0], preferred_element_type=jnp.float32) * scale
        )
        allowed = (key_idx < cols) & (first_row + index > 0) | (key_idx >= cols) & (
            key_idx - cols <= query_idx
        )
        masked = jnp.where(allowed[None], scores, jnp.float32(-1e30))
        peak = jnp.max(masked, axis=-1)
        weights = jnp.where(allowed[None], jnp.exp(masked - peak[..., None]), jnp.float32(0.0))
        total = jnp.sum(weights, axis=-1)
        rounded = weights.astype(jnp.bfloat16)
        mixed = jnp.einsum("hqk,khd->qhd", rounded, pair[1], preferred_element_type=jnp.float32)
        return (mixed / jnp.transpose(total)[..., None], jnp.transpose(peak + jnp.log(total)))

    return lax.map(one_row, jnp.arange(rows_dev, dtype=jnp.int32))


def body_any(qkv, out_weight):
    rows_dev, cols, features = (qkv.shape[1], qkv.shape[2], qkv.shape[3])
    head_size = HEAD
    heads_local = features // head_size
    local = qkv.reshape(3, rows_dev, cols, heads_local, head_size)
    previous = shifted(local[1:3, rows_dev - 1 : rows_dev], "seq", 1)
    first_row = lax.axis_index("seq") * rows_dev
    row_out, row_lse = row_part(local, previous, first_row)
    columns = lax.all_to_all(local, "seq", split_axis=2, concat_axis=1, tiled=True)
    col_part_out, col_part_lse = column_part(columns)
    col_out, col_lse = (
        lax.all_to_all(col_part_out, "seq", split_axis=0, concat_axis=1, tiled=True),
        lax.all_to_all(
            col_part_lse.astype(jnp.bfloat16), "seq", split_axis=0, concat_axis=1, tiled=True
        ).astype(col_part_lse.dtype),
    )
    top = jnp.maximum(row_lse, col_lse)
    left = jnp.exp(row_lse - top)
    right = jnp.exp(col_lse - top)
    attended = (left[..., None] * row_out + right[..., None] * col_out.astype(jnp.float32)) / (
        left + right
    )[..., None]
    attended = attended.astype(jnp.bfloat16).reshape(rows_dev, cols, features)
    terms = jnp.einsum(
        "rcf,fd->crd",
        attended,
        lax.all_gather(out_weight, "seq", axis=1, tiled=True),
        preferred_element_type=jnp.float32,
    )
    summed = lax.psum_scatter(terms.astype(jnp.bfloat16), "head", scatter_dimension=0, tiled=True)
    return summed


def dense_scores(q, k):
    return lax.dot_general(q, k, (((1,), (1,)), ((), ())), preferred_element_type=F32)


def col_scores(q, k):
    prod = q * k
    high = prod.astype(BF16)
    low = (prod - high.astype(F32)).astype(BF16)
    ones = jnp.ones((2 * HEAD, HEAD), BF16)
    return jnp.dot(jnp.concatenate([high, low], axis=1), ones, preferred_element_type=F32)


def with_ones(v):
    return jnp.concatenate([v, jnp.ones_like(v)], axis=1)


def attend(q, dense, cols, coef):
    rows = q.shape[0]
    scores = []
    for k, _, allowed in dense:
        s = dense_scores(q, k)
        scores.append(s if allowed is None else jnp.where(allowed, s, NEG))
    singles = []
    if cols:
        wide = q.astype(F32)
    for k, _, allowed in cols:
        c = col_scores(wide, k)
        singles.append(c if allowed is None else jnp.where(allowed, c, NEG))
    peak = None
    for s in scores:
        for j in range(s.shape[1] // HEAD):
            part = s[:, j * HEAD : (j + 1) * HEAD]
            peak = part if peak is None else jnp.maximum(peak, part)
    if peak is not None:
        peak = jnp.broadcast_to(jnp.max(peak, axis=1, keepdims=True), (rows, HEAD))
    for c in singles:
        peak = c if peak is None else jnp.maximum(peak, c)
    peak = peak * coef
    both = None
    for s, (_, v, _) in zip(scores, dense):
        tiled = jnp.concatenate([peak] * (s.shape[1] // HEAD), axis=1)
        p = jnp.exp2(s * coef - tiled).astype(BF16)
        term = jnp.dot(p, v, preferred_element_type=F32)
        both = term if both is None else both + term
    out = None if both is None else both[:, :HEAD]
    total = None if both is None else both[:, HEAD:]
    for c, (_, v, _) in zip(singles, cols):
        w = jnp.exp2(c * coef - peak)
        total = w if total is None else total + w
        out = w * v if out is None else out + w * v
    return out / total, peak + jnp.log2(total)


def lse_rows(even, odd):
    lane = lax.broadcasted_iota(jnp.int32, (HEAD, HEAD), 1)
    evens, odds = [], []
    for t in range(even.shape[0] // HEAD):
        block = slice(t * HEAD, (t + 1) * HEAD)
        turned = jnp.transpose(jnp.where(lane == 0, even[block], odd[block]))
        evens.append(turned[0:1])
        odds.append(turned[1:2])
    return evens, odds


def put_lse(ref, base, evens, odds):
    rows = jnp.concatenate(evens + odds, axis=0)
    pad = (-rows.shape[0]) % 16
    if pad:
        rows = jnp.concatenate([rows, jnp.zeros((pad, HEAD), F32)], axis=0)
    count = rows.shape[0]
    for piece in range(3):
        part = rows.astype(BF16)
        ref[pl.ds(base + piece * count, count), :] = part
        rows = rows - part.astype(F32)


def get_lse(ref, base, cols):
    blocks = cols // HEAD
    count = -(-2 * blocks // 16) * 16
    rows = sum(ref[pl.ds(base + piece * count, count), :].astype(F32) for piece in range(3))
    turned = [
        jnp.transpose(jnp.broadcast_to(rows[t : t + 1], (HEAD, HEAD))) for t in range(2 * blocks)
    ]
    return jnp.concatenate(turned[:blocks], axis=0), jnp.concatenate(turned[blocks:], axis=0)


def lse_height(cols):
    return 3 * (-(-2 * (cols // HEAD) // 16) * 16)


def stacked(refs):
    return [ref[i] for ref in refs for i in range(ref.shape[0])]


def own_kernel(coef, cols, at, q_m, q_o, kv_m, kv_o, *refs):
    x, z = at[0], at[1]
    below = z == 1
    block = 256
    tri = lax.broadcasted_iota(jnp.int32, (block, block), 1) <= lax.broadcasted_iota(
        jnp.int32, (block, block), 0
    )
    first = x == 0
    k_e, k_o = jnp.where(first, kv_m[0], kv_o[0]), jnp.where(first, kv_o[0], kv_m[0])
    v_e, v_o = jnp.where(first, kv_m[1], kv_o[1]), jnp.where(first, kv_o[1], kv_m[1])
    v_e, v_o = with_ones(v_e), with_ones(v_o)
    *low, out = refs
    m_k, m_v, o_k, o_v = stacked(low)
    lk_e, lk_o = jnp.where(first, m_k, o_k), jnp.where(first, o_k, m_k)
    lv_e, lv_o = jnp.where(first, m_v, o_v), jnp.where(first, o_v, m_v)
    lv_o1 = with_ones(lv_o)
    q_e, q_o = jnp.where(first, q_m[0], q_o[0]), jnp.where(first, q_o[0], q_m[0])
    evens, odds = [], []
    for part in range(cols // block):
        a, b = part * block, (part + 1) * block
        mine = slice(a, b)
        col_e = (lk_e[mine].astype(F32), lv_e[mine].astype(F32), below)
        col_o = (lk_o[mine].astype(F32), lv_o[mine].astype(F32), below)

        def causal(k, v):
            blocks = [(k[a:b], v[a:b], tri)]
            return blocks if part == 0 else [(k[:a], v[:a], None)] + blocks

        o1, l1 = attend(q_e[mine], causal(k_e, v_e) + [(lk_o, lv_o1, below)], [col_e], coef)
        o2, l2 = attend(q_o[mine], causal(k_o, v_o) + [(k_e, v_e, None)], [col_e, col_o], coef)
        out[mine] = o1.astype(BF16)
        out[cols + a : cols + b] = o2.astype(BF16)
        e, o = lse_rows(l1, l2)
        evens, odds = evens + e, odds + o
    put_lse(out, 2 * cols, evens, odds)


def upper_kernel(coef, cols, at, qa_m, qa_o, qb_m, qb_o, kv_m, kv_o, *refs):
    x, z = at[0], at[1]
    below = z == 1
    first = x == 0
    block = 256
    k_e, k_o = jnp.where(first, kv_m[0], kv_o[0]), jnp.where(first, kv_o[0], kv_m[0])
    v_e, v_o = jnp.where(first, kv_m[1], kv_o[1]), jnp.where(first, kv_o[1], kv_m[1])
    v_o1 = with_ones(v_o)
    *low, weight, out_a, out_b = refs
    lows = stacked(low)
    qa = jnp.where(first, qa_m[0], qa_o[0]), jnp.where(first, qa_o[0], qa_m[0])
    qb = jnp.where(first, qb_m[0], qb_o[0]), jnp.where(first, qb_o[0], qb_m[0])
    rows_a, rows_b = ([], []), ([], [])
    for index in range(cols // block):
        a, b = index * block, (index + 1) * block
        mine = slice(a, b)
        m_k, m_v, o_k, o_v = (part[mine].astype(F32) for part in lows)
        ce = (k_e[mine].astype(F32), v_e[mine].astype(F32), None)
        co = (k_o[mine].astype(F32), v_o[mine].astype(F32), None)
        low = [(m_k, m_v, below), (o_k, o_v, below)]
        for q, out, rows, dense, singles in (
            (qa, out_a, rows_a, [(k_o, v_o1, None)], [ce]),
            (qb, out_b, rows_b, [], [ce, co]),
        ):
            o1, l1 = attend(q[0][mine], dense, singles + low, coef)
            o2, l2 = attend(q[1][mine], [], [ce, co] + low, coef)
            o1, o2 = o1.astype(BF16), o2.astype(BF16)
            other = slice(cols + a, cols + b)
            if out is out_b:
                o1, o2 = jnp.where(below, o1, weight[mine]), jnp.where(below, o2, weight[other])
            out[mine] = o1
            out[other] = o2
            e, o = lse_rows(l1, l2)
            rows[0].extend(e)
            rows[1].extend(o)
    put_lse(out_a, 2 * cols, *rows_a)
    put_lse(out_b, 2 * cols, *rows_b)


def merge_kernel(cols, at, own, oa, ob, out):
    z = at[1]
    own_l, a_l, b_l = (get_lse(ref, 2 * cols, cols) for ref in (own, oa, ob))
    for row in range(2):
        tokens = slice(row * cols, (row + 1) * cols)
        l0 = own_l[row]
        l1 = jnp.where(z >= 2, a_l[row], NEG)
        l2 = jnp.where(z >= 3, b_l[row], NEG)
        top = jnp.maximum(l0, jnp.maximum(l1, l2))
        w0, w1, w2 = jnp.exp2(l0 - top), jnp.exp2(l1 - top), jnp.exp2(l2 - top)
        mixed = w0 * own[tokens].astype(F32) + w1 * oa[tokens].astype(F32) + w2 * ob[tokens].astype(F32)
        out[row] = (mixed / (w0 + w1 + w2)).astype(BF16)


def cost(us):
    return pl.CostEstimate(flops=int(us * 1e8), bytes_accessed=1024, transcendentals=0)


def head_call(kernel, at, args, outs, heads, name, us):
    def spec(shape, start=0):
        lead = len(shape) - 1
        return pl.BlockSpec(tuple(shape[:-1]) + (HEAD,), lambda h, at: (0,) * lead + (start + h,))

    return pl.pallas_call(
        kernel,
        out_shape=outs,
        grid_spec=pltpu.PrefetchScalarGridSpec(
            num_scalar_prefetch=1,
            grid=(heads,),
            in_specs=[spec(a.shape, start) for a, start in args],
            out_specs=[spec(o.shape) for o in outs],
        ),
        compiler_params=pltpu.CompilerParams(vmem_limit_bytes=VMEM),
        cost_estimate=cost(us),
        name=name,
    )(at, *(a for a, _ in args))


def project_kernel(chunks, at, *refs):
    x, core = at[0], at[2]
    near, far = refs[:chunks], refs[chunks : 2 * chunks]
    weights, send, keep = refs[2 * chunks : -2], refs[-2], refs[-1]
    tokens = near[0].shape[3]
    half = sum(ref.shape[4] for ref in near)
    for who, out in ((1 - core, send), (core, keep)):

        def rows(ref):
            return jnp.concatenate([ref[r, y, who] for y in range(2) for r in range(2)], axis=0)

        left = jnp.concatenate([rows(ref) for ref in near], axis=1)
        right = jnp.concatenate([rows(ref) for ref in far], axis=1)
        base = 0
        for weight in weights:
            top = weight[pl.ds(pl.multiple_of(x * half, half), half)]
            bottom = weight[pl.ds(pl.multiple_of((1 - x) * half, half), half)]
            c = jnp.dot(left, top, preferred_element_type=F32) + jnp.dot(right, bottom, preferred_element_type=F32)
            width = weight.shape[1]
            s, lane = base // out.shape[4], base % out.shape[4]
            out[s, :, :, :, lane : lane + width] = c.astype(BF16).reshape(2, 2, tokens, width)
            base += width


def project(at, near, far, weights, out_width):
    cols = near[0].shape[1]
    args = [a.reshape(2, 2, 2, cols // 4, a.shape[2]) for a in near + far] + weights
    layers = sum(w.shape[1] for w in weights) // out_width
    out = jax.ShapeDtypeStruct((layers, 2, 2, cols // 4, out_width), BF16)
    return whole_call(
        functools.partial(project_kernel, len(near)), at, args, [out, out], "project", 2 * layers)


def whole_call(kernel, at, args, outs, name, us):
    return pl.pallas_call(
        kernel,
        out_shape=outs,
        in_specs=[pl.BlockSpec(memory_space=pltpu.SMEM)] + [pl.BlockSpec(memory_space=pltpu.VMEM)] * len(args),
        out_specs=[pl.BlockSpec(memory_space=pltpu.VMEM)] * len(outs),
        compiler_params=pltpu.CompilerParams(vmem_limit_bytes=VMEM),
        cost_estimate=cost(us),
        name=name,
    )(at, *args)


def total(a, b):
    return (a.astype(F32) + b.astype(F32)).astype(BF16)


def split_kernel(at, kept, got, stay, to_y, to_x, to_xy):
    x, y = at[0], at[3]
    for s in range(kept.shape[0]):
        for out, yy, xx in ((to_xy, 1 - y, 1 - x), (to_y, 1 - y, x), (to_x, y, 1 - x), (stay, y, x)):
            out[s] = total(kept[s, yy, xx], got[s, yy, xx])


def place_kernel(at, *refs):
    x, z, out = at[0], at[1], refs[-1]
    layers = [z, z + 1 - 2 * (z % 2), (z + 2) % 4, 3 - z]
    for stay, from_y, from_x, from_xy in zip(*(refs[i:-1:4] for i in range(4))):
        width = stay.shape[-1]
        for s in range(stay.shape[0]):
            base = 2 * layers.pop(0)
            mine = pl.ds(pl.multiple_of((base + x) * width, width), width)
            theirs = pl.ds(pl.multiple_of((base + 1 - x) * width, width), width)
            out[:, mine] = total(stay[s], from_y[s])
            out[:, theirs] = total(from_x[s], from_xy[s])


def after(value, *earlier):
    return lax.optimization_barrier((value, earlier))[0]


def body_eight(qkv, out_weight):
    _, _, cols, features = qkv.shape
    half = features // 2
    chunks = 2
    width = half // chunks
    heads = width // HEAD
    coef = HEAD ** (-0.5) * LOG2E
    me = lax.axis_index("seq")
    who = lax.axis_index("head")
    z, x, core, y = me // 2, me % 2, who % 2, who // 2
    at = jnp.stack([x, z, core, y]).astype(jnp.int32)
    local = qkv.reshape(3, cols, features)
    first = x == 0

    def seq_perm(array, *layers, cross=False):
        pairs = [(2 * a + i, 2 * b + (1 - i if cross else i)) for a, b in layers for i in range(2)]
        return lax.ppermute(array, "seq", pairs)

    def swap(array):
        return seq_perm(array, (0, 0), (1, 1), (2, 2), (3, 3), cross=True)

    def head_perm(array, flip):
        return lax.ppermute(array, "head", [(i, i ^ flip) for i in range(4)])

    def lanes(lo, hi, part, source=local):
        return lax.dynamic_slice(source, (lo, 0, part * half), (hi - lo, cols, half))

    def with_weight(array, part):
        return jnp.where(z == 3, array, out_weight[part * cols : (part + 1) * cols].reshape(array.shape))

    down, two_down = [(2, 1), (3, 2)], [(3, 1), (1, 0), (2, 3)]
    q_m = lanes(0, 1, x)
    q_o = swap(lanes(0, 1, 1 - x))
    qs = [seq_perm(q_m, *down), None, seq_perm(with_weight(q_m, 0), *two_down), None]
    kv_m, kv_give = lanes(1, 3, x), lanes(1, 3, 1 - x)
    low_m = seq_perm(jnp.where(z == 0, kv_m, out_weight.reshape(kv_m.shape)), (0, 1), (1, 3))
    low_o = seq_perm(kv_give, (0, 1), cross=True)
    kv_o = swap(after(kv_give, q_o, qs[0]))
    qs[1], qs[3] = seq_perm(q_o, *down), seq_perm(with_weight(q_o, 1), *two_down)

    w_second = seq_perm(after(out_weight, *qs), (0, 2))

    struct = jax.ShapeDtypeStruct
    partial = struct((2 * cols + lse_height(cols), width), BF16)
    oa, ob, own = [], [], []
    turn = at
    kvs = [kv_m, kv_o, low_m, low_o]
    for c in range(chunks):
        a, b = head_call(
            functools.partial(upper_kernel, coef, cols), turn, [(a, c * heads) for a in qs + kvs + [out_weight]],
            [partial] * 2, heads, "upper_rows", 7)
        turn = after(at, a)
        oa.append(seq_perm(a, (1, 2), (2, 3)))
        ob.append(seq_perm(b, (1, 3), (0, 1), (3, 2)))
    for c in range(chunks):
        (mine,) = head_call(
            functools.partial(own_kernel, coef, cols), turn, [(a, c * heads) for a in [q_m, q_o] + kvs],
            [partial], heads, "own_rows", 6)
        own.append(mine)
        turn = after(at, mine, w_second)

    w_down = seq_perm(after(out_weight, *qs), (2, 0), (3, 1))
    depth = out_weight.shape[0]
    ridden = jnp.concatenate([qs[2], qs[3]], axis=1).reshape(out_weight.shape)
    w_near = jnp.where((z == 0) | (z == 3), ridden, jnp.concatenate([o[:depth] for o in ob], axis=1))

    def merged(c, earlier):
        (a,) = head_call(
            functools.partial(merge_kernel, cols), after(at, earlier), [(a[c], 0) for a in (own, oa, ob)],
            [struct((2, cols, width), BF16)], heads, "merge", 2)
        return a, swap(a)

    first_half = merged(0, own[1])
    w_far = jnp.where(
        z >= 2, jnp.where(z == 2, w_second, low_m.reshape(out_weight.shape)), after(w_down, first_half[0], own[1]))
    near, far = map(list, zip(first_half, merged(1, (w_far, first_half[1]))))
    w_other = seq_perm(w_far, (0, 1), (1, 0), (2, 3), (3, 2))

    parts = []
    turn = after(at, w_other)
    for weights in (
        [out_weight, w_near],
        [w_far, w_other],
    ):
        send, kept = project(turn, near, far, weights, out_weight.shape[1])
        got = head_perm(send, 1)
        piece = struct(send.shape[:1] + send.shape[3:], BF16)
        stay, to_y, to_x, to_xy = whole_call(split_kernel, at, [kept, got], [piece] * 4, "split", 2)
        turn = after(at, send)
        diagonal = [((2 * i + j) * 4 + h, (2 * i + 1 - j) * 4 + (h ^ 2)) for i in range(4) for j in range(2) for h in range(4)]
        from_xy = lax.ppermute(to_xy, ("seq", "head"), diagonal)
        parts += [stay, head_perm(to_y, 2), swap(to_x), from_xy]
    (out,) = whole_call(
        place_kernel, at, parts, [struct((cols // 4, 8 * out_weight.shape[1]), BF16)], "place", 2)
    return out.reshape(cols // 4, 1, 8 * out_weight.shape[1])


def solution(mesh):
    in_specs = (P(None, "seq", None, "head"), P("head", "seq"))
    out_specs = P("head", "seq", None)
    small = mesh.shape["seq"] == 8 and mesh.shape["head"] == 4

    def body(qkv, out_weight):
        if small and qkv.shape[1] == 1:
            return body_eight(qkv, out_weight)
        return body_any(qkv, out_weight)

    return jax.shard_map(body, mesh=mesh, in_specs=in_specs, out_specs=out_specs, check_vma=False)
```

```python
import functools
import jax
import jax.numpy as jnp
from jax import lax
from jax.experimental import pallas as pl
from jax.experimental.pallas import tpu as pltpu
from jax.sharding import PartitionSpec as P

HEAD = 128
LOG2E = 1.4426950408889634
NEG = -1e30
QB = 128
VMEM = 24 * 1024 * 1024
F32, BF16 = jnp.float32, jnp.bfloat16


def shifted(shard, axis, by):
    size = lax.axis_size(axis)
    pairs = [(i, i + by) for i in range(size) if 0 <= i + by < size]
    return lax.ppermute(shard, axis, pairs)


def column_part(part):
    queries, keys_part, values = (part[0], part[1], part[2])
    rows = queries.shape[0]
    scale = queries.shape[-1] ** (-0.5)
    scores = (
        jnp.einsum("rchd,schd->chrs", queries, keys_part, preferred_element_type=jnp.float32)
        * scale
    )
    r_idx = lax.broadcasted_iota(jnp.int32, (rows, rows), 0)
    s_idx = lax.broadcasted_iota(jnp.int32, (rows, rows), 1)
    allowed = s_idx <= r_idx - 2
    masked = jnp.where(allowed, scores, jnp.float32(-1e30))
    peak = jnp.max(masked, axis=-1)
    weights = jnp.where(allowed, jnp.exp(masked - peak[..., None]), jnp.float32(0.0))
    total = jnp.maximum(jnp.sum(weights, axis=-1), jnp.float32(1.0))
    rounded = weights.astype(jnp.bfloat16)
    mixed = jnp.einsum("chrs,schd->rchd", rounded, values, preferred_element_type=jnp.float32)
    col_out = (mixed / jnp.transpose(total, (2, 0, 1))[..., None]).astype(jnp.bfloat16)
    col_lse = jnp.transpose(peak + jnp.log(total), (2, 0, 1))
    return (col_out, col_lse)


def row_part(local, previous, first_row):
    rows_dev, cols, heads_local, head_size = (
        local.shape[1],
        local.shape[2],
        local.shape[3],
        local.shape[4],
    )
    scale = head_size ** (-0.5)
    keys_ext = jnp.concatenate([previous, local[1:3]], axis=1)
    key_idx = lax.broadcasted_iota(jnp.int32, (cols, 2 * cols), 1)
    query_idx = lax.broadcasted_iota(jnp.int32, (cols, 2 * cols), 0)

    def one_row(index):
        queries = lax.dynamic_index_in_dim(local[0], index, 0, keepdims=False)
        pair = keys_ext.reshape(2, 2 * cols, heads_local, head_size)
        scores = (
            jnp.einsum("qhd,khd->hqk", queries, pair[0], preferred_element_type=jnp.float32) * scale
        )
        allowed = (key_idx < cols) & (first_row + index > 0) | (key_idx >= cols) & (
            key_idx - cols <= query_idx
        )
        masked = jnp.where(allowed[None], scores, jnp.float32(-1e30))
        peak = jnp.max(masked, axis=-1)
        weights = jnp.where(allowed[None], jnp.exp(masked - peak[..., None]), jnp.float32(0.0))
        total = jnp.sum(weights, axis=-1)
        rounded = weights.astype(jnp.bfloat16)
        mixed = jnp.einsum("hqk,khd->qhd", rounded, pair[1], preferred_element_type=jnp.float32)
        return (mixed / jnp.transpose(total)[..., None], jnp.transpose(peak + jnp.log(total)))

    return lax.map(one_row, jnp.arange(rows_dev, dtype=jnp.int32))


def body_any(qkv, out_weight):
    rows_dev, cols, features = (qkv.shape[1], qkv.shape[2], qkv.shape[3])
    head_size = HEAD
    heads_local = features // head_size
    local = qkv.reshape(3, rows_dev, cols, heads_local, head_size)
    previous = shifted(local[1:3, rows_dev - 1 : rows_dev], "seq", 1)
    first_row = lax.axis_index("seq") * rows_dev
    row_out, row_lse = row_part(local, previous, first_row)
    columns = lax.all_to_all(local, "seq", split_axis=2, concat_axis=1, tiled=True)
    col_part_out, col_part_lse = column_part(columns)
    col_out, col_lse = (
        lax.all_to_all(col_part_out, "seq", split_axis=0, concat_axis=1, tiled=True),
        lax.all_to_all(
            col_part_lse.astype(jnp.bfloat16), "seq", split_axis=0, concat_axis=1, tiled=True
        ).astype(col_part_lse.dtype),
    )
    top = jnp.maximum(row_lse, col_lse)
    left = jnp.exp(row_lse - top)
    right = jnp.exp(col_lse - top)
    attended = (left[..., None] * row_out + right[..., None] * col_out.astype(jnp.float32)) / (
        left + right
    )[..., None]
    attended = attended.astype(jnp.bfloat16).reshape(rows_dev, cols, features)
    terms = jnp.einsum(
        "rcf,fd->crd",
        attended,
        lax.all_gather(out_weight, "seq", axis=1, tiled=True),
        preferred_element_type=jnp.float32,
    )
    summed = lax.psum_scatter(terms.astype(jnp.bfloat16), "head", scatter_dimension=0, tiled=True)
    return summed


def dense_scores(q, k):
    return lax.dot_general(q, k, (((1,), (1,)), ((), ())), preferred_element_type=F32)


def col_scores(q, k):
    prod = q * k
    high = prod.astype(BF16)
    low = (prod - high.astype(F32)).astype(BF16)
    ones = jnp.ones((2 * HEAD, HEAD), BF16)
    return jnp.dot(jnp.concatenate([high, low], axis=1), ones, preferred_element_type=F32)


def with_ones(v):
    return jnp.concatenate([v, jnp.ones_like(v)], axis=1)


def attend(q, dense, cols, coef):
    rows = q.shape[0]
    scores = []
    for k, _, allowed in dense:
        s = dense_scores(q, k)
        scores.append(s if allowed is None else jnp.where(allowed, s, NEG))
    singles = []
    if cols:
        wide = q.astype(F32)
    for k, _, allowed in cols:
        c = col_scores(wide, k)
        singles.append(c if allowed is None else jnp.where(allowed, c, NEG))
    peak = None
    for s in scores:
        for j in range(s.shape[1] // HEAD):
            part = s[:, j * HEAD : (j + 1) * HEAD]
            peak = part if peak is None else jnp.maximum(peak, part)
    if peak is not None:
        peak = jnp.broadcast_to(jnp.max(peak, axis=1, keepdims=True), (rows, HEAD))
    for c in singles:
        peak = c if peak is None else jnp.maximum(peak, c)
    peak = peak * coef
    both = None
    for s, (_, v, _) in zip(scores, dense):
        tiled = jnp.concatenate([peak] * (s.shape[1] // HEAD), axis=1)
        p = jnp.exp2(s * coef - tiled).astype(BF16)
        term = jnp.dot(p, v, preferred_element_type=F32)
        both = term if both is None else both + term
    out = None if both is None else both[:, :HEAD]
    total = None if both is None else both[:, HEAD:]
    for c, (_, v, _) in zip(singles, cols):
        w = jnp.exp2(c * coef - peak)
        total = w if total is None else total + w
        out = w * v if out is None else out + w * v
    return out / total, peak + jnp.log2(total)


def lse_rows(even, odd):
    lane = lax.broadcasted_iota(jnp.int32, (HEAD, HEAD), 1)
    evens, odds = [], []
    for t in range(even.shape[0] // HEAD):
        block = slice(t * HEAD, (t + 1) * HEAD)
        turned = jnp.transpose(jnp.where(lane == 0, even[block], odd[block]))
        evens.append(turned[0:1])
        odds.append(turned[1:2])
    return evens, odds


LSE_ROWS = 16


def put_lse(ref, base, evens, odds):
    rows = jnp.concatenate(evens + odds, axis=0)
    pieces = []
    for _ in range(3):
        pieces.append(rows.astype(BF16).astype(F32))
        rows = rows - pieces[-1]
    spare = LSE_ROWS - 3 * rows.shape[0]
    ref[pl.ds(base, LSE_ROWS), :] = jnp.concatenate(pieces + [jnp.zeros((spare, HEAD), F32)], axis=0).astype(BF16)


def get_lse(ref, base, tokens):
    blocks = tokens // HEAD
    packed = ref[pl.ds(base, LSE_ROWS), :].astype(F32)
    rows = sum(packed[i * 2 * blocks : (i + 1) * 2 * blocks] for i in range(3))
    turned = [
        jnp.transpose(jnp.broadcast_to(rows[t : t + 1], (HEAD, HEAD))) for t in range(2 * blocks)
    ]
    return jnp.concatenate(turned[:blocks], axis=0), jnp.concatenate(turned[blocks:], axis=0)


def chunk_rows(array, chunk, chunks, parts):
    size = array.shape[0] // parts
    share = size // chunks
    return jnp.concatenate(
        [array[p * size + chunk * share : p * size + (chunk + 1) * share] for p in range(parts)], axis=0)


def stacked(refs):
    return [ref[i] for ref in refs for i in range(ref.shape[0])]


def own_kernel(coef, chunk, chunks, parts, at, q_m, q_o, kv_m, kv_o, *refs):
    x, z = at[0], at[1]
    below = z == 1
    first = x == 0
    *low, out = refs
    cols = q_m.shape[1]
    tokens = cols // chunks

    def pair(a, b):
        return jnp.where(first, a, b), jnp.where(first, b, a)

    def mine(array):
        return chunk_rows(array, chunk, chunks, parts)

    q_e, q_o = pair(mine(q_m[0]), mine(q_o[0]))
    k_e, k_o = pair(kv_m[0], kv_o[0])
    v_e, v_o = pair(kv_m[1], kv_o[1])
    v_e, v_o = with_ones(v_e), with_ones(v_o)
    m_k, m_v, o_k, o_v = stacked(low)
    lk_e, lk_o = pair(m_k, o_k)
    lv_e, lv_o = pair(m_v, o_v)
    col_e = (mine(lk_e).astype(F32), mine(lv_e).astype(F32), below)
    col_o = (mine(lk_o).astype(F32), mine(lv_o).astype(F32), below)
    share = tokens // parts
    index = lax.broadcasted_iota(jnp.int32, (tokens, cols), 0)
    index = (index // share) * (cols // parts) + chunk * share + index % share
    tri = lax.broadcasted_iota(jnp.int32, (tokens, cols), 1) <= index
    o1, l1 = attend(q_e, [(k_e, v_e, tri), (lk_o, with_ones(lv_o), below)], [col_e], coef)
    o2, l2 = attend(q_o, [(k_o, v_o, tri), (k_e, v_e, None)], [col_e, col_o], coef)
    out[:tokens] = o1.astype(BF16)
    out[tokens : 2 * tokens] = o2.astype(BF16)
    put_lse(out, 2 * tokens, *lse_rows(l1, l2))


def upper_kernel(coef, chunk, chunks, parts, at, qa_m, qa_o, qb_m, qb_o, kv_m, kv_o, *refs):
    x, z = at[0], at[1]
    below = z == 1
    first = x == 0
    *low, weight, out_a, out_b = refs
    tokens = qa_m.shape[1] // chunks

    def pair(a, b):
        return jnp.where(first, a, b), jnp.where(first, b, a)

    def mine(array):
        return chunk_rows(array, chunk, chunks, parts)

    k_e, k_o = pair(kv_m[0], kv_o[0])
    v_e, v_o = pair(kv_m[1], kv_o[1])
    m_k, m_v, o_k, o_v = (mine(part).astype(F32) for part in stacked(low))
    lower = [(m_k, m_v, below), (o_k, o_v, below)]
    ce = (mine(k_e).astype(F32), mine(v_e).astype(F32), None)
    co = (mine(k_o).astype(F32), mine(v_o).astype(F32), None)
    base = chunk * 2 * tokens
    for q_m, q_o, out, dense, singles in (
        (qa_m, qa_o, out_a, [(k_o, with_ones(v_o), None)], [ce]),
        (qb_m, qb_o, out_b, [], [ce, co]),
    ):
        q_e, q_odd = pair(mine(q_m[0]), mine(q_o[0]))
        o1, l1 = attend(q_e, dense, singles + lower, coef)
        o2, l2 = attend(q_odd, [], [ce, co] + lower, coef)
        o1, o2 = o1.astype(BF16), o2.astype(BF16)
        if out is out_b:
            o1 = jnp.where(below, o1, weight[base : base + tokens])
            o2 = jnp.where(below, o2, weight[base + tokens : base + 2 * tokens])
        out[:tokens] = o1
        out[tokens : 2 * tokens] = o2
        put_lse(out, 2 * tokens, *lse_rows(l1, l2))


def merge_kernel(at, own, oa, ob, out):
    z = at[1]
    count = out.shape[1]
    own_l, a_l, b_l = (get_lse(ref, 2 * count, count) for ref in (own, oa, ob))
    for row in range(2):
        tokens = slice(row * count, (row + 1) * count)
        l0 = own_l[row]
        l1 = jnp.where(z >= 2, a_l[row], NEG)
        l2 = jnp.where(z >= 3, b_l[row], NEG)
        top = jnp.maximum(l0, jnp.maximum(l1, l2))
        w0, w1, w2 = jnp.exp2(l0 - top), jnp.exp2(l1 - top), jnp.exp2(l2 - top)
        mixed = w0 * own[tokens].astype(F32) + w1 * oa[tokens].astype(F32) + w2 * ob[tokens].astype(F32)
        out[row] = (mixed / (w0 + w1 + w2)).astype(BF16)


def cost(us):
    return pl.CostEstimate(flops=int(us * 1e8), bytes_accessed=1024, transcendentals=0)


def head_call(kernel, at, args, outs, heads, name, us):
    def spec(shape, start=0):
        lead = len(shape) - 1
        return pl.BlockSpec(tuple(shape[:-1]) + (HEAD,), lambda h, at: (0,) * lead + (start + h,))

    return pl.pallas_call(
        kernel,
        out_shape=outs,
        grid_spec=pltpu.PrefetchScalarGridSpec(
            num_scalar_prefetch=1,
            grid=(heads,),
            in_specs=[spec(a.shape, start) for a, start in args],
            out_specs=[spec(o.shape) for o in outs],
        ),
        compiler_params=pltpu.CompilerParams(vmem_limit_bytes=VMEM),
        cost_estimate=cost(us),
        name=name,
    )(at, *(a for a, _ in args))


def project_kernel(plan, at, *refs):
    x, core = at[0], at[2]
    *arrays, send, keep = refs
    for who, out in ((1 - core, send), (core, keep)):
        for s, (near, far, weight) in enumerate(plan):
            left, right = (
                jnp.concatenate([arrays[i][r, y, who] for y in range(2) for r in range(2)], axis=0)
                for i in (near, far)
            )
            weight = arrays[weight]
            half = left.shape[1]
            top = weight[pl.ds(pl.multiple_of(x * half, half), half)]
            bottom = weight[pl.ds(pl.multiple_of((1 - x) * half, half), half)]
            c = jnp.dot(left, top, preferred_element_type=F32) + jnp.dot(right, bottom, preferred_element_type=F32)
            out[s] = c.astype(BF16).reshape(out.shape[1:])


def project(at, attended, items):
    arrays, plan = [], []

    def place_of(array):
        for i, other in enumerate(arrays):
            if other is array:
                return i
        arrays.append(array)
        return len(arrays) - 1

    for chunk, weight in items:
        plan.append(tuple(place_of(a) for a in attended[chunk] + (weight,)))
    _, _, _, tokens, _ = attended[0][0].shape
    out = jax.ShapeDtypeStruct((len(items), 2, 2, tokens, items[0][1].shape[1]), BF16)
    return whole_call(functools.partial(project_kernel, plan), at, arrays, [out, out], "project", len(items))


def whole_call(kernel, at, args, outs, name, us):
    return pl.pallas_call(
        kernel,
        out_shape=outs,
        in_specs=[pl.BlockSpec(memory_space=pltpu.SMEM)] + [pl.BlockSpec(memory_space=pltpu.VMEM)] * len(args),
        out_specs=[pl.BlockSpec(memory_space=pltpu.VMEM)] * len(outs),
        compiler_params=pltpu.CompilerParams(vmem_limit_bytes=VMEM),
        cost_estimate=cost(us),
        name=name,
    )(at, *args)


def total(a, b):
    return (a.astype(F32) + b.astype(F32)).astype(BF16)


def split_kernel(at, kept, got, stay, to_y, to_x, to_xy):
    x, y = at[0], at[3]
    for s in range(kept.shape[0]):
        for out, yy, xx in ((to_xy, 1 - y, 1 - x), (to_y, 1 - y, x), (to_x, y, 1 - x), (stay, y, x)):
            out[s] = total(kept[s, yy, xx], got[s, yy, xx])


def place_kernel(plan, at, *refs):
    x, z, out = at[0], at[1], refs[-1]
    layers = [z, z + 1 - 2 * (z % 2), (z + 2) % 4, 3 - z]
    slabs = iter(plan)
    for stay, from_y, from_x, from_xy in zip(*(refs[i:-1:4] for i in range(4))):
        _, tokens, width = stay.shape
        for s in range(stay.shape[0]):
            chunk, layer = next(slabs)
            rows = pl.ds(chunk * tokens, tokens)
            base = 2 * layers[layer]
            mine = pl.ds(pl.multiple_of((base + x) * width, width), width)
            theirs = pl.ds(pl.multiple_of((base + 1 - x) * width, width), width)
            out[rows, mine] = total(stay[s], from_y[s])
            out[rows, theirs] = total(from_x[s], from_xy[s])


def after(value, *earlier):
    return lax.optimization_barrier((value, earlier))[0]


def body_eight(qkv, out_weight):
    _, _, cols, features = qkv.shape
    half = features // 2
    chunks = 2
    heads = half // HEAD
    parts = lax.axis_size("head")
    tokens = cols // chunks
    coef = HEAD ** (-0.5) * LOG2E
    me = lax.axis_index("seq")
    who = lax.axis_index("head")
    z, x, core, y = me // 2, me % 2, who % 2, who // 2
    at = jnp.stack([x, z, core, y]).astype(jnp.int32)
    local = qkv.reshape(3, cols, features)
    first = x == 0

    def seq_perm(array, *layers, cross=False):
        pairs = [(2 * a + i, 2 * b + (1 - i if cross else i)) for a, b in layers for i in range(2)]
        return lax.ppermute(array, "seq", pairs)

    def swap(array):
        return seq_perm(array, (0, 0), (1, 1), (2, 2), (3, 3), cross=True)

    def head_perm(array, flip):
        return lax.ppermute(array, "head", [(i, i ^ flip) for i in range(4)])

    def lanes(lo, hi, part, source=local):
        return lax.dynamic_slice(source, (lo, 0, part * half), (hi - lo, cols, half))

    down, two_down = [(2, 1), (3, 2)], [(3, 1)]
    q_m = lanes(0, 1, x)
    q_o = swap(lanes(0, 1, 1 - x))
    qs = [seq_perm(q_m, *down), None, seq_perm(q_m, *two_down), None]
    kv_m, kv_give = lanes(1, 3, x), lanes(1, 3, 1 - x)
    block = out_weight.reshape(kv_m.shape)
    low_m = seq_perm(jnp.where(z == 0, kv_m, block), (0, 1), (1, 3))
    pairs = [(i, 2 + 1 - i) for i in range(2)] + [(2 + i, i) for i in range(2)] + [(4 + i, 6 + i) for i in range(2)]
    low_o = lax.ppermute(jnp.where(z == 0, kv_give, block), "seq", pairs)
    kv_o = swap(after(kv_give, q_o, qs[0]))
    qs[1], qs[3] = seq_perm(q_o, *down), seq_perm(q_o, *two_down)
    w_second = seq_perm(after(out_weight, *qs), (0, 2))

    struct = jax.ShapeDtypeStruct
    partial = struct((2 * tokens + LSE_ROWS, half), BF16)
    oa, ob, own = [], [], []
    turn = at
    kvs = [kv_m, kv_o, low_m, low_o]
    for c in range(chunks):
        a, b = head_call(
            functools.partial(upper_kernel, coef, c, chunks, parts), turn, [(a, 0) for a in qs + kvs + [out_weight]],
            [partial] * 2, heads, "upper_rows", 7)
        turn = after(at, a)
        oa.append(seq_perm(a, (1, 2), (2, 3)))
        ob.append(seq_perm(b, (1, 3), (0, 1), (3, 2)))
    for c in range(chunks):
        (mine,) = head_call(
            functools.partial(own_kernel, coef, c, chunks, parts), turn, [(a, 0) for a in [q_m, q_o] + kvs],
            [partial], heads, "own_rows", 6)
        own.append(mine)
        turn = after(at, mine, w_second)

    w_down = seq_perm(after(out_weight, *qs), (2, 0), (3, 1))

    def merged(c, earlier):
        (a,) = head_call(
            merge_kernel, after(at, earlier), [(a[c], 0) for a in (own, oa, ob)],
            [struct((2, tokens, half), BF16)], heads, "merge", 2)
        shape = (2, 2, 2, tokens // 4, half)
        return a.reshape(shape), swap(a).reshape(shape)

    attended = [merged(0, own[1])]
    ridden = jnp.where(z == 2, w_second, low_m.reshape(out_weight.shape))
    w_far = jnp.where(z >= 2, ridden, after(w_down, attended[0][0], own[1]))
    w_other = seq_perm(w_far, (0, 1), (1, 0), (2, 3), (3, 2))
    parts_out, plan = [], []

    def send_out(turn, names):
        send, kept = project(turn, attended, [(c, weights[layer]) for c, layer in names])
        got = head_perm(send, 1)
        piece = struct(send.shape[:1] + send.shape[3:], BF16)
        stay, to_y, to_x, to_xy = whole_call(split_kernel, at, [kept, got], [piece] * 4, "split", 2)
        diagonal = [
            ((2 * i + j) * 4 + h, (2 * i + 1 - j) * 4 + (h ^ 2)) for i in range(4) for j in range(2) for h in range(4)
        ]
        from_xy = lax.ppermute(to_xy, ("seq", "head"), diagonal)
        parts_out.extend([stay, head_perm(to_y, 2), swap(to_x), from_xy])
        plan.extend(names)
        return send

    weights = {0: out_weight, 2: w_far, 3: w_other}
    attended.append(merged(1, (w_far, attended[0][1])))
    weights[1] = jnp.where(
        (z == 0) | (z == 3), low_o.reshape(out_weight.shape), jnp.concatenate([o[: 2 * tokens] for o in ob]))
    send_out(after(at, attended[1][0]), [(0, 0), (0, 2), (0, 1)])
    send_out(after(at, *parts_out), [(1, 0), (1, 1), (1, 2), (1, 3), (0, 3)])
    (out,) = whole_call(
        functools.partial(place_kernel, plan), at, parts_out,
        [struct((cols // 4, 8 * out_weight.shape[1]), BF16)], "place", 2)
    return out.reshape(cols // 4, 1, 8 * out_weight.shape[1])


def solution(mesh):
    in_specs = (P(None, "seq", None, "head"), P("head", "seq"))
    out_specs = P("head", "seq", None)
    small = mesh.shape["seq"] == 8 and mesh.shape["head"] == 4

    def body(qkv, out_weight):
        _, rows, cols, features = qkv.shape
        even = features == 2 * cols and out_weight.shape == (features, cols) and cols % 512 == 0
        if small and rows == 1 and even:
            return body_eight(qkv, out_weight)
        return body_any(qkv, out_weight)

    return jax.shard_map(body, mesh=mesh, in_specs=in_specs, out_specs=out_specs, check_vma=False)
```

```python
import functools
import jax
import jax.numpy as jnp
from jax import lax
from jax.experimental import pallas as pl
from jax.experimental.pallas import tpu as pltpu
from jax.sharding import PartitionSpec as P

HEAD = 128
LOG2E = 1.4426950408889634
NEG = -1e30
QB = 128
VMEM = 24 * 1024 * 1024
F32, BF16 = jnp.float32, jnp.bfloat16


def shifted(shard, axis, by):
    size = lax.axis_size(axis)
    pairs = [(i, i + by) for i in range(size) if 0 <= i + by < size]
    return lax.ppermute(shard, axis, pairs)


def column_part(part):
    queries, keys_part, values = (part[0], part[1], part[2])
    rows = queries.shape[0]
    scale = queries.shape[-1] ** (-0.5)
    scores = (
        jnp.einsum("rchd,schd->chrs", queries, keys_part, preferred_element_type=jnp.float32)
        * scale
    )
    r_idx = lax.broadcasted_iota(jnp.int32, (rows, rows), 0)
    s_idx = lax.broadcasted_iota(jnp.int32, (rows, rows), 1)
    allowed = s_idx <= r_idx - 2
    masked = jnp.where(allowed, scores, jnp.float32(-1e30))
    peak = jnp.max(masked, axis=-1)
    weights = jnp.where(allowed, jnp.exp(masked - peak[..., None]), jnp.float32(0.0))
    total = jnp.maximum(jnp.sum(weights, axis=-1), jnp.float32(1.0))
    rounded = weights.astype(jnp.bfloat16)
    mixed = jnp.einsum("chrs,schd->rchd", rounded, values, preferred_element_type=jnp.float32)
    col_out = (mixed / jnp.transpose(total, (2, 0, 1))[..., None]).astype(jnp.bfloat16)
    col_lse = jnp.transpose(peak + jnp.log(total), (2, 0, 1))
    return (col_out, col_lse)


def row_part(local, previous, first_row):
    rows_dev, cols, heads_local, head_size = (
        local.shape[1],
        local.shape[2],
        local.shape[3],
        local.shape[4],
    )
    scale = head_size ** (-0.5)
    keys_ext = jnp.concatenate([previous, local[1:3]], axis=1)
    key_idx = lax.broadcasted_iota(jnp.int32, (cols, 2 * cols), 1)
    query_idx = lax.broadcasted_iota(jnp.int32, (cols, 2 * cols), 0)

    def one_row(index):
        queries = lax.dynamic_index_in_dim(local[0], index, 0, keepdims=False)
        pair = keys_ext.reshape(2, 2 * cols, heads_local, head_size)
        scores = (
            jnp.einsum("qhd,khd->hqk", queries, pair[0], preferred_element_type=jnp.float32) * scale
        )
        allowed = (key_idx < cols) & (first_row + index > 0) | (key_idx >= cols) & (
            key_idx - cols <= query_idx
        )
        masked = jnp.where(allowed[None], scores, jnp.float32(-1e30))
        peak = jnp.max(masked, axis=-1)
        weights = jnp.where(allowed[None], jnp.exp(masked - peak[..., None]), jnp.float32(0.0))
        total = jnp.sum(weights, axis=-1)
        rounded = weights.astype(jnp.bfloat16)
        mixed = jnp.einsum("hqk,khd->qhd", rounded, pair[1], preferred_element_type=jnp.float32)
        return (mixed / jnp.transpose(total)[..., None], jnp.transpose(peak + jnp.log(total)))

    return lax.map(one_row, jnp.arange(rows_dev, dtype=jnp.int32))


def body_any(qkv, out_weight):
    rows_dev, cols, features = (qkv.shape[1], qkv.shape[2], qkv.shape[3])
    head_size = HEAD
    heads_local = features // head_size
    local = qkv.reshape(3, rows_dev, cols, heads_local, head_size)
    previous = shifted(local[1:3, rows_dev - 1 : rows_dev], "seq", 1)
    first_row = lax.axis_index("seq") * rows_dev
    row_out, row_lse = row_part(local, previous, first_row)
    columns = lax.all_to_all(local, "seq", split_axis=2, concat_axis=1, tiled=True)
    col_part_out, col_part_lse = column_part(columns)
    col_out, col_lse = (
        lax.all_to_all(col_part_out, "seq", split_axis=0, concat_axis=1, tiled=True),
        lax.all_to_all(
            col_part_lse.astype(jnp.bfloat16), "seq", split_axis=0, concat_axis=1, tiled=True
        ).astype(col_part_lse.dtype),
    )
    top = jnp.maximum(row_lse, col_lse)
    left = jnp.exp(row_lse - top)
    right = jnp.exp(col_lse - top)
    attended = (left[..., None] * row_out + right[..., None] * col_out.astype(jnp.float32)) / (
        left + right
    )[..., None]
    attended = attended.astype(jnp.bfloat16).reshape(rows_dev, cols, features)
    terms = jnp.einsum(
        "rcf,fd->crd",
        attended,
        lax.all_gather(out_weight, "seq", axis=1, tiled=True),
        preferred_element_type=jnp.float32,
    )
    summed = lax.psum_scatter(terms.astype(jnp.bfloat16), "head", scatter_dimension=0, tiled=True)
    return summed


def dense_scores(q, k):
    return lax.dot_general(q, k, (((1,), (1,)), ((), ())), preferred_element_type=F32)


def col_scores(q, k):
    prod = q * k
    high = prod.astype(BF16)
    low = (prod - high.astype(F32)).astype(BF16)
    ones = jnp.ones((2 * HEAD, HEAD), BF16)
    return jnp.dot(jnp.concatenate([high, low], axis=1), ones, preferred_element_type=F32)


def with_ones(v):
    return jnp.concatenate([v, jnp.ones_like(v)], axis=1)


def attend(q, dense, cols, coef):
    rows = q.shape[0]
    scores = []
    for k, _, allowed in dense:
        s = dense_scores(q, k)
        scores.append(s if allowed is None else jnp.where(allowed, s, NEG))
    singles = []
    if cols:
        wide = q.astype(F32)
    for k, _, allowed in cols:
        c = col_scores(wide, k)
        singles.append(c if allowed is None else jnp.where(allowed, c, NEG))
    peak = None
    for s in scores:
        for j in range(s.shape[1] // HEAD):
            part = s[:, j * HEAD : (j + 1) * HEAD]
            peak = part if peak is None else jnp.maximum(peak, part)
    if peak is not None:
        peak = jnp.broadcast_to(jnp.max(peak, axis=1, keepdims=True), (rows, HEAD))
    for c in singles:
        peak = c if peak is None else jnp.maximum(peak, c)
    peak = peak * coef
    both = None
    for s, (_, v, _) in zip(scores, dense):
        tiled = jnp.concatenate([peak] * (s.shape[1] // HEAD), axis=1)
        p = jnp.exp2(s * coef - tiled).astype(BF16)
        term = jnp.dot(p, v, preferred_element_type=F32)
        both = term if both is None else both + term
    out = None if both is None else both[:, :HEAD]
    total = None if both is None else both[:, HEAD:]
    for c, (_, v, _) in zip(singles, cols):
        w = jnp.exp2(c * coef - peak)
        total = w if total is None else total + w
        out = w * v if out is None else out + w * v
    return out / total, peak + jnp.log2(total)


def lse_rows(even, odd):
    lane = lax.broadcasted_iota(jnp.int32, (HEAD, HEAD), 1)
    evens, odds = [], []
    for t in range(even.shape[0] // HEAD):
        block = slice(t * HEAD, (t + 1) * HEAD)
        turned = jnp.transpose(jnp.where(lane == 0, even[block], odd[block]))
        evens.append(turned[0:1])
        odds.append(turned[1:2])
    return evens, odds


LSE_ROWS = 16


def put_lse(ref, base, evens, odds):
    rows = jnp.concatenate(evens + odds, axis=0)
    pieces = []
    for _ in range(3):
        pieces.append(rows.astype(BF16).astype(F32))
        rows = rows - pieces[-1]
    spare = LSE_ROWS - 3 * rows.shape[0]
    ref[pl.ds(base, LSE_ROWS), :] = jnp.concatenate(pieces + [jnp.zeros((spare, HEAD), F32)], axis=0).astype(BF16)


def get_lse(ref, base, tokens):
    blocks = tokens // HEAD
    packed = ref[pl.ds(base, LSE_ROWS), :].astype(F32)
    rows = sum(packed[i * 2 * blocks : (i + 1) * 2 * blocks] for i in range(3))
    turned = [
        jnp.transpose(jnp.broadcast_to(rows[t : t + 1], (HEAD, HEAD))) for t in range(2 * blocks)
    ]
    return jnp.concatenate(turned[:blocks], axis=0), jnp.concatenate(turned[blocks:], axis=0)


def chunk_rows(array, chunk, chunks, parts):
    size = array.shape[0] // parts
    share = size // chunks
    return jnp.concatenate(
        [array[p * size + chunk * share : p * size + (chunk + 1) * share] for p in range(parts)], axis=0)


def stacked(refs):
    return [ref[i] for ref in refs for i in range(ref.shape[0])]


def own_kernel(coef, chunk, chunks, parts, at, q_m, q_o, kv_m, kv_o, *refs):
    x, z = at[0], at[1]
    below = z == 1
    first = x == 0
    *low, out = refs
    cols = q_m.shape[1]
    tokens = cols // chunks

    def pair(a, b):
        return jnp.where(first, a, b), jnp.where(first, b, a)

    def mine(array):
        return chunk_rows(array, chunk, chunks, parts)

    q_e, q_o = pair(mine(q_m[0]), mine(q_o[0]))
    k_e, k_o = pair(kv_m[0], kv_o[0])
    v_e, v_o = pair(kv_m[1], kv_o[1])
    v_e, v_o = with_ones(v_e), with_ones(v_o)
    m_k, m_v, o_k, o_v = stacked(low)
    lk_e, lk_o = pair(m_k, o_k)
    lv_e, lv_o = pair(m_v, o_v)
    col_e = (mine(lk_e).astype(F32), mine(lv_e).astype(F32), below)
    col_o = (mine(lk_o).astype(F32), mine(lv_o).astype(F32), below)
    share = tokens // parts
    index = lax.broadcasted_iota(jnp.int32, (tokens, cols), 0)
    index = (index // share) * (cols // parts) + chunk * share + index % share
    tri = lax.broadcasted_iota(jnp.int32, (tokens, cols), 1) <= index
    o1, l1 = attend(q_e, [(k_e, v_e, tri), (lk_o, with_ones(lv_o), below)], [col_e], coef)
    o2, l2 = attend(q_o, [(k_o, v_o, tri), (k_e, v_e, None)], [col_e, col_o], coef)
    out[:tokens] = o1.astype(BF16)
    out[tokens : 2 * tokens] = o2.astype(BF16)
    put_lse(out, 2 * tokens, *lse_rows(l1, l2))


def upper_kernel(coef, chunk, chunks, parts, at, qa_m, qa_o, qb_m, qb_o, kv_m, kv_o, *refs):
    x, z = at[0], at[1]
    below = z == 1
    first = x == 0
    *low, weight, out_a, out_b = refs
    tokens = qa_m.shape[1] // chunks

    def pair(a, b):
        return jnp.where(first, a, b), jnp.where(first, b, a)

    def mine(array):
        return chunk_rows(array, chunk, chunks, parts)

    k_e, k_o = pair(kv_m[0], kv_o[0])
    v_e, v_o = pair(kv_m[1], kv_o[1])
    m_k, m_v, o_k, o_v = (mine(part).astype(F32) for part in stacked(low))
    lower = [(m_k, m_v, below), (o_k, o_v, below)]
    ce = (mine(k_e).astype(F32), mine(v_e).astype(F32), None)
    co = (mine(k_o).astype(F32), mine(v_o).astype(F32), None)
    base = chunk * 2 * tokens
    for q_m, q_o, out, dense, singles in (
        (qa_m, qa_o, out_a, [(k_o, with_ones(v_o), None)], [ce]),
        (qb_m, qb_o, out_b, [], [ce, co]),
    ):
        q_e, q_odd = pair(mine(q_m[0]), mine(q_o[0]))
        o1, l1 = attend(q_e, dense, singles + lower, coef)
        o2, l2 = attend(q_odd, [], [ce, co] + lower, coef)
        o1, o2 = o1.astype(BF16), o2.astype(BF16)
        if out is out_b:
            o1 = jnp.where(below, o1, weight[base : base + tokens])
            o2 = jnp.where(below, o2, weight[base + tokens : base + 2 * tokens])
        out[:tokens] = o1
        out[tokens : 2 * tokens] = o2
        put_lse(out, 2 * tokens, *lse_rows(l1, l2))


def merge_kernel(at, own, oa, ob, out):
    z = at[1]
    count = out.shape[1]
    own_l, a_l, b_l = (get_lse(ref, 2 * count, count) for ref in (own, oa, ob))
    for row in range(2):
        tokens = slice(row * count, (row + 1) * count)
        l0 = own_l[row]
        l1 = jnp.where(z >= 2, a_l[row], NEG)
        l2 = jnp.where(z >= 3, b_l[row], NEG)
        top = jnp.maximum(l0, jnp.maximum(l1, l2))
        w0, w1, w2 = jnp.exp2(l0 - top), jnp.exp2(l1 - top), jnp.exp2(l2 - top)
        mixed = w0 * own[tokens].astype(F32) + w1 * oa[tokens].astype(F32) + w2 * ob[tokens].astype(F32)
        out[row] = (mixed / (w0 + w1 + w2)).astype(BF16)


def cost(us):
    return pl.CostEstimate(flops=int(us * 1e8), bytes_accessed=1024, transcendentals=0)


def head_call(kernel, at, args, outs, heads, name, us):
    def spec(shape, start=0):
        lead = len(shape) - 1
        return pl.BlockSpec(tuple(shape[:-1]) + (HEAD,), lambda h, at: (0,) * lead + (start + h,))

    return pl.pallas_call(
        kernel,
        out_shape=outs,
        grid_spec=pltpu.PrefetchScalarGridSpec(
            num_scalar_prefetch=1,
            grid=(heads,),
            in_specs=[spec(a.shape, start) for a, start in args],
            out_specs=[spec(o.shape) for o in outs],
        ),
        compiler_params=pltpu.CompilerParams(vmem_limit_bytes=VMEM),
        cost_estimate=cost(us),
        name=name,
    )(at, *(a for a, _ in args))


def project_kernel(plan, at, *refs):
    x, core = at[0], at[2]
    *arrays, send, keep = refs
    for who, out in ((1 - core, send), (core, keep)):
        for s, (near, far, weight) in enumerate(plan):
            left, right = (
                jnp.concatenate([arrays[i][r, y, who] for y in range(2) for r in range(2)], axis=0)
                for i in (near, far)
            )
            weight = arrays[weight]
            half = left.shape[1]
            top = weight[pl.ds(pl.multiple_of(x * half, half), half)]
            bottom = weight[pl.ds(pl.multiple_of((1 - x) * half, half), half)]
            c = jnp.dot(left, top, preferred_element_type=F32) + jnp.dot(right, bottom, preferred_element_type=F32)
            out[s] = c.astype(BF16).reshape(out.shape[1:])


def project(at, attended, items):
    arrays, plan = [], []

    def place_of(array):
        for i, other in enumerate(arrays):
            if other is array:
                return i
        arrays.append(array)
        return len(arrays) - 1

    for chunk, weight in items:
        plan.append(tuple(place_of(a) for a in attended[chunk] + (weight,)))
    _, _, _, tokens, _ = attended[0][0].shape
    out = jax.ShapeDtypeStruct((len(items), 2, 2, tokens, items[0][1].shape[1]), BF16)
    return whole_call(functools.partial(project_kernel, plan), at, arrays, [out, out], "project", 1 * len(items))


def whole_call(kernel, at, args, outs, name, us):
    return pl.pallas_call(
        kernel,
        out_shape=outs,
        in_specs=[pl.BlockSpec(memory_space=pltpu.SMEM)] + [pl.BlockSpec(memory_space=pltpu.VMEM)] * len(args),
        out_specs=[pl.BlockSpec(memory_space=pltpu.VMEM)] * len(outs),
        compiler_params=pltpu.CompilerParams(vmem_limit_bytes=VMEM),
        cost_estimate=cost(us),
        name=name,
    )(at, *args)


def total(a, b):
    return (a.astype(F32) + b.astype(F32)).astype(BF16)


def split_kernel(at, kept, got, stay, to_y, to_x, to_xy):
    x, y = at[0], at[3]
    for s in range(kept.shape[0]):
        for out, yy, xx in ((to_xy, 1 - y, 1 - x), (to_y, 1 - y, x), (to_x, y, 1 - x), (stay, y, x)):
            out[s] = total(kept[s, yy, xx], got[s, yy, xx])


def halve_kernel(at, kept, got, stay, to_y):
    y = at[3]
    for s in range(kept.shape[0]):
        for r in range(2):
            to_y[s, r] = total(kept[s, 1 - y, r], got[s, 1 - y, r])
            stay[s, r] = total(kept[s, y, r], got[s, y, r])


def row_kernel(at, stay, got, mine, to_x):
    x = at[0]
    for s in range(stay.shape[0]):
        to_x[s] = total(stay[s, 1 - x], got[s, 1 - x])
        mine[s] = total(stay[s, x], got[s, x])


def place_kernel(plan, at, *refs):
    x, z, out = at[0], at[1], refs[-1]
    layers = [z, z + 1 - 2 * (z % 2), (z + 2) % 4, 3 - z]
    refs = iter(refs[:-1])
    for names, hops in plan:
        group = [next(refs) for _ in range(2 * hops)]
        _, tokens, width = group[0].shape
        for s, (chunk, layer) in enumerate(names):
            rows = pl.ds(chunk * tokens, tokens)
            base = 2 * layers[layer]
            mine = pl.ds(pl.multiple_of((base + x) * width, width), width)
            theirs = pl.ds(pl.multiple_of((base + 1 - x) * width, width), width)
            if hops == 1:
                out[rows, mine], out[rows, theirs] = group[0][s], group[1][s]
            else:
                out[rows, mine] = total(group[0][s], group[1][s])
                out[rows, theirs] = total(group[2][s], group[3][s])


def after(value, *earlier):
    return lax.optimization_barrier((value, earlier))[0]


def body_eight(qkv, out_weight):
    _, _, cols, features = qkv.shape
    half = features // 2
    chunks = 2
    heads = half // HEAD
    parts = lax.axis_size("head")
    tokens = cols // chunks
    coef = HEAD ** (-0.5) * LOG2E
    me = lax.axis_index("seq")
    who = lax.axis_index("head")
    z, x, core, y = me // 2, me % 2, who % 2, who // 2
    at = jnp.stack([x, z, core, y]).astype(jnp.int32)
    local = qkv.reshape(3, cols, features)
    first = x == 0

    def seq_perm(array, *layers, cross=False):
        pairs = [(2 * a + i, 2 * b + (1 - i if cross else i)) for a, b in layers for i in range(2)]
        return lax.ppermute(array, "seq", pairs)

    def swap(array):
        return seq_perm(array, (0, 0), (1, 1), (2, 2), (3, 3), cross=True)

    def head_perm(array, flip):
        return lax.ppermute(array, "head", [(i, i ^ flip) for i in range(4)])

    def lanes(lo, hi, part, source=local):
        return lax.dynamic_slice(source, (lo, 0, part * half), (hi - lo, cols, half))

    down, two_down = [(2, 1), (3, 2)], [(3, 1)]
    q_m = lanes(0, 1, x)
    q_o = swap(lanes(0, 1, 1 - x))
    qs = [seq_perm(q_m, *down), None, seq_perm(q_m, *two_down), None]
    kv_m, kv_give = lanes(1, 3, x), lanes(1, 3, 1 - x)
    block = out_weight.reshape(kv_m.shape)
    low_m = seq_perm(jnp.where(z == 0, kv_m, block), (0, 1), (1, 3))
    pairs = [(i, 2 + 1 - i) for i in range(2)] + [(2 + i, i) for i in range(2)] + [(4 + i, 6 + i) for i in range(2)]
    low_o = lax.ppermute(jnp.where(z == 0, kv_give, block), "seq", pairs)
    kv_o = swap(after(kv_give, q_o, qs[0]))
    qs[1], qs[3] = seq_perm(q_o, *down), seq_perm(q_o, *two_down)
    w_second = seq_perm(after(out_weight, *qs), (0, 2))

    struct = jax.ShapeDtypeStruct
    partial = struct((2 * tokens + LSE_ROWS, half), BF16)
    oa, ob, own = [], [], []
    turn = at
    kvs = [kv_m, kv_o, low_m, low_o]
    for c in range(chunks):
        a, b = head_call(
            functools.partial(upper_kernel, coef, c, chunks, parts), turn, [(a, 0) for a in qs + kvs + [out_weight]],
            [partial] * 2, heads, "upper_rows", 7)
        turn = after(at, a)
        oa.append(seq_perm(a, (1, 2), (2, 3)))
        ob.append(seq_perm(b, (1, 3), (0, 1), (3, 2)))
    for c in range(chunks):
        (mine,) = head_call(
            functools.partial(own_kernel, coef, c, chunks, parts), turn, [(a, 0) for a in [q_m, q_o] + kvs],
            [partial], heads, "own_rows", 6)
        own.append(mine)
        turn = after(at, mine, w_second)

    w_down = seq_perm(after(out_weight, *qs), (2, 0), (3, 1))

    def merged(c, earlier):
        (a,) = head_call(
            merge_kernel, after(at, earlier), [(a[c], 0) for a in (own, oa, ob)],
            [struct((2, tokens, half), BF16)], heads, "merge", 2)
        shape = (2, 2, 2, tokens // 4, half)
        return a.reshape(shape), swap(a).reshape(shape)

    attended = [merged(0, own[1])]
    ridden = jnp.where(z == 2, w_second, low_m.reshape(out_weight.shape))
    w_far = jnp.where(z >= 2, ridden, after(w_down, attended[0][0], own[1]))
    w_other = seq_perm(w_far, (0, 1), (1, 0), (2, 3), (3, 2))
    parts_out, plan = [], []

    def summed(turn, names):
        send, kept = project(turn, attended, [(c, weights[layer]) for c, layer in names])
        return send.shape[:1] + send.shape[3:], [kept, head_perm(send, 1)]

    attended.append(merged(1, (w_far, attended[0][1])))
    w_near = jnp.where(
        (z == 0) | (z == 3), low_o.reshape(out_weight.shape), jnp.concatenate([o[: 2 * tokens] for o in ob]))
    weights = {0: out_weight, 1: w_near, 2: w_far, 3: w_other}
    names = [(0, 0), (0, 1)]
    size, pair = summed(after(at, attended[1][0]), names)
    both = struct(size[:1] + (2,) + size[1:], BF16)
    stay, to_y = whole_call(halve_kernel, at, pair, [both] * 2, "halve", 2)
    from_y = head_perm(to_y, 2)
    mine, to_x = whole_call(row_kernel, at, [stay, from_y], [struct(size, BF16)] * 2, "rows", 1)
    parts_out += [mine, swap(to_x)]
    plan.append((names, 1))

    names = [(1, 0), (1, 1), (1, 2), (1, 3), (0, 2), (0, 3)]
    size, pair = summed(after(at, mine), names)
    stay, to_y, to_x, to_xy = whole_call(split_kernel, at, pair, [struct(size, BF16)] * 4, "split", 2)
    diagonal = [
        ((2 * i + j) * 4 + h, (2 * i + 1 - j) * 4 + (h ^ 2)) for i in range(4) for j in range(2) for h in range(4)
    ]
    parts_out += [stay, head_perm(to_y, 2), swap(to_x), lax.ppermute(to_xy, ("seq", "head"), diagonal)]
    plan.append((names, 2))
    (out,) = whole_call(
        functools.partial(place_kernel, plan), at, parts_out,
        [struct((cols // 4, 8 * out_weight.shape[1]), BF16)], "place", 2)
    return out.reshape(cols // 4, 1, 8 * out_weight.shape[1])


def solution(mesh):
    in_specs = (P(None, "seq", None, "head"), P("head", "seq"))
    out_specs = P("head", "seq", None)
    small = mesh.shape["seq"] == 8 and mesh.shape["head"] == 4

    def body(qkv, out_weight):
        _, rows, cols, features = qkv.shape
        even = features == 2 * cols and out_weight.shape == (features, cols) and cols % 512 == 0
        if small and rows == 1 and even:
            return body_eight(qkv, out_weight)
        return body_any(qkv, out_weight)

    return jax.shard_map(body, mesh=mesh, in_specs=in_specs, out_specs=out_specs, check_vma=False)
```

```python
import functools
import jax
import jax.numpy as jnp
from jax import lax
from jax.experimental import pallas as pl
from jax.experimental.pallas import tpu as pltpu
from jax.sharding import PartitionSpec as P

HEAD = 128
LOG2E = 1.4426950408889634
NEG = -1e30
QB = 128
VMEM = 24 * 1024 * 1024
F32, BF16 = jnp.float32, jnp.bfloat16


def shifted(shard, axis, by):
    size = lax.axis_size(axis)
    pairs = [(i, i + by) for i in range(size) if 0 <= i + by < size]
    return lax.ppermute(shard, axis, pairs)


def column_part(part):
    queries, keys_part, values = (part[0], part[1], part[2])
    rows = queries.shape[0]
    scale = queries.shape[-1] ** (-0.5)
    scores = (
        jnp.einsum("rchd,schd->chrs", queries, keys_part, preferred_element_type=jnp.float32)
        * scale
    )
    r_idx = lax.broadcasted_iota(jnp.int32, (rows, rows), 0)
    s_idx = lax.broadcasted_iota(jnp.int32, (rows, rows), 1)
    allowed = s_idx <= r_idx - 2
    masked = jnp.where(allowed, scores, jnp.float32(-1e30))
    peak = jnp.max(masked, axis=-1)
    weights = jnp.where(allowed, jnp.exp(masked - peak[..., None]), jnp.float32(0.0))
    total = jnp.maximum(jnp.sum(weights, axis=-1), jnp.float32(1.0))
    rounded = weights.astype(jnp.bfloat16)
    mixed = jnp.einsum("chrs,schd->rchd", rounded, values, preferred_element_type=jnp.float32)
    col_out = (mixed / jnp.transpose(total, (2, 0, 1))[..., None]).astype(jnp.bfloat16)
    col_lse = jnp.transpose(peak + jnp.log(total), (2, 0, 1))
    return (col_out, col_lse)


def row_part(local, previous, first_row):
    rows_dev, cols, heads_local, head_size = (
        local.shape[1],
        local.shape[2],
        local.shape[3],
        local.shape[4],
    )
    scale = head_size ** (-0.5)
    keys_ext = jnp.concatenate([previous, local[1:3]], axis=1)
    key_idx = lax.broadcasted_iota(jnp.int32, (cols, 2 * cols), 1)
    query_idx = lax.broadcasted_iota(jnp.int32, (cols, 2 * cols), 0)

    def one_row(index):
        queries = lax.dynamic_index_in_dim(local[0], index, 0, keepdims=False)
        pair = keys_ext.reshape(2, 2 * cols, heads_local, head_size)
        scores = (
            jnp.einsum("qhd,khd->hqk", queries, pair[0], preferred_element_type=jnp.float32) * scale
        )
        allowed = (key_idx < cols) & (first_row + index > 0) | (key_idx >= cols) & (
            key_idx - cols <= query_idx
        )
        masked = jnp.where(allowed[None], scores, jnp.float32(-1e30))
        peak = jnp.max(masked, axis=-1)
        weights = jnp.where(allowed[None], jnp.exp(masked - peak[..., None]), jnp.float32(0.0))
        total = jnp.sum(weights, axis=-1)
        rounded = weights.astype(jnp.bfloat16)
        mixed = jnp.einsum("hqk,khd->qhd", rounded, pair[1], preferred_element_type=jnp.float32)
        return (mixed / jnp.transpose(total)[..., None], jnp.transpose(peak + jnp.log(total)))

    return lax.map(one_row, jnp.arange(rows_dev, dtype=jnp.int32))


def body_any(qkv, out_weight):
    rows_dev, cols, features = (qkv.shape[1], qkv.shape[2], qkv.shape[3])
    head_size = HEAD
    heads_local = features // head_size
    local = qkv.reshape(3, rows_dev, cols, heads_local, head_size)
    previous = shifted(local[1:3, rows_dev - 1 : rows_dev], "seq", 1)
    first_row = lax.axis_index("seq") * rows_dev
    row_out, row_lse = row_part(local, previous, first_row)
    columns = lax.all_to_all(local, "seq", split_axis=2, concat_axis=1, tiled=True)
    col_part_out, col_part_lse = column_part(columns)
    col_out, col_lse = (
        lax.all_to_all(col_part_out, "seq", split_axis=0, concat_axis=1, tiled=True),
        lax.all_to_all(
            col_part_lse.astype(jnp.bfloat16), "seq", split_axis=0, concat_axis=1, tiled=True
        ).astype(col_part_lse.dtype),
    )
    top = jnp.maximum(row_lse, col_lse)
    left = jnp.exp(row_lse - top)
    right = jnp.exp(col_lse - top)
    attended = (left[..., None] * row_out + right[..., None] * col_out.astype(jnp.float32)) / (
        left + right
    )[..., None]
    attended = attended.astype(jnp.bfloat16).reshape(rows_dev, cols, features)
    terms = jnp.einsum(
        "rcf,fd->crd",
        attended,
        lax.all_gather(out_weight, "seq", axis=1, tiled=True),
        preferred_element_type=jnp.float32,
    )
    summed = lax.psum_scatter(terms.astype(jnp.bfloat16), "head", scatter_dimension=0, tiled=True)
    return summed


def dense_scores(q, k):
    return lax.dot_general(q, k, (((1,), (1,)), ((), ())), preferred_element_type=F32)


def col_scores(q, k):
    prod = q * k
    high = prod.astype(BF16)
    low = (prod - high.astype(F32)).astype(BF16)
    ones = jnp.ones((2 * HEAD, HEAD), BF16)
    return jnp.dot(jnp.concatenate([high, low], axis=1), ones, preferred_element_type=F32)


def with_ones(v):
    return jnp.concatenate([v, jnp.ones_like(v)], axis=1)


def attend(q, dense, cols, coef):
    rows = q.shape[0]
    scores = []
    for k, _, allowed in dense:
        s = dense_scores(q, k)
        scores.append(s if allowed is None else jnp.where(allowed, s, NEG))
    singles = []
    if cols:
        wide = q.astype(F32)
    for k, _, allowed in cols:
        c = col_scores(wide, k)
        singles.append(c if allowed is None else jnp.where(allowed, c, NEG))
    peak = None
    for s in scores:
        for j in range(s.shape[1] // HEAD):
            part = s[:, j * HEAD : (j + 1) * HEAD]
            peak = part if peak is None else jnp.maximum(peak, part)
    if peak is not None:
        peak = jnp.broadcast_to(jnp.max(peak, axis=1, keepdims=True), (rows, HEAD))
    for c in singles:
        peak = c if peak is None else jnp.maximum(peak, c)
    peak = peak * coef
    both = None
    for s, (_, v, _) in zip(scores, dense):
        tiled = jnp.concatenate([peak] * (s.shape[1] // HEAD), axis=1)
        p = jnp.exp2(s * coef - tiled).astype(BF16)
        term = jnp.dot(p, v, preferred_element_type=F32)
        both = term if both is None else both + term
    out = None if both is None else both[:, :HEAD]
    total = None if both is None else both[:, HEAD:]
    for c, (_, v, _) in zip(singles, cols):
        w = jnp.exp2(c * coef - peak)
        total = w if total is None else total + w
        out = w * v if out is None else out + w * v
    return out / total, peak + jnp.log2(total)


def lse_rows(even, odd):
    lane = lax.broadcasted_iota(jnp.int32, (HEAD, HEAD), 1)
    evens, odds = [], []
    for t in range(even.shape[0] // HEAD):
        block = slice(t * HEAD, (t + 1) * HEAD)
        turned = jnp.transpose(jnp.where(lane == 0, even[block], odd[block]))
        evens.append(turned[0:1])
        odds.append(turned[1:2])
    return evens, odds


LSE_ROWS = 16


def put_lse(ref, base, evens, odds):
    rows = jnp.concatenate(evens + odds, axis=0)
    pieces = []
    for _ in range(3):
        pieces.append(rows.astype(BF16).astype(F32))
        rows = rows - pieces[-1]
    spare = LSE_ROWS - 3 * rows.shape[0]
    ref[pl.ds(base, LSE_ROWS), :] = jnp.concatenate(pieces + [jnp.zeros((spare, HEAD), F32)], axis=0).astype(BF16)


def chunk_rows(array, chunk, chunks, parts):
    size = array.shape[0] // parts
    share = size // chunks
    return jnp.concatenate(
        [array[p * size + chunk * share : p * size + (chunk + 1) * share] for p in range(parts)], axis=0)


def stacked(refs):
    return [ref[i] for ref in refs for i in range(ref.shape[0])]


def own_kernel(coef, chunk, chunks, parts, at, q_m, q_o, kv_m, kv_o, *refs):
    x, z = at[0], at[1]
    below = z == 1
    first = x == 0
    *low, out = refs
    cols = q_m.shape[1]
    tokens = cols // chunks

    def pair(a, b):
        return jnp.where(first, a, b), jnp.where(first, b, a)

    def mine(array):
        return chunk_rows(array, chunk, chunks, parts)

    q_e, q_o = pair(mine(q_m[0]), mine(q_o[0]))
    k_e, k_o = pair(kv_m[0], kv_o[0])
    v_e, v_o = pair(kv_m[1], kv_o[1])
    v_e, v_o = with_ones(v_e), with_ones(v_o)
    m_k, m_v, o_k, o_v = stacked(low)
    lk_e, lk_o = pair(m_k, o_k)
    lv_e, lv_o = pair(m_v, o_v)
    col_e = (mine(lk_e).astype(F32), mine(lv_e).astype(F32), below)
    col_o = (mine(lk_o).astype(F32), mine(lv_o).astype(F32), below)
    share = tokens // parts
    index = lax.broadcasted_iota(jnp.int32, (tokens, cols), 0)
    index = (index // share) * (cols // parts) + chunk * share + index % share
    tri = lax.broadcasted_iota(jnp.int32, (tokens, cols), 1) <= index
    o1, l1 = attend(q_e, [(k_e, v_e, tri), (lk_o, with_ones(lv_o), below)], [col_e], coef)
    o2, l2 = attend(q_o, [(k_o, v_o, tri), (k_e, v_e, None)], [col_e, col_o], coef)
    out[:tokens] = o1.astype(BF16)
    out[tokens : 2 * tokens] = o2.astype(BF16)
    put_lse(out, 2 * tokens, *lse_rows(l1, l2))


def upper_kernel(coef, chunk, chunks, parts, at, qa_m, qa_o, qb_m, qb_o, kv_m, kv_o, *refs):
    x, z = at[0], at[1]
    below = z == 1
    first = x == 0
    *low, weight, out_a, out_b = refs
    tokens = qa_m.shape[1] // chunks

    def pair(a, b):
        return jnp.where(first, a, b), jnp.where(first, b, a)

    def mine(array):
        return chunk_rows(array, chunk, chunks, parts)

    k_e, k_o = pair(kv_m[0], kv_o[0])
    v_e, v_o = pair(kv_m[1], kv_o[1])
    m_k, m_v, o_k, o_v = (mine(part).astype(F32) for part in stacked(low))
    lower = [(m_k, m_v, below), (o_k, o_v, below)]
    ce = (mine(k_e).astype(F32), mine(v_e).astype(F32), None)
    co = (mine(k_o).astype(F32), mine(v_o).astype(F32), None)
    base = chunk * 2 * tokens
    for q_m, q_o, out, dense, singles in (
        (qa_m, qa_o, out_a, [(k_o, with_ones(v_o), None)], [ce]),
        (qb_m, qb_o, out_b, [], [ce, co]),
    ):
        q_e, q_odd = pair(mine(q_m[0]), mine(q_o[0]))
        o1, l1 = attend(q_e, dense, singles + lower, coef)
        o2, l2 = attend(q_odd, [], [ce, co] + lower, coef)
        o1, o2 = o1.astype(BF16), o2.astype(BF16)
        if out is out_b:
            o1 = jnp.where(below, o1, weight[base : base + tokens])
            o2 = jnp.where(below, o2, weight[base + tokens : base + 2 * tokens])
        out[:tokens] = o1
        out[tokens : 2 * tokens] = o2
        put_lse(out, 2 * tokens, *lse_rows(l1, l2))


def lse_packed(ref, base, rows):
    packed = ref[pl.ds(base, LSE_ROWS), :].astype(F32)
    return sum(packed[i * rows : (i + 1) * rows] for i in range(3))


def merge_kernel(at, own, oa, ob, out):
    z = at[1]
    tokens = out.shape[1]
    blocks = tokens // HEAD
    rows = 2 * blocks
    l0, l1, l2 = (lse_packed(ref, 2 * tokens, rows) for ref in (own, oa, ob))
    l1, l2 = jnp.where(z >= 2, l1, NEG), jnp.where(z >= 3, l2, NEG)
    top = jnp.maximum(l0, jnp.maximum(l1, l2))
    shares = [jnp.exp2(l - top) for l in (l0, l1, l2)]
    whole = shares[0] + shares[1] + shares[2]
    shares = jnp.concatenate([share / whole for share in shares], axis=0)
    high = shares.astype(BF16).astype(F32)
    spare = jnp.zeros((32 - 6 * rows, HEAD), F32)
    pieces = jnp.concatenate([high, shares - high, spare], axis=0).astype(BF16)
    line = lax.broadcasted_iota(jnp.int32, (32, 3 * HEAD), 0)
    group = lax.broadcasted_iota(jnp.int32, (32, 3 * HEAD), 1) // HEAD
    for row in range(2):
        for block in range(blocks):
            first = row * blocks + block + group * rows
            pick = ((line == first) | (line == first + 3 * rows)).astype(BF16)
            spread = lax.dot_general(pieces, pick, (((0,), (0,)), ((), ())), preferred_element_type=F32)
            mine = slice(row * tokens + block * HEAD, row * tokens + (block + 1) * HEAD)
            mixed = spread[:, :HEAD] * own[mine].astype(F32)
            mixed = mixed + spread[:, HEAD : 2 * HEAD] * oa[mine].astype(F32)
            mixed = mixed + spread[:, 2 * HEAD :] * ob[mine].astype(F32)
            out[row, block * HEAD : (block + 1) * HEAD] = mixed.astype(BF16)


def cost(us):
    return pl.CostEstimate(flops=int(us * 1e8), bytes_accessed=1024, transcendentals=0)


def head_call(kernel, at, args, outs, heads, name, us):
    def spec(shape, start=0):
        lead = len(shape) - 1
        return pl.BlockSpec(tuple(shape[:-1]) + (HEAD,), lambda h, at: (0,) * lead + (start + h,))

    return pl.pallas_call(
        kernel,
        out_shape=outs,
        grid_spec=pltpu.PrefetchScalarGridSpec(
            num_scalar_prefetch=1,
            grid=(heads,),
            in_specs=[spec(a.shape, start) for a, start in args],
            out_specs=[spec(o.shape) for o in outs],
        ),
        compiler_params=pltpu.CompilerParams(vmem_limit_bytes=VMEM),
        cost_estimate=cost(us),
        name=name,
    )(at, *(a for a, _ in args))


def project_kernel(plan, at, *refs):
    x, core = at[0], at[2]
    *arrays, send, keep = refs
    for who, out in ((1 - core, send), (core, keep)):
        for s, (near, far, weight) in enumerate(plan):
            left, right = (
                jnp.concatenate([arrays[i][r, y, who] for y in range(2) for r in range(2)], axis=0)
                for i in (near, far)
            )
            weight = arrays[weight]
            half = left.shape[1]
            top = weight[pl.ds(pl.multiple_of(x * half, half), half)]
            bottom = weight[pl.ds(pl.multiple_of((1 - x) * half, half), half)]
            c = jnp.dot(left, top, preferred_element_type=F32) + jnp.dot(right, bottom, preferred_element_type=F32)
            out[s] = c.astype(BF16).reshape(out.shape[1:])


def project(at, attended, items):
    arrays, plan = [], []

    def place_of(array):
        for i, other in enumerate(arrays):
            if other is array:
                return i
        arrays.append(array)
        return len(arrays) - 1

    for chunk, weight in items:
        plan.append(tuple(place_of(a) for a in attended[chunk] + (weight,)))
    _, _, _, tokens, _ = attended[0][0].shape
    out = jax.ShapeDtypeStruct((len(items), 2, 2, tokens, items[0][1].shape[1]), BF16)
    return whole_call(functools.partial(project_kernel, plan), at, arrays, [out, out], "project", 1 * len(items))


def whole_call(kernel, at, args, outs, name, us):
    return pl.pallas_call(
        kernel,
        out_shape=outs,
        in_specs=[pl.BlockSpec(memory_space=pltpu.SMEM)] + [pl.BlockSpec(memory_space=pltpu.VMEM)] * len(args),
        out_specs=[pl.BlockSpec(memory_space=pltpu.VMEM)] * len(outs),
        compiler_params=pltpu.CompilerParams(vmem_limit_bytes=VMEM),
        cost_estimate=cost(us),
        name=name,
    )(at, *args)


def total(a, b):
    return (a.astype(F32) + b.astype(F32)).astype(BF16)


def split_kernel(at, kept, got, stay, to_y, to_x, to_xy):
    x, y = at[0], at[3]
    for s in range(kept.shape[0]):
        for out, yy, xx in ((to_xy, 1 - y, 1 - x), (to_y, 1 - y, x), (to_x, y, 1 - x), (stay, y, x)):
            out[s] = total(kept[s, yy, xx], got[s, yy, xx])


def halve_kernel(at, kept, got, stay, to_y):
    y = at[3]
    for s in range(kept.shape[0]):
        for r in range(2):
            to_y[s, r] = total(kept[s, 1 - y, r], got[s, 1 - y, r])
            stay[s, r] = total(kept[s, y, r], got[s, y, r])


def row_kernel(at, stay, got, mine, to_x):
    x = at[0]
    for s in range(stay.shape[0]):
        to_x[s] = total(stay[s, 1 - x], got[s, 1 - x])
        mine[s] = total(stay[s, x], got[s, x])


def place_kernel(plan, at, *refs):
    x, z, out = at[0], at[1], refs[-1]
    layers = [z, z + 1 - 2 * (z % 2), (z + 2) % 4, 3 - z]
    refs = iter(refs[:-1])
    for names, hops in plan:
        group = [next(refs) for _ in range(2 * hops)]
        _, tokens, width = group[0].shape
        for s, (chunk, layer) in enumerate(names):
            rows = pl.ds(chunk * tokens, tokens)
            base = 2 * layers[layer]
            mine = pl.ds(pl.multiple_of((base + x) * width, width), width)
            theirs = pl.ds(pl.multiple_of((base + 1 - x) * width, width), width)
            if hops == 1:
                out[rows, mine], out[rows, theirs] = group[0][s], group[1][s]
            else:
                out[rows, mine] = total(group[0][s], group[1][s])
                out[rows, theirs] = total(group[2][s], group[3][s])


def after(value, *earlier):
    return lax.optimization_barrier((value, earlier))[0]


def body_eight(qkv, out_weight):
    _, _, cols, features = qkv.shape
    half = features // 2
    chunks = 2
    heads = half // HEAD
    parts = lax.axis_size("head")
    tokens = cols // chunks
    coef = HEAD ** (-0.5) * LOG2E
    me = lax.axis_index("seq")
    who = lax.axis_index("head")
    z, x, core, y = me // 2, me % 2, who % 2, who // 2
    at = jnp.stack([x, z, core, y]).astype(jnp.int32)
    local = qkv.reshape(3, cols, features)
    first = x == 0

    def seq_perm(array, *layers, cross=False):
        pairs = [(2 * a + i, 2 * b + (1 - i if cross else i)) for a, b in layers for i in range(2)]
        return lax.ppermute(array, "seq", pairs)

    def swap(array):
        return seq_perm(array, (0, 0), (1, 1), (2, 2), (3, 3), cross=True)

    def head_perm(array, flip):
        return lax.ppermute(array, "head", [(i, i ^ flip) for i in range(4)])

    def lanes(lo, hi, part, source=local):
        return lax.dynamic_slice(source, (lo, 0, part * half), (hi - lo, cols, half))

    down, two_down = [(2, 1), (3, 2)], [(3, 1)]
    q_m = lanes(0, 1, x)
    q_o = swap(lanes(0, 1, 1 - x))
    qs = [seq_perm(q_m, *down), None, seq_perm(q_m, *two_down), None]
    kv_m, kv_give = lanes(1, 3, x), lanes(1, 3, 1 - x)
    block = out_weight.reshape(kv_m.shape)
    low_m = seq_perm(jnp.where(z == 0, kv_m, block), (0, 1), (1, 3))
    pairs = [(i, 2 + 1 - i) for i in range(2)] + [(2 + i, i) for i in range(2)] + [(4 + i, 6 + i) for i in range(2)]
    low_o = lax.ppermute(jnp.where(z == 0, kv_give, block), "seq", pairs)
    kv_o = swap(after(kv_give, q_o, qs[0]))
    qs[1], qs[3] = seq_perm(q_o, *down), seq_perm(q_o, *two_down)
    w_second = seq_perm(after(out_weight, *qs), (0, 2))

    struct = jax.ShapeDtypeStruct
    partial = struct((2 * tokens + LSE_ROWS, half), BF16)
    oa, ob, own = [], [], []
    turn = at
    kvs = [kv_m, kv_o, low_m, low_o]
    for c in range(chunks):
        a, b = head_call(
            functools.partial(upper_kernel, coef, c, chunks, parts), turn, [(a, 0) for a in qs + kvs + [out_weight]],
            [partial] * 2, heads, "upper_rows", 7)
        turn = after(at, a)
        oa.append(seq_perm(a, (1, 2), (2, 3)))
        ob.append(seq_perm(b, (1, 3), (0, 1), (3, 2)))
    def own_rows(c, turn):
        (mine,) = head_call(
            functools.partial(own_kernel, coef, c, chunks, parts), turn, [(a, 0) for a in [q_m, q_o] + kvs],
            [partial], heads, "own_rows", 6)
        return mine

    own.append(own_rows(0, turn))
    w_down = seq_perm(after(out_weight, *qs), (2, 0), (3, 1))

    def merged(c, earlier):
        (a,) = head_call(
            merge_kernel, after(at, earlier), [(a[c], 0) for a in (own, oa, ob)],
            [struct((2, tokens, half), BF16)], heads, "merge", 2)
        shape = (2, 2, 2, tokens // 4, half)
        return a.reshape(shape), swap(a).reshape(shape)

    attended = [merged(0, own[0])]
    own.append(own_rows(1, after(at, attended[0][0], w_second)))
    ridden = jnp.where(z == 2, w_second, low_m.reshape(out_weight.shape))
    w_far = jnp.where(z >= 2, ridden, after(w_down, own[1]))
    w_other = seq_perm(w_far, (0, 1), (1, 0), (2, 3), (3, 2))
    parts_out, plan = [], []

    def summed(turn, names):
        send, kept = project(turn, attended, [(c, weights[layer]) for c, layer in names])
        return send.shape[:1] + send.shape[3:], [kept, head_perm(send, 1)]

    attended.append(merged(1, (w_far, attended[0][1])))
    w_near = jnp.where(
        (z == 0) | (z == 3), low_o.reshape(out_weight.shape), jnp.concatenate([o[: 2 * tokens] for o in ob]))
    weights = {0: out_weight, 1: w_near, 2: w_far, 3: w_other}
    names = [(0, 0), (0, 1)]
    size, pair = summed(after(at, attended[1][0]), names)
    both = struct(size[:1] + (2,) + size[1:], BF16)
    stay, to_y = whole_call(halve_kernel, at, pair, [both] * 2, "halve", 2)
    from_y = head_perm(to_y, 2)
    mine, to_x = whole_call(row_kernel, at, [stay, from_y], [struct(size, BF16)] * 2, "rows", 1)
    parts_out += [mine, swap(to_x)]
    plan.append((names, 1))

    names = [(1, 0), (1, 1), (1, 2), (1, 3), (0, 2), (0, 3)]
    size, pair = summed(after(at, mine), names)
    stay, to_y, to_x, to_xy = whole_call(split_kernel, at, pair, [struct(size, BF16)] * 4, "split", 2)
    diagonal = [
        ((2 * i + j) * 4 + h, (2 * i + 1 - j) * 4 + (h ^ 2)) for i in range(4) for j in range(2) for h in range(4)
    ]
    parts_out += [stay, head_perm(to_y, 2), swap(to_x), lax.ppermute(to_xy, ("seq", "head"), diagonal)]
    plan.append((names, 2))
    (out,) = whole_call(
        functools.partial(place_kernel, plan), at, parts_out,
        [struct((cols // 4, 8 * out_weight.shape[1]), BF16)], "place", 2)
    return out.reshape(cols // 4, 1, 8 * out_weight.shape[1])


def solution(mesh):
    in_specs = (P(None, "seq", None, "head"), P("head", "seq"))
    out_specs = P("head", "seq", None)
    small = mesh.shape["seq"] == 8 and mesh.shape["head"] == 4

    def body(qkv, out_weight):
        _, rows, cols, features = qkv.shape
        even = features == 2 * cols and out_weight.shape == (features, cols) and cols % 512 == 0
        if small and rows == 1 and even:
            return body_eight(qkv, out_weight)
        return body_any(qkv, out_weight)

    return jax.shard_map(body, mesh=mesh, in_specs=in_specs, out_specs=out_specs, check_vma=False)
```

```python
import functools
import jax
import jax.numpy as jnp
from jax import lax
from jax.experimental import pallas as pl
from jax.experimental.pallas import tpu as pltpu
from jax.sharding import PartitionSpec as P

HEAD = 128
LOG2E = 1.4426950408889634
NEG = -1e30
QB = 128
VMEM = 14 * 1024 * 1024
F32, BF16 = jnp.float32, jnp.bfloat16


def shifted(shard, axis, by):
    size = lax.axis_size(axis)
    pairs = [(i, i + by) for i in range(size) if 0 <= i + by < size]
    return lax.ppermute(shard, axis, pairs)


def column_part(part):
    queries, keys_part, values = (part[0], part[1], part[2])
    rows = queries.shape[0]
    scale = queries.shape[-1] ** (-0.5)
    scores = (
        jnp.einsum("rchd,schd->chrs", queries, keys_part, preferred_element_type=jnp.float32)
        * scale
    )
    r_idx = lax.broadcasted_iota(jnp.int32, (rows, rows), 0)
    s_idx = lax.broadcasted_iota(jnp.int32, (rows, rows), 1)
    allowed = s_idx <= r_idx - 2
    masked = jnp.where(allowed, scores, jnp.float32(-1e30))
    peak = jnp.max(masked, axis=-1)
    weights = jnp.where(allowed, jnp.exp(masked - peak[..., None]), jnp.float32(0.0))
    total = jnp.maximum(jnp.sum(weights, axis=-1), jnp.float32(1.0))
    rounded = weights.astype(jnp.bfloat16)
    mixed = jnp.einsum("chrs,schd->rchd", rounded, values, preferred_element_type=jnp.float32)
    col_out = (mixed / jnp.transpose(total, (2, 0, 1))[..., None]).astype(jnp.bfloat16)
    col_lse = jnp.transpose(peak + jnp.log(total), (2, 0, 1))
    return (col_out, col_lse)


def row_part(local, previous, first_row):
    rows_dev, cols, heads_local, head_size = (
        local.shape[1],
        local.shape[2],
        local.shape[3],
        local.shape[4],
    )
    scale = head_size ** (-0.5)
    keys_ext = jnp.concatenate([previous, local[1:3]], axis=1)
    key_idx = lax.broadcasted_iota(jnp.int32, (cols, 2 * cols), 1)
    query_idx = lax.broadcasted_iota(jnp.int32, (cols, 2 * cols), 0)

    def one_row(index):
        queries = lax.dynamic_index_in_dim(local[0], index, 0, keepdims=False)
        pair = keys_ext.reshape(2, 2 * cols, heads_local, head_size)
        scores = (
            jnp.einsum("qhd,khd->hqk", queries, pair[0], preferred_element_type=jnp.float32) * scale
        )
        allowed = (key_idx < cols) & (first_row + index > 0) | (key_idx >= cols) & (
            key_idx - cols <= query_idx
        )
        masked = jnp.where(allowed[None], scores, jnp.float32(-1e30))
        peak = jnp.max(masked, axis=-1)
        weights = jnp.where(allowed[None], jnp.exp(masked - peak[..., None]), jnp.float32(0.0))
        total = jnp.sum(weights, axis=-1)
        rounded = weights.astype(jnp.bfloat16)
        mixed = jnp.einsum("hqk,khd->qhd", rounded, pair[1], preferred_element_type=jnp.float32)
        return (mixed / jnp.transpose(total)[..., None], jnp.transpose(peak + jnp.log(total)))

    return lax.map(one_row, jnp.arange(rows_dev, dtype=jnp.int32))


def body_any(qkv, out_weight):
    rows_dev, cols, features = (qkv.shape[1], qkv.shape[2], qkv.shape[3])
    head_size = HEAD
    heads_local = features // head_size
    local = qkv.reshape(3, rows_dev, cols, heads_local, head_size)
    previous = shifted(local[1:3, rows_dev - 1 : rows_dev], "seq", 1)
    first_row = lax.axis_index("seq") * rows_dev
    row_out, row_lse = row_part(local, previous, first_row)
    columns = lax.all_to_all(local, "seq", split_axis=2, concat_axis=1, tiled=True)
    col_part_out, col_part_lse = column_part(columns)
    col_out, col_lse = (
        lax.all_to_all(col_part_out, "seq", split_axis=0, concat_axis=1, tiled=True),
        lax.all_to_all(
            col_part_lse.astype(jnp.bfloat16), "seq", split_axis=0, concat_axis=1, tiled=True
        ).astype(col_part_lse.dtype),
    )
    top = jnp.maximum(row_lse, col_lse)
    left = jnp.exp(row_lse - top)
    right = jnp.exp(col_lse - top)
    attended = (left[..., None] * row_out + right[..., None] * col_out.astype(jnp.float32)) / (
        left + right
    )[..., None]
    attended = attended.astype(jnp.bfloat16).reshape(rows_dev, cols, features)
    terms = jnp.einsum(
        "rcf,fd->crd",
        attended,
        lax.all_gather(out_weight, "seq", axis=1, tiled=True),
        preferred_element_type=jnp.float32,
    )
    summed = lax.psum_scatter(terms.astype(jnp.bfloat16), "head", scatter_dimension=0, tiled=True)
    return summed


def dense_scores(q, k):
    return lax.dot_general(q, k, (((1,), (1,)), ((), ())), preferred_element_type=F32)


def col_scores(q, k):
    prod = q * k
    high = prod.astype(BF16)
    low = (prod - high.astype(F32)).astype(BF16)
    ones = jnp.ones((2 * HEAD, HEAD), BF16)
    return jnp.dot(jnp.concatenate([high, low], axis=1), ones, preferred_element_type=F32)


def with_ones(v):
    return jnp.concatenate([v, jnp.ones_like(v)], axis=1)


def attend(q, dense, cols, coef):
    rows = q.shape[0]
    scores = []
    for k, _, allowed in dense:
        s = dense_scores(q, k)
        scores.append(s if allowed is None else jnp.where(allowed, s, NEG))
    singles = []
    if cols:
        wide = q.astype(F32)
    for k, _, allowed in cols:
        c = col_scores(wide, k)
        singles.append(c if allowed is None else jnp.where(allowed, c, NEG))
    peak = None
    for s in scores:
        for j in range(s.shape[1] // HEAD):
            part = s[:, j * HEAD : (j + 1) * HEAD]
            peak = part if peak is None else jnp.maximum(peak, part)
    if peak is not None:
        peak = jnp.broadcast_to(jnp.max(peak, axis=1, keepdims=True), (rows, HEAD))
    for c in singles:
        peak = c if peak is None else jnp.maximum(peak, c)
    peak = peak * coef
    both = None
    for s, (_, v, _) in zip(scores, dense):
        tiled = jnp.concatenate([peak] * (s.shape[1] // HEAD), axis=1)
        p = jnp.exp2(s * coef - tiled).astype(BF16)
        term = jnp.dot(p, v, preferred_element_type=F32)
        both = term if both is None else both + term
    out = None if both is None else both[:, :HEAD]
    total = None if both is None else both[:, HEAD:]
    for c, (_, v, _) in zip(singles, cols):
        w = jnp.exp2(c * coef - peak)
        total = w if total is None else total + w
        out = w * v if out is None else out + w * v
    return out / total, peak + jnp.log2(total)


def lse_rows(even, odd):
    lane = lax.broadcasted_iota(jnp.int32, (HEAD, HEAD), 1)
    evens, odds = [], []
    for t in range(even.shape[0] // HEAD):
        block = slice(t * HEAD, (t + 1) * HEAD)
        turned = jnp.transpose(jnp.where(lane == 0, even[block], odd[block]))
        evens.append(turned[0:1])
        odds.append(turned[1:2])
    return evens, odds


LSE_ROWS = 16


def put_lse(ref, base, evens, odds):
    rows = jnp.concatenate(evens + odds, axis=0)
    pieces = []
    for _ in range(3):
        pieces.append(rows.astype(BF16).astype(F32))
        rows = rows - pieces[-1]
    spare = LSE_ROWS - 3 * rows.shape[0]
    ref[pl.ds(base, LSE_ROWS), :] = jnp.concatenate(pieces + [jnp.zeros((spare, HEAD), F32)], axis=0).astype(BF16)


def chunk_rows(array, chunk, chunks, parts):
    size = array.shape[0] // parts
    share = size // chunks
    return jnp.concatenate(
        [array[p * size + chunk * share : p * size + (chunk + 1) * share] for p in range(parts)], axis=0)


def stacked(refs):
    return [ref[i] for ref in refs for i in range(ref.shape[0])]


def own_kernel(coef, chunk, chunks, parts, at, q_m, q_o, kv_m, kv_o, *refs):
    x, z = at[0], at[1]
    below = z == 1
    first = x == 0
    *low, out = refs
    cols = q_m.shape[1]
    tokens = cols // chunks

    def pair(a, b):
        return jnp.where(first, a, b), jnp.where(first, b, a)

    def mine(array):
        return chunk_rows(array, chunk, chunks, parts)

    q_e, q_o = pair(mine(q_m[0]), mine(q_o[0]))
    k_e, k_o = pair(kv_m[0], kv_o[0])
    v_e, v_o = pair(kv_m[1], kv_o[1])
    v_e, v_o = with_ones(v_e), with_ones(v_o)
    m_k, m_v, o_k, o_v = stacked(low)
    lk_e, lk_o = pair(m_k, o_k)
    lv_e, lv_o = pair(m_v, o_v)
    col_e = (mine(lk_e).astype(F32), mine(lv_e).astype(F32), below)
    col_o = (mine(lk_o).astype(F32), mine(lv_o).astype(F32), below)
    share = tokens // parts
    index = lax.broadcasted_iota(jnp.int32, (tokens, cols), 0)
    index = (index // share) * (cols // parts) + chunk * share + index % share
    tri = lax.broadcasted_iota(jnp.int32, (tokens, cols), 1) <= index
    o1, l1 = attend(q_e, [(k_e, v_e, tri), (lk_o, with_ones(lv_o), below)], [col_e], coef)
    o2, l2 = attend(q_o, [(k_o, v_o, tri), (k_e, v_e, None)], [col_e, col_o], coef)
    out[:tokens] = o1.astype(BF16)
    out[tokens : 2 * tokens] = o2.astype(BF16)
    put_lse(out, 2 * tokens, *lse_rows(l1, l2))


def upper_kernel(coef, chunk, chunks, parts, at, qa_m, qa_o, qb_m, qb_o, kv_m, kv_o, *refs):
    x, z = at[0], at[1]
    below = z == 1
    first = x == 0
    *low, weight, out_a, out_b = refs
    tokens = qa_m.shape[1] // chunks

    def pair(a, b):
        return jnp.where(first, a, b), jnp.where(first, b, a)

    def mine(array):
        return chunk_rows(array, chunk, chunks, parts)

    k_e, k_o = pair(kv_m[0], kv_o[0])
    v_e, v_o = pair(kv_m[1], kv_o[1])
    m_k, m_v, o_k, o_v = (mine(part).astype(F32) for part in stacked(low))
    lower = [(m_k, m_v, below), (o_k, o_v, below)]
    ce = (mine(k_e).astype(F32), mine(v_e).astype(F32), None)
    co = (mine(k_o).astype(F32), mine(v_o).astype(F32), None)
    base = chunk * 2 * tokens
    for q_m, q_o, out, dense, singles in (
        (qa_m, qa_o, out_a, [(k_o, with_ones(v_o), None)], [ce]),
        (qb_m, qb_o, out_b, [], [ce, co]),
    ):
        q_e, q_odd = pair(mine(q_m[0]), mine(q_o[0]))
        o1, l1 = attend(q_e, dense, singles + lower, coef)
        o2, l2 = attend(q_odd, [], [ce, co] + lower, coef)
        o1, o2 = o1.astype(BF16), o2.astype(BF16)
        if out is out_b:
            o1 = jnp.where(below, o1, weight[base : base + tokens])
            o2 = jnp.where(below, o2, weight[base + tokens : base + 2 * tokens])
        out[:tokens] = o1
        out[tokens : 2 * tokens] = o2
        put_lse(out, 2 * tokens, *lse_rows(l1, l2))


def lse_packed(ref, base, rows):
    packed = ref[pl.ds(base, LSE_ROWS), :].astype(F32)
    return sum(packed[i * rows : (i + 1) * rows] for i in range(3))


def merge_kernel(at, own, oa, ob, out):
    z = at[1]
    tokens = out.shape[1]
    blocks = tokens // HEAD
    rows = 2 * blocks
    l0, l1, l2 = (lse_packed(ref, 2 * tokens, rows) for ref in (own, oa, ob))
    l1, l2 = jnp.where(z >= 2, l1, NEG), jnp.where(z >= 3, l2, NEG)
    top = jnp.maximum(l0, jnp.maximum(l1, l2))
    shares = [jnp.exp2(l - top) for l in (l0, l1, l2)]
    whole = shares[0] + shares[1] + shares[2]
    shares = jnp.concatenate([share / whole for share in shares], axis=0)
    high = shares.astype(BF16).astype(F32)
    spare = jnp.zeros((32 - 6 * rows, HEAD), F32)
    pieces = jnp.concatenate([high, shares - high, spare], axis=0).astype(BF16)
    line = lax.broadcasted_iota(jnp.int32, (32, 3 * HEAD), 0)
    group = lax.broadcasted_iota(jnp.int32, (32, 3 * HEAD), 1) // HEAD
    for row in range(2):
        for block in range(blocks):
            first = row * blocks + block + group * rows
            pick = ((line == first) | (line == first + 3 * rows)).astype(BF16)
            spread = lax.dot_general(pieces, pick, (((0,), (0,)), ((), ())), preferred_element_type=F32)
            mine = slice(row * tokens + block * HEAD, row * tokens + (block + 1) * HEAD)
            mixed = spread[:, :HEAD] * own[mine].astype(F32)
            mixed = mixed + spread[:, HEAD : 2 * HEAD] * oa[mine].astype(F32)
            mixed = mixed + spread[:, 2 * HEAD :] * ob[mine].astype(F32)
            out[row, block * HEAD : (block + 1) * HEAD] = mixed.astype(BF16)


def cost(us):
    return pl.CostEstimate(flops=int(us * 1e8), bytes_accessed=1024, transcendentals=0)


def head_call(kernel, at, args, outs, heads, name, us):
    def spec(shape, start=0):
        lead = len(shape) - 1
        return pl.BlockSpec(tuple(shape[:-1]) + (HEAD,), lambda h, at: (0,) * lead + (start + h,))

    return pl.pallas_call(
        kernel,
        out_shape=outs,
        grid_spec=pltpu.PrefetchScalarGridSpec(
            num_scalar_prefetch=1,
            grid=(heads,),
            in_specs=[spec(a.shape, start) for a, start in args],
            out_specs=[spec(o.shape) for o in outs],
        ),
        compiler_params=pltpu.CompilerParams(vmem_limit_bytes=VMEM),
        cost_estimate=cost(us),
        name=name,
    )(at, *(a for a, _ in args))


def project_kernel(plan, at, *refs):
    x, core = at[0], at[2]
    *arrays, send, keep = refs
    for who, out in ((1 - core, send), (core, keep)):
        for s, (near, far, weight) in enumerate(plan):
            left, right = (
                jnp.concatenate([arrays[i][r, y, who] for y in range(2) for r in range(2)], axis=0)
                for i in (near, far)
            )
            weight = arrays[weight]
            half = left.shape[1]
            top = weight[pl.ds(pl.multiple_of(x * half, half), half)]
            bottom = weight[pl.ds(pl.multiple_of((1 - x) * half, half), half)]
            c = jnp.dot(left, top, preferred_element_type=F32) + jnp.dot(right, bottom, preferred_element_type=F32)
            out[s] = c.astype(BF16).reshape(out.shape[1:])


def project(at, attended, items):
    arrays, plan = [], []

    def place_of(array):
        for i, other in enumerate(arrays):
            if other is array:
                return i
        arrays.append(array)
        return len(arrays) - 1

    for chunk, weight in items:
        plan.append(tuple(place_of(a) for a in attended[chunk] + (weight,)))
    _, _, _, tokens, _ = attended[0][0].shape
    out = jax.ShapeDtypeStruct((len(items), 2, 2, tokens, items[0][1].shape[1]), BF16)
    return whole_call(functools.partial(project_kernel, plan), at, arrays, [out, out], "project", 1 * len(items))


def whole_call(kernel, at, args, outs, name, us):
    return pl.pallas_call(
        kernel,
        out_shape=outs,
        in_specs=[pl.BlockSpec(memory_space=pltpu.SMEM)] + [pl.BlockSpec(memory_space=pltpu.VMEM)] * len(args),
        out_specs=[pl.BlockSpec(memory_space=pltpu.VMEM)] * len(outs),
        compiler_params=pltpu.CompilerParams(vmem_limit_bytes=VMEM),
        cost_estimate=cost(us),
        name=name,
    )(at, *args)


def total(a, b):
    return (a.astype(F32) + b.astype(F32)).astype(BF16)


def split_kernel(at, kept, got, stay, to_y, to_x, to_xy):
    x, y = at[0], at[3]
    for s in range(kept.shape[0]):
        for out, yy, xx in ((to_xy, 1 - y, 1 - x), (to_y, 1 - y, x), (to_x, y, 1 - x), (stay, y, x)):
            out[s] = total(kept[s, yy, xx], got[s, yy, xx])


def halve_kernel(at, kept, got, stay, to_y):
    y = at[3]
    for s in range(kept.shape[0]):
        for r in range(2):
            to_y[s, r] = total(kept[s, 1 - y, r], got[s, 1 - y, r])
            stay[s, r] = total(kept[s, y, r], got[s, y, r])


def row_kernel(at, stay, got, mine, to_x):
    x = at[0]
    for s in range(stay.shape[0]):
        to_x[s] = total(stay[s, 1 - x], got[s, 1 - x])
        mine[s] = total(stay[s, x], got[s, x])


def place_kernel(plan, at, *refs):
    x, z, out = at[0], at[1], refs[-1]
    layers = [z, z + 1 - 2 * (z % 2), (z + 2) % 4, 3 - z]
    refs = iter(refs[:-1])
    for names, hops in plan:
        group = [next(refs) for _ in range(2 * hops)]
        _, tokens, width = group[0].shape
        for s, (chunk, layer) in enumerate(names):
            rows = pl.ds(chunk * tokens, tokens)
            base = 2 * layers[layer]
            mine = pl.ds(pl.multiple_of((base + x) * width, width), width)
            theirs = pl.ds(pl.multiple_of((base + 1 - x) * width, width), width)
            if hops == 1:
                out[rows, mine], out[rows, theirs] = group[0][s], group[1][s]
            else:
                out[rows, mine] = total(group[0][s], group[1][s])
                out[rows, theirs] = total(group[2][s], group[3][s])


def after(value, *earlier):
    return lax.optimization_barrier((value, earlier))[0]


def body_eight(qkv, out_weight):
    _, _, cols, features = qkv.shape
    half = features // 2
    chunks = 2
    heads = half // HEAD
    parts = lax.axis_size("head")
    tokens = cols // chunks
    coef = HEAD ** (-0.5) * LOG2E
    me = lax.axis_index("seq")
    who = lax.axis_index("head")
    z, x, core, y = me // 2, me % 2, who % 2, who // 2
    at = jnp.stack([x, z, core, y]).astype(jnp.int32)
    local = qkv.reshape(3, cols, features)
    first = x == 0

    def seq_perm(array, *layers, cross=False):
        pairs = [(2 * a + i, 2 * b + (1 - i if cross else i)) for a, b in layers for i in range(2)]
        return lax.ppermute(array, "seq", pairs)

    def swap(array):
        return seq_perm(array, (0, 0), (1, 1), (2, 2), (3, 3), cross=True)

    def head_perm(array, flip):
        return lax.ppermute(array, "head", [(i, i ^ flip) for i in range(4)])

    def lanes(lo, hi, part, source=local):
        return lax.dynamic_slice(source, (lo, 0, part * half), (hi - lo, cols, half))

    down, two_down = [(2, 1), (3, 2)], [(3, 1)]
    q_m = lanes(0, 1, x)
    q_o = swap(lanes(0, 1, 1 - x))
    qs = [seq_perm(q_m, *down), None, seq_perm(q_m, *two_down), None]
    kv_m, kv_give = lanes(1, 3, x), lanes(1, 3, 1 - x)
    block = out_weight.reshape(kv_m.shape)
    low_m = seq_perm(jnp.where(z == 0, kv_m, block), (0, 1), (1, 3))
    pairs = [(i, 2 + 1 - i) for i in range(2)] + [(2 + i, i) for i in range(2)] + [(4 + i, 6 + i) for i in range(2)]
    low_o = lax.ppermute(jnp.where(z == 0, kv_give, block), "seq", pairs)
    kv_o = swap(after(kv_give, q_o, qs[0]))
    qs[1], qs[3] = seq_perm(q_o, *down), seq_perm(q_o, *two_down)
    w_second = seq_perm(after(out_weight, *qs), (0, 2))

    struct = jax.ShapeDtypeStruct
    partial = struct((2 * tokens + LSE_ROWS, half), BF16)
    oa, ob, own = [], [], []
    turn = at
    kvs = [kv_m, kv_o, low_m, low_o]
    for c in range(chunks):
        a, b = head_call(
            functools.partial(upper_kernel, coef, c, chunks, parts), turn, [(a, 0) for a in qs + kvs + [out_weight]],
            [partial] * 2, heads, "upper_rows", 7)
        turn = after(at, a, w_second)
        oa.append(seq_perm(a, (1, 2), (2, 3)))
        ob.append(seq_perm(b, (1, 3), (0, 1), (3, 2)))
    def own_rows(c, turn):
        (mine,) = head_call(
            functools.partial(own_kernel, coef, c, chunks, parts), turn, [(a, 0) for a in [q_m, q_o] + kvs],
            [partial], heads, "own_rows", 6)
        return mine

    own.append(own_rows(0, turn))
    w_down = seq_perm(after(out_weight, *qs), (2, 0), (3, 1))

    def merged(c, earlier):
        (a,) = head_call(
            merge_kernel, after(at, earlier), [(a[c], 0) for a in (own, oa, ob)],
            [struct((2, tokens, half), BF16)], heads, "merge", 2)
        shape = (2, 2, 2, tokens // 4, half)
        return a.reshape(shape), swap(a).reshape(shape)

    attended = [merged(0, own[0])]
    own.append(own_rows(1, after(at, attended[0][0], w_second)))
    ridden = jnp.where(z == 2, w_second, low_m.reshape(out_weight.shape))
    w_far = jnp.where(z >= 2, ridden, after(w_down, attended[0][0]))
    w_other = seq_perm(w_far, (0, 1), (1, 0), (2, 3), (3, 2))
    parts_out, plan = [], []

    def summed(turn, names):
        send, kept = project(turn, attended, [(c, weights[layer]) for c, layer in names])
        return send.shape[:1] + send.shape[3:], [kept, head_perm(send, 1)]

    w_near = jnp.where(
        (z == 0) | (z == 3), low_o.reshape(out_weight.shape), jnp.concatenate([o[: 2 * tokens] for o in after(ob, own[1])]))
    attended.append(merged(1, (w_far, attended[0][1], w_near)))
    weights = {0: out_weight, 1: w_near, 2: w_far, 3: w_other}
    names = [(0, 0), (0, 1)]
    size, pair = summed(at, names)
    both = struct(size[:1] + (2,) + size[1:], BF16)
    stay, to_y = whole_call(halve_kernel, at, pair, [both] * 2, "halve", 2)
    from_y = head_perm(to_y, 2)
    mine, to_x = whole_call(row_kernel, at, [stay, from_y], [struct(size, BF16)] * 2, "rows", 1)
    parts_out += [mine, swap(to_x)]
    plan.append((names, 1))

    names = [(1, 0), (1, 1), (1, 2), (1, 3), (0, 2), (0, 3)]
    size, pair = summed(after(at, mine), names)
    stay, to_y, to_x, to_xy = whole_call(split_kernel, at, pair, [struct(size, BF16)] * 4, "split", 2)
    diagonal = [
        ((2 * i + j) * 4 + h, (2 * i + 1 - j) * 4 + (h ^ 2)) for i in range(4) for j in range(2) for h in range(4)
    ]
    parts_out += [stay, head_perm(to_y, 2), swap(to_x), lax.ppermute(to_xy, ("seq", "head"), diagonal)]
    plan.append((names, 2))
    (out,) = whole_call(
        functools.partial(place_kernel, plan), at, parts_out,
        [struct((cols // 4, 8 * out_weight.shape[1]), BF16)], "place", 2)
    return out.reshape(cols // 4, 1, 8 * out_weight.shape[1])


def solution(mesh):
    in_specs = (P(None, "seq", None, "head"), P("head", "seq"))
    out_specs = P("head", "seq", None)
    small = mesh.shape["seq"] == 8 and mesh.shape["head"] == 4

    def body(qkv, out_weight):
        _, rows, cols, features = qkv.shape
        even = features == 2 * cols and out_weight.shape == (features, cols) and cols % 512 == 0
        if small and rows == 1 and even:
            return body_eight(qkv, out_weight)
        return body_any(qkv, out_weight)

    return jax.shard_map(body, mesh=mesh, in_specs=in_specs, out_specs=out_specs, check_vma=False)
```

```python
import functools
import jax
import jax.numpy as jnp
from jax import lax
from jax.experimental import pallas as pl
from jax.experimental.pallas import tpu as pltpu
from jax.sharding import PartitionSpec as P

HEAD = 128
LOG2E = 1.4426950408889634
NEG = -1e30
QB = 128
VMEM = 24 * 1024 * 1024
F32, BF16 = jnp.float32, jnp.bfloat16


def shifted(shard, axis, by):
    size = lax.axis_size(axis)
    pairs = [(i, i + by) for i in range(size) if 0 <= i + by < size]
    return lax.ppermute(shard, axis, pairs)


def column_part(part):
    queries, keys_part, values = (part[0], part[1], part[2])
    rows = queries.shape[0]
    scale = queries.shape[-1] ** (-0.5)
    scores = (
        jnp.einsum("rchd,schd->chrs", queries, keys_part, preferred_element_type=jnp.float32)
        * scale
    )
    r_idx = lax.broadcasted_iota(jnp.int32, (rows, rows), 0)
    s_idx = lax.broadcasted_iota(jnp.int32, (rows, rows), 1)
    allowed = s_idx <= r_idx - 2
    masked = jnp.where(allowed, scores, jnp.float32(-1e30))
    peak = jnp.max(masked, axis=-1)
    weights = jnp.where(allowed, jnp.exp(masked - peak[..., None]), jnp.float32(0.0))
    total = jnp.maximum(jnp.sum(weights, axis=-1), jnp.float32(1.0))
    rounded = weights.astype(jnp.bfloat16)
    mixed = jnp.einsum("chrs,schd->rchd", rounded, values, preferred_element_type=jnp.float32)
    col_out = (mixed / jnp.transpose(total, (2, 0, 1))[..., None]).astype(jnp.bfloat16)
    col_lse = jnp.transpose(peak + jnp.log(total), (2, 0, 1))
    return (col_out, col_lse)


def row_part(local, previous, first_row):
    rows_dev, cols, heads_local, head_size = (
        local.shape[1],
        local.shape[2],
        local.shape[3],
        local.shape[4],
    )
    scale = head_size ** (-0.5)
    keys_ext = jnp.concatenate([previous, local[1:3]], axis=1)
    key_idx = lax.broadcasted_iota(jnp.int32, (cols, 2 * cols), 1)
    query_idx = lax.broadcasted_iota(jnp.int32, (cols, 2 * cols), 0)

    def one_row(index):
        queries = lax.dynamic_index_in_dim(local[0], index, 0, keepdims=False)
        pair = keys_ext.reshape(2, 2 * cols, heads_local, head_size)
        scores = (
            jnp.einsum("qhd,khd->hqk", queries, pair[0], preferred_element_type=jnp.float32) * scale
        )
        allowed = (key_idx < cols) & (first_row + index > 0) | (key_idx >= cols) & (
            key_idx - cols <= query_idx
        )
        masked = jnp.where(allowed[None], scores, jnp.float32(-1e30))
        peak = jnp.max(masked, axis=-1)
        weights = jnp.where(allowed[None], jnp.exp(masked - peak[..., None]), jnp.float32(0.0))
        total = jnp.sum(weights, axis=-1)
        rounded = weights.astype(jnp.bfloat16)
        mixed = jnp.einsum("hqk,khd->qhd", rounded, pair[1], preferred_element_type=jnp.float32)
        return (mixed / jnp.transpose(total)[..., None], jnp.transpose(peak + jnp.log(total)))

    return lax.map(one_row, jnp.arange(rows_dev, dtype=jnp.int32))


def body_any(qkv, out_weight):
    rows_dev, cols, features = (qkv.shape[1], qkv.shape[2], qkv.shape[3])
    head_size = HEAD
    heads_local = features // head_size
    local = qkv.reshape(3, rows_dev, cols, heads_local, head_size)
    previous = shifted(local[1:3, rows_dev - 1 : rows_dev], "seq", 1)
    first_row = lax.axis_index("seq") * rows_dev
    row_out, row_lse = row_part(local, previous, first_row)
    columns = lax.all_to_all(local, "seq", split_axis=2, concat_axis=1, tiled=True)
    col_part_out, col_part_lse = column_part(columns)
    col_out, col_lse = (
        lax.all_to_all(col_part_out, "seq", split_axis=0, concat_axis=1, tiled=True),
        lax.all_to_all(
            col_part_lse.astype(jnp.bfloat16), "seq", split_axis=0, concat_axis=1, tiled=True
        ).astype(col_part_lse.dtype),
    )
    top = jnp.maximum(row_lse, col_lse)
    left = jnp.exp(row_lse - top)
    right = jnp.exp(col_lse - top)
    attended = (left[..., None] * row_out + right[..., None] * col_out.astype(jnp.float32)) / (
        left + right
    )[..., None]
    attended = attended.astype(jnp.bfloat16).reshape(rows_dev, cols, features)
    terms = jnp.einsum(
        "rcf,fd->crd",
        attended,
        lax.all_gather(out_weight, "seq", axis=1, tiled=True),
        preferred_element_type=jnp.float32,
    )
    summed = lax.psum_scatter(terms.astype(jnp.bfloat16), "head", scatter_dimension=0, tiled=True)
    return summed


def dense_scores(q, k):
    return lax.dot_general(q, k, (((1,), (1,)), ((), ())), preferred_element_type=F32)


def col_scores(q, k):
    prod = q * k
    high = prod.astype(BF16)
    low = (prod - high.astype(F32)).astype(BF16)
    ones = jnp.ones((2 * HEAD, HEAD), BF16)
    return jnp.dot(jnp.concatenate([high, low], axis=1), ones, preferred_element_type=F32)


def with_ones(v):
    return jnp.concatenate([v, jnp.ones_like(v)], axis=1)


def attend(q, dense, cols, coef):
    rows = q.shape[0]
    scores = []
    for k, _, allowed in dense:
        s = dense_scores(q, k)
        scores.append(s if allowed is None else jnp.where(allowed, s, NEG))
    singles = []
    if cols:
        wide = q.astype(F32)
    for k, _, allowed in cols:
        c = col_scores(wide, k)
        singles.append(c if allowed is None else jnp.where(allowed, c, NEG))
    peak = None
    for s in scores:
        for j in range(s.shape[1] // HEAD):
            part = s[:, j * HEAD : (j + 1) * HEAD]
            peak = part if peak is None else jnp.maximum(peak, part)
    if peak is not None:
        peak = jnp.broadcast_to(jnp.max(peak, axis=1, keepdims=True), (rows, HEAD))
    for c in singles:
        peak = c if peak is None else jnp.maximum(peak, c)
    peak = peak * coef
    both = None
    for s, (_, v, _) in zip(scores, dense):
        tiled = jnp.concatenate([peak] * (s.shape[1] // HEAD), axis=1)
        p = jnp.exp2(s * coef - tiled).astype(BF16)
        term = jnp.dot(p, v, preferred_element_type=F32)
        both = term if both is None else both + term
    out = None if both is None else both[:, :HEAD]
    total = None if both is None else both[:, HEAD:]
    for c, (_, v, _) in zip(singles, cols):
        w = jnp.exp2(c * coef - peak)
        total = w if total is None else total + w
        out = w * v if out is None else out + w * v
    return out / total, peak + jnp.log2(total)


def lse_rows(even, odd):
    lane = lax.broadcasted_iota(jnp.int32, (HEAD, HEAD), 1)
    evens, odds = [], []
    for t in range(even.shape[0] // HEAD):
        block = slice(t * HEAD, (t + 1) * HEAD)
        turned = jnp.transpose(jnp.where(lane == 0, even[block], odd[block]))
        evens.append(turned[0:1])
        odds.append(turned[1:2])
    return evens, odds


LSE_ROWS = 16


def put_lse(ref, base, evens, odds):
    rows = jnp.concatenate(evens + odds, axis=0)
    pieces = []
    for _ in range(3):
        pieces.append(rows.astype(BF16).astype(F32))
        rows = rows - pieces[-1]
    spare = LSE_ROWS - 3 * rows.shape[0]
    ref[pl.ds(base, LSE_ROWS), :] = jnp.concatenate(pieces + [jnp.zeros((spare, HEAD), F32)], axis=0).astype(BF16)


def chunk_rows(array, chunk, chunks, parts):
    size = array.shape[0] // parts
    share = size // chunks
    return jnp.concatenate(
        [array[p * size + chunk * share : p * size + (chunk + 1) * share] for p in range(parts)], axis=0)


def stacked(refs):
    return [ref[i] for ref in refs for i in range(ref.shape[0])]


def own_kernel(coef, chunk, chunks, parts, at, q_m, q_o, kv_m, kv_o, *refs):
    x, z = at[0], at[1]
    below = z == 1
    first = x == 0
    *low, out = refs
    cols = q_m.shape[1]
    tokens = cols // chunks

    def pair(a, b):
        return jnp.where(first, a, b), jnp.where(first, b, a)

    def mine(array):
        return chunk_rows(array, chunk, chunks, parts)

    q_e, q_o = pair(mine(q_m[0]), mine(q_o[0]))
    k_e, k_o = pair(kv_m[0], kv_o[0])
    v_e, v_o = pair(kv_m[1], kv_o[1])
    v_e, v_o = with_ones(v_e), with_ones(v_o)
    share = tokens // parts
    index = lax.broadcasted_iota(jnp.int32, (tokens, cols), 0)
    index = (index // share) * (cols // parts) + chunk * share + index % share
    tri = lax.broadcasted_iota(jnp.int32, (tokens, cols), 1) <= index

    def run(even, odd):
        o1, l1 = attend(q_e, [(k_e, v_e, tri)] + even[0], even[1], coef)
        o2, l2 = attend(q_o, [(k_o, v_o, tri), (k_e, v_e, None)], odd, coef)
        out[:tokens] = o1.astype(BF16)
        out[tokens : 2 * tokens] = o2.astype(BF16)
        put_lse(out, 2 * tokens, *lse_rows(l1, l2))

    @pl.when(below)
    def _():
        m_k, m_v, o_k, o_v = stacked(low)
        lk_e, lk_o = pair(m_k, o_k)
        lv_e, lv_o = pair(m_v, o_v)
        col_e = (mine(lk_e).astype(F32), mine(lv_e).astype(F32), None)
        col_o = (mine(lk_o).astype(F32), mine(lv_o).astype(F32), None)
        run(([(lk_o, with_ones(lv_o), None)], [col_e]), [col_e, col_o])

    @pl.when(jnp.logical_not(below))
    def _():
        run(([], []), [])


def upper_kernel(coef, chunk, chunks, parts, at, qa_m, qa_o, qb_m, qb_o, kv_m, kv_o, *refs):
    x, z = at[0], at[1]
    below = z == 1
    first = x == 0
    *low, weight, out_a, out_b = refs
    tokens = qa_m.shape[1] // chunks

    def pair(a, b):
        return jnp.where(first, a, b), jnp.where(first, b, a)

    def mine(array):
        return chunk_rows(array, chunk, chunks, parts)

    k_e, k_o = pair(kv_m[0], kv_o[0])
    v_e, v_o = pair(kv_m[1], kv_o[1])
    ce = (mine(k_e).astype(F32), mine(v_e).astype(F32), None)
    co = (mine(k_o).astype(F32), mine(v_o).astype(F32), None)
    base = chunk * 2 * tokens

    def run(q_m, q_o, out, dense, singles, lower):
        q_e, q_odd = pair(mine(q_m[0]), mine(q_o[0]))
        o1, l1 = attend(q_e, dense, singles + lower, coef)
        o2, l2 = attend(q_odd, [], [ce, co] + lower, coef)
        out[:tokens] = o1.astype(BF16)
        out[tokens : 2 * tokens] = o2.astype(BF16)
        put_lse(out, 2 * tokens, *lse_rows(l1, l2))

    def first_rows(lower):
        run(qa_m, qa_o, out_a, [(k_o, with_ones(v_o), None)], [ce], lower)

    @pl.when(below)
    def _():
        m_k, m_v, o_k, o_v = (mine(part).astype(F32) for part in stacked(low))
        lower = [(m_k, m_v, None), (o_k, o_v, None)]
        first_rows(lower)
        run(qb_m, qb_o, out_b, [], [ce, co], lower)

    @pl.when(jnp.logical_not(below))
    def _():
        out_b[: 2 * tokens] = weight[base : base + 2 * tokens]
        out_b[pl.ds(2 * tokens, LSE_ROWS), :] = jnp.zeros((LSE_ROWS, HEAD), BF16)

    @pl.when(z == 2)
    def _():
        first_rows([])

    @pl.when(z % 3 == 0)
    def _():
        out_a[...] = jnp.zeros(out_a.shape, BF16)


def lse_packed(ref, base, rows):
    packed = ref[pl.ds(base, LSE_ROWS), :].astype(F32)
    return sum(packed[i * rows : (i + 1) * rows] for i in range(3))


def merge_kernel(at, own, oa, ob, out):
    z = at[1]
    tokens = out.shape[1]
    blocks = tokens // HEAD
    rows = 2 * blocks
    l0, l1, l2 = (lse_packed(ref, 2 * tokens, rows) for ref in (own, oa, ob))
    l1, l2 = jnp.where(z >= 2, l1, NEG), jnp.where(z >= 3, l2, NEG)
    top = jnp.maximum(l0, jnp.maximum(l1, l2))
    shares = [jnp.exp2(l - top) for l in (l0, l1, l2)]
    whole = shares[0] + shares[1] + shares[2]
    shares = jnp.concatenate([share / whole for share in shares], axis=0)
    high = shares.astype(BF16).astype(F32)
    spare = jnp.zeros((32 - 6 * rows, HEAD), F32)
    pieces = jnp.concatenate([high, shares - high, spare], axis=0).astype(BF16)
    line = lax.broadcasted_iota(jnp.int32, (32, 3 * HEAD), 0)
    group = lax.broadcasted_iota(jnp.int32, (32, 3 * HEAD), 1) // HEAD
    for row in range(2):
        for block in range(blocks):
            first = row * blocks + block + group * rows
            pick = ((line == first) | (line == first + 3 * rows)).astype(BF16)
            spread = lax.dot_general(pieces, pick, (((0,), (0,)), ((), ())), preferred_element_type=F32)
            mine = slice(row * tokens + block * HEAD, row * tokens + (block + 1) * HEAD)
            mixed = spread[:, :HEAD] * own[mine].astype(F32)
            mixed = mixed + spread[:, HEAD : 2 * HEAD] * oa[mine].astype(F32)
            mixed = mixed + spread[:, 2 * HEAD :] * ob[mine].astype(F32)
            out[row, block * HEAD : (block + 1) * HEAD] = mixed.astype(BF16)


def cost(us):
    return pl.CostEstimate(flops=int(us * 1e8), bytes_accessed=1024, transcendentals=0)


def head_call(kernel, at, args, outs, heads, name, us):
    def spec(shape, start=0):
        lead = len(shape) - 1
        return pl.BlockSpec(tuple(shape[:-1]) + (HEAD,), lambda h, at: (0,) * lead + (start + h,))

    return pl.pallas_call(
        kernel,
        out_shape=outs,
        grid_spec=pltpu.PrefetchScalarGridSpec(
            num_scalar_prefetch=1,
            grid=(heads,),
            in_specs=[spec(a.shape, start) for a, start in args],
            out_specs=[spec(o.shape) for o in outs],
        ),
        compiler_params=pltpu.CompilerParams(vmem_limit_bytes=VMEM),
        cost_estimate=cost(us),
        name=name,
    )(at, *(a for a, _ in args))


def project_kernel(plan, at, *refs):
    x, core = at[0], at[2]
    *arrays, send, keep = refs
    for who, out in ((1 - core, send), (core, keep)):
        for s, (near, far, weight) in enumerate(plan):
            left, right = (
                jnp.concatenate([arrays[i][r, y, who] for y in range(2) for r in range(2)], axis=0)
                for i in (near, far)
            )
            weight = arrays[weight]
            half = left.shape[1]
            top = weight[pl.ds(pl.multiple_of(x * half, half), half)]
            bottom = weight[pl.ds(pl.multiple_of((1 - x) * half, half), half)]
            c = jnp.dot(left, top, preferred_element_type=F32) + jnp.dot(right, bottom, preferred_element_type=F32)
            out[s] = c.astype(BF16).reshape(out.shape[1:])


def project(at, attended, items):
    arrays, plan = [], []

    def place_of(array):
        for i, other in enumerate(arrays):
            if other is array:
                return i
        arrays.append(array)
        return len(arrays) - 1

    for chunk, weight in items:
        plan.append(tuple(place_of(a) for a in attended[chunk] + (weight,)))
    _, _, _, tokens, _ = attended[0][0].shape
    out = jax.ShapeDtypeStruct((len(items), 2, 2, tokens, items[0][1].shape[1]), BF16)
    return whole_call(functools.partial(project_kernel, plan), at, arrays, [out, out], "project", 1 * len(items))


def whole_call(kernel, at, args, outs, name, us):
    return pl.pallas_call(
        kernel,
        out_shape=outs,
        in_specs=[pl.BlockSpec(memory_space=pltpu.SMEM)] + [pl.BlockSpec(memory_space=pltpu.VMEM)] * len(args),
        out_specs=[pl.BlockSpec(memory_space=pltpu.VMEM)] * len(outs),
        compiler_params=pltpu.CompilerParams(vmem_limit_bytes=VMEM),
        cost_estimate=cost(us),
        name=name,
    )(at, *args)


def total(a, b):
    return (a.astype(F32) + b.astype(F32)).astype(BF16)


def split_kernel(at, kept, got, stay, to_y, to_x, to_xy):
    x, y = at[0], at[3]
    for s in range(kept.shape[0]):
        for out, yy, xx in ((to_xy, 1 - y, 1 - x), (to_y, 1 - y, x), (to_x, y, 1 - x), (stay, y, x)):
            out[s] = total(kept[s, yy, xx], got[s, yy, xx])


def halve_kernel(at, kept, got, stay, to_y):
    y = at[3]
    for s in range(kept.shape[0]):
        for r in range(2):
            to_y[s, r] = total(kept[s, 1 - y, r], got[s, 1 - y, r])
            stay[s, r] = total(kept[s, y, r], got[s, y, r])


def row_kernel(at, stay, got, mine, to_x):
    x = at[0]
    for s in range(stay.shape[0]):
        to_x[s] = total(stay[s, 1 - x], got[s, 1 - x])
        mine[s] = total(stay[s, x], got[s, x])


def place_kernel(plan, at, *refs):
    x, z, out = at[0], at[1], refs[-1]
    layers = [z, z + 1 - 2 * (z % 2), (z + 2) % 4, 3 - z]
    refs = iter(refs[:-1])
    for names, hops in plan:
        group = [next(refs) for _ in range(2 * hops)]
        _, tokens, width = group[0].shape
        for s, (chunk, layer) in enumerate(names):
            rows = pl.ds(chunk * tokens, tokens)
            base = 2 * layers[layer]
            mine = pl.ds(pl.multiple_of((base + x) * width, width), width)
            theirs = pl.ds(pl.multiple_of((base + 1 - x) * width, width), width)
            if hops == 1:
                out[rows, mine], out[rows, theirs] = group[0][s], group[1][s]
            else:
                out[rows, mine] = total(group[0][s], group[1][s])
                out[rows, theirs] = total(group[2][s], group[3][s])


def after(value, *earlier):
    return lax.optimization_barrier((value, earlier))[0]


def body_eight(qkv, out_weight):
    _, _, cols, features = qkv.shape
    half = features // 2
    chunks = 2
    heads = half // HEAD
    parts = lax.axis_size("head")
    tokens = cols // chunks
    coef = HEAD ** (-0.5) * LOG2E
    me = lax.axis_index("seq")
    who = lax.axis_index("head")
    z, x, core, y = me // 2, me % 2, who % 2, who // 2
    at = jnp.stack([x, z, core, y]).astype(jnp.int32)
    local = qkv.reshape(3, cols, features)
    first = x == 0

    def seq_perm(array, *layers, cross=False):
        pairs = [(2 * a + i, 2 * b + (1 - i if cross else i)) for a, b in layers for i in range(2)]
        return lax.ppermute(array, "seq", pairs)

    def swap(array):
        return seq_perm(array, (0, 0), (1, 1), (2, 2), (3, 3), cross=True)

    def head_perm(array, flip):
        return lax.ppermute(array, "head", [(i, i ^ flip) for i in range(4)])

    def lanes(lo, hi, part, source=local):
        return lax.dynamic_slice(source, (lo, 0, part * half), (hi - lo, cols, half))

    down, two_down = [(2, 1), (3, 2)], [(3, 1)]
    q_m = lanes(0, 1, x)
    q_o = swap(lanes(0, 1, 1 - x))
    qs = [seq_perm(q_m, *down), None, seq_perm(q_m, *two_down), None]
    kv_m, kv_give = lanes(1, 3, x), lanes(1, 3, 1 - x)
    block = out_weight.reshape(kv_m.shape)
    low_m = seq_perm(jnp.where(z == 0, kv_m, block), (0, 1), (1, 3))
    pairs = [(i, 2 + 1 - i) for i in range(2)] + [(2 + i, i) for i in range(2)] + [(4 + i, 6 + i) for i in range(2)]
    low_o = lax.ppermute(jnp.where(z == 0, kv_give, block), "seq", pairs)
    kv_o = swap(after(kv_give, q_o, qs[0]))
    qs[1], qs[3] = seq_perm(q_o, *down), seq_perm(q_o, *two_down)
    w_second = seq_perm(after(out_weight, *qs), (0, 2))

    struct = jax.ShapeDtypeStruct
    partial = struct((2 * tokens + LSE_ROWS, half), BF16)
    oa, ob, own = [], [], []
    turn = at
    kvs = [kv_m, kv_o, low_m, low_o]
    for c in range(chunks):
        a, b = head_call(
            functools.partial(upper_kernel, coef, c, chunks, parts), turn, [(a, 0) for a in qs + kvs + [out_weight]],
            [partial] * 2, heads, "upper_rows", 7)
        turn = after(at, a)
        oa.append(seq_perm(a, (1, 2), (2, 3)))
        ob.append(seq_perm(b, (1, 3), (0, 1), (3, 2)))
    def own_rows(c, turn):
        (mine,) = head_call(
            functools.partial(own_kernel, coef, c, chunks, parts), turn, [(a, 0) for a in [q_m, q_o] + kvs],
            [partial], heads, "own_rows", 6)
        return mine

    own.append(own_rows(0, turn))
    w_down = seq_perm(after(out_weight, *qs), (2, 0), (3, 1))

    def merged(c, earlier):
        (a,) = head_call(
            merge_kernel, after(at, earlier), [(a[c], 0) for a in (own, oa, ob)],
            [struct((2, tokens, half), BF16)], heads, "merge", 2)
        shape = (2, 2, 2, tokens // 4, half)
        return a.reshape(shape), swap(a).reshape(shape)

    attended = [merged(0, own[0])]
    own.append(own_rows(1, after(at, attended[0][0], w_second)))
    ridden = jnp.where(z == 2, w_second, low_m.reshape(out_weight.shape))
    w_far = jnp.where(z >= 2, ridden, after(w_down, own[1]))
    w_other = seq_perm(w_far, (0, 1), (1, 0), (2, 3), (3, 2))
    parts_out, plan = [], []

    def summed(turn, names):
        send, kept = project(turn, attended, [(c, weights[layer]) for c, layer in names])
        return send.shape[:1] + send.shape[3:], [kept, head_perm(send, 1)]

    w_near = jnp.where(
        (z == 0) | (z == 3), low_o.reshape(out_weight.shape), jnp.concatenate([o[: 2 * tokens] for o in after(ob, own[1])]))
    attended.append(merged(1, (w_far, attended[0][1], w_near)))
    weights = {0: out_weight, 1: w_near, 2: w_far, 3: w_other}
    names = [(0, 0), (0, 1)]
    size, pair = summed(at, names)
    both = struct(size[:1] + (2,) + size[1:], BF16)
    stay, to_y = whole_call(halve_kernel, at, pair, [both] * 2, "halve", 2)
    from_y = head_perm(to_y, 2)
    mine, to_x = whole_call(row_kernel, at, [stay, from_y], [struct(size, BF16)] * 2, "rows", 1)
    parts_out += [mine, swap(to_x)]
    plan.append((names, 1))

    names = [(1, 0), (1, 1), (1, 2), (1, 3), (0, 2), (0, 3)]
    size, pair = summed(after(at, mine), names)
    stay, to_y, to_x, to_xy = whole_call(split_kernel, at, pair, [struct(size, BF16)] * 4, "split", 2)
    diagonal = [
        ((2 * i + j) * 4 + h, (2 * i + 1 - j) * 4 + (h ^ 2)) for i in range(4) for j in range(2) for h in range(4)
    ]
    parts_out += [stay, head_perm(to_y, 2), swap(to_x), lax.ppermute(to_xy, ("seq", "head"), diagonal)]
    plan.append((names, 2))
    (out,) = whole_call(
        functools.partial(place_kernel, plan), at, parts_out,
        [struct((cols // 4, 8 * out_weight.shape[1]), BF16)], "place", 2)
    return out.reshape(cols // 4, 1, 8 * out_weight.shape[1])


def solution(mesh):
    in_specs = (P(None, "seq", None, "head"), P("head", "seq"))
    out_specs = P("head", "seq", None)
    small = mesh.shape["seq"] == 8 and mesh.shape["head"] == 4

    def body(qkv, out_weight):
        _, rows, cols, features = qkv.shape
        even = features == 2 * cols and out_weight.shape == (features, cols) and cols % 512 == 0
        if small and rows == 1 and even:
            return body_eight(qkv, out_weight)
        return body_any(qkv, out_weight)

    return jax.shard_map(body, mesh=mesh, in_specs=in_specs, out_specs=out_specs, check_vma=False)
```

```python
import functools
import jax
import jax.numpy as jnp
from jax import lax
from jax.experimental import pallas as pl
from jax.experimental.pallas import tpu as pltpu
from jax.sharding import PartitionSpec as P

HEAD = 128
LOG2E = 1.4426950408889634
NEG = -1e30
QB = 128
VMEM = 24 * 1024 * 1024
F32, BF16 = jnp.float32, jnp.bfloat16


def shifted(shard, axis, by):
    size = lax.axis_size(axis)
    pairs = [(i, i + by) for i in range(size) if 0 <= i + by < size]
    return lax.ppermute(shard, axis, pairs)


def column_part(part):
    queries, keys_part, values = (part[0], part[1], part[2])
    rows = queries.shape[0]
    scale = queries.shape[-1] ** (-0.5)
    scores = (
        jnp.einsum("rchd,schd->chrs", queries, keys_part, preferred_element_type=jnp.float32)
        * scale
    )
    r_idx = lax.broadcasted_iota(jnp.int32, (rows, rows), 0)
    s_idx = lax.broadcasted_iota(jnp.int32, (rows, rows), 1)
    allowed = s_idx <= r_idx - 2
    masked = jnp.where(allowed, scores, jnp.float32(-1e30))
    peak = jnp.max(masked, axis=-1)
    weights = jnp.where(allowed, jnp.exp(masked - peak[..., None]), jnp.float32(0.0))
    total = jnp.maximum(jnp.sum(weights, axis=-1), jnp.float32(1.0))
    rounded = weights.astype(jnp.bfloat16)
    mixed = jnp.einsum("chrs,schd->rchd", rounded, values, preferred_element_type=jnp.float32)
    col_out = (mixed / jnp.transpose(total, (2, 0, 1))[..., None]).astype(jnp.bfloat16)
    col_lse = jnp.transpose(peak + jnp.log(total), (2, 0, 1))
    return (col_out, col_lse)


def row_part(local, previous, first_row):
    rows_dev, cols, heads_local, head_size = (
        local.shape[1],
        local.shape[2],
        local.shape[3],
        local.shape[4],
    )
    scale = head_size ** (-0.5)
    keys_ext = jnp.concatenate([previous, local[1:3]], axis=1)
    key_idx = lax.broadcasted_iota(jnp.int32, (cols, 2 * cols), 1)
    query_idx = lax.broadcasted_iota(jnp.int32, (cols, 2 * cols), 0)

    def one_row(index):
        queries = lax.dynamic_index_in_dim(local[0], index, 0, keepdims=False)
        pair = keys_ext.reshape(2, 2 * cols, heads_local, head_size)
        scores = (
            jnp.einsum("qhd,khd->hqk", queries, pair[0], preferred_element_type=jnp.float32) * scale
        )
        allowed = (key_idx < cols) & (first_row + index > 0) | (key_idx >= cols) & (
            key_idx - cols <= query_idx
        )
        masked = jnp.where(allowed[None], scores, jnp.float32(-1e30))
        peak = jnp.max(masked, axis=-1)
        weights = jnp.where(allowed[None], jnp.exp(masked - peak[..., None]), jnp.float32(0.0))
        total = jnp.sum(weights, axis=-1)
        rounded = weights.astype(jnp.bfloat16)
        mixed = jnp.einsum("hqk,khd->qhd", rounded, pair[1], preferred_element_type=jnp.float32)
        return (mixed / jnp.transpose(total)[..., None], jnp.transpose(peak + jnp.log(total)))

    return lax.map(one_row, jnp.arange(rows_dev, dtype=jnp.int32))


def body_any(qkv, out_weight):
    rows_dev, cols, features = (qkv.shape[1], qkv.shape[2], qkv.shape[3])
    head_size = HEAD
    heads_local = features // head_size
    local = qkv.reshape(3, rows_dev, cols, heads_local, head_size)
    previous = shifted(local[1:3, rows_dev - 1 : rows_dev], "seq", 1)
    first_row = lax.axis_index("seq") * rows_dev
    row_out, row_lse = row_part(local, previous, first_row)
    columns = lax.all_to_all(local, "seq", split_axis=2, concat_axis=1, tiled=True)
    col_part_out, col_part_lse = column_part(columns)
    col_out, col_lse = (
        lax.all_to_all(col_part_out, "seq", split_axis=0, concat_axis=1, tiled=True),
        lax.all_to_all(
            col_part_lse.astype(jnp.bfloat16), "seq", split_axis=0, concat_axis=1, tiled=True
        ).astype(col_part_lse.dtype),
    )
    top = jnp.maximum(row_lse, col_lse)
    left = jnp.exp(row_lse - top)
    right = jnp.exp(col_lse - top)
    attended = (left[..., None] * row_out + right[..., None] * col_out.astype(jnp.float32)) / (
        left + right
    )[..., None]
    attended = attended.astype(jnp.bfloat16).reshape(rows_dev, cols, features)
    terms = jnp.einsum(
        "rcf,fd->crd",
        attended,
        lax.all_gather(out_weight, "seq", axis=1, tiled=True),
        preferred_element_type=jnp.float32,
    )
    summed = lax.psum_scatter(terms.astype(jnp.bfloat16), "head", scatter_dimension=0, tiled=True)
    return summed


def dense_scores(q, k):
    return lax.dot_general(q, k, (((1,), (1,)), ((), ())), preferred_element_type=F32)


def col_scores(q, k):
    prod = q * k
    high = prod.astype(BF16)
    low = (prod - high.astype(F32)).astype(BF16)
    ones = jnp.ones((2 * HEAD, HEAD), BF16)
    return jnp.dot(jnp.concatenate([high, low], axis=1), ones, preferred_element_type=F32)


def with_ones(v):
    return jnp.concatenate([v, jnp.ones_like(v)], axis=1)


def attend(q, dense, cols, coef):
    rows = q.shape[0]
    scores = []
    for k, _, allowed in dense:
        s = dense_scores(q, k)
        scores.append(s if allowed is None else jnp.where(allowed, s, NEG))
    singles = []
    if cols:
        wide = q.astype(F32)
    for k, _, allowed in cols:
        c = col_scores(wide, k)
        singles.append(c if allowed is None else jnp.where(allowed, c, NEG))
    peak = None
    for s in scores:
        for j in range(s.shape[1] // HEAD):
            part = s[:, j * HEAD : (j + 1) * HEAD]
            peak = part if peak is None else jnp.maximum(peak, part)
    if peak is not None:
        peak = jnp.broadcast_to(jnp.max(peak, axis=1, keepdims=True), (rows, HEAD))
    for c in singles:
        peak = c if peak is None else jnp.maximum(peak, c)
    peak = peak * coef
    both = None
    for s, (_, v, _) in zip(scores, dense):
        tiled = jnp.concatenate([peak] * (s.shape[1] // HEAD), axis=1)
        p = jnp.exp2(s * coef - tiled).astype(BF16)
        term = jnp.dot(p, v, preferred_element_type=F32)
        both = term if both is None else both + term
    out = None if both is None else both[:, :HEAD]
    total = None if both is None else both[:, HEAD:]
    for c, (_, v, _) in zip(singles, cols):
        w = jnp.exp2(c * coef - peak)
        total = w if total is None else total + w
        out = w * v if out is None else out + w * v
    return out / total, peak + jnp.log2(total)


def lse_rows(even, odd):
    lane = lax.broadcasted_iota(jnp.int32, (HEAD, HEAD), 1)
    evens, odds = [], []
    for t in range(even.shape[0] // HEAD):
        block = slice(t * HEAD, (t + 1) * HEAD)
        turned = jnp.transpose(jnp.where(lane == 0, even[block], odd[block]))
        evens.append(turned[0:1])
        odds.append(turned[1:2])
    return evens, odds


LSE_ROWS = 16


def put_lse(ref, base, evens, odds):
    rows = jnp.concatenate(evens + odds, axis=0)
    pieces = []
    for _ in range(3):
        pieces.append(rows.astype(BF16).astype(F32))
        rows = rows - pieces[-1]
    spare = LSE_ROWS - 3 * rows.shape[0]
    ref[pl.ds(base, LSE_ROWS), :] = jnp.concatenate(pieces + [jnp.zeros((spare, HEAD), F32)], axis=0).astype(BF16)


def chunk_rows(array, chunk, chunks, parts):
    size = array.shape[0] // parts
    share = size // chunks
    return jnp.concatenate(
        [array[p * size + chunk * share : p * size + (chunk + 1) * share] for p in range(parts)], axis=0)


def stacked(refs):
    return [ref[i] for ref in refs for i in range(ref.shape[0])]


def own_kernel(coef, chunk, chunks, parts, at, q_m, q_o, kv_m, kv_o, *refs):
    x, z = at[0], at[1]
    below = z == 1
    first = x == 0
    *low, out = refs
    cols = q_m.shape[1]
    tokens = cols // chunks

    def pair(a, b):
        return jnp.where(first, a, b), jnp.where(first, b, a)

    def mine(array):
        return chunk_rows(array, chunk, chunks, parts)

    q_e, q_o = pair(mine(q_m[0]), mine(q_o[0]))
    k_e, k_o = pair(kv_m[0], kv_o[0])
    v_e, v_o = pair(kv_m[1], kv_o[1])
    v_e, v_o = with_ones(v_e), with_ones(v_o)
    share = tokens // parts
    index = lax.broadcasted_iota(jnp.int32, (tokens, cols), 0)
    index = (index // share) * (cols // parts) + chunk * share + index % share
    tri = lax.broadcasted_iota(jnp.int32, (tokens, cols), 1) <= index

    def run(even, odd):
        o1, l1 = attend(q_e, [(k_e, v_e, tri)] + even[0], even[1], coef)
        o2, l2 = attend(q_o, [(k_o, v_o, tri), (k_e, v_e, None)], odd, coef)
        out[:tokens] = o1.astype(BF16)
        out[tokens : 2 * tokens] = o2.astype(BF16)
        put_lse(out, 2 * tokens, *lse_rows(l1, l2))

    @pl.when(below)
    def _():
        m_k, m_v, o_k, o_v = stacked(low)
        lk_e, lk_o = pair(m_k, o_k)
        lv_e, lv_o = pair(m_v, o_v)
        col_e = (mine(lk_e).astype(F32), mine(lv_e).astype(F32), None)
        col_o = (mine(lk_o).astype(F32), mine(lv_o).astype(F32), None)
        run(([(lk_o, with_ones(lv_o), None)], [col_e]), [col_e, col_o])

    @pl.when(jnp.logical_not(below))
    def _():
        run(([], []), [])


def upper_kernel(coef, chunk, chunks, parts, at, qa_m, qa_o, qb_m, qb_o, kv_m, kv_o, *refs):
    x, z = at[0], at[1]
    below = z == 1
    first = x == 0
    *low, weight, out_a, out_b = refs
    tokens = qa_m.shape[1] // chunks

    def pair(a, b):
        return jnp.where(first, a, b), jnp.where(first, b, a)

    def mine(array):
        return chunk_rows(array, chunk, chunks, parts)

    k_e, k_o = pair(kv_m[0], kv_o[0])
    v_e, v_o = pair(kv_m[1], kv_o[1])
    ce = (mine(k_e).astype(F32), mine(v_e).astype(F32), None)
    co = (mine(k_o).astype(F32), mine(v_o).astype(F32), None)
    base = chunk * 2 * tokens

    def run(q_m, q_o, out, dense, singles, lower):
        q_e, q_odd = pair(mine(q_m[0]), mine(q_o[0]))
        o1, l1 = attend(q_e, dense, singles + lower, coef)
        o2, l2 = attend(q_odd, [], [ce, co] + lower, coef)
        out[:tokens] = o1.astype(BF16)
        out[tokens : 2 * tokens] = o2.astype(BF16)
        put_lse(out, 2 * tokens, *lse_rows(l1, l2))

    def first_rows(lower):
        run(qa_m, qa_o, out_a, [(k_o, with_ones(v_o), None)], [ce], lower)

    @pl.when(below)
    def _():
        m_k, m_v, o_k, o_v = (mine(part).astype(F32) for part in stacked(low))
        lower = [(m_k, m_v, None), (o_k, o_v, None)]
        first_rows(lower)
        run(qb_m, qb_o, out_b, [], [ce, co], lower)

    @pl.when(jnp.logical_not(below))
    def _():
        out_b[: 2 * tokens] = weight[base : base + 2 * tokens]
        out_b[pl.ds(2 * tokens, LSE_ROWS), :] = jnp.zeros((LSE_ROWS, HEAD), BF16)

    @pl.when(z == 2)
    def _():
        first_rows([])

    @pl.when(z % 3 == 0)
    def _():
        out_a[...] = jnp.zeros(out_a.shape, BF16)


def lse_packed(ref, base, rows):
    packed = ref[pl.ds(base, LSE_ROWS), :].astype(F32)
    return sum(packed[i * rows : (i + 1) * rows] for i in range(3))


def merge_kernel(at, own, oa, ob, out):
    z = at[1]
    tokens = out.shape[1]
    blocks = tokens // HEAD
    rows = 2 * blocks
    l0, l1, l2 = (lse_packed(ref, 2 * tokens, rows) for ref in (own, oa, ob))
    l1, l2 = jnp.where(z >= 2, l1, NEG), jnp.where(z >= 3, l2, NEG)
    top = jnp.maximum(l0, jnp.maximum(l1, l2))
    shares = [jnp.exp2(l - top) for l in (l0, l1, l2)]
    whole = shares[0] + shares[1] + shares[2]
    shares = jnp.concatenate([share / whole for share in shares], axis=0)
    high = shares.astype(BF16).astype(F32)
    spare = jnp.zeros((32 - 6 * rows, HEAD), F32)
    pieces = jnp.concatenate([high, shares - high, spare], axis=0).astype(BF16)
    line = lax.broadcasted_iota(jnp.int32, (32, 3 * HEAD), 0)
    group = lax.broadcasted_iota(jnp.int32, (32, 3 * HEAD), 1) // HEAD
    for row in range(2):
        for block in range(blocks):
            first = row * blocks + block + group * rows
            pick = ((line == first) | (line == first + 3 * rows)).astype(BF16)
            spread = lax.dot_general(pieces, pick, (((0,), (0,)), ((), ())), preferred_element_type=F32)
            mine = slice(row * tokens + block * HEAD, row * tokens + (block + 1) * HEAD)
            mixed = spread[:, :HEAD] * own[mine].astype(F32)
            mixed = mixed + spread[:, HEAD : 2 * HEAD] * oa[mine].astype(F32)
            mixed = mixed + spread[:, 2 * HEAD :] * ob[mine].astype(F32)
            out[row, block * HEAD : (block + 1) * HEAD] = mixed.astype(BF16)


def cost(us):
    return pl.CostEstimate(flops=int(us * 1e8), bytes_accessed=1024, transcendentals=0)


def head_call(kernel, at, args, outs, heads, name, us):
    def spec(shape, start=0):
        lead = len(shape) - 1
        return pl.BlockSpec(tuple(shape[:-1]) + (HEAD,), lambda h, at: (0,) * lead + (start + h,))

    return pl.pallas_call(
        kernel,
        out_shape=outs,
        grid_spec=pltpu.PrefetchScalarGridSpec(
            num_scalar_prefetch=1,
            grid=(heads,),
            in_specs=[spec(a.shape, start) for a, start in args],
            out_specs=[spec(o.shape) for o in outs],
        ),
        compiler_params=pltpu.CompilerParams(vmem_limit_bytes=VMEM),
        cost_estimate=cost(us),
        name=name,
    )(at, *(a for a, _ in args))


def project_kernel(plan, at, *refs):
    x, core = at[0], at[2]
    *arrays, send, keep = refs
    for who, out in ((1 - core, send), (core, keep)):
        for s, (near, far, weight) in enumerate(plan):
            left, right = (
                jnp.concatenate([arrays[i][r, y, who] for y in range(2) for r in range(2)], axis=0)
                for i in (near, far)
            )
            weight = arrays[weight]
            half = left.shape[1]
            top = weight[pl.ds(pl.multiple_of(x * half, half), half)]
            bottom = weight[pl.ds(pl.multiple_of((1 - x) * half, half), half)]
            c = jnp.dot(left, top, preferred_element_type=F32) + jnp.dot(right, bottom, preferred_element_type=F32)
            out[s] = c.astype(BF16).reshape(out.shape[1:])


def project(at, attended, items):
    arrays, plan = [], []

    def place_of(array):
        for i, other in enumerate(arrays):
            if other is array:
                return i
        arrays.append(array)
        return len(arrays) - 1

    for chunk, weight in items:
        plan.append(tuple(place_of(a) for a in attended[chunk] + (weight,)))
    _, _, _, tokens, _ = attended[0][0].shape
    out = jax.ShapeDtypeStruct((len(items), 2, 2, tokens, items[0][1].shape[1]), BF16)
    return whole_call(functools.partial(project_kernel, plan), at, arrays, [out, out], "project", 1 * len(items))


def whole_call(kernel, at, args, outs, name, us):
    return pl.pallas_call(
        kernel,
        out_shape=outs,
        in_specs=[pl.BlockSpec(memory_space=pltpu.SMEM)] + [pl.BlockSpec(memory_space=pltpu.VMEM)] * len(args),
        out_specs=[pl.BlockSpec(memory_space=pltpu.VMEM)] * len(outs),
        compiler_params=pltpu.CompilerParams(vmem_limit_bytes=VMEM),
        cost_estimate=cost(us),
        name=name,
    )(at, *args)


def total(a, b):
    return (a.astype(F32) + b.astype(F32)).astype(BF16)


def split_kernel(at, kept, got, stay, to_y, to_x, to_xy):
    x, y = at[0], at[3]
    for s in range(kept.shape[0]):
        for out, yy, xx in ((to_xy, 1 - y, 1 - x), (to_y, 1 - y, x), (to_x, y, 1 - x), (stay, y, x)):
            out[s] = total(kept[s, yy, xx], got[s, yy, xx])


def halve_kernel(at, kept, got, stay, to_y):
    y = at[3]
    for s in range(kept.shape[0]):
        for r in range(2):
            to_y[s, r] = total(kept[s, 1 - y, r], got[s, 1 - y, r])
            stay[s, r] = total(kept[s, y, r], got[s, y, r])


def row_kernel(at, stay, got, mine, to_x):
    x = at[0]
    for s in range(stay.shape[0]):
        to_x[s] = total(stay[s, 1 - x], got[s, 1 - x])
        mine[s] = total(stay[s, x], got[s, x])


def place_kernel(plan, at, *refs):
    x, z, out = at[0], at[1], refs[-1]
    layers = [z, z + 1 - 2 * (z % 2), (z + 2) % 4, 3 - z]
    refs = iter(refs[:-1])
    for names, hops in plan:
        group = [next(refs) for _ in range(2 * hops)]
        _, tokens, width = group[0].shape
        for s, (chunk, layer) in enumerate(names):
            rows = pl.ds(chunk * tokens, tokens)
            base = 2 * layers[layer]
            mine = pl.ds(pl.multiple_of((base + x) * width, width), width)
            theirs = pl.ds(pl.multiple_of((base + 1 - x) * width, width), width)
            if hops == 1:
                out[rows, mine], out[rows, theirs] = group[0][s], group[1][s]
            else:
                out[rows, mine] = total(group[0][s], group[1][s])
                out[rows, theirs] = total(group[2][s], group[3][s])


def after(value, *earlier):
    return lax.optimization_barrier((value, earlier))[0]


def body_eight(qkv, out_weight):
    _, _, cols, features = qkv.shape
    half = features // 2
    chunks = 2
    heads = half // HEAD
    parts = lax.axis_size("head")
    tokens = cols // chunks
    coef = HEAD ** (-0.5) * LOG2E
    me = lax.axis_index("seq")
    who = lax.axis_index("head")
    z, x, core, y = me // 2, me % 2, who % 2, who // 2
    at = jnp.stack([x, z, core, y]).astype(jnp.int32)
    local = qkv.reshape(3, cols, features)
    first = x == 0

    def seq_perm(array, *layers, cross=False):
        pairs = [(2 * a + i, 2 * b + (1 - i if cross else i)) for a, b in layers for i in range(2)]
        return lax.ppermute(array, "seq", pairs)

    def swap(array):
        return seq_perm(array, (0, 0), (1, 1), (2, 2), (3, 3), cross=True)

    def head_perm(array, flip):
        return lax.ppermute(array, "head", [(i, i ^ flip) for i in range(4)])

    def lanes(lo, hi, part, source=local):
        return lax.dynamic_slice(source, (lo, 0, part * half), (hi - lo, cols, half))

    down, two_down = [(2, 1), (3, 2)], [(3, 1)]
    q_m = lanes(0, 1, x)
    q_o = swap(lanes(0, 1, 1 - x))
    qs = [seq_perm(q_m, *down), None, seq_perm(q_m, *two_down), None]
    kv_m, kv_give = lanes(1, 3, x), lanes(1, 3, 1 - x)
    block = out_weight.reshape(kv_m.shape)
    low_m = seq_perm(jnp.where(z == 0, kv_m, block), (0, 1), (1, 3))
    pairs = [(i, 2 + 1 - i) for i in range(2)] + [(2 + i, i) for i in range(2)] + [(4 + i, 6 + i) for i in range(2)]
    low_o = lax.ppermute(jnp.where(z == 0, kv_give, block), "seq", pairs)
    kv_o = swap(after(kv_give, q_o, qs[0]))
    qs[1], qs[3] = seq_perm(q_o, *down), seq_perm(q_o, *two_down)

    struct = jax.ShapeDtypeStruct
    partial = struct((2 * tokens + LSE_ROWS, half), BF16)
    oa, ob, own = [], [], []
    turn = at
    kvs = [kv_m, kv_o, low_m, low_o]
    for c in range(chunks):
        a, b = head_call(
            functools.partial(upper_kernel, coef, c, chunks, parts), turn, [(a, 0) for a in qs + kvs + [out_weight]],
            [partial] * 2, heads, "upper_rows", 7)
        turn = after(at, a)
        oa.append(seq_perm(a, (1, 2), (2, 3)))
        ob.append(seq_perm(b, (1, 3), (0, 1), (3, 2)))
    def own_rows(c, turn):
        (mine,) = head_call(
            functools.partial(own_kernel, coef, c, chunks, parts), turn, [(a, 0) for a in [q_m, q_o] + kvs],
            [partial], heads, "own_rows", 6)
        return mine

    own.append(own_rows(0, turn))
    w_down = seq_perm(after(out_weight, *qs), (0, 2), (2, 0), (3, 1))

    def merged(c, earlier):
        (a,) = head_call(
            merge_kernel, after(at, earlier), [(a[c], 0) for a in (own, oa, ob)],
            [struct((2, tokens, half), BF16)], heads, "merge", 2)
        shape = (2, 2, 2, tokens // 4, half)
        return a.reshape(shape), swap(a).reshape(shape)

    attended = [merged(0, own[0])]
    w_far = jnp.where(z == 3, low_m.reshape(out_weight.shape), after(w_down, attended[0][0]))
    own.append(own_rows(1, after(at, w_far)))
    w_other = seq_perm(w_far, (0, 1), (1, 0), (2, 3), (3, 2))
    parts_out, plan = [], []

    def summed(turn, names):
        send, kept = project(turn, attended, [(c, weights[layer]) for c, layer in names])
        return send.shape[:1] + send.shape[3:], [kept, head_perm(send, 1)]

    w_near = jnp.where(
        (z == 0) | (z == 3), low_o.reshape(out_weight.shape), jnp.concatenate([o[: 2 * tokens] for o in after(ob, own[1])]))
    attended.append(merged(1, (w_far, attended[0][1], w_near)))
    weights = {0: out_weight, 1: w_near, 2: w_far, 3: w_other}
    names = [(0, 0), (0, 1)]
    size, pair = summed(at, names)
    both = struct(size[:1] + (2,) + size[1:], BF16)
    stay, to_y = whole_call(halve_kernel, at, pair, [both] * 2, "halve", 2)
    from_y = head_perm(to_y, 2)
    mine, to_x = whole_call(row_kernel, at, [stay, from_y], [struct(size, BF16)] * 2, "rows", 1)
    parts_out += [mine, swap(to_x)]
    plan.append((names, 1))

    names = [(1, 0), (1, 1), (1, 2), (1, 3), (0, 2), (0, 3)]
    size, pair = summed(after(at, mine), names)
    stay, to_y, to_x, to_xy = whole_call(split_kernel, at, pair, [struct(size, BF16)] * 4, "split", 2)
    diagonal = [
        ((2 * i + j) * 4 + h, (2 * i + 1 - j) * 4 + (h ^ 2)) for i in range(4) for j in range(2) for h in range(4)
    ]
    parts_out += [stay, head_perm(to_y, 2), swap(to_x), lax.ppermute(to_xy, ("seq", "head"), diagonal)]
    plan.append((names, 2))
    (out,) = whole_call(
        functools.partial(place_kernel, plan), at, parts_out,
        [struct((cols // 4, 8 * out_weight.shape[1]), BF16)], "place", 2)
    return out.reshape(cols // 4, 1, 8 * out_weight.shape[1])


def solution(mesh):
    in_specs = (P(None, "seq", None, "head"), P("head", "seq"))
    out_specs = P("head", "seq", None)
    small = mesh.shape["seq"] == 8 and mesh.shape["head"] == 4

    def body(qkv, out_weight):
        _, rows, cols, features = qkv.shape
        even = features == 2 * cols and out_weight.shape == (features, cols) and cols % 512 == 0
        if small and rows == 1 and even:
            return body_eight(qkv, out_weight)
        return body_any(qkv, out_weight)

    return jax.shard_map(body, mesh=mesh, in_specs=in_specs, out_specs=out_specs, check_vma=False)
```

```python
import functools
import jax
import jax.numpy as jnp
from jax import lax
from jax.experimental import pallas as pl
from jax.experimental.pallas import tpu as pltpu
from jax.sharding import PartitionSpec as P

HEAD = 128
LOG2E = 1.4426950408889634
NEG = -1e30
QB = 128
VMEM = 24 * 1024 * 1024
F32, BF16 = jnp.float32, jnp.bfloat16


def shifted(shard, axis, by):
    size = lax.axis_size(axis)
    pairs = [(i, i + by) for i in range(size) if 0 <= i + by < size]
    return lax.ppermute(shard, axis, pairs)


def column_part(part):
    queries, keys_part, values = (part[0], part[1], part[2])
    rows = queries.shape[0]
    scale = queries.shape[-1] ** (-0.5)
    scores = (
        jnp.einsum("rchd,schd->chrs", queries, keys_part, preferred_element_type=jnp.float32)
        * scale
    )
    r_idx = lax.broadcasted_iota(jnp.int32, (rows, rows), 0)
    s_idx = lax.broadcasted_iota(jnp.int32, (rows, rows), 1)
    allowed = s_idx <= r_idx - 2
    masked = jnp.where(allowed, scores, jnp.float32(-1e30))
    peak = jnp.max(masked, axis=-1)
    weights = jnp.where(allowed, jnp.exp(masked - peak[..., None]), jnp.float32(0.0))
    total = jnp.maximum(jnp.sum(weights, axis=-1), jnp.float32(1.0))
    rounded = weights.astype(jnp.bfloat16)
    mixed = jnp.einsum("chrs,schd->rchd", rounded, values, preferred_element_type=jnp.float32)
    col_out = (mixed / jnp.transpose(total, (2, 0, 1))[..., None]).astype(jnp.bfloat16)
    col_lse = jnp.transpose(peak + jnp.log(total), (2, 0, 1))
    return (col_out, col_lse)


def row_part(local, previous, first_row):
    rows_dev, cols, heads_local, head_size = (
        local.shape[1],
        local.shape[2],
        local.shape[3],
        local.shape[4],
    )
    scale = head_size ** (-0.5)
    keys_ext = jnp.concatenate([previous, local[1:3]], axis=1)
    key_idx = lax.broadcasted_iota(jnp.int32, (cols, 2 * cols), 1)
    query_idx = lax.broadcasted_iota(jnp.int32, (cols, 2 * cols), 0)

    def one_row(index):
        queries = lax.dynamic_index_in_dim(local[0], index, 0, keepdims=False)
        pair = keys_ext.reshape(2, 2 * cols, heads_local, head_size)
        scores = (
            jnp.einsum("qhd,khd->hqk", queries, pair[0], preferred_element_type=jnp.float32) * scale
        )
        allowed = (key_idx < cols) & (first_row + index > 0) | (key_idx >= cols) & (
            key_idx - cols <= query_idx
        )
        masked = jnp.where(allowed[None], scores, jnp.float32(-1e30))
        peak = jnp.max(masked, axis=-1)
        weights = jnp.where(allowed[None], jnp.exp(masked - peak[..., None]), jnp.float32(0.0))
        total = jnp.sum(weights, axis=-1)
        rounded = weights.astype(jnp.bfloat16)
        mixed = jnp.einsum("hqk,khd->qhd", rounded, pair[1], preferred_element_type=jnp.float32)
        return (mixed / jnp.transpose(total)[..., None], jnp.transpose(peak + jnp.log(total)))

    return lax.map(one_row, jnp.arange(rows_dev, dtype=jnp.int32))


def body_any(qkv, out_weight):
    rows_dev, cols, features = (qkv.shape[1], qkv.shape[2], qkv.shape[3])
    head_size = HEAD
    heads_local = features // head_size
    local = qkv.reshape(3, rows_dev, cols, heads_local, head_size)
    previous = shifted(local[1:3, rows_dev - 1 : rows_dev], "seq", 1)
    first_row = lax.axis_index("seq") * rows_dev
    row_out, row_lse = row_part(local, previous, first_row)
    columns = lax.all_to_all(local, "seq", split_axis=2, concat_axis=1, tiled=True)
    col_part_out, col_part_lse = column_part(columns)
    col_out, col_lse = (
        lax.all_to_all(col_part_out, "seq", split_axis=0, concat_axis=1, tiled=True),
        lax.all_to_all(
            col_part_lse.astype(jnp.bfloat16), "seq", split_axis=0, concat_axis=1, tiled=True
        ).astype(col_part_lse.dtype),
    )
    top = jnp.maximum(row_lse, col_lse)
    left = jnp.exp(row_lse - top)
    right = jnp.exp(col_lse - top)
    attended = (left[..., None] * row_out + right[..., None] * col_out.astype(jnp.float32)) / (
        left + right
    )[..., None]
    attended = attended.astype(jnp.bfloat16).reshape(rows_dev, cols, features)
    terms = jnp.einsum(
        "rcf,fd->crd",
        attended,
        lax.all_gather(out_weight, "seq", axis=1, tiled=True),
        preferred_element_type=jnp.float32,
    )
    summed = lax.psum_scatter(terms.astype(jnp.bfloat16), "head", scatter_dimension=0, tiled=True)
    return summed


def dense_scores(q, k):
    return lax.dot_general(q, k, (((1,), (1,)), ((), ())), preferred_element_type=F32)


def col_scores(q, k):
    prod = q * k
    high = prod.astype(BF16)
    low = (prod - high.astype(F32)).astype(BF16)
    ones = jnp.ones((2 * HEAD, HEAD), BF16)
    return jnp.dot(jnp.concatenate([high, low], axis=1), ones, preferred_element_type=F32)


def with_ones(v):
    return jnp.concatenate([v, jnp.ones_like(v)], axis=1)


def attend(q, dense, cols, coef):
    rows = q.shape[0]
    scores = []
    for k, _, allowed in dense:
        s = dense_scores(q, k)
        scores.append(s if allowed is None else jnp.where(allowed, s, NEG))
    singles = []
    if cols:
        wide = q.astype(F32)
    for k, _, allowed in cols:
        c = col_scores(wide, k)
        singles.append(c if allowed is None else jnp.where(allowed, c, NEG))
    peak = None
    for s in scores:
        for j in range(s.shape[1] // HEAD):
            part = s[:, j * HEAD : (j + 1) * HEAD]
            peak = part if peak is None else jnp.maximum(peak, part)
    if peak is not None:
        peak = jnp.broadcast_to(jnp.max(peak, axis=1, keepdims=True), (rows, HEAD))
    for c in singles:
        peak = c if peak is None else jnp.maximum(peak, c)
    peak = peak * coef
    both = None
    for s, (_, v, _) in zip(scores, dense):
        tiled = jnp.concatenate([peak] * (s.shape[1] // HEAD), axis=1)
        p = jnp.exp2(s * coef - tiled).astype(BF16)
        term = jnp.dot(p, v, preferred_element_type=F32)
        both = term if both is None else both + term
    out = None if both is None else both[:, :HEAD]
    total = None if both is None else both[:, HEAD:]
    for c, (_, v, _) in zip(singles, cols):
        w = jnp.exp2(c * coef - peak)
        total = w if total is None else total + w
        out = w * v if out is None else out + w * v
    return out / total, peak + jnp.log2(total)


def lse_rows(even, odd):
    lane = lax.broadcasted_iota(jnp.int32, (HEAD, HEAD), 1)
    evens, odds = [], []
    for t in range(even.shape[0] // HEAD):
        block = slice(t * HEAD, (t + 1) * HEAD)
        turned = jnp.transpose(jnp.where(lane == 0, even[block], odd[block]))
        evens.append(turned[0:1])
        odds.append(turned[1:2])
    return evens, odds


LSE_ROWS = 16


def put_lse(ref, base, evens, odds):
    rows = jnp.concatenate(evens + odds, axis=0)
    pieces = []
    for _ in range(3):
        pieces.append(rows.astype(BF16).astype(F32))
        rows = rows - pieces[-1]
    spare = LSE_ROWS - 3 * rows.shape[0]
    ref[pl.ds(base, LSE_ROWS), :] = jnp.concatenate(pieces + [jnp.zeros((spare, HEAD), F32)], axis=0).astype(BF16)


def chunk_rows(array, chunk, chunks, parts):
    size = array.shape[0] // parts
    share = size // chunks
    return jnp.concatenate(
        [array[p * size + chunk * share : p * size + (chunk + 1) * share] for p in range(parts)], axis=0)


def stacked(refs):
    return [ref[i] for ref in refs for i in range(ref.shape[0])]


def own_kernel(coef, chunk, chunks, parts, at, q_m, q_o, kv_m, kv_o, *refs):
    x, z = at[0], at[1]
    below = z == 1
    first = x == 0
    *low, out = refs
    cols = q_m.shape[1]
    tokens = cols // chunks

    def pair(a, b):
        return jnp.where(first, a, b), jnp.where(first, b, a)

    def mine(array):
        return chunk_rows(array, chunk, chunks, parts)

    q_e, q_o = pair(mine(q_m[0]), mine(q_o[0]))
    k_e, k_o = pair(kv_m[0], kv_o[0])
    v_e, v_o = pair(kv_m[1], kv_o[1])
    v_e, v_o = with_ones(v_e), with_ones(v_o)
    share = tokens // parts
    index = lax.broadcasted_iota(jnp.int32, (tokens, cols), 0)
    index = (index // share) * (cols // parts) + chunk * share + index % share
    tri = lax.broadcasted_iota(jnp.int32, (tokens, cols), 1) <= index

    def run(even, odd):
        o1, l1 = attend(q_e, [(k_e, v_e, tri)] + even[0], even[1], coef)
        o2, l2 = attend(q_o, [(k_o, v_o, tri), (k_e, v_e, None)], odd, coef)
        out[:tokens] = o1.astype(BF16)
        out[tokens : 2 * tokens] = o2.astype(BF16)
        put_lse(out, 2 * tokens, *lse_rows(l1, l2))

    @pl.when(below)
    def _():
        m_k, m_v, o_k, o_v = stacked(low)
        lk_e, lk_o = pair(m_k, o_k)
        lv_e, lv_o = pair(m_v, o_v)
        col_e = (mine(lk_e).astype(F32), mine(lv_e).astype(F32), None)
        col_o = (mine(lk_o).astype(F32), mine(lv_o).astype(F32), None)
        run(([(lk_o, with_ones(lv_o), None)], [col_e]), [col_e, col_o])

    @pl.when(jnp.logical_not(below))
    def _():
        run(([], []), [])


def upper_kernel(coef, chunk, chunks, parts, at, qa_m, qa_o, qb_m, qb_o, kv_m, kv_o, *refs):
    x, z = at[0], at[1]
    below = z == 1
    first = x == 0
    *low, weight, out_a, out_b = refs
    tokens = qa_m.shape[1] // chunks

    def pair(a, b):
        return jnp.where(first, a, b), jnp.where(first, b, a)

    def mine(array):
        return chunk_rows(array, chunk, chunks, parts)

    k_e, k_o = pair(kv_m[0], kv_o[0])
    v_e, v_o = pair(kv_m[1], kv_o[1])
    ce = (mine(k_e).astype(F32), mine(v_e).astype(F32), None)
    co = (mine(k_o).astype(F32), mine(v_o).astype(F32), None)
    base = chunk * 2 * tokens

    def run(q_m, q_o, out, dense, singles, lower):
        q_e, q_odd = pair(mine(q_m[0]), mine(q_o[0]))
        o1, l1 = attend(q_e, dense, singles + lower, coef)
        o2, l2 = attend(q_odd, [], [ce, co] + lower, coef)
        out[:tokens] = o1.astype(BF16)
        out[tokens : 2 * tokens] = o2.astype(BF16)
        put_lse(out, 2 * tokens, *lse_rows(l1, l2))

    def first_rows(lower):
        run(qa_m, qa_o, out_a, [(k_o, with_ones(v_o), None)], [ce], lower)

    @pl.when(below)
    def _():
        m_k, m_v, o_k, o_v = (mine(part).astype(F32) for part in stacked(low))
        lower = [(m_k, m_v, None), (o_k, o_v, None)]
        first_rows(lower)
        run(qb_m, qb_o, out_b, [], [ce, co], lower)

    @pl.when(jnp.logical_not(below))
    def _():
        out_b[: 2 * tokens] = weight[base : base + 2 * tokens]
        out_b[pl.ds(2 * tokens, LSE_ROWS), :] = jnp.zeros((LSE_ROWS, HEAD), BF16)

    @pl.when(z == 2)
    def _():
        first_rows([])

    @pl.when(z % 3 == 0)
    def _():
        out_a[...] = jnp.zeros(out_a.shape, BF16)


def lse_packed(ref, base, rows):
    packed = ref[pl.ds(base, LSE_ROWS), :].astype(F32)
    return sum(packed[i * rows : (i + 1) * rows] for i in range(3))


def merge_kernel(at, own, oa, ob, out):
    z = at[1]
    tokens = out.shape[1]
    blocks = tokens // HEAD
    rows = 2 * blocks
    l0, l1, l2 = (lse_packed(ref, 2 * tokens, rows) for ref in (own, oa, ob))
    l1, l2 = jnp.where(z >= 2, l1, NEG), jnp.where(z >= 3, l2, NEG)
    top = jnp.maximum(l0, jnp.maximum(l1, l2))
    shares = [jnp.exp2(l - top) for l in (l0, l1, l2)]
    whole = shares[0] + shares[1] + shares[2]
    shares = jnp.concatenate([share / whole for share in shares], axis=0)
    high = shares.astype(BF16).astype(F32)
    spare = jnp.zeros((32 - 6 * rows, HEAD), F32)
    pieces = jnp.concatenate([high, shares - high, spare], axis=0).astype(BF16)
    line = lax.broadcasted_iota(jnp.int32, (32, 3 * HEAD), 0)
    group = lax.broadcasted_iota(jnp.int32, (32, 3 * HEAD), 1) // HEAD
    for row in range(2):
        for block in range(blocks):
            first = row * blocks + block + group * rows
            pick = ((line == first) | (line == first + 3 * rows)).astype(BF16)
            spread = lax.dot_general(pieces, pick, (((0,), (0,)), ((), ())), preferred_element_type=F32)
            mine = slice(row * tokens + block * HEAD, row * tokens + (block + 1) * HEAD)
            mixed = spread[:, :HEAD] * own[mine].astype(F32)
            mixed = mixed + spread[:, HEAD : 2 * HEAD] * oa[mine].astype(F32)
            mixed = mixed + spread[:, 2 * HEAD :] * ob[mine].astype(F32)
            out[row, block * HEAD : (block + 1) * HEAD] = mixed.astype(BF16)


def cost(us):
    return pl.CostEstimate(flops=int(us * 1e8), bytes_accessed=1024, transcendentals=0)


def head_call(kernel, at, args, outs, heads, name, us):
    def spec(shape, start=0):
        lead = len(shape) - 1
        return pl.BlockSpec(tuple(shape[:-1]) + (HEAD,), lambda h, at: (0,) * lead + (start + h,))

    return pl.pallas_call(
        kernel,
        out_shape=outs,
        grid_spec=pltpu.PrefetchScalarGridSpec(
            num_scalar_prefetch=1,
            grid=(heads,),
            in_specs=[spec(a.shape, start) for a, start in args],
            out_specs=[spec(o.shape) for o in outs],
        ),
        compiler_params=pltpu.CompilerParams(vmem_limit_bytes=VMEM),
        cost_estimate=cost(us),
        name=name,
    )(at, *(a for a, _ in args))


def project_kernel(plan, at, *refs):
    x, core = at[0], at[2]
    *arrays, send, keep = refs
    for who, out in ((1 - core, send), (core, keep)):
        for s, (near, far, weight) in enumerate(plan):
            left, right = (
                jnp.concatenate([arrays[i][r, y, who] for y in range(2) for r in range(2)], axis=0)
                for i in (near, far)
            )
            weight = arrays[weight]
            half = left.shape[1]
            top = weight[pl.ds(pl.multiple_of(x * half, half), half)]
            bottom = weight[pl.ds(pl.multiple_of((1 - x) * half, half), half)]
            c = jnp.dot(left, top, preferred_element_type=F32) + jnp.dot(right, bottom, preferred_element_type=F32)
            out[s] = c.astype(BF16).reshape(out.shape[1:])


def project(at, attended, items):
    arrays, plan = [], []

    def place_of(array):
        for i, other in enumerate(arrays):
            if other is array:
                return i
        arrays.append(array)
        return len(arrays) - 1

    for chunk, weight in items:
        plan.append(tuple(place_of(a) for a in attended[chunk] + (weight,)))
    _, _, _, tokens, _ = attended[0][0].shape
    out = jax.ShapeDtypeStruct((len(items), 2, 2, tokens, items[0][1].shape[1]), BF16)
    return whole_call(functools.partial(project_kernel, plan), at, arrays, [out, out], "project", 1 * len(items))


def whole_call(kernel, at, args, outs, name, us):
    return pl.pallas_call(
        kernel,
        out_shape=outs,
        in_specs=[pl.BlockSpec(memory_space=pltpu.SMEM)] + [pl.BlockSpec(memory_space=pltpu.VMEM)] * len(args),
        out_specs=[pl.BlockSpec(memory_space=pltpu.VMEM)] * len(outs),
        compiler_params=pltpu.CompilerParams(vmem_limit_bytes=VMEM),
        cost_estimate=cost(us),
        name=name,
    )(at, *args)


def total(a, b):
    return (a.astype(F32) + b.astype(F32)).astype(BF16)


def split_kernel(at, kept, got, stay, to_y, to_x, to_xy):
    x, y = at[0], at[3]
    for s in range(kept.shape[0]):
        for out, yy, xx in ((to_xy, 1 - y, 1 - x), (to_y, 1 - y, x), (to_x, y, 1 - x), (stay, y, x)):
            out[s] = total(kept[s, yy, xx], got[s, yy, xx])


def halve_kernel(at, kept, got, stay, to_y):
    y = at[3]
    for s in range(kept.shape[0]):
        for r in range(2):
            to_y[s, r] = total(kept[s, 1 - y, r], got[s, 1 - y, r])
            stay[s, r] = total(kept[s, y, r], got[s, y, r])


def row_kernel(at, stay, got, mine, to_x):
    x = at[0]
    for s in range(stay.shape[0]):
        to_x[s] = total(stay[s, 1 - x], got[s, 1 - x])
        mine[s] = total(stay[s, x], got[s, x])


def place_kernel(plan, at, *refs):
    x, z, out = at[0], at[1], refs[-1]
    layers = [z, z + 1 - 2 * (z % 2), (z + 2) % 4, 3 - z]
    refs = iter(refs[:-1])
    for names, hops in plan:
        group = [next(refs) for _ in range(2 * hops)]
        _, tokens, width = group[0].shape
        for s, (chunk, layer) in enumerate(names):
            rows = pl.ds(chunk * tokens, tokens)
            base = 2 * layers[layer]
            mine = pl.ds(pl.multiple_of((base + x) * width, width), width)
            theirs = pl.ds(pl.multiple_of((base + 1 - x) * width, width), width)
            if hops == 1:
                out[rows, mine], out[rows, theirs] = group[0][s], group[1][s]
            else:
                out[rows, mine] = total(group[0][s], group[1][s])
                out[rows, theirs] = total(group[2][s], group[3][s])


def after(value, *earlier):
    return lax.optimization_barrier((value, earlier))[0]


def body_eight(qkv, out_weight):
    _, _, cols, features = qkv.shape
    half = features // 2
    chunks = 2
    heads = half // HEAD
    parts = lax.axis_size("head")
    tokens = cols // chunks
    coef = HEAD ** (-0.5) * LOG2E
    me = lax.axis_index("seq")
    who = lax.axis_index("head")
    z, x, core, y = me // 2, me % 2, who % 2, who // 2
    at = jnp.stack([x, z, core, y]).astype(jnp.int32)
    local = qkv.reshape(3, cols, features)
    first = x == 0

    def seq_perm(array, *layers, cross=False):
        pairs = [(2 * a + i, 2 * b + (1 - i if cross else i)) for a, b in layers for i in range(2)]
        return lax.ppermute(array, "seq", pairs)

    def swap(array):
        return seq_perm(array, (0, 0), (1, 1), (2, 2), (3, 3), cross=True)

    def head_perm(array, flip):
        return lax.ppermute(array, "head", [(i, i ^ flip) for i in range(4)])

    def lanes(lo, hi, part, source=local):
        return lax.dynamic_slice(source, (lo, 0, part * half), (hi - lo, cols, half))

    down, two_down = [(2, 1), (3, 2)], [(3, 1)]
    q_m = lanes(0, 1, x)
    q_o = swap(lanes(0, 1, 1 - x))
    qs = [seq_perm(q_m, *down), None, seq_perm(q_m, *two_down), None]
    kv_m, kv_give = lanes(1, 3, x), lanes(1, 3, 1 - x)
    block = out_weight.reshape(kv_m.shape)
    low_m = seq_perm(jnp.where(z == 0, kv_m, block), (0, 1), (1, 3))
    pairs = [(i, 2 + 1 - i) for i in range(2)] + [(2 + i, i) for i in range(2)] + [(4 + i, 6 + i) for i in range(2)]
    low_o = lax.ppermute(after(jnp.where(z == 0, kv_give, block), q_o), "seq", pairs)
    kv_o = swap(after(kv_give, q_o, qs[0]))
    qs[1], qs[3] = seq_perm(q_o, *down), seq_perm(q_o, *two_down)

    struct = jax.ShapeDtypeStruct
    partial = struct((2 * tokens + LSE_ROWS, half), BF16)
    oa, ob, own = [], [], []
    turn = at
    kvs = [kv_m, kv_o, low_m, low_o]
    for c in range(chunks):
        a, b = head_call(
            functools.partial(upper_kernel, coef, c, chunks, parts), turn, [(a, 0) for a in qs + kvs + [out_weight]],
            [partial] * 2, heads, "upper_rows", 7)
        turn = after(at, a)
        oa.append(seq_perm(a, (1, 2), (2, 3)))
        ob.append(seq_perm(b, (1, 3), (0, 1), (3, 2)))
    def own_rows(c, turn):
        (mine,) = head_call(
            functools.partial(own_kernel, coef, c, chunks, parts), turn, [(a, 0) for a in [q_m, q_o] + kvs],
            [partial], heads, "own_rows", 6)
        return mine

    own.append(own_rows(0, turn))
    w_down = seq_perm(after(out_weight, *qs), (0, 2), (2, 0), (3, 1))

    def merged(c, earlier):
        (a,) = head_call(
            merge_kernel, after(at, earlier), [(a[c], 0) for a in (own, oa, ob)],
            [struct((2, tokens, half), BF16)], heads, "merge", 2)
        shape = (2, 2, 2, tokens // 4, half)
        return a.reshape(shape), swap(a).reshape(shape)

    attended = [merged(0, own[0])]
    w_far = jnp.where(z == 3, low_m.reshape(out_weight.shape), after(w_down, attended[0][0]))
    own.append(own_rows(1, after(at, w_far)))
    w_other = seq_perm(w_far, (0, 1), (1, 0), (2, 3), (3, 2))
    parts_out, plan = [], []

    def summed(turn, names):
        send, kept = project(turn, attended, [(c, weights[layer]) for c, layer in names])
        return send.shape[:1] + send.shape[3:], [kept, head_perm(send, 1)]

    w_near = jnp.where(
        (z == 0) | (z == 3), low_o.reshape(out_weight.shape), jnp.concatenate([o[: 2 * tokens] for o in after(ob, own[1])]))
    attended.append(merged(1, (w_far, attended[0][1], w_near)))
    weights = {0: out_weight, 1: w_near, 2: w_far, 3: w_other}
    names = [(0, 0), (0, 1)]
    size, pair = summed(at, names)
    both = struct(size[:1] + (2,) + size[1:], BF16)
    stay, to_y = whole_call(halve_kernel, at, pair, [both] * 2, "halve", 2)
    from_y = head_perm(to_y, 2)
    mine, to_x = whole_call(row_kernel, at, [stay, from_y], [struct(size, BF16)] * 2, "rows", 1)
    parts_out += [mine, swap(to_x)]
    plan.append((names, 1))

    names = [(1, 0), (1, 1), (1, 2), (1, 3), (0, 2), (0, 3)]
    size, pair = summed(after(at, mine), names)
    stay, to_y, to_x, to_xy = whole_call(split_kernel, at, pair, [struct(size, BF16)] * 4, "split", 2)
    diagonal = [
        ((2 * i + j) * 4 + h, (2 * i + 1 - j) * 4 + (h ^ 2)) for i in range(4) for j in range(2) for h in range(4)
    ]
    parts_out += [stay, head_perm(to_y, 2), swap(to_x), lax.ppermute(to_xy, ("seq", "head"), diagonal)]
    plan.append((names, 2))
    (out,) = whole_call(
        functools.partial(place_kernel, plan), at, parts_out,
        [struct((cols // 4, 8 * out_weight.shape[1]), BF16)], "place", 2)
    return out.reshape(cols // 4, 1, 8 * out_weight.shape[1])


def solution(mesh):
    in_specs = (P(None, "seq", None, "head"), P("head", "seq"))
    out_specs = P("head", "seq", None)
    small = mesh.shape["seq"] == 8 and mesh.shape["head"] == 4

    def body(qkv, out_weight):
        _, rows, cols, features = qkv.shape
        even = features == 2 * cols and out_weight.shape == (features, cols) and cols % 512 == 0
        if small and rows == 1 and even:
            return body_eight(qkv, out_weight)
        return body_any(qkv, out_weight)

    return jax.shard_map(body, mesh=mesh, in_specs=in_specs, out_specs=out_specs, check_vma=False)
```

```python
import functools
import jax
import jax.numpy as jnp
from jax import lax
from jax.experimental import pallas as pl
from jax.experimental.pallas import tpu as pltpu
from jax.sharding import PartitionSpec as P

HEAD = 128
LOG2E = 1.4426950408889634
NEG = -1e30
QB = 128
VMEM = 24 * 1024 * 1024
F32, BF16 = jnp.float32, jnp.bfloat16


def shifted(shard, axis, by):
    size = lax.axis_size(axis)
    pairs = [(i, i + by) for i in range(size) if 0 <= i + by < size]
    return lax.ppermute(shard, axis, pairs)


def column_part(part):
    queries, keys_part, values = (part[0], part[1], part[2])
    rows = queries.shape[0]
    scale = queries.shape[-1] ** (-0.5)
    scores = (
        jnp.einsum("rchd,schd->chrs", queries, keys_part, preferred_element_type=jnp.float32)
        * scale
    )
    r_idx = lax.broadcasted_iota(jnp.int32, (rows, rows), 0)
    s_idx = lax.broadcasted_iota(jnp.int32, (rows, rows), 1)
    allowed = s_idx <= r_idx - 2
    masked = jnp.where(allowed, scores, jnp.float32(-1e30))
    peak = jnp.max(masked, axis=-1)
    weights = jnp.where(allowed, jnp.exp(masked - peak[..., None]), jnp.float32(0.0))
    total = jnp.maximum(jnp.sum(weights, axis=-1), jnp.float32(1.0))
    rounded = weights.astype(jnp.bfloat16)
    mixed = jnp.einsum("chrs,schd->rchd", rounded, values, preferred_element_type=jnp.float32)
    col_out = (mixed / jnp.transpose(total, (2, 0, 1))[..., None]).astype(jnp.bfloat16)
    col_lse = jnp.transpose(peak + jnp.log(total), (2, 0, 1))
    return (col_out, col_lse)


def row_part(local, previous, first_row):
    rows_dev, cols, heads_local, head_size = (
        local.shape[1],
        local.shape[2],
        local.shape[3],
        local.shape[4],
    )
    scale = head_size ** (-0.5)
    keys_ext = jnp.concatenate([previous, local[1:3]], axis=1)
    key_idx = lax.broadcasted_iota(jnp.int32, (cols, 2 * cols), 1)
    query_idx = lax.broadcasted_iota(jnp.int32, (cols, 2 * cols), 0)

    def one_row(index):
        queries = lax.dynamic_index_in_dim(local[0], index, 0, keepdims=False)
        pair = keys_ext.reshape(2, 2 * cols, heads_local, head_size)
        scores = (
            jnp.einsum("qhd,khd->hqk", queries, pair[0], preferred_element_type=jnp.float32) * scale
        )
        allowed = (key_idx < cols) & (first_row + index > 0) | (key_idx >= cols) & (
            key_idx - cols <= query_idx
        )
        masked = jnp.where(allowed[None], scores, jnp.float32(-1e30))
        peak = jnp.max(masked, axis=-1)
        weights = jnp.where(allowed[None], jnp.exp(masked - peak[..., None]), jnp.float32(0.0))
        total = jnp.sum(weights, axis=-1)
        rounded = weights.astype(jnp.bfloat16)
        mixed = jnp.einsum("hqk,khd->qhd", rounded, pair[1], preferred_element_type=jnp.float32)
        return (mixed / jnp.transpose(total)[..., None], jnp.transpose(peak + jnp.log(total)))

    return lax.map(one_row, jnp.arange(rows_dev, dtype=jnp.int32))


def body_any(qkv, out_weight):
    rows_dev, cols, features = (qkv.shape[1], qkv.shape[2], qkv.shape[3])
    head_size = HEAD
    heads_local = features // head_size
    local = qkv.reshape(3, rows_dev, cols, heads_local, head_size)
    previous = shifted(local[1:3, rows_dev - 1 : rows_dev], "seq", 1)
    first_row = lax.axis_index("seq") * rows_dev
    row_out, row_lse = row_part(local, previous, first_row)
    columns = lax.all_to_all(local, "seq", split_axis=2, concat_axis=1, tiled=True)
    col_part_out, col_part_lse = column_part(columns)
    col_out, col_lse = (
        lax.all_to_all(col_part_out, "seq", split_axis=0, concat_axis=1, tiled=True),
        lax.all_to_all(
            col_part_lse.astype(jnp.bfloat16), "seq", split_axis=0, concat_axis=1, tiled=True
        ).astype(col_part_lse.dtype),
    )
    top = jnp.maximum(row_lse, col_lse)
    left = jnp.exp(row_lse - top)
    right = jnp.exp(col_lse - top)
    attended = (left[..., None] * row_out + right[..., None] * col_out.astype(jnp.float32)) / (
        left + right
    )[..., None]
    attended = attended.astype(jnp.bfloat16).reshape(rows_dev, cols, features)
    terms = jnp.einsum(
        "rcf,fd->crd",
        attended,
        lax.all_gather(out_weight, "seq", axis=1, tiled=True),
        preferred_element_type=jnp.float32,
    )
    summed = lax.psum_scatter(terms.astype(jnp.bfloat16), "head", scatter_dimension=0, tiled=True)
    return summed


def dense_scores(q, k):
    return lax.dot_general(q, k, (((1,), (1,)), ((), ())), preferred_element_type=F32)


def col_scores(q, k):
    prod = q * k
    high = prod.astype(BF16)
    low = (prod - high.astype(F32)).astype(BF16)
    ones = jnp.ones((2 * HEAD, HEAD), BF16)
    return jnp.dot(jnp.concatenate([high, low], axis=1), ones, preferred_element_type=F32)


def with_ones(v):
    return jnp.concatenate([v, jnp.ones_like(v)], axis=1)


def attend(q, dense, cols, coef):
    rows = q.shape[0]
    scores = []
    for k, _, allowed in dense:
        s = dense_scores(q, k)
        scores.append(s if allowed is None else jnp.where(allowed, s, NEG))
    singles = []
    if cols:
        wide = q.astype(F32)
    for k, _, allowed in cols:
        c = col_scores(wide, k)
        singles.append(c if allowed is None else jnp.where(allowed, c, NEG))
    peak = None
    for s in scores:
        for j in range(s.shape[1] // HEAD):
            part = s[:, j * HEAD : (j + 1) * HEAD]
            peak = part if peak is None else jnp.maximum(peak, part)
    if peak is not None:
        peak = jnp.broadcast_to(jnp.max(peak, axis=1, keepdims=True), (rows, HEAD))
    for c in singles:
        peak = c if peak is None else jnp.maximum(peak, c)
    peak = peak * coef
    both = None
    for s, (_, v, _) in zip(scores, dense):
        tiled = jnp.concatenate([peak] * (s.shape[1] // HEAD), axis=1)
        p = jnp.exp2(s * coef - tiled).astype(BF16)
        term = jnp.dot(p, v, preferred_element_type=F32)
        both = term if both is None else both + term
    out = None if both is None else both[:, :HEAD]
    total = None if both is None else both[:, HEAD:]
    for c, (_, v, _) in zip(singles, cols):
        w = jnp.exp2(c * coef - peak)
        total = w if total is None else total + w
        out = w * v if out is None else out + w * v
    return out / total, peak + jnp.log2(total)


def lse_rows(even, odd):
    lane = lax.broadcasted_iota(jnp.int32, (HEAD, HEAD), 1)
    evens, odds = [], []
    for t in range(even.shape[0] // HEAD):
        block = slice(t * HEAD, (t + 1) * HEAD)
        turned = jnp.transpose(jnp.where(lane == 0, even[block], odd[block]))
        evens.append(turned[0:1])
        odds.append(turned[1:2])
    return evens, odds


LSE_ROWS = 16


def put_lse(ref, base, evens, odds):
    rows = jnp.concatenate(evens + odds, axis=0)
    pieces = []
    for _ in range(3):
        pieces.append(rows.astype(BF16).astype(F32))
        rows = rows - pieces[-1]
    spare = LSE_ROWS - 3 * rows.shape[0]
    ref[pl.ds(base, LSE_ROWS), :] = jnp.concatenate(pieces + [jnp.zeros((spare, HEAD), F32)], axis=0).astype(BF16)


def chunk_rows(array, chunk, chunks, parts):
    size = array.shape[0] // parts
    share = size // chunks
    return jnp.concatenate(
        [array[p * size + chunk * share : p * size + (chunk + 1) * share] for p in range(parts)], axis=0)


def stacked(refs):
    return [ref[i] for ref in refs for i in range(ref.shape[0])]


def own_kernel(coef, chunk, chunks, parts, at, q_m, q_o, kv_m, kv_o, *refs):
    x, z = at[0], at[1]
    below = z == 1
    first = x == 0
    *low, out = refs
    cols = q_m.shape[1]
    tokens = cols // chunks

    def pair(a, b):
        return jnp.where(first, a, b), jnp.where(first, b, a)

    def mine(array):
        return chunk_rows(array, chunk, chunks, parts)

    q_e, q_o = pair(mine(q_m[0]), mine(q_o[0]))
    k_e, k_o = pair(kv_m[0], kv_o[0])
    v_e, v_o = pair(kv_m[1], kv_o[1])
    v_e, v_o = with_ones(v_e), with_ones(v_o)
    share = tokens // parts
    index = lax.broadcasted_iota(jnp.int32, (tokens, cols), 0)
    index = (index // share) * (cols // parts) + chunk * share + index % share
    tri = lax.broadcasted_iota(jnp.int32, (tokens, cols), 1) <= index

    def run(even, odd):
        o1, l1 = attend(q_e, [(k_e, v_e, tri)] + even[0], even[1], coef)
        o2, l2 = attend(q_o, [(k_o, v_o, tri), (k_e, v_e, None)], odd, coef)
        out[:tokens] = o1.astype(BF16)
        out[tokens : 2 * tokens] = o2.astype(BF16)
        put_lse(out, 2 * tokens, *lse_rows(l1, l2))

    @pl.when(below)
    def _():
        m_k, m_v, o_k, o_v = stacked(low)
        lk_e, lk_o = pair(m_k, o_k)
        lv_e, lv_o = pair(m_v, o_v)
        col_e = (mine(lk_e).astype(F32), mine(lv_e).astype(F32), None)
        col_o = (mine(lk_o).astype(F32), mine(lv_o).astype(F32), None)
        run(([(lk_o, with_ones(lv_o), None)], [col_e]), [col_e, col_o])

    @pl.when(jnp.logical_not(below))
    def _():
        run(([], []), [])


def upper_kernel(coef, chunk, chunks, parts, at, qa_m, qa_o, qb_m, qb_o, kv_m, kv_o, *refs):
    x, z = at[0], at[1]
    below = z == 1
    first = x == 0
    *low, weight, out_a, out_b = refs
    tokens = qa_m.shape[1] // chunks

    def pair(a, b):
        return jnp.where(first, a, b), jnp.where(first, b, a)

    def mine(array):
        return chunk_rows(array, chunk, chunks, parts)

    k_e, k_o = pair(kv_m[0], kv_o[0])
    v_e, v_o = pair(kv_m[1], kv_o[1])
    ce = (mine(k_e).astype(F32), mine(v_e).astype(F32), None)
    co = (mine(k_o).astype(F32), mine(v_o).astype(F32), None)
    base = chunk * 2 * tokens

    def run(q_m, q_o, out, dense, singles, lower):
        q_e, q_odd = pair(mine(q_m[0]), mine(q_o[0]))
        o1, l1 = attend(q_e, dense, singles + lower, coef)
        o2, l2 = attend(q_odd, [], [ce, co] + lower, coef)
        out[:tokens] = o1.astype(BF16)
        out[tokens : 2 * tokens] = o2.astype(BF16)
        put_lse(out, 2 * tokens, *lse_rows(l1, l2))

    def first_rows(lower):
        run(qa_m, qa_o, out_a, [(k_o, with_ones(v_o), None)], [ce], lower)

    @pl.when(below)
    def _():
        m_k, m_v, o_k, o_v = (mine(part).astype(F32) for part in stacked(low))
        lower = [(m_k, m_v, None), (o_k, o_v, None)]
        first_rows(lower)
        run(qb_m, qb_o, out_b, [], [ce, co], lower)

    @pl.when(jnp.logical_not(below))
    def _():
        out_b[: 2 * tokens] = weight[base : base + 2 * tokens]
        out_b[pl.ds(2 * tokens, LSE_ROWS), :] = jnp.zeros((LSE_ROWS, HEAD), BF16)

    @pl.when(z == 2)
    def _():
        first_rows([])

    @pl.when(z % 3 == 0)
    def _():
        out_a[...] = jnp.zeros(out_a.shape, BF16)


def lse_packed(ref, base, rows):
    packed = ref[pl.ds(base, LSE_ROWS), :].astype(F32)
    return sum(packed[i * rows : (i + 1) * rows] for i in range(3))


def merge_kernel(at, own, oa, ob, out):
    z = at[1]
    tokens = out.shape[1]
    blocks = tokens // HEAD
    rows = 2 * blocks
    l0, l1, l2 = (lse_packed(ref, 2 * tokens, rows) for ref in (own, oa, ob))
    l1, l2 = jnp.where(z >= 2, l1, NEG), jnp.where(z >= 3, l2, NEG)
    top = jnp.maximum(l0, jnp.maximum(l1, l2))
    shares = [jnp.exp2(l - top) for l in (l0, l1, l2)]
    whole = shares[0] + shares[1] + shares[2]
    shares = jnp.concatenate([share / whole for share in shares], axis=0)
    high = shares.astype(BF16).astype(F32)
    spare = jnp.zeros((32 - 6 * rows, HEAD), F32)
    pieces = jnp.concatenate([high, shares - high, spare], axis=0).astype(BF16)
    line = lax.broadcasted_iota(jnp.int32, (32, 3 * HEAD), 0)
    group = lax.broadcasted_iota(jnp.int32, (32, 3 * HEAD), 1) // HEAD
    for row in range(2):
        for block in range(blocks):
            first = row * blocks + block + group * rows
            pick = ((line == first) | (line == first + 3 * rows)).astype(BF16)
            spread = lax.dot_general(pieces, pick, (((0,), (0,)), ((), ())), preferred_element_type=F32)
            mine = slice(row * tokens + block * HEAD, row * tokens + (block + 1) * HEAD)
            mixed = spread[:, :HEAD] * own[mine].astype(F32)
            mixed = mixed + spread[:, HEAD : 2 * HEAD] * oa[mine].astype(F32)
            mixed = mixed + spread[:, 2 * HEAD :] * ob[mine].astype(F32)
            out[row, block * HEAD : (block + 1) * HEAD] = mixed.astype(BF16)


def cost(us):
    return pl.CostEstimate(flops=int(us * 1e8), bytes_accessed=1024, transcendentals=0)


def head_call(kernel, at, args, outs, heads, name, us):
    def spec(shape, start=0):
        lead = len(shape) - 1
        return pl.BlockSpec(tuple(shape[:-1]) + (HEAD,), lambda h, at: (0,) * lead + (start + h,))

    return pl.pallas_call(
        kernel,
        out_shape=outs,
        grid_spec=pltpu.PrefetchScalarGridSpec(
            num_scalar_prefetch=1,
            grid=(heads,),
            in_specs=[spec(a.shape, start) for a, start in args],
            out_specs=[spec(o.shape) for o in outs],
        ),
        compiler_params=pltpu.CompilerParams(vmem_limit_bytes=VMEM),
        cost_estimate=cost(us),
        name=name,
    )(at, *(a for a, _ in args))


def project_kernel(plan, at, *refs):
    x, core = at[0], at[2]
    *arrays, send, keep = refs
    for who, out in ((1 - core, send), (core, keep)):
        for s, (near, far, weight) in enumerate(plan):
            left, right = (
                jnp.concatenate([arrays[i][r, y, who] for y in range(2) for r in range(2)], axis=0)
                for i in (near, far)
            )
            weight = arrays[weight]
            half = left.shape[1]
            top = weight[pl.ds(pl.multiple_of(x * half, half), half)]
            bottom = weight[pl.ds(pl.multiple_of((1 - x) * half, half), half)]
            c = jnp.dot(left, top, preferred_element_type=F32) + jnp.dot(right, bottom, preferred_element_type=F32)
            out[s] = c.astype(BF16).reshape(out.shape[1:])


def project(at, attended, items):
    arrays, plan = [], []

    def place_of(array):
        for i, other in enumerate(arrays):
            if other is array:
                return i
        arrays.append(array)
        return len(arrays) - 1

    for chunk, weight in items:
        plan.append(tuple(place_of(a) for a in attended[chunk] + (weight,)))
    _, _, _, tokens, _ = attended[0][0].shape
    out = jax.ShapeDtypeStruct((len(items), 2, 2, tokens, items[0][1].shape[1]), BF16)
    return whole_call(functools.partial(project_kernel, plan), at, arrays, [out, out], "project", 1 * len(items))


def whole_call(kernel, at, args, outs, name, us):
    return pl.pallas_call(
        kernel,
        out_shape=outs,
        in_specs=[pl.BlockSpec(memory_space=pltpu.SMEM)] + [pl.BlockSpec(memory_space=pltpu.VMEM)] * len(args),
        out_specs=[pl.BlockSpec(memory_space=pltpu.VMEM)] * len(outs),
        compiler_params=pltpu.CompilerParams(vmem_limit_bytes=VMEM),
        cost_estimate=cost(us),
        name=name,
    )(at, *args)


def total(a, b):
    return (a.astype(F32) + b.astype(F32)).astype(BF16)


def split_kernel(at, kept, got, stay, to_y, to_x, to_xy):
    x, y = at[0], at[3]
    for s in range(kept.shape[0]):
        for out, yy, xx in ((to_xy, 1 - y, 1 - x), (to_y, 1 - y, x), (to_x, y, 1 - x), (stay, y, x)):
            out[s] = total(kept[s, yy, xx], got[s, yy, xx])


def halve_kernel(at, kept, got, stay, to_y):
    y = at[3]
    for s in range(kept.shape[0]):
        for r in range(2):
            to_y[s, r] = total(kept[s, 1 - y, r], got[s, 1 - y, r])
            stay[s, r] = total(kept[s, y, r], got[s, y, r])


def row_kernel(at, stay, got, mine, to_x):
    x = at[0]
    for s in range(stay.shape[0]):
        to_x[s] = total(stay[s, 1 - x], got[s, 1 - x])
        mine[s] = total(stay[s, x], got[s, x])


def place_kernel(plan, at, *refs):
    x, z, out = at[0], at[1], refs[-1]
    layers = [z, z + 1 - 2 * (z % 2), (z + 2) % 4, 3 - z]
    refs = iter(refs[:-1])
    for names, hops in plan:
        group = [next(refs) for _ in range(2 * hops)]
        _, tokens, width = group[0].shape
        for s, (chunk, layer) in enumerate(names):
            rows = pl.ds(chunk * tokens, tokens)
            base = 2 * layers[layer]
            mine = pl.ds(pl.multiple_of((base + x) * width, width), width)
            theirs = pl.ds(pl.multiple_of((base + 1 - x) * width, width), width)
            if hops == 1:
                out[rows, mine], out[rows, theirs] = group[0][s], group[1][s]
            else:
                out[rows, mine] = total(group[0][s], group[1][s])
                out[rows, theirs] = total(group[2][s], group[3][s])


def after(value, *earlier):
    return lax.optimization_barrier((value, earlier))[0]


def body_eight(qkv, out_weight):
    _, _, cols, features = qkv.shape
    half = features // 2
    chunks = 2
    heads = half // HEAD
    parts = lax.axis_size("head")
    tokens = cols // chunks
    coef = HEAD ** (-0.5) * LOG2E
    me = lax.axis_index("seq")
    who = lax.axis_index("head")
    z, x, core, y = me // 2, me % 2, who % 2, who // 2
    at = jnp.stack([x, z, core, y]).astype(jnp.int32)
    local = qkv.reshape(3, cols, features)
    first = x == 0

    def seq_perm(array, *layers, cross=False):
        pairs = [(2 * a + i, 2 * b + (1 - i if cross else i)) for a, b in layers for i in range(2)]
        return lax.ppermute(array, "seq", pairs)

    def swap(array):
        return seq_perm(array, (0, 0), (1, 1), (2, 2), (3, 3), cross=True)

    def head_perm(array, flip):
        return lax.ppermute(array, "head", [(i, i ^ flip) for i in range(4)])

    def lanes(lo, hi, part, source=local):
        return lax.dynamic_slice(source, (lo, 0, part * half), (hi - lo, cols, half))

    down, two_down = [(2, 1), (3, 2)], [(3, 1)]
    q_m = lanes(0, 1, x)
    q_o = swap(lanes(0, 1, 1 - x))
    qs = [seq_perm(q_m, *down), None, seq_perm(q_m, *two_down), None]
    kv_m, kv_give = lanes(1, 3, x), lanes(1, 3, 1 - x)
    block = out_weight.reshape(kv_m.shape)
    low_m = seq_perm(jnp.where(z == 0, kv_m, block), (0, 1), (1, 3))
    pairs = [(i, 2 + 1 - i) for i in range(2)] + [(2 + i, i) for i in range(2)] + [(4 + i, 6 + i) for i in range(2)]
    low_o = lax.ppermute(after(jnp.where(z == 0, kv_give, block), q_o), "seq", pairs)
    kv_o = swap(after(kv_give, q_o, qs[0]))
    qs[1], qs[3] = seq_perm(q_o, *down), seq_perm(q_o, *two_down)

    struct = jax.ShapeDtypeStruct
    partial = struct((2 * tokens + LSE_ROWS, half), BF16)
    oa, ob, own = [], [], []
    turn = at
    kvs = [kv_m, kv_o, low_m, low_o]
    for c in range(chunks):
        a, b = head_call(
            functools.partial(upper_kernel, coef, c, chunks, parts), turn, [(a, 0) for a in qs + kvs + [out_weight]],
            [partial] * 2, heads, "upper_rows", 7)
        turn = after(at, a)
        oa.append(seq_perm(a, (1, 2), (2, 3)))
        ob.append(seq_perm(b, (1, 3), (0, 1), (3, 2)))
    def own_rows(c, turn):
        (mine,) = head_call(
            functools.partial(own_kernel, coef, c, chunks, parts), turn, [(a, 0) for a in [q_m, q_o] + kvs],
            [partial], heads, "own_rows", 6)
        return mine

    own.append(own_rows(0, turn))
    w_down = seq_perm(after(out_weight, *qs), (0, 2), (2, 0), (3, 1))

    def merged(c, earlier):
        (a,) = head_call(
            merge_kernel, after(at, earlier), [(a[c], 0) for a in (own, oa, ob)],
            [struct((2, tokens, half), BF16)], heads, "merge", 2)
        shape = (2, 2, 2, tokens // 4, half)
        return a.reshape(shape), swap(a).reshape(shape)

    attended = [merged(0, own[0])]
    w_far = jnp.where(z == 3, low_m.reshape(out_weight.shape), after(w_down, attended[0][0]))
    own.append(own_rows(1, after(at, w_far)))
    w_other = seq_perm(w_far, (0, 1), (1, 0), (2, 3), (3, 2))
    parts_out, plan = [], []

    def summed(turn, names):
        send, kept = project(turn, attended, [(c, weights[layer]) for c, layer in names])
        return send.shape[:1] + send.shape[3:], [kept, head_perm(send, 1)]

    w_near = jnp.where(
        (z == 0) | (z == 3), low_o.reshape(out_weight.shape), jnp.concatenate([o[: 2 * tokens] for o in after(ob, own[1])]))
    attended.append(merged(1, (w_far, attended[0][1], w_near)))
    weights = {0: out_weight, 1: w_near, 2: w_far, 3: w_other}
    names = [(0, 0), (0, 1)]
    size, pair = summed(at, names)
    both = struct(size[:1] + (2,) + size[1:], BF16)
    stay, to_y = whole_call(halve_kernel, at, pair, [both] * 2, "halve", 2)
    from_y = head_perm(to_y, 2)
    mine, to_x = whole_call(row_kernel, at, [stay, from_y], [struct(size, BF16)] * 2, "rows", 1)
    parts_out += [mine, swap(to_x)]
    plan.append((names, 1))

    diagonal = [
        ((2 * i + j) * 4 + h, (2 * i + 1 - j) * 4 + (h ^ 2)) for i in range(4) for j in range(2) for h in range(4)
    ]
    turn = after(at, mine)
    for names in ([(1, 0), (1, 1), (0, 2)], [(1, 2), (1, 3), (0, 3)]):
        size, pair = summed(turn, names)
        turn = after(at, pair[0])
        stay, to_y, to_x, to_xy = whole_call(split_kernel, at, pair, [struct(size, BF16)] * 4, "split", 2)
        parts_out += [stay, head_perm(to_y, 2), swap(to_x), lax.ppermute(to_xy, ("seq", "head"), diagonal)]
        plan.append((names, 2))
    (out,) = whole_call(
        functools.partial(place_kernel, plan), at, parts_out,
        [struct((cols // 4, 8 * out_weight.shape[1]), BF16)], "place", 2)
    return out.reshape(cols // 4, 1, 8 * out_weight.shape[1])


def solution(mesh):
    in_specs = (P(None, "seq", None, "head"), P("head", "seq"))
    out_specs = P("head", "seq", None)
    small = mesh.shape["seq"] == 8 and mesh.shape["head"] == 4

    def body(qkv, out_weight):
        _, rows, cols, features = qkv.shape
        even = features == 2 * cols and out_weight.shape == (features, cols) and cols % 512 == 0
        if small and rows == 1 and even:
            return body_eight(qkv, out_weight)
        return body_any(qkv, out_weight)

    return jax.shard_map(body, mesh=mesh, in_specs=in_specs, out_specs=out_specs, check_vma=False)
```

```python
import functools
import jax
import jax.numpy as jnp
from jax import lax
from jax.experimental import pallas as pl
from jax.experimental.pallas import tpu as pltpu
from jax.sharding import PartitionSpec as P

HEAD = 128
LOG2E = 1.4426950408889634
NEG = -1e30
QB = 128
VMEM = 24 * 1024 * 1024
F32, BF16 = jnp.float32, jnp.bfloat16


def shifted(shard, axis, by):
    size = lax.axis_size(axis)
    pairs = [(i, i + by) for i in range(size) if 0 <= i + by < size]
    return lax.ppermute(shard, axis, pairs)


def column_part(part):
    queries, keys_part, values = (part[0], part[1], part[2])
    rows = queries.shape[0]
    scale = queries.shape[-1] ** (-0.5)
    scores = (
        jnp.einsum("rchd,schd->chrs", queries, keys_part, preferred_element_type=jnp.float32)
        * scale
    )
    r_idx = lax.broadcasted_iota(jnp.int32, (rows, rows), 0)
    s_idx = lax.broadcasted_iota(jnp.int32, (rows, rows), 1)
    allowed = s_idx <= r_idx - 2
    masked = jnp.where(allowed, scores, jnp.float32(-1e30))
    peak = jnp.max(masked, axis=-1)
    weights = jnp.where(allowed, jnp.exp(masked - peak[..., None]), jnp.float32(0.0))
    total = jnp.maximum(jnp.sum(weights, axis=-1), jnp.float32(1.0))
    rounded = weights.astype(jnp.bfloat16)
    mixed = jnp.einsum("chrs,schd->rchd", rounded, values, preferred_element_type=jnp.float32)
    col_out = (mixed / jnp.transpose(total, (2, 0, 1))[..., None]).astype(jnp.bfloat16)
    col_lse = jnp.transpose(peak + jnp.log(total), (2, 0, 1))
    return (col_out, col_lse)


def row_part(local, previous, first_row):
    rows_dev, cols, heads_local, head_size = (
        local.shape[1],
        local.shape[2],
        local.shape[3],
        local.shape[4],
    )
    scale = head_size ** (-0.5)
    keys_ext = jnp.concatenate([previous, local[1:3]], axis=1)
    key_idx = lax.broadcasted_iota(jnp.int32, (cols, 2 * cols), 1)
    query_idx = lax.broadcasted_iota(jnp.int32, (cols, 2 * cols), 0)

    def one_row(index):
        queries = lax.dynamic_index_in_dim(local[0], index, 0, keepdims=False)
        pair = keys_ext.reshape(2, 2 * cols, heads_local, head_size)
        scores = (
            jnp.einsum("qhd,khd->hqk", queries, pair[0], preferred_element_type=jnp.float32) * scale
        )
        allowed = (key_idx < cols) & (first_row + index > 0) | (key_idx >= cols) & (
            key_idx - cols <= query_idx
        )
        masked = jnp.where(allowed[None], scores, jnp.float32(-1e30))
        peak = jnp.max(masked, axis=-1)
        weights = jnp.where(allowed[None], jnp.exp(masked - peak[..., None]), jnp.float32(0.0))
        total = jnp.sum(weights, axis=-1)
        rounded = weights.astype(jnp.bfloat16)
        mixed = jnp.einsum("hqk,khd->qhd", rounded, pair[1], preferred_element_type=jnp.float32)
        return (mixed / jnp.transpose(total)[..., None], jnp.transpose(peak + jnp.log(total)))

    return lax.map(one_row, jnp.arange(rows_dev, dtype=jnp.int32))


def body_any(qkv, out_weight):
    rows_dev, cols, features = (qkv.shape[1], qkv.shape[2], qkv.shape[3])
    head_size = HEAD
    heads_local = features // head_size
    local = qkv.reshape(3, rows_dev, cols, heads_local, head_size)
    previous = shifted(local[1:3, rows_dev - 1 : rows_dev], "seq", 1)
    first_row = lax.axis_index("seq") * rows_dev
    row_out, row_lse = row_part(local, previous, first_row)
    columns = lax.all_to_all(local, "seq", split_axis=2, concat_axis=1, tiled=True)
    col_part_out, col_part_lse = column_part(columns)
    col_out, col_lse = (
        lax.all_to_all(col_part_out, "seq", split_axis=0, concat_axis=1, tiled=True),
        lax.all_to_all(
            col_part_lse.astype(jnp.bfloat16), "seq", split_axis=0, concat_axis=1, tiled=True
        ).astype(col_part_lse.dtype),
    )
    top = jnp.maximum(row_lse, col_lse)
    left = jnp.exp(row_lse - top)
    right = jnp.exp(col_lse - top)
    attended = (left[..., None] * row_out + right[..., None] * col_out.astype(jnp.float32)) / (
        left + right
    )[..., None]
    attended = attended.astype(jnp.bfloat16).reshape(rows_dev, cols, features)
    terms = jnp.einsum(
        "rcf,fd->crd",
        attended,
        lax.all_gather(out_weight, "seq", axis=1, tiled=True),
        preferred_element_type=jnp.float32,
    )
    summed = lax.psum_scatter(terms.astype(jnp.bfloat16), "head", scatter_dimension=0, tiled=True)
    return summed


def dense_scores(q, k):
    return lax.dot_general(q, k, (((1,), (1,)), ((), ())), preferred_element_type=F32)


def col_scores(q, k):
    prod = q * k
    high = prod.astype(BF16)
    low = (prod - high.astype(F32)).astype(BF16)
    ones = jnp.ones((2 * HEAD, HEAD), BF16)
    return jnp.dot(jnp.concatenate([high, low], axis=1), ones, preferred_element_type=F32)


def with_ones(v):
    return jnp.concatenate([v, jnp.ones_like(v)], axis=1)


def attend(q, dense, cols, coef):
    rows = q.shape[0]
    scores = []
    for k, _, allowed in dense:
        s = dense_scores(q, k)
        scores.append(s if allowed is None else jnp.where(allowed, s, NEG))
    singles = []
    if cols:
        wide = q.astype(F32)
    for k, _, allowed in cols:
        c = col_scores(wide, k)
        singles.append(c if allowed is None else jnp.where(allowed, c, NEG))
    peak = None
    for s in scores:
        for j in range(s.shape[1] // HEAD):
            part = s[:, j * HEAD : (j + 1) * HEAD]
            peak = part if peak is None else jnp.maximum(peak, part)
    if peak is not None:
        peak = jnp.broadcast_to(jnp.max(peak, axis=1, keepdims=True), (rows, HEAD))
    for c in singles:
        peak = c if peak is None else jnp.maximum(peak, c)
    peak = peak * coef
    both = None
    for s, (_, v, _) in zip(scores, dense):
        tiled = jnp.concatenate([peak] * (s.shape[1] // HEAD), axis=1)
        p = jnp.exp2(s * coef - tiled).astype(BF16)
        term = jnp.dot(p, v, preferred_element_type=F32)
        both = term if both is None else both + term
    out = None if both is None else both[:, :HEAD]
    total = None if both is None else both[:, HEAD:]
    for c, (_, v, _) in zip(singles, cols):
        w = jnp.exp2(c * coef - peak)
        total = w if total is None else total + w
        out = w * v if out is None else out + w * v
    return out / total, peak + jnp.log2(total)


def lse_rows(even, odd):
    lane = lax.broadcasted_iota(jnp.int32, (HEAD, HEAD), 1)
    evens, odds = [], []
    for t in range(even.shape[0] // HEAD):
        block = slice(t * HEAD, (t + 1) * HEAD)
        turned = jnp.transpose(jnp.where(lane == 0, even[block], odd[block]))
        evens.append(turned[0:1])
        odds.append(turned[1:2])
    return evens, odds


LSE_ROWS = 16


def put_lse(ref, base, evens, odds):
    rows = jnp.concatenate(evens + odds, axis=0)
    pieces = []
    for _ in range(3):
        pieces.append(rows.astype(BF16).astype(F32))
        rows = rows - pieces[-1]
    spare = LSE_ROWS - 3 * rows.shape[0]
    ref[pl.ds(base, LSE_ROWS), :] = jnp.concatenate(pieces + [jnp.zeros((spare, HEAD), F32)], axis=0).astype(BF16)


def chunk_rows(array, chunk, chunks, parts):
    size = array.shape[0] // parts
    share = size // chunks
    return jnp.concatenate(
        [array[p * size + chunk * share : p * size + (chunk + 1) * share] for p in range(parts)], axis=0)


def stacked(refs):
    return [ref[i] for ref in refs for i in range(ref.shape[0])]


def own_kernel(coef, chunk, chunks, parts, at, q_m, q_o, kv_m, kv_o, *refs):
    x, z = at[0], at[1]
    below = z == 1
    first = x == 0
    *low, out = refs
    cols = q_m.shape[1]
    tokens = cols // chunks

    def pair(a, b):
        return jnp.where(first, a, b), jnp.where(first, b, a)

    def mine(array):
        return chunk_rows(array, chunk, chunks, parts)

    q_e, q_o = pair(mine(q_m[0]), mine(q_o[0]))
    k_e, k_o = pair(kv_m[0], kv_o[0])
    v_e, v_o = pair(kv_m[1], kv_o[1])
    v_e, v_o = with_ones(v_e), with_ones(v_o)
    share = tokens // parts
    index = lax.broadcasted_iota(jnp.int32, (tokens, cols), 0)
    index = (index // share) * (cols // parts) + chunk * share + index % share
    tri = lax.broadcasted_iota(jnp.int32, (tokens, cols), 1) <= index

    def run(even, odd):
        o1, l1 = attend(q_e, [(k_e, v_e, tri)] + even[0], even[1], coef)
        o2, l2 = attend(q_o, [(k_o, v_o, tri), (k_e, v_e, None)], odd, coef)
        out[:tokens] = o1.astype(BF16)
        out[tokens : 2 * tokens] = o2.astype(BF16)
        put_lse(out, 2 * tokens, *lse_rows(l1, l2))

    @pl.when(below)
    def _():
        m_k, m_v, o_k, o_v = stacked(low)
        lk_e, lk_o = pair(m_k, o_k)
        lv_e, lv_o = pair(m_v, o_v)
        col_e = (mine(lk_e).astype(F32), mine(lv_e).astype(F32), None)
        col_o = (mine(lk_o).astype(F32), mine(lv_o).astype(F32), None)
        run(([(lk_o, with_ones(lv_o), None)], [col_e]), [col_e, col_o])

    @pl.when(jnp.logical_not(below))
    def _():
        run(([], []), [])


def upper_kernel(coef, chunk, chunks, parts, at, qa_m, qa_o, qb_m, qb_o, kv_m, kv_o, *refs):
    x, z = at[0], at[1]
    below = z == 1
    first = x == 0
    *low, weight, out_a, out_b = refs
    tokens = qa_m.shape[1] // chunks

    def pair(a, b):
        return jnp.where(first, a, b), jnp.where(first, b, a)

    def mine(array):
        return chunk_rows(array, chunk, chunks, parts)

    k_e, k_o = pair(kv_m[0], kv_o[0])
    v_e, v_o = pair(kv_m[1], kv_o[1])
    ce = (mine(k_e).astype(F32), mine(v_e).astype(F32), None)
    co = (mine(k_o).astype(F32), mine(v_o).astype(F32), None)
    base = chunk * 2 * tokens

    def run(q_m, q_o, out, dense, singles, lower):
        q_e, q_odd = pair(mine(q_m[0]), mine(q_o[0]))
        o1, l1 = attend(q_e, dense, singles + lower, coef)
        o2, l2 = attend(q_odd, [], [ce, co] + lower, coef)
        out[:tokens] = o1.astype(BF16)
        out[tokens : 2 * tokens] = o2.astype(BF16)
        put_lse(out, 2 * tokens, *lse_rows(l1, l2))

    def first_rows(lower):
        run(qa_m, qa_o, out_a, [(k_o, with_ones(v_o), None)], [ce], lower)

    @pl.when(below)
    def _():
        m_k, m_v, o_k, o_v = (mine(part).astype(F32) for part in stacked(low))
        lower = [(m_k, m_v, None), (o_k, o_v, None)]
        first_rows(lower)
        run(qb_m, qb_o, out_b, [], [ce, co], lower)

    @pl.when(jnp.logical_not(below))
    def _():
        out_b[: 2 * tokens] = weight[base : base + 2 * tokens]
        out_b[pl.ds(2 * tokens, LSE_ROWS), :] = jnp.zeros((LSE_ROWS, HEAD), BF16)

    @pl.when(z == 2)
    def _():
        first_rows([])

    @pl.when(z % 3 == 0)
    def _():
        out_a[...] = jnp.zeros(out_a.shape, BF16)


def merge_kernel(heads, at, own, oa, ob, out):
    z = at[1]
    tokens = out.shape[1]
    blocks = tokens // HEAD
    rows = 2 * blocks
    line = lax.broadcasted_iota(jnp.int32, (32, 3 * HEAD), 0)
    group = lax.broadcasted_iota(jnp.int32, (32, 3 * HEAD), 1) // HEAD
    picks = []
    for first in range(rows):
        at_line = first + group * rows
        picks.append(((line == at_line) | (line == at_line + 3 * rows)).astype(BF16))
    for head in range(heads):
        lanes = slice(head * HEAD, (head + 1) * HEAD)

        def totals(ref):
            packed = ref[pl.ds(2 * tokens, LSE_ROWS), lanes].astype(F32)
            return sum(packed[i * rows : (i + 1) * rows] for i in range(3))

        l0, l1, l2 = (totals(ref) for ref in (own, oa, ob))
        l1, l2 = jnp.where(z >= 2, l1, NEG), jnp.where(z >= 3, l2, NEG)
        top = jnp.maximum(l0, jnp.maximum(l1, l2))
        shares = [jnp.exp2(l - top) for l in (l0, l1, l2)]
        whole = shares[0] + shares[1] + shares[2]
        shares = jnp.concatenate([share / whole for share in shares], axis=0)
        high = shares.astype(BF16).astype(F32)
        spare = jnp.zeros((32 - 6 * rows, HEAD), F32)
        pieces = jnp.concatenate([high, shares - high, spare], axis=0).astype(BF16)
        for row in range(2):
            for block in range(blocks):
                pick = picks[row * blocks + block]
                spread = lax.dot_general(pieces, pick, (((0,), (0,)), ((), ())), preferred_element_type=F32)
                mine = slice(row * tokens + block * HEAD, row * tokens + (block + 1) * HEAD)
                mixed = spread[:, :HEAD] * own[mine, lanes].astype(F32)
                mixed = mixed + spread[:, HEAD : 2 * HEAD] * oa[mine, lanes].astype(F32)
                mixed = mixed + spread[:, 2 * HEAD :] * ob[mine, lanes].astype(F32)
                out[row, block * HEAD : (block + 1) * HEAD, lanes] = mixed.astype(BF16)


def cost(us):
    return pl.CostEstimate(flops=int(us * 1e8), bytes_accessed=1024, transcendentals=0)


def head_call(kernel, at, args, outs, heads, name, us):
    def spec(shape, start=0):
        lead = len(shape) - 1
        return pl.BlockSpec(tuple(shape[:-1]) + (HEAD,), lambda h, at: (0,) * lead + (start + h,))

    return pl.pallas_call(
        kernel,
        out_shape=outs,
        grid_spec=pltpu.PrefetchScalarGridSpec(
            num_scalar_prefetch=1,
            grid=(heads,),
            in_specs=[spec(a.shape, start) for a, start in args],
            out_specs=[spec(o.shape) for o in outs],
        ),
        compiler_params=pltpu.CompilerParams(vmem_limit_bytes=VMEM),
        cost_estimate=cost(us),
        name=name,
    )(at, *(a for a, _ in args))


def project_kernel(plan, at, *refs):
    x, core = at[0], at[2]
    *arrays, send, keep = refs
    for who, out in ((1 - core, send), (core, keep)):
        for s, (near, far, weight) in enumerate(plan):
            left, right = (
                jnp.concatenate([arrays[i][r, y, who] for y in range(2) for r in range(2)], axis=0)
                for i in (near, far)
            )
            weight = arrays[weight]
            half = left.shape[1]
            top = weight[pl.ds(pl.multiple_of(x * half, half), half)]
            bottom = weight[pl.ds(pl.multiple_of((1 - x) * half, half), half)]
            c = jnp.dot(left, top, preferred_element_type=F32) + jnp.dot(right, bottom, preferred_element_type=F32)
            out[s] = c.astype(BF16).reshape(out.shape[1:])


def project(at, attended, items):
    arrays, plan = [], []

    def place_of(array):
        for i, other in enumerate(arrays):
            if other is array:
                return i
        arrays.append(array)
        return len(arrays) - 1

    for chunk, weight in items:
        plan.append(tuple(place_of(a) for a in attended[chunk] + (weight,)))
    _, _, _, tokens, _ = attended[0][0].shape
    out = jax.ShapeDtypeStruct((len(items), 2, 2, tokens, items[0][1].shape[1]), BF16)
    return whole_call(functools.partial(project_kernel, plan), at, arrays, [out, out], "project", 1 * len(items))


def whole_call(kernel, at, args, outs, name, us):
    return pl.pallas_call(
        kernel,
        out_shape=outs,
        in_specs=[pl.BlockSpec(memory_space=pltpu.SMEM)] + [pl.BlockSpec(memory_space=pltpu.VMEM)] * len(args),
        out_specs=[pl.BlockSpec(memory_space=pltpu.VMEM)] * len(outs),
        compiler_params=pltpu.CompilerParams(vmem_limit_bytes=VMEM),
        cost_estimate=cost(us),
        name=name,
    )(at, *args)


def total(a, b):
    return (a.astype(F32) + b.astype(F32)).astype(BF16)


def split_kernel(at, kept, got, stay, to_y, to_x, to_xy):
    x, y = at[0], at[3]
    for s in range(kept.shape[0]):
        for out, yy, xx in ((to_xy, 1 - y, 1 - x), (to_y, 1 - y, x), (to_x, y, 1 - x), (stay, y, x)):
            out[s] = total(kept[s, yy, xx], got[s, yy, xx])


def halve_kernel(at, kept, got, stay, to_y):
    y = at[3]
    for s in range(kept.shape[0]):
        for r in range(2):
            to_y[s, r] = total(kept[s, 1 - y, r], got[s, 1 - y, r])
            stay[s, r] = total(kept[s, y, r], got[s, y, r])


def row_kernel(at, stay, got, mine, to_x):
    x = at[0]
    for s in range(stay.shape[0]):
        to_x[s] = total(stay[s, 1 - x], got[s, 1 - x])
        mine[s] = total(stay[s, x], got[s, x])


def place_kernel(plan, at, *refs):
    x, z, out = at[0], at[1], refs[-1]
    layers = [z, z + 1 - 2 * (z % 2), (z + 2) % 4, 3 - z]
    refs = iter(refs[:-1])
    for names, hops in plan:
        group = [next(refs) for _ in range(2 * hops)]
        _, tokens, width = group[0].shape
        for s, (chunk, layer) in enumerate(names):
            rows = pl.ds(chunk * tokens, tokens)
            base = 2 * layers[layer]
            mine = pl.ds(pl.multiple_of((base + x) * width, width), width)
            theirs = pl.ds(pl.multiple_of((base + 1 - x) * width, width), width)
            if hops == 1:
                out[rows, mine], out[rows, theirs] = group[0][s], group[1][s]
            else:
                out[rows, mine] = total(group[0][s], group[1][s])
                out[rows, theirs] = total(group[2][s], group[3][s])


def after(value, *earlier):
    return lax.optimization_barrier((value, earlier))[0]


def body_eight(qkv, out_weight):
    _, _, cols, features = qkv.shape
    half = features // 2
    chunks = 2
    heads = half // HEAD
    parts = lax.axis_size("head")
    tokens = cols // chunks
    coef = HEAD ** (-0.5) * LOG2E
    me = lax.axis_index("seq")
    who = lax.axis_index("head")
    z, x, core, y = me // 2, me % 2, who % 2, who // 2
    at = jnp.stack([x, z, core, y]).astype(jnp.int32)
    local = qkv.reshape(3, cols, features)
    first = x == 0

    def seq_perm(array, *layers, cross=False):
        pairs = [(2 * a + i, 2 * b + (1 - i if cross else i)) for a, b in layers for i in range(2)]
        return lax.ppermute(array, "seq", pairs)

    def swap(array):
        return seq_perm(array, (0, 0), (1, 1), (2, 2), (3, 3), cross=True)

    def head_perm(array, flip):
        return lax.ppermute(array, "head", [(i, i ^ flip) for i in range(4)])

    def lanes(lo, hi, part, source=local):
        return lax.dynamic_slice(source, (lo, 0, part * half), (hi - lo, cols, half))

    down, two_down = [(2, 1), (3, 2)], [(3, 1)]
    q_m = lanes(0, 1, x)
    q_o = swap(lanes(0, 1, 1 - x))
    qs = [seq_perm(q_m, *down), None, seq_perm(q_m, *two_down), None]
    kv_m, kv_give = lanes(1, 3, x), lanes(1, 3, 1 - x)
    block = out_weight.reshape(kv_m.shape)
    low_m = seq_perm(jnp.where(z == 0, kv_m, block), (0, 1), (1, 3))
    pairs = [(i, 2 + 1 - i) for i in range(2)] + [(2 + i, i) for i in range(2)] + [(4 + i, 6 + i) for i in range(2)]
    low_o = lax.ppermute(after(jnp.where(z == 0, kv_give, block), q_o), "seq", pairs)
    kv_o = swap(after(kv_give, q_o, qs[0]))
    qs[1], qs[3] = seq_perm(q_o, *down), seq_perm(q_o, *two_down)

    struct = jax.ShapeDtypeStruct
    partial = struct((2 * tokens + LSE_ROWS, half), BF16)
    oa, ob, own = [], [], []
    turn = at
    kvs = [kv_m, kv_o, low_m, low_o]
    for c in range(chunks):
        a, b = head_call(
            functools.partial(upper_kernel, coef, c, chunks, parts), turn, [(a, 0) for a in qs + kvs + [out_weight]],
            [partial] * 2, heads, "upper_rows", 7)
        turn = after(at, a)
        oa.append(seq_perm(a, (1, 2), (2, 3)))
        ob.append(seq_perm(b, (1, 3), (0, 1), (3, 2)))
    def own_rows(c, turn):
        (mine,) = head_call(
            functools.partial(own_kernel, coef, c, chunks, parts), turn, [(a, 0) for a in [q_m, q_o] + kvs],
            [partial], heads, "own_rows", 6)
        return mine

    own.append(own_rows(0, turn))
    w_down = seq_perm(after(out_weight, *qs), (0, 2), (2, 0), (3, 1))

    def merged(c, earlier):
        (a,) = whole_call(
            functools.partial(merge_kernel, heads), after(at, earlier), [own[c], oa[c], ob[c]],
            [struct((2, tokens, half), BF16)], "merge", 2)
        shape = (2, 2, 2, tokens // 4, half)
        return a.reshape(shape), swap(a).reshape(shape)

    attended = [merged(0, own[0])]
    w_far = jnp.where(z == 3, low_m.reshape(out_weight.shape), after(w_down, attended[0][0]))
    own.append(own_rows(1, after(at, w_far)))
    w_other = seq_perm(w_far, (0, 1), (1, 0), (2, 3), (3, 2))
    parts_out, plan = [], []

    def summed(turn, names):
        send, kept = project(turn, attended, [(c, weights[layer]) for c, layer in names])
        return send.shape[:1] + send.shape[3:], [kept, head_perm(send, 1)]

    w_near = jnp.where(
        (z == 0) | (z == 3), low_o.reshape(out_weight.shape), jnp.concatenate([o[: 2 * tokens] for o in after(ob, own[1])]))
    attended.append(merged(1, (w_far, attended[0][1], w_near)))
    weights = {0: out_weight, 1: w_near, 2: w_far, 3: w_other}
    names = [(0, 0), (0, 1)]
    size, pair = summed(at, names)
    both = struct(size[:1] + (2,) + size[1:], BF16)
    stay, to_y = whole_call(halve_kernel, at, pair, [both] * 2, "halve", 2)
    from_y = head_perm(to_y, 2)
    mine, to_x = whole_call(row_kernel, at, [stay, from_y], [struct(size, BF16)] * 2, "rows", 1)
    parts_out += [mine, swap(to_x)]
    plan.append((names, 1))

    diagonal = [
        ((2 * i + j) * 4 + h, (2 * i + 1 - j) * 4 + (h ^ 2)) for i in range(4) for j in range(2) for h in range(4)
    ]
    turn = after(at, mine)
    for names in ([(1, 0), (1, 1), (0, 2)], [(1, 2), (1, 3), (0, 3)]):
        size, pair = summed(turn, names)
        turn = after(at, pair[0])
        stay, to_y, to_x, to_xy = whole_call(split_kernel, at, pair, [struct(size, BF16)] * 4, "split", 2)
        parts_out += [stay, head_perm(to_y, 2), swap(to_x), lax.ppermute(to_xy, ("seq", "head"), diagonal)]
        plan.append((names, 2))
    (out,) = whole_call(
        functools.partial(place_kernel, plan), at, parts_out,
        [struct((cols // 4, 8 * out_weight.shape[1]), BF16)], "place", 2)
    return out.reshape(cols // 4, 1, 8 * out_weight.shape[1])


def solution(mesh):
    in_specs = (P(None, "seq", None, "head"), P("head", "seq"))
    out_specs = P("head", "seq", None)
    small = mesh.shape["seq"] == 8 and mesh.shape["head"] == 4

    def body(qkv, out_weight):
        _, rows, cols, features = qkv.shape
        even = features == 2 * cols and out_weight.shape == (features, cols) and cols % 512 == 0
        if small and rows == 1 and even:
            return body_eight(qkv, out_weight)
        return body_any(qkv, out_weight)

    return jax.shard_map(body, mesh=mesh, in_specs=in_specs, out_specs=out_specs, check_vma=False)
```

```python
import functools
import jax
import jax.numpy as jnp
from jax import lax
from jax.experimental import pallas as pl
from jax.experimental.pallas import tpu as pltpu
from jax.sharding import PartitionSpec as P

HEAD = 128
LOG2E = 1.4426950408889634
NEG = -1e30
QB = 128
VMEM = 24 * 1024 * 1024
F32, BF16 = jnp.float32, jnp.bfloat16


def shifted(shard, axis, by):
    size = lax.axis_size(axis)
    pairs = [(i, i + by) for i in range(size) if 0 <= i + by < size]
    return lax.ppermute(shard, axis, pairs)


def column_part(part):
    queries, keys_part, values = (part[0], part[1], part[2])
    rows = queries.shape[0]
    scale = queries.shape[-1] ** (-0.5)
    scores = (
        jnp.einsum("rchd,schd->chrs", queries, keys_part, preferred_element_type=jnp.float32)
        * scale
    )
    r_idx = lax.broadcasted_iota(jnp.int32, (rows, rows), 0)
    s_idx = lax.broadcasted_iota(jnp.int32, (rows, rows), 1)
    allowed = s_idx <= r_idx - 2
    masked = jnp.where(allowed, scores, jnp.float32(-1e30))
    peak = jnp.max(masked, axis=-1)
    weights = jnp.where(allowed, jnp.exp(masked - peak[..., None]), jnp.float32(0.0))
    total = jnp.maximum(jnp.sum(weights, axis=-1), jnp.float32(1.0))
    rounded = weights.astype(jnp.bfloat16)
    mixed = jnp.einsum("chrs,schd->rchd", rounded, values, preferred_element_type=jnp.float32)
    col_out = (mixed / jnp.transpose(total, (2, 0, 1))[..., None]).astype(jnp.bfloat16)
    col_lse = jnp.transpose(peak + jnp.log(total), (2, 0, 1))
    return (col_out, col_lse)


def row_part(local, previous, first_row):
    rows_dev, cols, heads_local, head_size = (
        local.shape[1],
        local.shape[2],
        local.shape[3],
        local.shape[4],
    )
    scale = head_size ** (-0.5)
    keys_ext = jnp.concatenate([previous, local[1:3]], axis=1)
    key_idx = lax.broadcasted_iota(jnp.int32, (cols, 2 * cols), 1)
    query_idx = lax.broadcasted_iota(jnp.int32, (cols, 2 * cols), 0)

    def one_row(index):
        queries = lax.dynamic_index_in_dim(local[0], index, 0, keepdims=False)
        pair = keys_ext.reshape(2, 2 * cols, heads_local, head_size)
        scores = (
            jnp.einsum("qhd,khd->hqk", queries, pair[0], preferred_element_type=jnp.float32) * scale
        )
        allowed = (key_idx < cols) & (first_row + index > 0) | (key_idx >= cols) & (
            key_idx - cols <= query_idx
        )
        masked = jnp.where(allowed[None], scores, jnp.float32(-1e30))
        peak = jnp.max(masked, axis=-1)
        weights = jnp.where(allowed[None], jnp.exp(masked - peak[..., None]), jnp.float32(0.0))
        total = jnp.sum(weights, axis=-1)
        rounded = weights.astype(jnp.bfloat16)
        mixed = jnp.einsum("hqk,khd->qhd", rounded, pair[1], preferred_element_type=jnp.float32)
        return (mixed / jnp.transpose(total)[..., None], jnp.transpose(peak + jnp.log(total)))

    return lax.map(one_row, jnp.arange(rows_dev, dtype=jnp.int32))


def body_any(qkv, out_weight):
    rows_dev, cols, features = (qkv.shape[1], qkv.shape[2], qkv.shape[3])
    head_size = HEAD
    heads_local = features // head_size
    local = qkv.reshape(3, rows_dev, cols, heads_local, head_size)
    previous = shifted(local[1:3, rows_dev - 1 : rows_dev], "seq", 1)
    first_row = lax.axis_index("seq") * rows_dev
    row_out, row_lse = row_part(local, previous, first_row)
    columns = lax.all_to_all(local, "seq", split_axis=2, concat_axis=1, tiled=True)
    col_part_out, col_part_lse = column_part(columns)
    col_out, col_lse = (
        lax.all_to_all(col_part_out, "seq", split_axis=0, concat_axis=1, tiled=True),
        lax.all_to_all(
            col_part_lse.astype(jnp.bfloat16), "seq", split_axis=0, concat_axis=1, tiled=True
        ).astype(col_part_lse.dtype),
    )
    top = jnp.maximum(row_lse, col_lse)
    left = jnp.exp(row_lse - top)
    right = jnp.exp(col_lse - top)
    attended = (left[..., None] * row_out + right[..., None] * col_out.astype(jnp.float32)) / (
        left + right
    )[..., None]
    attended = attended.astype(jnp.bfloat16).reshape(rows_dev, cols, features)
    terms = jnp.einsum(
        "rcf,fd->crd",
        attended,
        lax.all_gather(out_weight, "seq", axis=1, tiled=True),
        preferred_element_type=jnp.float32,
    )
    summed = lax.psum_scatter(terms.astype(jnp.bfloat16), "head", scatter_dimension=0, tiled=True)
    return summed


def dense_scores(q, k):
    return lax.dot_general(q, k, (((1,), (1,)), ((), ())), preferred_element_type=F32)


def col_scores(q, k):
    prod = q * k
    high = prod.astype(BF16)
    low = (prod - high.astype(F32)).astype(BF16)
    ones = jnp.ones((2 * HEAD, HEAD), BF16)
    return jnp.dot(jnp.concatenate([high, low], axis=1), ones, preferred_element_type=F32)


def with_ones(v):
    return jnp.concatenate([v, jnp.ones_like(v)], axis=1)


def attend(q, dense, cols, coef):
    rows = q.shape[0]
    scores = []
    for k, _, allowed in dense:
        s = dense_scores(q, k)
        scores.append(s if allowed is None else jnp.where(allowed, s, NEG))
    singles = []
    if cols:
        wide = q.astype(F32)
    for k, _, allowed in cols:
        c = col_scores(wide, k)
        singles.append(c if allowed is None else jnp.where(allowed, c, NEG))
    peak = None
    for s in scores:
        for j in range(s.shape[1] // HEAD):
            part = s[:, j * HEAD : (j + 1) * HEAD]
            peak = part if peak is None else jnp.maximum(peak, part)
    if peak is not None:
        peak = jnp.broadcast_to(jnp.max(peak, axis=1, keepdims=True), (rows, HEAD))
    for c in singles:
        peak = c if peak is None else jnp.maximum(peak, c)
    peak = peak * coef
    both = None
    for s, (_, v, _) in zip(scores, dense):
        tiled = jnp.concatenate([peak] * (s.shape[1] // HEAD), axis=1)
        p = jnp.exp2(s * coef - tiled).astype(BF16)
        term = jnp.dot(p, v, preferred_element_type=F32)
        both = term if both is None else both + term
    out = None if both is None else both[:, :HEAD]
    total = None if both is None else both[:, HEAD:]
    for c, (_, v, _) in zip(singles, cols):
        w = jnp.exp2(c * coef - peak)
        total = w if total is None else total + w
        out = w * v if out is None else out + w * v
    return out / total, peak + jnp.log2(total)


def lse_rows(even, odd):
    lane = lax.broadcasted_iota(jnp.int32, (HEAD, HEAD), 1)
    evens, odds = [], []
    for t in range(even.shape[0] // HEAD):
        block = slice(t * HEAD, (t + 1) * HEAD)
        turned = jnp.transpose(jnp.where(lane == 0, even[block], odd[block]))
        evens.append(turned[0:1])
        odds.append(turned[1:2])
    return evens, odds


LSE_ROWS = 16


def put_lse(ref, base, evens, odds):
    rows = jnp.concatenate(evens + odds, axis=0)
    pieces = []
    for _ in range(3):
        pieces.append(rows.astype(BF16).astype(F32))
        rows = rows - pieces[-1]
    spare = LSE_ROWS - 3 * rows.shape[0]
    ref[pl.ds(base, LSE_ROWS), :] = jnp.concatenate(pieces + [jnp.zeros((spare, HEAD), F32)], axis=0).astype(BF16)


def chunk_rows(array, chunk, chunks, parts):
    size = array.shape[0] // parts
    share = size // chunks
    return jnp.concatenate(
        [array[p * size + chunk * share : p * size + (chunk + 1) * share] for p in range(parts)], axis=0)


def stacked(refs):
    return [ref[i] for ref in refs for i in range(ref.shape[0])]


def own_kernel(coef, chunk, chunks, parts, at, q_m, q_o, kv_m, kv_o, *refs):
    x, z = at[0], at[1]
    below = z == 1
    first = x == 0
    *low, out = refs
    cols = q_m.shape[1]
    tokens = cols // chunks

    def pair(a, b):
        return jnp.where(first, a, b), jnp.where(first, b, a)

    def mine(array):
        return chunk_rows(array, chunk, chunks, parts)

    q_e, q_o = pair(mine(q_m[0]), mine(q_o[0]))
    k_e, k_o = pair(kv_m[0], kv_o[0])
    v_e, v_o = pair(kv_m[1], kv_o[1])
    v_e, v_o = with_ones(v_e), with_ones(v_o)
    share = tokens // parts
    index = lax.broadcasted_iota(jnp.int32, (tokens, cols), 0)
    index = (index // share) * (cols // parts) + chunk * share + index % share
    tri = lax.broadcasted_iota(jnp.int32, (tokens, cols), 1) <= index

    def run(even, odd):
        o1, l1 = attend(q_e, [(k_e, v_e, tri)] + even[0], even[1], coef)
        o2, l2 = attend(q_o, [(k_o, v_o, tri), (k_e, v_e, None)], odd, coef)
        out[:tokens] = o1.astype(BF16)
        out[tokens : 2 * tokens] = o2.astype(BF16)
        put_lse(out, 2 * tokens, *lse_rows(l1, l2))

    @pl.when(below)
    def _():
        m_k, m_v, o_k, o_v = stacked(low)
        lk_e, lk_o = pair(m_k, o_k)
        lv_e, lv_o = pair(m_v, o_v)
        col_e = (mine(lk_e).astype(F32), mine(lv_e).astype(F32), None)
        col_o = (mine(lk_o).astype(F32), mine(lv_o).astype(F32), None)
        run(([(lk_o, with_ones(lv_o), None)], [col_e]), [col_e, col_o])

    @pl.when(jnp.logical_not(below))
    def _():
        run(([], []), [])


def upper_kernel(coef, chunk, chunks, parts, at, qa_m, qa_o, qb_m, qb_o, kv_m, kv_o, *refs):
    x, z = at[0], at[1]
    below = z == 1
    first = x == 0
    *low, weight, out_a, out_b = refs
    tokens = qa_m.shape[1] // chunks

    def pair(a, b):
        return jnp.where(first, a, b), jnp.where(first, b, a)

    def mine(array):
        return chunk_rows(array, chunk, chunks, parts)

    k_e, k_o = pair(kv_m[0], kv_o[0])
    v_e, v_o = pair(kv_m[1], kv_o[1])
    ce = (mine(k_e).astype(F32), mine(v_e).astype(F32), None)
    co = (mine(k_o).astype(F32), mine(v_o).astype(F32), None)
    base = chunk * 2 * tokens

    def run(q_m, q_o, out, dense, singles, lower):
        q_e, q_odd = pair(mine(q_m[0]), mine(q_o[0]))
        o1, l1 = attend(q_e, dense, singles + lower, coef)
        o2, l2 = attend(q_odd, [], [ce, co] + lower, coef)
        out[:tokens] = o1.astype(BF16)
        out[tokens : 2 * tokens] = o2.astype(BF16)
        put_lse(out, 2 * tokens, *lse_rows(l1, l2))

    def first_rows(lower):
        run(qa_m, qa_o, out_a, [(k_o, with_ones(v_o), None)], [ce], lower)

    @pl.when(below)
    def _():
        m_k, m_v, o_k, o_v = (mine(part).astype(F32) for part in stacked(low))
        lower = [(m_k, m_v, None), (o_k, o_v, None)]
        first_rows(lower)
        run(qb_m, qb_o, out_b, [], [ce, co], lower)

    @pl.when(jnp.logical_not(below))
    def _():
        out_b[: 2 * tokens] = weight[base : base + 2 * tokens]
        out_b[pl.ds(2 * tokens, LSE_ROWS), :] = jnp.zeros((LSE_ROWS, HEAD), BF16)

    @pl.when(z == 2)
    def _():
        first_rows([])

    @pl.when(z % 3 == 0)
    def _():
        out_a[...] = jnp.zeros(out_a.shape, BF16)


def merge_kernel(heads, at, own, oa, ob, out):
    z = at[1]
    tokens = out.shape[1]
    blocks = tokens // HEAD
    rows = 2 * blocks
    line = lax.broadcasted_iota(jnp.int32, (32, 3 * HEAD), 0)
    group = lax.broadcasted_iota(jnp.int32, (32, 3 * HEAD), 1) // HEAD
    picks = []
    for first in range(rows):
        at_line = first + group * rows
        picks.append(((line == at_line) | (line == at_line + 3 * rows)).astype(BF16))
    for head in range(heads):
        lanes = slice(head * HEAD, (head + 1) * HEAD)

        def totals(ref):
            packed = ref[pl.ds(2 * tokens, LSE_ROWS), lanes].astype(F32)
            return sum(packed[i * rows : (i + 1) * rows] for i in range(3))

        l0, l1, l2 = (totals(ref) for ref in (own, oa, ob))
        l1, l2 = jnp.where(z >= 2, l1, NEG), jnp.where(z >= 3, l2, NEG)
        top = jnp.maximum(l0, jnp.maximum(l1, l2))
        shares = [jnp.exp2(l - top) for l in (l0, l1, l2)]
        whole = shares[0] + shares[1] + shares[2]
        shares = jnp.concatenate([share / whole for share in shares], axis=0)
        high = shares.astype(BF16).astype(F32)
        spare = jnp.zeros((32 - 6 * rows, HEAD), F32)
        pieces = jnp.concatenate([high, shares - high, spare], axis=0).astype(BF16)
        for row in range(2):
            for block in range(blocks):
                pick = picks[row * blocks + block]
                spread = lax.dot_general(pieces, pick, (((0,), (0,)), ((), ())), preferred_element_type=F32)
                mine = slice(row * tokens + block * HEAD, row * tokens + (block + 1) * HEAD)
                mixed = spread[:, :HEAD] * own[mine, lanes].astype(F32)
                mixed = mixed + spread[:, HEAD : 2 * HEAD] * oa[mine, lanes].astype(F32)
                mixed = mixed + spread[:, 2 * HEAD :] * ob[mine, lanes].astype(F32)
                out[row, block * HEAD : (block + 1) * HEAD, lanes] = mixed.astype(BF16)


def cost(us):
    return pl.CostEstimate(flops=int(us * 1e8), bytes_accessed=1024, transcendentals=0)


def head_call(kernel, at, args, outs, heads, name, us):
    def spec(shape, start=0):
        lead = len(shape) - 1
        return pl.BlockSpec(tuple(shape[:-1]) + (HEAD,), lambda h, at: (0,) * lead + (start + h,))

    return pl.pallas_call(
        kernel,
        out_shape=outs,
        grid_spec=pltpu.PrefetchScalarGridSpec(
            num_scalar_prefetch=1,
            grid=(heads,),
            in_specs=[spec(a.shape, start) for a, start in args],
            out_specs=[spec(o.shape) for o in outs],
        ),
        compiler_params=pltpu.CompilerParams(vmem_limit_bytes=VMEM),
        cost_estimate=cost(us),
        name=name,
    )(at, *(a for a, _ in args))


def project_kernel(plan, at, *refs):
    x, core = at[0], at[2]
    *arrays, send, keep = refs
    for who, out in ((1 - core, send), (core, keep)):
        for s, (near, far, weight) in enumerate(plan):
            left, right = (
                jnp.concatenate([arrays[i][r, y, who] for y in range(2) for r in range(2)], axis=0)
                for i in (near, far)
            )
            weight = arrays[weight]
            half = left.shape[1]
            top = weight[pl.ds(pl.multiple_of(x * half, half), half)]
            bottom = weight[pl.ds(pl.multiple_of((1 - x) * half, half), half)]
            c = jnp.dot(left, top, preferred_element_type=F32) + jnp.dot(right, bottom, preferred_element_type=F32)
            out[s] = c.astype(BF16).reshape(out.shape[1:])


def project(at, attended, items):
    arrays, plan = [], []

    def place_of(array):
        for i, other in enumerate(arrays):
            if other is array:
                return i
        arrays.append(array)
        return len(arrays) - 1

    for chunk, weight in items:
        plan.append(tuple(place_of(a) for a in attended[chunk] + (weight,)))
    _, _, _, tokens, _ = attended[0][0].shape
    out = jax.ShapeDtypeStruct((len(items), 2, 2, tokens, items[0][1].shape[1]), BF16)
    return whole_call(functools.partial(project_kernel, plan), at, arrays, [out, out], "project", 1 * len(items))


def whole_call(kernel, at, args, outs, name, us):
    return pl.pallas_call(
        kernel,
        out_shape=outs,
        in_specs=[pl.BlockSpec(memory_space=pltpu.SMEM)] + [pl.BlockSpec(memory_space=pltpu.VMEM)] * len(args),
        out_specs=[pl.BlockSpec(memory_space=pltpu.VMEM)] * len(outs),
        compiler_params=pltpu.CompilerParams(vmem_limit_bytes=VMEM),
        cost_estimate=cost(us),
        name=name,
    )(at, *args)


def total(a, b):
    return (a.astype(F32) + b.astype(F32)).astype(BF16)


def split_kernel(at, kept, got, stay, to_y, to_x, to_xy):
    x, y = at[0], at[3]
    for s in range(kept.shape[0]):
        for out, yy, xx in ((to_xy, 1 - y, 1 - x), (to_y, 1 - y, x), (to_x, y, 1 - x), (stay, y, x)):
            out[s] = total(kept[s, yy, xx], got[s, yy, xx])


def halve_kernel(at, kept, got, stay, to_y):
    y = at[3]
    for s in range(kept.shape[0]):
        for r in range(2):
            to_y[s, r] = total(kept[s, 1 - y, r], got[s, 1 - y, r])
            stay[s, r] = total(kept[s, y, r], got[s, y, r])


def row_kernel(at, stay, got, mine, to_x):
    x = at[0]
    for s in range(stay.shape[0]):
        to_x[s] = total(stay[s, 1 - x], got[s, 1 - x])
        mine[s] = total(stay[s, x], got[s, x])


def place_kernel(plan, at, *refs):
    x, z, out = at[0], at[1], refs[-1]
    layers = [z, z + 1 - 2 * (z % 2), (z + 2) % 4, 3 - z]
    refs = iter(refs[:-1])
    for names, hops in plan:
        group = [next(refs) for _ in range(2 * hops)]
        _, tokens, width = group[0].shape
        for s, (chunk, layer) in enumerate(names):
            rows = pl.ds(chunk * tokens, tokens)
            base = 2 * layers[layer]
            mine = pl.ds(pl.multiple_of((base + x) * width, width), width)
            theirs = pl.ds(pl.multiple_of((base + 1 - x) * width, width), width)
            if hops == 1:
                out[rows, mine], out[rows, theirs] = group[0][s], group[1][s]
            else:
                out[rows, mine] = total(group[0][s], group[1][s])
                out[rows, theirs] = total(group[2][s], group[3][s])


def after(value, *earlier):
    return lax.optimization_barrier((value, earlier))[0]


def body_eight(qkv, out_weight):
    _, _, cols, features = qkv.shape
    half = features // 2
    chunks = 2
    heads = half // HEAD
    parts = lax.axis_size("head")
    tokens = cols // chunks
    coef = HEAD ** (-0.5) * LOG2E
    me = lax.axis_index("seq")
    who = lax.axis_index("head")
    z, x, core, y = me // 2, me % 2, who % 2, who // 2
    at = jnp.stack([x, z, core, y]).astype(jnp.int32)
    local = qkv.reshape(3, cols, features)
    first = x == 0

    def seq_perm(array, *layers, cross=False):
        pairs = [(2 * a + i, 2 * b + (1 - i if cross else i)) for a, b in layers for i in range(2)]
        return lax.ppermute(array, "seq", pairs)

    def swap(array):
        return seq_perm(array, (0, 0), (1, 1), (2, 2), (3, 3), cross=True)

    def head_perm(array, flip):
        return lax.ppermute(array, "head", [(i, i ^ flip) for i in range(4)])

    def lanes(lo, hi, part, source=local):
        return lax.dynamic_slice(source, (lo, 0, part * half), (hi - lo, cols, half))

    down, two_down = [(2, 1), (3, 2)], [(3, 1)]
    q_m = lanes(0, 1, x)
    q_o = swap(lanes(0, 1, 1 - x))
    qs = [seq_perm(q_m, *down), None, seq_perm(q_m, *two_down), None]
    kv_m, kv_give = lanes(1, 3, x), lanes(1, 3, 1 - x)
    block = out_weight.reshape(kv_m.shape)
    low_m = seq_perm(jnp.where(z == 0, kv_m, block), (0, 1), (1, 3))
    pairs = [(i, 2 + 1 - i) for i in range(2)] + [(2 + i, i) for i in range(2)] + [(4 + i, 6 + i) for i in range(2)]
    low_o = lax.ppermute(after(jnp.where(z == 0, kv_give, block), q_o), "seq", pairs)
    kv_o = swap(after(kv_give, q_o, qs[0]))
    qs[1], qs[3] = seq_perm(q_o, *down), seq_perm(q_o, *two_down)

    struct = jax.ShapeDtypeStruct
    partial = struct((2 * tokens + LSE_ROWS, half), BF16)
    oa, ob, own = [], [], []
    turn = at
    kvs = [kv_m, kv_o, low_m, low_o]
    for c in range(chunks):
        a, b = head_call(
            functools.partial(upper_kernel, coef, c, chunks, parts), turn, [(a, 0) for a in qs + kvs + [out_weight]],
            [partial] * 2, heads, "upper_rows", 7)
        turn = after(at, a)
        oa.append(seq_perm(a, (1, 2), (2, 3)))
        ob.append(seq_perm(b, (1, 3), (0, 1), (3, 2)))
    def own_rows(c, turn):
        (mine,) = head_call(
            functools.partial(own_kernel, coef, c, chunks, parts), turn, [(a, 0) for a in [q_m, q_o] + kvs],
            [partial], heads, "own_rows", 6)
        return mine

    own.append(own_rows(0, turn))
    w_down = seq_perm(after(out_weight, *qs), (0, 2), (2, 0), (3, 1))

    def merged(c, earlier):
        (a,) = whole_call(
            functools.partial(merge_kernel, heads), after(at, earlier), [own[c], oa[c], ob[c]],
            [struct((2, tokens, half), BF16)], "merge", 2)
        shape = (2, 2, 2, tokens // 4, half)
        return a.reshape(shape), swap(a).reshape(shape)

    attended = [merged(0, own[0])]
    w_far = jnp.where(z == 3, low_m.reshape(out_weight.shape), after(w_down, attended[0][0]))
    own.append(own_rows(1, after(at, w_far)))
    w_other = seq_perm(w_far, (0, 1), (1, 0), (2, 3), (3, 2))
    parts_out, plan = [], []

    def summed(turn, names):
        send, kept = project(turn, attended, [(c, weights[layer]) for c, layer in names])
        return send.shape[:1] + send.shape[3:], [kept, head_perm(send, 1)]

    w_near = jnp.where(
        (z == 0) | (z == 3), low_o.reshape(out_weight.shape), jnp.concatenate([o[: 2 * tokens] for o in after(ob, own[1])]))
    attended.append(merged(1, (w_far, attended[0][1], w_near)))
    weights = {0: out_weight, 1: w_near, 2: w_far, 3: w_other}
    diagonal = [
        ((2 * i + j) * 4 + h, (2 * i + 1 - j) * 4 + (h ^ 2)) for i in range(4) for j in range(2) for h in range(4)
    ]
    turn = at
    groups = [
        ([(0, 0), (0, 1)], 1),
        ([(1, 0), (1, 1), (0, 2)], 1),
        ([(1, 2), (1, 3), (0, 3)], 2),
    ]
    for index, (names, hops) in enumerate(groups):
        size, pair = summed(turn, names)
        plan.append((names, hops))
        if hops == 1:
            both = struct(size[:1] + (2,) + size[1:], BF16)
            stay, to_y = whole_call(halve_kernel, at, pair, [both] * 2, "halve", 2)
            from_y = head_perm(to_y, 2)
            mine, to_x = whole_call(row_kernel, at, [stay, from_y], [struct(size, BF16)] * 2, "rows", 1)
            parts_out += [mine, swap(to_x)]
        else:
            stay, to_y, to_x, to_xy = whole_call(split_kernel, at, pair, [struct(size, BF16)] * 4, "split", 2)
            parts_out += [stay, head_perm(to_y, 2), swap(to_x), lax.ppermute(to_xy, ("seq", "head"), diagonal)]
        turn = after(at, mine if index == 0 else pair[0])
    (out,) = whole_call(
        functools.partial(place_kernel, plan), at, parts_out,
        [struct((cols // 4, 8 * out_weight.shape[1]), BF16)], "place", 2)
    return out.reshape(cols // 4, 1, 8 * out_weight.shape[1])


def solution(mesh):
    in_specs = (P(None, "seq", None, "head"), P("head", "seq"))
    out_specs = P("head", "seq", None)
    small = mesh.shape["seq"] == 8 and mesh.shape["head"] == 4

    def body(qkv, out_weight):
        _, rows, cols, features = qkv.shape
        even = features == 2 * cols and out_weight.shape == (features, cols) and cols % 512 == 0
        if small and rows == 1 and even:
            return body_eight(qkv, out_weight)
        return body_any(qkv, out_weight)

    return jax.shard_map(body, mesh=mesh, in_specs=in_specs, out_specs=out_specs, check_vma=False)
```

```python
import functools
import jax
import jax.numpy as jnp
from jax import lax
from jax.experimental import pallas as pl
from jax.experimental.pallas import tpu as pltpu
from jax.sharding import PartitionSpec as P

HEAD = 128
LOG2E = 1.4426950408889634
NEG = -1e30
QB = 128
VMEM = 24 * 1024 * 1024
F32, BF16 = jnp.float32, jnp.bfloat16


def shifted(shard, axis, by):
    size = lax.axis_size(axis)
    pairs = [(i, i + by) for i in range(size) if 0 <= i + by < size]
    return lax.ppermute(shard, axis, pairs)


def column_part(part):
    queries, keys_part, values = (part[0], part[1], part[2])
    rows = queries.shape[0]
    scale = queries.shape[-1] ** (-0.5)
    scores = (
        jnp.einsum("rchd,schd->chrs", queries, keys_part, preferred_element_type=jnp.float32)
        * scale
    )
    r_idx = lax.broadcasted_iota(jnp.int32, (rows, rows), 0)
    s_idx = lax.broadcasted_iota(jnp.int32, (rows, rows), 1)
    allowed = s_idx <= r_idx - 2
    masked = jnp.where(allowed, scores, jnp.float32(-1e30))
    peak = jnp.max(masked, axis=-1)
    weights = jnp.where(allowed, jnp.exp(masked - peak[..., None]), jnp.float32(0.0))
    total = jnp.maximum(jnp.sum(weights, axis=-1), jnp.float32(1.0))
    rounded = weights.astype(jnp.bfloat16)
    mixed = jnp.einsum("chrs,schd->rchd", rounded, values, preferred_element_type=jnp.float32)
    col_out = (mixed / jnp.transpose(total, (2, 0, 1))[..., None]).astype(jnp.bfloat16)
    col_lse = jnp.transpose(peak + jnp.log(total), (2, 0, 1))
    return (col_out, col_lse)


def row_part(local, previous, first_row):
    rows_dev, cols, heads_local, head_size = (
        local.shape[1],
        local.shape[2],
        local.shape[3],
        local.shape[4],
    )
    scale = head_size ** (-0.5)
    keys_ext = jnp.concatenate([previous, local[1:3]], axis=1)
    key_idx = lax.broadcasted_iota(jnp.int32, (cols, 2 * cols), 1)
    query_idx = lax.broadcasted_iota(jnp.int32, (cols, 2 * cols), 0)

    def one_row(index):
        queries = lax.dynamic_index_in_dim(local[0], index, 0, keepdims=False)
        pair = keys_ext.reshape(2, 2 * cols, heads_local, head_size)
        scores = (
            jnp.einsum("qhd,khd->hqk", queries, pair[0], preferred_element_type=jnp.float32) * scale
        )
        allowed = (key_idx < cols) & (first_row + index > 0) | (key_idx >= cols) & (
            key_idx - cols <= query_idx
        )
        masked = jnp.where(allowed[None], scores, jnp.float32(-1e30))
        peak = jnp.max(masked, axis=-1)
        weights = jnp.where(allowed[None], jnp.exp(masked - peak[..., None]), jnp.float32(0.0))
        total = jnp.sum(weights, axis=-1)
        rounded = weights.astype(jnp.bfloat16)
        mixed = jnp.einsum("hqk,khd->qhd", rounded, pair[1], preferred_element_type=jnp.float32)
        return (mixed / jnp.transpose(total)[..., None], jnp.transpose(peak + jnp.log(total)))

    return lax.map(one_row, jnp.arange(rows_dev, dtype=jnp.int32))


def body_any(qkv, out_weight):
    rows_dev, cols, features = (qkv.shape[1], qkv.shape[2], qkv.shape[3])
    head_size = HEAD
    heads_local = features // head_size
    local = qkv.reshape(3, rows_dev, cols, heads_local, head_size)
    previous = shifted(local[1:3, rows_dev - 1 : rows_dev], "seq", 1)
    first_row = lax.axis_index("seq") * rows_dev
    row_out, row_lse = row_part(local, previous, first_row)
    columns = lax.all_to_all(local, "seq", split_axis=2, concat_axis=1, tiled=True)
    col_part_out, col_part_lse = column_part(columns)
    col_out, col_lse = (
        lax.all_to_all(col_part_out, "seq", split_axis=0, concat_axis=1, tiled=True),
        lax.all_to_all(
            col_part_lse.astype(jnp.bfloat16), "seq", split_axis=0, concat_axis=1, tiled=True
        ).astype(col_part_lse.dtype),
    )
    top = jnp.maximum(row_lse, col_lse)
    left = jnp.exp(row_lse - top)
    right = jnp.exp(col_lse - top)
    attended = (left[..., None] * row_out + right[..., None] * col_out.astype(jnp.float32)) / (
        left + right
    )[..., None]
    attended = attended.astype(jnp.bfloat16).reshape(rows_dev, cols, features)
    terms = jnp.einsum(
        "rcf,fd->crd",
        attended,
        lax.all_gather(out_weight, "seq", axis=1, tiled=True),
        preferred_element_type=jnp.float32,
    )
    summed = lax.psum_scatter(terms.astype(jnp.bfloat16), "head", scatter_dimension=0, tiled=True)
    return summed


def dense_scores(q, k):
    return lax.dot_general(q, k, (((1,), (1,)), ((), ())), preferred_element_type=F32)


def col_scores(q, k):
    prod = q * k
    high = prod.astype(BF16)
    low = (prod - high.astype(F32)).astype(BF16)
    ones = jnp.ones((2 * HEAD, HEAD), BF16)
    return jnp.dot(jnp.concatenate([high, low], axis=1), ones, preferred_element_type=F32)


def with_ones(v):
    return jnp.concatenate([v, jnp.ones_like(v)], axis=1)


def attend(q, dense, cols, coef):
    rows = q.shape[0]
    scores = []
    for k, _, allowed in dense:
        s = dense_scores(q, k)
        scores.append(s if allowed is None else jnp.where(allowed, s, NEG))
    singles = []
    if cols:
        wide = q.astype(F32)
    for k, _, allowed in cols:
        c = col_scores(wide, k)
        singles.append(c if allowed is None else jnp.where(allowed, c, NEG))
    peak = None
    for s in scores:
        for j in range(s.shape[1] // HEAD):
            part = s[:, j * HEAD : (j + 1) * HEAD]
            peak = part if peak is None else jnp.maximum(peak, part)
    if peak is not None:
        peak = jnp.broadcast_to(jnp.max(peak, axis=1, keepdims=True), (rows, HEAD))
    for c in singles:
        peak = c if peak is None else jnp.maximum(peak, c)
    peak = peak * coef
    both = None
    for s, (_, v, _) in zip(scores, dense):
        tiled = jnp.concatenate([peak] * (s.shape[1] // HEAD), axis=1)
        p = jnp.exp2(s * coef - tiled).astype(BF16)
        term = jnp.dot(p, v, preferred_element_type=F32)
        both = term if both is None else both + term
    out = None if both is None else both[:, :HEAD]
    total = None if both is None else both[:, HEAD:]
    for c, (_, v, _) in zip(singles, cols):
        w = jnp.exp2(c * coef - peak)
        total = w if total is None else total + w
        out = w * v if out is None else out + w * v
    return out / total, peak + jnp.log2(total)


def lse_rows(even, odd):
    lane = lax.broadcasted_iota(jnp.int32, (HEAD, HEAD), 1)
    evens, odds = [], []
    for t in range(even.shape[0] // HEAD):
        block = slice(t * HEAD, (t + 1) * HEAD)
        turned = jnp.transpose(jnp.where(lane == 0, even[block], odd[block]))
        evens.append(turned[0:1])
        odds.append(turned[1:2])
    return evens, odds


LSE_ROWS = 16


def put_lse(ref, base, evens, odds):
    rows = jnp.concatenate(evens + odds, axis=0)
    pieces = []
    for _ in range(3):
        pieces.append(rows.astype(BF16).astype(F32))
        rows = rows - pieces[-1]
    spare = LSE_ROWS - 3 * rows.shape[0]
    ref[pl.ds(base, LSE_ROWS), :] = jnp.concatenate(pieces + [jnp.zeros((spare, HEAD), F32)], axis=0).astype(BF16)


def chunk_rows(array, chunk, chunks, parts):
    size = array.shape[0] // parts
    share = size // chunks
    return jnp.concatenate(
        [array[p * size + chunk * share : p * size + (chunk + 1) * share] for p in range(parts)], axis=0)


def stacked(refs):
    return [ref[i] for ref in refs for i in range(ref.shape[0])]


def own_kernel(coef, chunk, chunks, parts, at, q_m, q_o, kv_m, kv_o, *refs):
    x, z = at[0], at[1]
    below = z == 1
    first = x == 0
    *low, out = refs
    cols = q_m.shape[1]
    tokens = cols // chunks

    def pair(a, b):
        return jnp.where(first, a, b), jnp.where(first, b, a)

    def mine(array):
        return chunk_rows(array, chunk, chunks, parts)

    q_e, q_o = pair(mine(q_m[0]), mine(q_o[0]))
    k_e, k_o = pair(kv_m[0], kv_o[0])
    v_e, v_o = pair(kv_m[1], kv_o[1])
    v_e, v_o = with_ones(v_e), with_ones(v_o)
    share = tokens // parts
    index = lax.broadcasted_iota(jnp.int32, (tokens, cols), 0)
    index = (index // share) * (cols // parts) + chunk * share + index % share
    tri = lax.broadcasted_iota(jnp.int32, (tokens, cols), 1) <= index

    def run(even, odd):
        o1, l1 = attend(q_e, [(k_e, v_e, tri)] + even[0], even[1], coef)
        o2, l2 = attend(q_o, [(k_o, v_o, tri), (k_e, v_e, None)], odd, coef)
        out[:tokens] = o1.astype(BF16)
        out[tokens : 2 * tokens] = o2.astype(BF16)
        put_lse(out, 2 * tokens, *lse_rows(l1, l2))

    @pl.when(below)
    def _():
        m_k, m_v, o_k, o_v = stacked(low)
        lk_e, lk_o = pair(m_k, o_k)
        lv_e, lv_o = pair(m_v, o_v)
        col_e = (mine(lk_e).astype(F32), mine(lv_e).astype(F32), None)
        col_o = (mine(lk_o).astype(F32), mine(lv_o).astype(F32), None)
        run(([(lk_o, with_ones(lv_o), None)], [col_e]), [col_e, col_o])

    @pl.when(jnp.logical_not(below))
    def _():
        run(([], []), [])


def upper_kernel(coef, chunk, chunks, parts, at, qa_m, qa_o, qb_m, qb_o, kv_m, kv_o, *refs):
    x, z = at[0], at[1]
    below = z == 1
    first = x == 0
    *low, weight, out_a, out_b = refs
    tokens = qa_m.shape[1] // chunks

    def pair(a, b):
        return jnp.where(first, a, b), jnp.where(first, b, a)

    def mine(array):
        return chunk_rows(array, chunk, chunks, parts)

    k_e, k_o = pair(kv_m[0], kv_o[0])
    v_e, v_o = pair(kv_m[1], kv_o[1])
    ce = (mine(k_e).astype(F32), mine(v_e).astype(F32), None)
    co = (mine(k_o).astype(F32), mine(v_o).astype(F32), None)
    base = chunk * 2 * tokens

    def run(q_m, q_o, out, dense, singles, lower):
        q_e, q_odd = pair(mine(q_m[0]), mine(q_o[0]))
        o1, l1 = attend(q_e, dense, singles + lower, coef)
        o2, l2 = attend(q_odd, [], [ce, co] + lower, coef)
        out[:tokens] = o1.astype(BF16)
        out[tokens : 2 * tokens] = o2.astype(BF16)
        put_lse(out, 2 * tokens, *lse_rows(l1, l2))

    def first_rows(lower):
        run(qa_m, qa_o, out_a, [(k_o, with_ones(v_o), None)], [ce], lower)

    @pl.when(below)
    def _():
        m_k, m_v, o_k, o_v = (mine(part).astype(F32) for part in stacked(low))
        lower = [(m_k, m_v, None), (o_k, o_v, None)]
        first_rows(lower)
        run(qb_m, qb_o, out_b, [], [ce, co], lower)

    @pl.when(jnp.logical_not(below))
    def _():
        out_b[: 2 * tokens] = weight[base : base + 2 * tokens]
        out_b[pl.ds(2 * tokens, LSE_ROWS), :] = jnp.zeros((LSE_ROWS, HEAD), BF16)

    @pl.when(z == 2)
    def _():
        first_rows([])

    @pl.when(z % 3 == 0)
    def _():
        out_a[...] = jnp.zeros(out_a.shape, BF16)


def merge_kernel(heads, at, own, oa, ob, out):
    z = at[1]
    tokens = out.shape[1]
    blocks = tokens // HEAD
    rows = 2 * blocks
    line = lax.broadcasted_iota(jnp.int32, (32, 3 * HEAD), 0)
    group = lax.broadcasted_iota(jnp.int32, (32, 3 * HEAD), 1) // HEAD
    picks = []
    for first in range(rows):
        at_line = first + group * rows
        picks.append(((line == at_line) | (line == at_line + 3 * rows)).astype(BF16))
    for head in range(heads):
        lanes = slice(head * HEAD, (head + 1) * HEAD)

        def totals(ref):
            packed = ref[pl.ds(2 * tokens, LSE_ROWS), lanes].astype(F32)
            return sum(packed[i * rows : (i + 1) * rows] for i in range(3))

        l0, l1, l2 = (totals(ref) for ref in (own, oa, ob))
        l1, l2 = jnp.where(z >= 2, l1, NEG), jnp.where(z >= 3, l2, NEG)
        top = jnp.maximum(l0, jnp.maximum(l1, l2))
        shares = [jnp.exp2(l - top) for l in (l0, l1, l2)]
        whole = shares[0] + shares[1] + shares[2]
        shares = jnp.concatenate([share / whole for share in shares], axis=0)
        high = shares.astype(BF16).astype(F32)
        spare = jnp.zeros((32 - 6 * rows, HEAD), F32)
        pieces = jnp.concatenate([high, shares - high, spare], axis=0).astype(BF16)
        for row in range(2):
            for block in range(blocks):
                pick = picks[row * blocks + block]
                spread = lax.dot_general(pieces, pick, (((0,), (0,)), ((), ())), preferred_element_type=F32)
                mine = slice(row * tokens + block * HEAD, row * tokens + (block + 1) * HEAD)
                mixed = spread[:, :HEAD] * own[mine, lanes].astype(F32)
                mixed = mixed + spread[:, HEAD : 2 * HEAD] * oa[mine, lanes].astype(F32)
                mixed = mixed + spread[:, 2 * HEAD :] * ob[mine, lanes].astype(F32)
                out[row, block * HEAD : (block + 1) * HEAD, lanes] = mixed.astype(BF16)


def cost(us):
    return pl.CostEstimate(flops=int(us * 1e8), bytes_accessed=1024, transcendentals=0)


def head_call(kernel, at, args, outs, heads, name, us):
    def spec(shape, start=0):
        lead = len(shape) - 1
        return pl.BlockSpec(tuple(shape[:-1]) + (HEAD,), lambda h, at: (0,) * lead + (start + h,))

    return pl.pallas_call(
        kernel,
        out_shape=outs,
        grid_spec=pltpu.PrefetchScalarGridSpec(
            num_scalar_prefetch=1,
            grid=(heads,),
            in_specs=[spec(a.shape, start) for a, start in args],
            out_specs=[spec(o.shape) for o in outs],
        ),
        compiler_params=pltpu.CompilerParams(vmem_limit_bytes=VMEM),
        cost_estimate=cost(us),
        name=name,
    )(at, *(a for a, _ in args))


def project_kernel(plan, at, *refs):
    x, core = at[0], at[2]
    *arrays, send, keep = refs
    for who, out in ((1 - core, send), (core, keep)):
        for s, (near, far, weight) in enumerate(plan):
            left, right = (
                jnp.concatenate([arrays[i][r, y, who] for y in range(2) for r in range(2)], axis=0)
                for i in (near, far)
            )
            weight = arrays[weight]
            half = left.shape[1]
            top = weight[pl.ds(pl.multiple_of(x * half, half), half)]
            bottom = weight[pl.ds(pl.multiple_of((1 - x) * half, half), half)]
            c = jnp.dot(left, top, preferred_element_type=F32) + jnp.dot(right, bottom, preferred_element_type=F32)
            out[s] = c.astype(BF16).reshape(out.shape[1:])


def project(at, attended, items):
    arrays, plan = [], []

    def place_of(array):
        for i, other in enumerate(arrays):
            if other is array:
                return i
        arrays.append(array)
        return len(arrays) - 1

    for chunk, weight in items:
        plan.append(tuple(place_of(a) for a in attended[chunk] + (weight,)))
    _, _, _, tokens, _ = attended[0][0].shape
    out = jax.ShapeDtypeStruct((len(items), 2, 2, tokens, items[0][1].shape[1]), BF16)
    return whole_call(functools.partial(project_kernel, plan), at, arrays, [out, out], "project", 1 * len(items))


def whole_call(kernel, at, args, outs, name, us):
    return pl.pallas_call(
        kernel,
        out_shape=outs,
        in_specs=[pl.BlockSpec(memory_space=pltpu.SMEM)] + [pl.BlockSpec(memory_space=pltpu.VMEM)] * len(args),
        out_specs=[pl.BlockSpec(memory_space=pltpu.VMEM)] * len(outs),
        compiler_params=pltpu.CompilerParams(vmem_limit_bytes=VMEM),
        cost_estimate=cost(us),
        name=name,
    )(at, *args)


def total(a, b):
    return (a.astype(F32) + b.astype(F32)).astype(BF16)


def split_kernel(at, kept, got, stay, to_y, to_x, to_xy):
    x, y = at[0], at[3]
    for s in range(kept.shape[0]):
        for out, yy, xx in ((to_xy, 1 - y, 1 - x), (to_y, 1 - y, x), (to_x, y, 1 - x), (stay, y, x)):
            out[s] = total(kept[s, yy, xx], got[s, yy, xx])


def halve_kernel(at, kept, got, stay, to_y):
    y = at[3]
    for s in range(kept.shape[0]):
        for r in range(2):
            to_y[s, r] = total(kept[s, 1 - y, r], got[s, 1 - y, r])
            stay[s, r] = total(kept[s, y, r], got[s, y, r])


def row_kernel(at, stay, got, mine, to_x):
    x = at[0]
    for s in range(stay.shape[0]):
        to_x[s] = total(stay[s, 1 - x], got[s, 1 - x])
        mine[s] = total(stay[s, x], got[s, x])


def place_kernel(plan, at, *refs):
    x, z, out = at[0], at[1], refs[-1]
    layers = [z, z + 1 - 2 * (z % 2), (z + 2) % 4, 3 - z]
    refs = iter(refs[:-1])
    for names, hops in plan:
        group = [next(refs) for _ in range(2 * hops)]
        _, tokens, width = group[0].shape
        for s, (chunk, layer) in enumerate(names):
            rows = pl.ds(chunk * tokens, tokens)
            base = 2 * layers[layer]
            mine = pl.ds(pl.multiple_of((base + x) * width, width), width)
            theirs = pl.ds(pl.multiple_of((base + 1 - x) * width, width), width)
            if hops == 1:
                out[rows, mine], out[rows, theirs] = group[0][s], group[1][s]
            else:
                out[rows, mine] = total(group[0][s], group[1][s])
                out[rows, theirs] = total(group[2][s], group[3][s])


def after(value, *earlier):
    return lax.optimization_barrier((value, earlier))[0]


def body_eight(qkv, out_weight):
    _, _, cols, features = qkv.shape
    half = features // 2
    chunks = 2
    heads = half // HEAD
    parts = lax.axis_size("head")
    tokens = cols // chunks
    coef = HEAD ** (-0.5) * LOG2E
    me = lax.axis_index("seq")
    who = lax.axis_index("head")
    z, x, core, y = me // 2, me % 2, who % 2, who // 2
    at = jnp.stack([x, z, core, y]).astype(jnp.int32)
    local = qkv.reshape(3, cols, features)
    first = x == 0

    def seq_perm(array, *layers, cross=False):
        pairs = [(2 * a + i, 2 * b + (1 - i if cross else i)) for a, b in layers for i in range(2)]
        return lax.ppermute(array, "seq", pairs)

    def swap(array):
        return seq_perm(array, (0, 0), (1, 1), (2, 2), (3, 3), cross=True)

    def head_perm(array, flip):
        return lax.ppermute(array, "head", [(i, i ^ flip) for i in range(4)])

    def lanes(lo, hi, part, source=local):
        return lax.dynamic_slice(source, (lo, 0, part * half), (hi - lo, cols, half))

    down, two_down = [(2, 1), (3, 2)], [(3, 1)]
    q_m = lanes(0, 1, x)
    q_o = swap(lanes(0, 1, 1 - x))
    qs = [seq_perm(q_m, *down), None, seq_perm(q_m, *two_down), None]
    kv_m, kv_give = lanes(1, 3, x), lanes(1, 3, 1 - x)
    block = out_weight.reshape(kv_m.shape)
    low_m = seq_perm(jnp.where(z == 0, kv_m, block), (0, 1), (1, 3))
    pairs = [(i, 2 + 1 - i) for i in range(2)] + [(2 + i, i) for i in range(2)] + [(4 + i, 6 + i) for i in range(2)]
    low_o = lax.ppermute(after(jnp.where(z == 0, kv_give, block), q_o), "seq", pairs)
    kv_o = swap(after(kv_give, q_o, qs[0]))
    qs[1], qs[3] = seq_perm(q_o, *down), seq_perm(q_o, *two_down)

    struct = jax.ShapeDtypeStruct
    partial = struct((2 * tokens + LSE_ROWS, half), BF16)
    oa, ob, own = [], [], []
    turn = at
    kvs = [kv_m, kv_o, low_m, low_o]
    for c in range(chunks):
        a, b = head_call(
            functools.partial(upper_kernel, coef, c, chunks, parts), turn, [(a, 0) for a in qs + kvs + [out_weight]],
            [partial] * 2, heads, "upper_rows", 7)
        turn = after(at, a)
        oa.append(seq_perm(a, (1, 2), (2, 3)))
        ob.append(seq_perm(b, (1, 3), (0, 1), (3, 2)))
    def own_rows(c, turn):
        (mine,) = head_call(
            functools.partial(own_kernel, coef, c, chunks, parts), turn, [(a, 0) for a in [q_m, q_o] + kvs],
            [partial], heads, "own_rows", 6)
        return mine

    own.append(own_rows(0, turn))
    w_down = seq_perm(after(out_weight, *qs), (0, 2), (2, 0), (3, 1))

    def merged(c, earlier):
        (a,) = whole_call(
            functools.partial(merge_kernel, heads), after(at, earlier), [own[c], oa[c], ob[c]],
            [struct((2, tokens, half), BF16)], "merge", 2)
        shape = (2, 2, 2, tokens // 4, half)
        return a.reshape(shape), swap(a).reshape(shape)

    attended = [merged(0, own[0])]
    w_far = jnp.where(z == 3, low_m.reshape(out_weight.shape), after(w_down, attended[0][0]))
    own.append(own_rows(1, after(at, w_far)))
    w_other = seq_perm(w_far, (0, 1), (1, 0), (2, 3), (3, 2))
    parts_out, plan = [], []

    def summed(turn, names):
        send, kept = project(turn, attended, [(c, weights[layer]) for c, layer in names])
        return send.shape[:1] + send.shape[3:], [kept, head_perm(send, 1)]

    w_near = jnp.where(
        (z == 0) | (z == 3), low_o.reshape(out_weight.shape), jnp.concatenate([o[: 2 * tokens] for o in after(ob, own[1])]))
    attended.append(merged(1, (w_far, attended[0][1], w_near)))
    weights = {0: out_weight, 1: w_near, 2: w_far, 3: w_other}
    names = [(0, 0), (0, 1)]
    size, pair = summed(at, names)
    both = struct(size[:1] + (2,) + size[1:], BF16)
    stay, to_y = whole_call(halve_kernel, at, pair, [both] * 2, "halve", 2)
    from_y = head_perm(to_y, 2)
    mine, to_x = whole_call(row_kernel, at, [stay, from_y], [struct(size, BF16)] * 2, "rows", 1)
    parts_out += [mine, swap(to_x)]
    plan.append((names, 1))

    diagonal = [
        ((2 * i + j) * 4 + h, (2 * i + 1 - j) * 4 + (h ^ 2)) for i in range(4) for j in range(2) for h in range(4)
    ]
    turn = after(at, mine)
    for names in ([(1, 0), (1, 1), (0, 2)], [(1, 2), (1, 3), (0, 3)]):
        size, pair = summed(turn, names)
        turn = after(at, pair[0], parts_out[1])
        stay, to_y, to_x, to_xy = whole_call(split_kernel, at, pair, [struct(size, BF16)] * 4, "split", 2)
        parts_out += [stay, head_perm(to_y, 2), swap(to_x), lax.ppermute(to_xy, ("seq", "head"), diagonal)]
        plan.append((names, 2))
    (out,) = whole_call(
        functools.partial(place_kernel, plan), at, parts_out,
        [struct((cols // 4, 8 * out_weight.shape[1]), BF16)], "place", 2)
    return out.reshape(cols // 4, 1, 8 * out_weight.shape[1])


def solution(mesh):
    in_specs = (P(None, "seq", None, "head"), P("head", "seq"))
    out_specs = P("head", "seq", None)
    small = mesh.shape["seq"] == 8 and mesh.shape["head"] == 4

    def body(qkv, out_weight):
        _, rows, cols, features = qkv.shape
        even = features == 2 * cols and out_weight.shape == (features, cols) and cols % 512 == 0
        if small and rows == 1 and even:
            return body_eight(qkv, out_weight)
        return body_any(qkv, out_weight)

    return jax.shard_map(body, mesh=mesh, in_specs=in_specs, out_specs=out_specs, check_vma=False)
```

```python
import functools
import jax
import jax.numpy as jnp
from jax import lax
from jax.experimental import pallas as pl
from jax.experimental.pallas import tpu as pltpu
from jax.sharding import PartitionSpec as P

HEAD = 128
LOG2E = 1.4426950408889634
NEG = -1e30
QB = 128
VMEM = 24 * 1024 * 1024
F32, BF16 = jnp.float32, jnp.bfloat16


def shifted(shard, axis, by):
    size = lax.axis_size(axis)
    pairs = [(i, i + by) for i in range(size) if 0 <= i + by < size]
    return lax.ppermute(shard, axis, pairs)


def column_part(part):
    queries, keys_part, values = (part[0], part[1], part[2])
    rows = queries.shape[0]
    scale = queries.shape[-1] ** (-0.5)
    scores = (
        jnp.einsum("rchd,schd->chrs", queries, keys_part, preferred_element_type=jnp.float32)
        * scale
    )
    r_idx = lax.broadcasted_iota(jnp.int32, (rows, rows), 0)
    s_idx = lax.broadcasted_iota(jnp.int32, (rows, rows), 1)
    allowed = s_idx <= r_idx - 2
    masked = jnp.where(allowed, scores, jnp.float32(-1e30))
    peak = jnp.max(masked, axis=-1)
    weights = jnp.where(allowed, jnp.exp(masked - peak[..., None]), jnp.float32(0.0))
    total = jnp.maximum(jnp.sum(weights, axis=-1), jnp.float32(1.0))
    rounded = weights.astype(jnp.bfloat16)
    mixed = jnp.einsum("chrs,schd->rchd", rounded, values, preferred_element_type=jnp.float32)
    col_out = (mixed / jnp.transpose(total, (2, 0, 1))[..., None]).astype(jnp.bfloat16)
    col_lse = jnp.transpose(peak + jnp.log(total), (2, 0, 1))
    return (col_out, col_lse)


def row_part(local, previous, first_row):
    rows_dev, cols, heads_local, head_size = (
        local.shape[1],
        local.shape[2],
        local.shape[3],
        local.shape[4],
    )
    scale = head_size ** (-0.5)
    keys_ext = jnp.concatenate([previous, local[1:3]], axis=1)
    key_idx = lax.broadcasted_iota(jnp.int32, (cols, 2 * cols), 1)
    query_idx = lax.broadcasted_iota(jnp.int32, (cols, 2 * cols), 0)

    def one_row(index):
        queries = lax.dynamic_index_in_dim(local[0], index, 0, keepdims=False)
        pair = keys_ext.reshape(2, 2 * cols, heads_local, head_size)
        scores = (
            jnp.einsum("qhd,khd->hqk", queries, pair[0], preferred_element_type=jnp.float32) * scale
        )
        allowed = (key_idx < cols) & (first_row + index > 0) | (key_idx >= cols) & (
            key_idx - cols <= query_idx
        )
        masked = jnp.where(allowed[None], scores, jnp.float32(-1e30))
        peak = jnp.max(masked, axis=-1)
        weights = jnp.where(allowed[None], jnp.exp(masked - peak[..., None]), jnp.float32(0.0))
        total = jnp.sum(weights, axis=-1)
        rounded = weights.astype(jnp.bfloat16)
        mixed = jnp.einsum("hqk,khd->qhd", rounded, pair[1], preferred_element_type=jnp.float32)
        return (mixed / jnp.transpose(total)[..., None], jnp.transpose(peak + jnp.log(total)))

    return lax.map(one_row, jnp.arange(rows_dev, dtype=jnp.int32))


def body_any(qkv, out_weight):
    rows_dev, cols, features = (qkv.shape[1], qkv.shape[2], qkv.shape[3])
    head_size = HEAD
    heads_local = features // head_size
    local = qkv.reshape(3, rows_dev, cols, heads_local, head_size)
    previous = shifted(local[1:3, rows_dev - 1 : rows_dev], "seq", 1)
    first_row = lax.axis_index("seq") * rows_dev
    row_out, row_lse = row_part(local, previous, first_row)
    columns = lax.all_to_all(local, "seq", split_axis=2, concat_axis=1, tiled=True)
    col_part_out, col_part_lse = column_part(columns)
    col_out, col_lse = (
        lax.all_to_all(col_part_out, "seq", split_axis=0, concat_axis=1, tiled=True),
        lax.all_to_all(
            col_part_lse.astype(jnp.bfloat16), "seq", split_axis=0, concat_axis=1, tiled=True
        ).astype(col_part_lse.dtype),
    )
    top = jnp.maximum(row_lse, col_lse)
    left = jnp.exp(row_lse - top)
    right = jnp.exp(col_lse - top)
    attended = (left[..., None] * row_out + right[..., None] * col_out.astype(jnp.float32)) / (
        left + right
    )[..., None]
    attended = attended.astype(jnp.bfloat16).reshape(rows_dev, cols, features)
    terms = jnp.einsum(
        "rcf,fd->crd",
        attended,
        lax.all_gather(out_weight, "seq", axis=1, tiled=True),
        preferred_element_type=jnp.float32,
    )
    summed = lax.psum_scatter(terms.astype(jnp.bfloat16), "head", scatter_dimension=0, tiled=True)
    return summed


def dense_scores(q, k):
    return lax.dot_general(q, k, (((1,), (1,)), ((), ())), preferred_element_type=F32)


def col_scores(q, k):
    prod = q * k
    high = prod.astype(BF16)
    low = (prod - high.astype(F32)).astype(BF16)
    ones = jnp.ones((2 * HEAD, HEAD), BF16)
    return jnp.dot(jnp.concatenate([high, low], axis=1), ones, preferred_element_type=F32)


def with_ones(v):
    return jnp.concatenate([v, jnp.ones_like(v)], axis=1)


def attend(q, dense, cols, coef):
    rows = q.shape[0]
    scores = []
    for k, _, allowed in dense:
        s = dense_scores(q, k)
        scores.append(s if allowed is None else jnp.where(allowed, s, NEG))
    singles = []
    if cols:
        wide = q.astype(F32)
    for k, _, allowed in cols:
        c = col_scores(wide, k)
        singles.append(c if allowed is None else jnp.where(allowed, c, NEG))
    peak = None
    for s in scores:
        for j in range(s.shape[1] // HEAD):
            part = s[:, j * HEAD : (j + 1) * HEAD]
            peak = part if peak is None else jnp.maximum(peak, part)
    if peak is not None:
        peak = jnp.broadcast_to(jnp.max(peak, axis=1, keepdims=True), (rows, HEAD))
    for c in singles:
        peak = c if peak is None else jnp.maximum(peak, c)
    peak = peak * coef
    both = None
    for s, (_, v, _) in zip(scores, dense):
        tiled = jnp.concatenate([peak] * (s.shape[1] // HEAD), axis=1)
        p = jnp.exp2(s * coef - tiled).astype(BF16)
        term = jnp.dot(p, v, preferred_element_type=F32)
        both = term if both is None else both + term
    out = None if both is None else both[:, :HEAD]
    total = None if both is None else both[:, HEAD:]
    for c, (_, v, _) in zip(singles, cols):
        w = jnp.exp2(c * coef - peak)
        total = w if total is None else total + w
        out = w * v if out is None else out + w * v
    return out / total, peak + jnp.log2(total)


def lse_rows(even, odd):
    lane = lax.broadcasted_iota(jnp.int32, (HEAD, HEAD), 1)
    evens, odds = [], []
    for t in range(even.shape[0] // HEAD):
        block = slice(t * HEAD, (t + 1) * HEAD)
        turned = jnp.transpose(jnp.where(lane == 0, even[block], odd[block]))
        evens.append(turned[0:1])
        odds.append(turned[1:2])
    return evens, odds


LSE_ROWS = 16


def put_lse(ref, base, evens, odds):
    rows = jnp.concatenate(evens + odds, axis=0)
    pieces = []
    for _ in range(3):
        pieces.append(rows.astype(BF16).astype(F32))
        rows = rows - pieces[-1]
    spare = LSE_ROWS - 3 * rows.shape[0]
    ref[pl.ds(base, LSE_ROWS), :] = jnp.concatenate(pieces + [jnp.zeros((spare, HEAD), F32)], axis=0).astype(BF16)


def chunk_rows(array, chunk, chunks, parts):
    size = array.shape[0] // parts
    share = size // chunks
    return jnp.concatenate(
        [array[p * size + chunk * share : p * size + (chunk + 1) * share] for p in range(parts)], axis=0)


def stacked(refs):
    return [ref[i] for ref in refs for i in range(ref.shape[0])]


def own_kernel(coef, chunk, chunks, parts, at, q_m, q_o, kv_m, kv_o, *refs):
    x, z = at[0], at[1]
    below = z == 1
    first = x == 0
    *low, out = refs
    cols = q_m.shape[1]
    tokens = cols // chunks

    def pair(a, b):
        return jnp.where(first, a, b), jnp.where(first, b, a)

    def mine(array):
        return chunk_rows(array, chunk, chunks, parts)

    q_e, q_o = pair(mine(q_m[0]), mine(q_o[0]))
    k_e, k_o = pair(kv_m[0], kv_o[0])
    v_e, v_o = pair(kv_m[1], kv_o[1])
    v_e, v_o = with_ones(v_e), with_ones(v_o)
    share = tokens // parts
    index = lax.broadcasted_iota(jnp.int32, (tokens, cols), 0)
    index = (index // share) * (cols // parts) + chunk * share + index % share
    tri = lax.broadcasted_iota(jnp.int32, (tokens, cols), 1) <= index

    def run(even, odd):
        o1, l1 = attend(q_e, [(k_e, v_e, tri)] + even[0], even[1], coef)
        o2, l2 = attend(q_o, [(k_o, v_o, tri), (k_e, v_e, None)], odd, coef)
        out[:tokens] = o1.astype(BF16)
        out[tokens : 2 * tokens] = o2.astype(BF16)
        put_lse(out, 2 * tokens, *lse_rows(l1, l2))

    @pl.when(below)
    def _():
        m_k, m_v, o_k, o_v = stacked(low)
        lk_e, lk_o = pair(m_k, o_k)
        lv_e, lv_o = pair(m_v, o_v)
        col_e = (mine(lk_e).astype(F32), mine(lv_e).astype(F32), None)
        col_o = (mine(lk_o).astype(F32), mine(lv_o).astype(F32), None)
        run(([(lk_o, with_ones(lv_o), None)], [col_e]), [col_e, col_o])

    @pl.when(jnp.logical_not(below))
    def _():
        run(([], []), [])


def upper_kernel(coef, chunk, chunks, parts, at, qa_m, qa_o, qb_m, qb_o, kv_m, kv_o, *refs):
    x, z = at[0], at[1]
    below = z == 1
    first = x == 0
    *low, weight, out_a, out_b = refs
    tokens = qa_m.shape[1] // chunks

    def pair(a, b):
        return jnp.where(first, a, b), jnp.where(first, b, a)

    def mine(array):
        return chunk_rows(array, chunk, chunks, parts)

    k_e, k_o = pair(kv_m[0], kv_o[0])
    v_e, v_o = pair(kv_m[1], kv_o[1])
    ce = (mine(k_e).astype(F32), mine(v_e).astype(F32), None)
    co = (mine(k_o).astype(F32), mine(v_o).astype(F32), None)
    base = chunk * 2 * tokens

    def run(q_m, q_o, out, dense, singles, lower):
        q_e, q_odd = pair(mine(q_m[0]), mine(q_o[0]))
        o1, l1 = attend(q_e, dense, singles + lower, coef)
        o2, l2 = attend(q_odd, [], [ce, co] + lower, coef)
        out[:tokens] = o1.astype(BF16)
        out[tokens : 2 * tokens] = o2.astype(BF16)
        put_lse(out, 2 * tokens, *lse_rows(l1, l2))

    def first_rows(lower):
        run(qa_m, qa_o, out_a, [(k_o, with_ones(v_o), None)], [ce], lower)

    @pl.when(below)
    def _():
        m_k, m_v, o_k, o_v = (mine(part).astype(F32) for part in stacked(low))
        lower = [(m_k, m_v, None), (o_k, o_v, None)]
        first_rows(lower)
        run(qb_m, qb_o, out_b, [], [ce, co], lower)

    @pl.when(jnp.logical_not(below))
    def _():
        out_b[: 2 * tokens] = weight[base : base + 2 * tokens]
        out_b[pl.ds(2 * tokens, LSE_ROWS), :] = jnp.zeros((LSE_ROWS, HEAD), BF16)

    @pl.when(z == 2)
    def _():
        first_rows([])

    @pl.when(z % 3 == 0)
    def _():
        out_a[...] = jnp.zeros(out_a.shape, BF16)


def merge_kernel(heads, at, own, oa, ob, out):
    z = at[1]
    tokens = out.shape[1]
    blocks = tokens // HEAD
    rows = 2 * blocks
    line = lax.broadcasted_iota(jnp.int32, (32, 3 * HEAD), 0)
    group = lax.broadcasted_iota(jnp.int32, (32, 3 * HEAD), 1) // HEAD
    picks = []
    for first in range(rows):
        at_line = first + group * rows
        picks.append(((line == at_line) | (line == at_line + 3 * rows)).astype(BF16))
    for head in range(heads):
        lanes = slice(head * HEAD, (head + 1) * HEAD)

        def totals(ref):
            packed = ref[pl.ds(2 * tokens, LSE_ROWS), lanes].astype(F32)
            return sum(packed[i * rows : (i + 1) * rows] for i in range(3))

        l0, l1, l2 = (totals(ref) for ref in (own, oa, ob))
        l1, l2 = jnp.where(z >= 2, l1, NEG), jnp.where(z >= 3, l2, NEG)
        top = jnp.maximum(l0, jnp.maximum(l1, l2))
        shares = [jnp.exp2(l - top) for l in (l0, l1, l2)]
        whole = shares[0] + shares[1] + shares[2]
        shares = jnp.concatenate([share / whole for share in shares], axis=0)
        high = shares.astype(BF16).astype(F32)
        spare = jnp.zeros((32 - 6 * rows, HEAD), F32)
        pieces = jnp.concatenate([high, shares - high, spare], axis=0).astype(BF16)
        for row in range(2):
            for block in range(blocks):
                pick = picks[row * blocks + block]
                spread = lax.dot_general(pieces, pick, (((0,), (0,)), ((), ())), preferred_element_type=F32)
                mine = slice(row * tokens + block * HEAD, row * tokens + (block + 1) * HEAD)
                mixed = spread[:, :HEAD] * own[mine, lanes].astype(F32)
                mixed = mixed + spread[:, HEAD : 2 * HEAD] * oa[mine, lanes].astype(F32)
                mixed = mixed + spread[:, 2 * HEAD :] * ob[mine, lanes].astype(F32)
                out[row, block * HEAD : (block + 1) * HEAD, lanes] = mixed.astype(BF16)


def cost(us):
    return pl.CostEstimate(flops=int(us * 1e8), bytes_accessed=1024, transcendentals=0)


def head_call(kernel, at, args, outs, heads, name, us):
    def spec(shape, start=0):
        lead = len(shape) - 1
        return pl.BlockSpec(tuple(shape[:-1]) + (HEAD,), lambda h, at: (0,) * lead + (start + h,))

    return pl.pallas_call(
        kernel,
        out_shape=outs,
        grid_spec=pltpu.PrefetchScalarGridSpec(
            num_scalar_prefetch=1,
            grid=(heads,),
            in_specs=[spec(a.shape, start) for a, start in args],
            out_specs=[spec(o.shape) for o in outs],
        ),
        compiler_params=pltpu.CompilerParams(vmem_limit_bytes=VMEM),
        cost_estimate=cost(us),
        name=name,
    )(at, *(a for a, _ in args))


def project_kernel(plan, at, *refs):
    x, core = at[0], at[2]
    *arrays, send, keep = refs
    for who, out in ((1 - core, send), (core, keep)):
        for s, (near, far, weight) in enumerate(plan):
            left, right = (
                jnp.concatenate([arrays[i][r, y, who] for y in range(2) for r in range(2)], axis=0)
                for i in (near, far)
            )
            weight = arrays[weight]
            half = left.shape[1]
            top = weight[pl.ds(pl.multiple_of(x * half, half), half)]
            bottom = weight[pl.ds(pl.multiple_of((1 - x) * half, half), half)]
            c = jnp.dot(left, top, preferred_element_type=F32) + jnp.dot(right, bottom, preferred_element_type=F32)
            out[s] = c.astype(BF16).reshape(out.shape[1:])


def project(at, attended, items):
    arrays, plan = [], []

    def place_of(array):
        for i, other in enumerate(arrays):
            if other is array:
                return i
        arrays.append(array)
        return len(arrays) - 1

    for chunk, weight in items:
        plan.append(tuple(place_of(a) for a in attended[chunk] + (weight,)))
    _, _, _, tokens, _ = attended[0][0].shape
    out = jax.ShapeDtypeStruct((len(items), 2, 2, tokens, items[0][1].shape[1]), BF16)
    return whole_call(functools.partial(project_kernel, plan), at, arrays, [out, out], "project", 1 * len(items))


def whole_call(kernel, at, args, outs, name, us):
    return pl.pallas_call(
        kernel,
        out_shape=outs,
        in_specs=[pl.BlockSpec(memory_space=pltpu.SMEM)] + [pl.BlockSpec(memory_space=pltpu.VMEM)] * len(args),
        out_specs=[pl.BlockSpec(memory_space=pltpu.VMEM)] * len(outs),
        compiler_params=pltpu.CompilerParams(vmem_limit_bytes=VMEM),
        cost_estimate=cost(us),
        name=name,
    )(at, *args)


def total(a, b):
    return (a.astype(F32) + b.astype(F32)).astype(BF16)


def split_kernel(at, kept, got, stay, to_y, to_x, to_xy):
    x, y = at[0], at[3]
    for s in range(kept.shape[0]):
        for out, yy, xx in ((to_xy, 1 - y, 1 - x), (to_y, 1 - y, x), (to_x, y, 1 - x), (stay, y, x)):
            out[s] = total(kept[s, yy, xx], got[s, yy, xx])


def halve_kernel(at, kept, got, stay, to_y):
    y = at[3]
    for s in range(kept.shape[0]):
        for r in range(2):
            to_y[s, r] = total(kept[s, 1 - y, r], got[s, 1 - y, r])
            stay[s, r] = total(kept[s, y, r], got[s, y, r])


def row_kernel(at, stay, got, mine, to_x):
    x = at[0]
    for s in range(stay.shape[0]):
        to_x[s] = total(stay[s, 1 - x], got[s, 1 - x])
        mine[s] = total(stay[s, x], got[s, x])


def place_kernel(plan, at, *refs):
    x, z, out = at[0], at[1], refs[-1]
    layers = [z, z + 1 - 2 * (z % 2), (z + 2) % 4, 3 - z]
    refs = iter(refs[:-1])
    for names, hops in plan:
        group = [next(refs) for _ in range(2 * hops)]
        _, tokens, width = group[0].shape
        for s, (chunk, layer) in enumerate(names):
            rows = pl.ds(chunk * tokens, tokens)
            base = 2 * layers[layer]
            mine = pl.ds(pl.multiple_of((base + x) * width, width), width)
            theirs = pl.ds(pl.multiple_of((base + 1 - x) * width, width), width)
            if hops == 1:
                out[rows, mine], out[rows, theirs] = group[0][s], group[1][s]
            else:
                out[rows, mine] = total(group[0][s], group[1][s])
                out[rows, theirs] = total(group[2][s], group[3][s])


def after(value, *earlier):
    return lax.optimization_barrier((value, earlier))[0]


def body_eight(qkv, out_weight):
    _, _, cols, features = qkv.shape
    half = features // 2
    chunks = 2
    heads = half // HEAD
    parts = lax.axis_size("head")
    tokens = cols // chunks
    coef = HEAD ** (-0.5) * LOG2E
    me = lax.axis_index("seq")
    who = lax.axis_index("head")
    z, x, core, y = me // 2, me % 2, who % 2, who // 2
    at = jnp.stack([x, z, core, y]).astype(jnp.int32)
    local = qkv.reshape(3, cols, features)
    first = x == 0

    def seq_perm(array, *layers, cross=False):
        pairs = [(2 * a + i, 2 * b + (1 - i if cross else i)) for a, b in layers for i in range(2)]
        return lax.ppermute(array, "seq", pairs)

    def swap(array):
        return seq_perm(array, (0, 0), (1, 1), (2, 2), (3, 3), cross=True)

    def head_perm(array, flip):
        return lax.ppermute(array, "head", [(i, i ^ flip) for i in range(4)])

    def lanes(lo, hi, part, source=local):
        return lax.dynamic_slice(source, (lo, 0, part * half), (hi - lo, cols, half))

    down, two_down = [(2, 1), (3, 2)], [(3, 1)]
    q_m = lanes(0, 1, x)
    q_o = swap(lanes(0, 1, 1 - x))
    qs = [seq_perm(q_m, *down), None, seq_perm(q_m, *two_down), None]
    kv_m, kv_give = lanes(1, 3, x), lanes(1, 3, 1 - x)
    block = out_weight.reshape(kv_m.shape)
    low_m = seq_perm(jnp.where(z == 0, kv_m, block), (0, 1), (1, 3))
    pairs = [(i, 2 + 1 - i) for i in range(2)] + [(2 + i, i) for i in range(2)] + [(4 + i, 6 + i) for i in range(2)]
    low_o = lax.ppermute(after(jnp.where(z == 0, kv_give, block), q_o), "seq", pairs)
    kv_o = swap(after(kv_give, q_o))
    qs[1], qs[3] = seq_perm(q_o, *down), seq_perm(q_o, *two_down)

    struct = jax.ShapeDtypeStruct
    partial = struct((2 * tokens + LSE_ROWS, half), BF16)
    oa, ob, own = [], [], []
    turn = at
    kvs = [kv_m, kv_o, low_m, low_o]
    for c in range(chunks):
        a, b = head_call(
            functools.partial(upper_kernel, coef, c, chunks, parts), turn, [(a, 0) for a in qs + kvs + [out_weight]],
            [partial] * 2, heads, "upper_rows", 7)
        turn = after(at, a)
        oa.append(seq_perm(a, (1, 2), (2, 3)))
        ob.append(seq_perm(b, (1, 3), (0, 1), (3, 2)))
    def own_rows(c, turn):
        (mine,) = head_call(
            functools.partial(own_kernel, coef, c, chunks, parts), turn, [(a, 0) for a in [q_m, q_o] + kvs],
            [partial], heads, "own_rows", 6)
        return mine

    own.append(own_rows(0, turn))
    w_down = seq_perm(after(out_weight, *qs), (0, 2), (2, 0), (3, 1))

    def merged(c, earlier):
        (a,) = whole_call(
            functools.partial(merge_kernel, heads), after(at, earlier), [own[c], oa[c], ob[c]],
            [struct((2, tokens, half), BF16)], "merge", 2)
        shape = (2, 2, 2, tokens // 4, half)
        return a.reshape(shape), swap(a).reshape(shape)

    attended = [merged(0, own[0])]
    w_far = jnp.where(z == 3, low_m.reshape(out_weight.shape), after(w_down, attended[0][0]))
    own.append(own_rows(1, after(at, w_far)))
    w_other = seq_perm(w_far, (0, 1), (1, 0), (2, 3), (3, 2))
    parts_out, plan = [], []

    def summed(turn, names):
        send, kept = project(turn, attended, [(c, weights[layer]) for c, layer in names])
        return send.shape[:1] + send.shape[3:], [kept, head_perm(send, 1)]

    w_near = jnp.where(
        (z == 0) | (z == 3), low_o.reshape(out_weight.shape), jnp.concatenate([o[: 2 * tokens] for o in after(ob, own[1])]))
    attended.append(merged(1, (w_far, attended[0][1], w_near)))
    weights = {0: out_weight, 1: w_near, 2: w_far, 3: w_other}
    names = [(0, 0), (0, 1)]
    size, pair = summed(at, names)
    both = struct(size[:1] + (2,) + size[1:], BF16)
    stay, to_y = whole_call(halve_kernel, at, pair, [both] * 2, "halve", 2)
    from_y = head_perm(to_y, 2)
    mine, to_x = whole_call(row_kernel, at, [stay, from_y], [struct(size, BF16)] * 2, "rows", 1)
    parts_out += [mine, swap(to_x)]
    plan.append((names, 1))

    diagonal = [
        ((2 * i + j) * 4 + h, (2 * i + 1 - j) * 4 + (h ^ 2)) for i in range(4) for j in range(2) for h in range(4)
    ]
    turn = after(at, mine)
    for names in ([(1, 0), (1, 1), (0, 2)], [(1, 2), (1, 3), (0, 3)]):
        size, pair = summed(turn, names)
        turn = after(at, pair[0])
        stay, to_y, to_x, to_xy = whole_call(split_kernel, at, pair, [struct(size, BF16)] * 4, "split", 2)
        parts_out += [stay, head_perm(to_y, 2), swap(to_x), lax.ppermute(to_xy, ("seq", "head"), diagonal)]
        plan.append((names, 2))
    (out,) = whole_call(
        functools.partial(place_kernel, plan), at, parts_out,
        [struct((cols // 4, 8 * out_weight.shape[1]), BF16)], "place", 2)
    return out.reshape(cols // 4, 1, 8 * out_weight.shape[1])


def solution(mesh):
    in_specs = (P(None, "seq", None, "head"), P("head", "seq"))
    out_specs = P("head", "seq", None)
    small = mesh.shape["seq"] == 8 and mesh.shape["head"] == 4

    def body(qkv, out_weight):
        _, rows, cols, features = qkv.shape
        even = features == 2 * cols and out_weight.shape == (features, cols) and cols % 512 == 0
        if small and rows == 1 and even:
            return body_eight(qkv, out_weight)
        return body_any(qkv, out_weight)

    return jax.shard_map(body, mesh=mesh, in_specs=in_specs, out_specs=out_specs, check_vma=False)
```

```python
import functools
import jax
import jax.numpy as jnp
from jax import lax
from jax.experimental import pallas as pl
from jax.experimental.pallas import tpu as pltpu
from jax.sharding import PartitionSpec as P

HEAD = 128
LOG2E = 1.4426950408889634
NEG = -1e30
QB = 128
VMEM = 24 * 1024 * 1024
F32, BF16 = jnp.float32, jnp.bfloat16


def shifted(shard, axis, by):
    size = lax.axis_size(axis)
    pairs = [(i, i + by) for i in range(size) if 0 <= i + by < size]
    return lax.ppermute(shard, axis, pairs)


def column_part(part):
    queries, keys_part, values = (part[0], part[1], part[2])
    rows = queries.shape[0]
    scale = queries.shape[-1] ** (-0.5)
    scores = (
        jnp.einsum("rchd,schd->chrs", queries, keys_part, preferred_element_type=jnp.float32)
        * scale
    )
    r_idx = lax.broadcasted_iota(jnp.int32, (rows, rows), 0)
    s_idx = lax.broadcasted_iota(jnp.int32, (rows, rows), 1)
    allowed = s_idx <= r_idx - 2
    masked = jnp.where(allowed, scores, jnp.float32(-1e30))
    peak = jnp.max(masked, axis=-1)
    weights = jnp.where(allowed, jnp.exp(masked - peak[..., None]), jnp.float32(0.0))
    total = jnp.maximum(jnp.sum(weights, axis=-1), jnp.float32(1.0))
    rounded = weights.astype(jnp.bfloat16)
    mixed = jnp.einsum("chrs,schd->rchd", rounded, values, preferred_element_type=jnp.float32)
    col_out = (mixed / jnp.transpose(total, (2, 0, 1))[..., None]).astype(jnp.bfloat16)
    col_lse = jnp.transpose(peak + jnp.log(total), (2, 0, 1))
    return (col_out, col_lse)


def row_part(local, previous, first_row):
    rows_dev, cols, heads_local, head_size = (
        local.shape[1],
        local.shape[2],
        local.shape[3],
        local.shape[4],
    )
    scale = head_size ** (-0.5)
    keys_ext = jnp.concatenate([previous, local[1:3]], axis=1)
    key_idx = lax.broadcasted_iota(jnp.int32, (cols, 2 * cols), 1)
    query_idx = lax.broadcasted_iota(jnp.int32, (cols, 2 * cols), 0)

    def one_row(index):
        queries = lax.dynamic_index_in_dim(local[0], index, 0, keepdims=False)
        pair = keys_ext.reshape(2, 2 * cols, heads_local, head_size)
        scores = (
            jnp.einsum("qhd,khd->hqk", queries, pair[0], preferred_element_type=jnp.float32) * scale
        )
        allowed = (key_idx < cols) & (first_row + index > 0) | (key_idx >= cols) & (
            key_idx - cols <= query_idx
        )
        masked = jnp.where(allowed[None], scores, jnp.float32(-1e30))
        peak = jnp.max(masked, axis=-1)
        weights = jnp.where(allowed[None], jnp.exp(masked - peak[..., None]), jnp.float32(0.0))
        total = jnp.sum(weights, axis=-1)
        rounded = weights.astype(jnp.bfloat16)
        mixed = jnp.einsum("hqk,khd->qhd", rounded, pair[1], preferred_element_type=jnp.float32)
        return (mixed / jnp.transpose(total)[..., None], jnp.transpose(peak + jnp.log(total)))

    return lax.map(one_row, jnp.arange(rows_dev, dtype=jnp.int32))


def body_any(qkv, out_weight):
    rows_dev, cols, features = (qkv.shape[1], qkv.shape[2], qkv.shape[3])
    head_size = HEAD
    heads_local = features // head_size
    local = qkv.reshape(3, rows_dev, cols, heads_local, head_size)
    previous = shifted(local[1:3, rows_dev - 1 : rows_dev], "seq", 1)
    first_row = lax.axis_index("seq") * rows_dev
    row_out, row_lse = row_part(local, previous, first_row)
    columns = lax.all_to_all(local, "seq", split_axis=2, concat_axis=1, tiled=True)
    col_part_out, col_part_lse = column_part(columns)
    col_out, col_lse = (
        lax.all_to_all(col_part_out, "seq", split_axis=0, concat_axis=1, tiled=True),
        lax.all_to_all(
            col_part_lse.astype(jnp.bfloat16), "seq", split_axis=0, concat_axis=1, tiled=True
        ).astype(col_part_lse.dtype),
    )
    top = jnp.maximum(row_lse, col_lse)
    left = jnp.exp(row_lse - top)
    right = jnp.exp(col_lse - top)
    attended = (left[..., None] * row_out + right[..., None] * col_out.astype(jnp.float32)) / (
        left + right
    )[..., None]
    attended = attended.astype(jnp.bfloat16).reshape(rows_dev, cols, features)
    terms = jnp.einsum(
        "rcf,fd->crd",
        attended,
        lax.all_gather(out_weight, "seq", axis=1, tiled=True),
        preferred_element_type=jnp.float32,
    )
    summed = lax.psum_scatter(terms.astype(jnp.bfloat16), "head", scatter_dimension=0, tiled=True)
    return summed


def dense_scores(q, k):
    return lax.dot_general(q, k, (((1,), (1,)), ((), ())), preferred_element_type=F32)


def col_scores(q, k):
    prod = q * k
    high = prod.astype(BF16)
    low = (prod - high.astype(F32)).astype(BF16)
    ones = jnp.ones((2 * HEAD, HEAD), BF16)
    return jnp.dot(jnp.concatenate([high, low], axis=1), ones, preferred_element_type=F32)


def with_ones(v):
    return jnp.concatenate([v, jnp.ones_like(v)], axis=1)


def attend(q, dense, cols, coef):
    rows = q.shape[0]
    scores = []
    for k, _, allowed in dense:
        s = dense_scores(q, k)
        scores.append(s if allowed is None else jnp.where(allowed, s, NEG))
    singles = []
    if cols:
        wide = q.astype(F32) * coef
    for k, _, allowed in cols:
        c = col_scores(wide, k)
        singles.append(c if allowed is None else jnp.where(allowed, c, NEG))
    peak = None
    for s in scores:
        for j in range(s.shape[1] // HEAD):
            part = s[:, j * HEAD : (j + 1) * HEAD]
            peak = part if peak is None else jnp.maximum(peak, part)
    if peak is not None:
        peak = jnp.broadcast_to(jnp.max(peak, axis=1, keepdims=True), (rows, HEAD))
        peak = peak * coef
    for c in singles:
        peak = c if peak is None else jnp.maximum(peak, c)
    both = None
    for s, (_, v, _) in zip(scores, dense):
        tiled = jnp.concatenate([peak] * (s.shape[1] // HEAD), axis=1)
        p = jnp.exp2(s * coef - tiled).astype(BF16)
        term = jnp.dot(p, v, preferred_element_type=F32)
        both = term if both is None else both + term
    out = None if both is None else both[:, :HEAD]
    total = None if both is None else both[:, HEAD:]
    for c, (_, v, _) in zip(singles, cols):
        w = jnp.exp2(c - peak)
        total = w if total is None else total + w
        out = w * v if out is None else out + w * v
    return out / total, peak + jnp.log2(total)


def lse_rows(even, odd):
    lane = lax.broadcasted_iota(jnp.int32, (HEAD, HEAD), 1)
    evens, odds = [], []
    for t in range(even.shape[0] // HEAD):
        block = slice(t * HEAD, (t + 1) * HEAD)
        turned = jnp.transpose(jnp.where(lane == 0, even[block], odd[block]))
        evens.append(turned[0:1])
        odds.append(turned[1:2])
    return evens, odds


LSE_ROWS = 16


def put_lse(ref, base, evens, odds):
    rows = jnp.concatenate(evens + odds, axis=0)
    pieces = []
    for _ in range(3):
        pieces.append(rows.astype(BF16).astype(F32))
        rows = rows - pieces[-1]
    spare = LSE_ROWS - 3 * rows.shape[0]
    ref[pl.ds(base, LSE_ROWS), :] = jnp.concatenate(pieces + [jnp.zeros((spare, HEAD), F32)], axis=0).astype(BF16)


def chunk_rows(array, chunk, chunks, parts):
    size = array.shape[0] // parts
    share = size // chunks
    return jnp.concatenate(
        [array[p * size + chunk * share : p * size + (chunk + 1) * share] for p in range(parts)], axis=0)


def stacked(refs):
    return [ref[i] for ref in refs for i in range(ref.shape[0])]


def own_kernel(coef, chunk, chunks, parts, at, q_m, q_o, kv_m, kv_o, *refs):
    x, z = at[0], at[1]
    below = z == 1
    first = x == 0
    *low, out = refs
    cols = q_m.shape[1]
    tokens = cols // chunks

    def pair(a, b):
        return jnp.where(first, a, b), jnp.where(first, b, a)

    def mine(array):
        return chunk_rows(array, chunk, chunks, parts)

    q_e, q_o = pair(mine(q_m[0]), mine(q_o[0]))
    k_e, k_o = pair(kv_m[0], kv_o[0])
    v_e, v_o = pair(kv_m[1], kv_o[1])
    v_e, v_o = with_ones(v_e), with_ones(v_o)
    share = tokens // parts
    index = lax.broadcasted_iota(jnp.int32, (tokens, cols), 0)
    index = (index // share) * (cols // parts) + chunk * share + index % share
    tri = lax.broadcasted_iota(jnp.int32, (tokens, cols), 1) <= index

    def run(even, odd):
        o1, l1 = attend(q_e, [(k_e, v_e, tri)] + even[0], even[1], coef)
        o2, l2 = attend(q_o, [(k_o, v_o, tri), (k_e, v_e, None)], odd, coef)
        out[:tokens] = o1.astype(BF16)
        out[tokens : 2 * tokens] = o2.astype(BF16)
        put_lse(out, 2 * tokens, *lse_rows(l1, l2))

    @pl.when(below)
    def _():
        m_k, m_v, o_k, o_v = stacked(low)
        lk_e, lk_o = pair(m_k, o_k)
        lv_e, lv_o = pair(m_v, o_v)
        col_e = (mine(lk_e).astype(F32), mine(lv_e).astype(F32), None)
        col_o = (mine(lk_o).astype(F32), mine(lv_o).astype(F32), None)
        run(([(lk_o, with_ones(lv_o), None)], [col_e]), [col_e, col_o])

    @pl.when(jnp.logical_not(below))
    def _():
        run(([], []), [])


def upper_kernel(coef, chunk, chunks, parts, at, qa_m, qa_o, qb_m, qb_o, kv_m, kv_o, *refs):
    x, z = at[0], at[1]
    below = z == 1
    first = x == 0
    *low, weight, out_a, out_b = refs
    tokens = qa_m.shape[1] // chunks

    def pair(a, b):
        return jnp.where(first, a, b), jnp.where(first, b, a)

    def mine(array):
        return chunk_rows(array, chunk, chunks, parts)

    k_e, k_o = pair(kv_m[0], kv_o[0])
    v_e, v_o = pair(kv_m[1], kv_o[1])
    ce = (mine(k_e).astype(F32), mine(v_e).astype(F32), None)
    co = (mine(k_o).astype(F32), mine(v_o).astype(F32), None)
    base = chunk * 2 * tokens

    def run(q_m, q_o, out, dense, singles, lower):
        q_e, q_odd = pair(mine(q_m[0]), mine(q_o[0]))
        o1, l1 = attend(q_e, dense, singles + lower, coef)
        o2, l2 = attend(q_odd, [], [ce, co] + lower, coef)
        out[:tokens] = o1.astype(BF16)
        out[tokens : 2 * tokens] = o2.astype(BF16)
        put_lse(out, 2 * tokens, *lse_rows(l1, l2))

    def first_rows(lower):
        run(qa_m, qa_o, out_a, [(k_o, with_ones(v_o), None)], [ce], lower)

    @pl.when(below)
    def _():
        m_k, m_v, o_k, o_v = (mine(part).astype(F32) for part in stacked(low))
        lower = [(m_k, m_v, None), (o_k, o_v, None)]
        first_rows(lower)
        run(qb_m, qb_o, out_b, [], [ce, co], lower)

    @pl.when(jnp.logical_not(below))
    def _():
        out_b[: 2 * tokens] = weight[base : base + 2 * tokens]
        out_b[pl.ds(2 * tokens, LSE_ROWS), :] = jnp.zeros((LSE_ROWS, HEAD), BF16)

    @pl.when(z == 2)
    def _():
        first_rows([])

    @pl.when(z % 3 == 0)
    def _():
        out_a[...] = jnp.zeros(out_a.shape, BF16)


def merge_kernel(heads, at, own, oa, ob, out):
    z = at[1]
    tokens = out.shape[1]
    blocks = tokens // HEAD
    rows = 2 * blocks
    line = lax.broadcasted_iota(jnp.int32, (32, 3 * HEAD), 0)
    group = lax.broadcasted_iota(jnp.int32, (32, 3 * HEAD), 1) // HEAD
    picks = []
    for first in range(rows):
        at_line = first + group * rows
        picks.append(((line == at_line) | (line == at_line + 3 * rows)).astype(BF16))
    for head in range(heads):
        lanes = slice(head * HEAD, (head + 1) * HEAD)

        def totals(ref):
            packed = ref[pl.ds(2 * tokens, LSE_ROWS), lanes].astype(F32)
            return sum(packed[i * rows : (i + 1) * rows] for i in range(3))

        l0, l1, l2 = (totals(ref) for ref in (own, oa, ob))
        l1, l2 = jnp.where(z >= 2, l1, NEG), jnp.where(z >= 3, l2, NEG)
        top = jnp.maximum(l0, jnp.maximum(l1, l2))
        shares = [jnp.exp2(l - top) for l in (l0, l1, l2)]
        whole = shares[0] + shares[1] + shares[2]
        shares = jnp.concatenate([share / whole for share in shares], axis=0)
        high = shares.astype(BF16).astype(F32)
        spare = jnp.zeros((32 - 6 * rows, HEAD), F32)
        pieces = jnp.concatenate([high, shares - high, spare], axis=0).astype(BF16)
        for row in range(2):
            for block in range(blocks):
                pick = picks[row * blocks + block]
                spread = lax.dot_general(pieces, pick, (((0,), (0,)), ((), ())), preferred_element_type=F32)
                mine = slice(row * tokens + block * HEAD, row * tokens + (block + 1) * HEAD)
                mixed = spread[:, :HEAD] * own[mine, lanes].astype(F32)
                mixed = mixed + spread[:, HEAD : 2 * HEAD] * oa[mine, lanes].astype(F32)
                mixed = mixed + spread[:, 2 * HEAD :] * ob[mine, lanes].astype(F32)
                out[row, block * HEAD : (block + 1) * HEAD, lanes] = mixed.astype(BF16)


def cost(us):
    return pl.CostEstimate(flops=int(us * 1e8), bytes_accessed=1024, transcendentals=0)


def head_call(kernel, at, args, outs, heads, name, us):
    def spec(shape, start=0):
        lead = len(shape) - 1
        return pl.BlockSpec(tuple(shape[:-1]) + (HEAD,), lambda h, at: (0,) * lead + (start + h,))

    return pl.pallas_call(
        kernel,
        out_shape=outs,
        grid_spec=pltpu.PrefetchScalarGridSpec(
            num_scalar_prefetch=1,
            grid=(heads,),
            in_specs=[spec(a.shape, start) for a, start in args],
            out_specs=[spec(o.shape) for o in outs],
        ),
        compiler_params=pltpu.CompilerParams(vmem_limit_bytes=VMEM),
        cost_estimate=cost(us),
        name=name,
    )(at, *(a for a, _ in args))


def project_kernel(plan, at, *refs):
    x, core = at[0], at[2]
    *arrays, send, keep = refs
    for who, out in ((1 - core, send), (core, keep)):
        for s, (near, far, weight) in enumerate(plan):
            left, right = (
                jnp.concatenate([arrays[i][r, y, who] for y in range(2) for r in range(2)], axis=0)
                for i in (near, far)
            )
            weight = arrays[weight]
            half = left.shape[1]
            top = weight[pl.ds(pl.multiple_of(x * half, half), half)]
            bottom = weight[pl.ds(pl.multiple_of((1 - x) * half, half), half)]
            c = jnp.dot(left, top, preferred_element_type=F32) + jnp.dot(right, bottom, preferred_element_type=F32)
            out[s] = c.astype(BF16).reshape(out.shape[1:])


def project(at, attended, items):
    arrays, plan = [], []

    def place_of(array):
        for i, other in enumerate(arrays):
            if other is array:
                return i
        arrays.append(array)
        return len(arrays) - 1

    for chunk, weight in items:
        plan.append(tuple(place_of(a) for a in attended[chunk] + (weight,)))
    _, _, _, tokens, _ = attended[0][0].shape
    out = jax.ShapeDtypeStruct((len(items), 2, 2, tokens, items[0][1].shape[1]), BF16)
    return whole_call(functools.partial(project_kernel, plan), at, arrays, [out, out], "project", 1 * len(items))


def whole_call(kernel, at, args, outs, name, us):
    return pl.pallas_call(
        kernel,
        out_shape=outs,
        in_specs=[pl.BlockSpec(memory_space=pltpu.SMEM)] + [pl.BlockSpec(memory_space=pltpu.VMEM)] * len(args),
        out_specs=[pl.BlockSpec(memory_space=pltpu.VMEM)] * len(outs),
        compiler_params=pltpu.CompilerParams(vmem_limit_bytes=VMEM),
        cost_estimate=cost(us),
        name=name,
    )(at, *args)


def total(a, b):
    return (a.astype(F32) + b.astype(F32)).astype(BF16)


def split_kernel(at, kept, got, stay, to_y, to_x, to_xy):
    x, y = at[0], at[3]
    for s in range(kept.shape[0]):
        for out, yy, xx in ((to_xy, 1 - y, 1 - x), (to_y, 1 - y, x), (to_x, y, 1 - x), (stay, y, x)):
            out[s] = total(kept[s, yy, xx], got[s, yy, xx])


def halve_kernel(at, kept, got, stay, to_y):
    y = at[3]
    for s in range(kept.shape[0]):
        for r in range(2):
            to_y[s, r] = total(kept[s, 1 - y, r], got[s, 1 - y, r])
            stay[s, r] = total(kept[s, y, r], got[s, y, r])


def row_kernel(at, stay, got, mine, to_x):
    x = at[0]
    for s in range(stay.shape[0]):
        to_x[s] = total(stay[s, 1 - x], got[s, 1 - x])
        mine[s] = total(stay[s, x], got[s, x])


def place_kernel(plan, at, *refs):
    x, z, out = at[0], at[1], refs[-1]
    layers = [z, z + 1 - 2 * (z % 2), (z + 2) % 4, 3 - z]
    refs = iter(refs[:-1])
    for names, hops in plan:
        group = [next(refs) for _ in range(2 * hops)]
        _, tokens, width = group[0].shape
        for s, (chunk, layer) in enumerate(names):
            rows = pl.ds(chunk * tokens, tokens)
            base = 2 * layers[layer]
            mine = pl.ds(pl.multiple_of((base + x) * width, width), width)
            theirs = pl.ds(pl.multiple_of((base + 1 - x) * width, width), width)
            if hops == 1:
                out[rows, mine], out[rows, theirs] = group[0][s], group[1][s]
            else:
                out[rows, mine] = total(group[0][s], group[1][s])
                out[rows, theirs] = total(group[2][s], group[3][s])


def after(value, *earlier):
    return lax.optimization_barrier((value, earlier))[0]


def body_eight(qkv, out_weight):
    _, _, cols, features = qkv.shape
    half = features // 2
    chunks = 2
    heads = half // HEAD
    parts = lax.axis_size("head")
    tokens = cols // chunks
    coef = HEAD ** (-0.5) * LOG2E
    me = lax.axis_index("seq")
    who = lax.axis_index("head")
    z, x, core, y = me // 2, me % 2, who % 2, who // 2
    at = jnp.stack([x, z, core, y]).astype(jnp.int32)
    local = qkv.reshape(3, cols, features)
    first = x == 0

    def seq_perm(array, *layers, cross=False):
        pairs = [(2 * a + i, 2 * b + (1 - i if cross else i)) for a, b in layers for i in range(2)]
        return lax.ppermute(array, "seq", pairs)

    def swap(array):
        return seq_perm(array, (0, 0), (1, 1), (2, 2), (3, 3), cross=True)

    def head_perm(array, flip):
        return lax.ppermute(array, "head", [(i, i ^ flip) for i in range(4)])

    def lanes(lo, hi, part, source=local):
        return lax.dynamic_slice(source, (lo, 0, part * half), (hi - lo, cols, half))

    down, two_down = [(2, 1), (3, 2)], [(3, 1)]
    q_m = lanes(0, 1, x)
    q_o = swap(lanes(0, 1, 1 - x))
    qs = [seq_perm(q_m, *down), None, seq_perm(q_m, *two_down), None]
    kv_m, kv_give = lanes(1, 3, x), lanes(1, 3, 1 - x)
    block = out_weight.reshape(kv_m.shape)
    low_m = seq_perm(jnp.where(z == 0, kv_m, block), (0, 1), (1, 3))
    pairs = [(i, 2 + 1 - i) for i in range(2)] + [(2 + i, i) for i in range(2)] + [(4 + i, 6 + i) for i in range(2)]
    low_o = lax.ppermute(after(jnp.where(z == 0, kv_give, block), q_o), "seq", pairs)
    kv_o = swap(after(kv_give, q_o))
    qs[1], qs[3] = seq_perm(q_o, *down), seq_perm(q_o, *two_down)

    struct = jax.ShapeDtypeStruct
    partial = struct((2 * tokens + LSE_ROWS, half), BF16)
    oa, ob, own = [], [], []
    turn = at
    kvs = [kv_m, kv_o, low_m, low_o]
    for c in range(chunks):
        a, b = head_call(
            functools.partial(upper_kernel, coef, c, chunks, parts), turn, [(a, 0) for a in qs + kvs + [out_weight]],
            [partial] * 2, heads, "upper_rows", 7)
        turn = after(at, a)
        oa.append(seq_perm(a, (1, 2), (2, 3)))
        ob.append(seq_perm(b, (1, 3), (0, 1), (3, 2)))
    def own_rows(c, turn):
        (mine,) = head_call(
            functools.partial(own_kernel, coef, c, chunks, parts), turn, [(a, 0) for a in [q_m, q_o] + kvs],
            [partial], heads, "own_rows", 6)
        return mine

    own.append(own_rows(0, turn))
    w_down = seq_perm(after(out_weight, *qs), (0, 2), (2, 0), (3, 1))

    def merged(c, earlier):
        (a,) = whole_call(
            functools.partial(merge_kernel, heads), after(at, earlier), [own[c], oa[c], ob[c]],
            [struct((2, tokens, half), BF16)], "merge", 2)
        shape = (2, 2, 2, tokens // 4, half)
        return a.reshape(shape), swap(a).reshape(shape)

    attended = [merged(0, own[0])]
    w_far = jnp.where(z == 3, low_m.reshape(out_weight.shape), after(w_down, attended[0][0]))
    own.append(own_rows(1, after(at, w_far)))
    w_other = seq_perm(w_far, (0, 1), (1, 0), (2, 3), (3, 2))
    parts_out, plan = [], []

    def summed(turn, names):
        send, kept = project(turn, attended, [(c, weights[layer]) for c, layer in names])
        return send.shape[:1] + send.shape[3:], [kept, head_perm(send, 1)]

    w_near = jnp.where(
        (z == 0) | (z == 3), low_o.reshape(out_weight.shape), jnp.concatenate([o[: 2 * tokens] for o in after(ob, own[1])]))
    attended.append(merged(1, (w_far, attended[0][1], w_near)))
    weights = {0: out_weight, 1: w_near, 2: w_far, 3: w_other}
    names = [(0, 0), (0, 1)]
    size, pair = summed(at, names)
    both = struct(size[:1] + (2,) + size[1:], BF16)
    stay, to_y = whole_call(halve_kernel, at, pair, [both] * 2, "halve", 2)
    from_y = head_perm(to_y, 2)
    mine, to_x = whole_call(row_kernel, at, [stay, from_y], [struct(size, BF16)] * 2, "rows", 1)
    parts_out += [mine, swap(to_x)]
    plan.append((names, 1))

    diagonal = [
        ((2 * i + j) * 4 + h, (2 * i + 1 - j) * 4 + (h ^ 2)) for i in range(4) for j in range(2) for h in range(4)
    ]
    turn = after(at, mine)
    for names in ([(1, 0), (1, 1), (0, 2)], [(1, 2), (1, 3), (0, 3)]):
        size, pair = summed(turn, names)
        turn = after(at, pair[0])
        stay, to_y, to_x, to_xy = whole_call(split_kernel, at, pair, [struct(size, BF16)] * 4, "split", 2)
        parts_out += [stay, head_perm(to_y, 2), swap(to_x), lax.ppermute(to_xy, ("seq", "head"), diagonal)]
        plan.append((names, 2))
    (out,) = whole_call(
        functools.partial(place_kernel, plan), at, parts_out,
        [struct((cols // 4, 8 * out_weight.shape[1]), BF16)], "place", 2)
    return out.reshape(cols // 4, 1, 8 * out_weight.shape[1])


def solution(mesh):
    in_specs = (P(None, "seq", None, "head"), P("head", "seq"))
    out_specs = P("head", "seq", None)
    small = mesh.shape["seq"] == 8 and mesh.shape["head"] == 4

    def body(qkv, out_weight):
        _, rows, cols, features = qkv.shape
        even = features == 2 * cols and out_weight.shape == (features, cols) and cols % 512 == 0
        if small and rows == 1 and even:
            return body_eight(qkv, out_weight)
        return body_any(qkv, out_weight)

    return jax.shard_map(body, mesh=mesh, in_specs=in_specs, out_specs=out_specs, check_vma=False)
```
